32 devices in a mesh: dp: 8 (over y, x, core), seq: 4 (over z).
Axes of the slice: x: 2, y: 2, z: 4, core: 2. Of those that a mesh axis runs over, the one named last changes fastest.
Arguments:
- block_in: bfloat16 [8, 2048, 1536], P('dp', 'seq'), may hold values from -6 to 6
- cotangent: bfloat16 [8, 2048, 1536], P('dp', 'seq'), may hold values from -6 to 6
- segment_ids: int32 [8, 2048], P('dp'), may hold values from 0 to 4, as said below
- input_proj: float32 [1536, 1792], P('seq'), may hold values from -0.21875 to 0.21875
- output_proj: float32 [1536, 1536], P('seq'), may hold values from -0.4375 to 0.4375
- gate_up: float32 [1536, 9216], P('seq'), may hold values from -0.15625 to 0.15625
- down_weight: float32 [4608, 1536], P('seq'), may hold values from -0.1875 to 0.1875
- norm_gains: float32 [2, 1536], P(None, 'seq'), may hold values from 0.5 to 1.5
- input_moments: float32 [2, 1536, 1792], P(None, 'seq'), may hold values from -1 to 1, as said below
- output_moments: float32 [2, 1536, 1536], P(None, 'seq'), may hold values from -1 to 1, as said below
- gate_moments: float32 [2, 1536, 9216], P(None, 'seq'), may hold values from -1 to 1, as said below
- down_moments: float32 [2, 4608, 1536], P(None, 'seq'), may hold values from -1 to 1, as said below
- gain_moments: float32 [2, 2, 1536], P(None, None, 'seq'), may hold values from -1 to 1, as said below
- update_count: int32 [1], replicated, may hold values from 1 to 4
- optimizer_rates: float32 [2], replicated, may hold values from 0.01 to 0.1
Outputs:
- block_out: bfloat16 [8, 2048, 1536], P('dp', 'seq')
- block_in_grad: bfloat16 [8, 2048, 1536], P('dp', 'seq')
- input_grad: float32 [1536, 1792], P('seq')
- output_grad: float32 [1536, 1536], P('seq')
- gate_grad: float32 [1536, 9216], P('seq')
- down_grad: float32 [4608, 1536], P('seq')
- gain_grad: float32 [2, 1536], P(None, 'seq')
- input_new: float32 [1536, 1792], P('seq')
- output_new: float32 [1536, 1536], P('seq')
- gate_new: float32 [1536, 9216], P('seq')
- down_new: float32 [4608, 1536], P('seq')
- gains_step: float32 [2, 1536], P(None, 'seq')
- input_moments_new: float32 [2, 1536, 1792], P(None, 'seq')
- output_moments_new: float32 [2, 1536, 1536], P(None, 'seq')
- gate_moments_new: float32 [2, 1536, 9216], P(None, 'seq')
- down_moments_new: float32 [2, 4608, 1536], P(None, 'seq')
- gain_moments_new: float32 [2, 2, 1536], P(None, None, 'seq')
The draws below stay inside these ranges and needn't reach their ends.
Inputs may be any that keep to these rules, and one draw needn't show every extreme that they name: `segment_ids`: within a sequence the ids are 1, 2, 3, 4 in order of the documents, never falling, followed by 0 over the last 1 to 63 tokens; document 2 starts within the first 256 tokens and ends within the last 256. `input_moments`: the first slice holds first moments, the second positive second moments. `output_moments`: Likewise. `gate_moments`: Likewise. `down_moments`: Likewise. `gain_moments`: Likewise.
All inputs are finite; a program needn't handle non-finite values.
Results may differ from the reference program's by a relative error of at most 0.022.
Values may be sent and summed in bfloat16 or wider, within the bound.
A program may use at most 448 MiB of HBM per device.

```python
import math
import jax
import jax.numpy as jnp
from jax import lax

D = 1536
HEADS = 12
HEAD = 128
FF = 4608
WINDOW = 1024
PIECE = 512
QW = 1536
RIM = 2
LENGTH = 2048
SEQUENCES = 8
TOKENS = 16384


def draw_segment_ids(key, part):
    key = jax.random.fold_in(key, 3)
    key_list = jax.random.split(key, 3)
    position = jnp.arange(LENGTH)[None, :]
    opening = jax.random.randint(key_list[0], (SEQUENCES, 1), 1, max(PIECE // 2, 2))
    closing = jax.random.randint(key_list[1], (SEQUENCES, 1), max(PIECE // 4, 2), max(PIECE // 2, 3))
    padding = jax.random.randint(key_list[2], (SEQUENCES, 1), 1, max(PIECE // 8, 2))
    last_start = LENGTH - closing
    fourth_start = last_start + closing // 2
    starts = (position == 0) | (position == opening) | (position == last_start) | (position == fourth_start)
    numbers = jnp.cumsum(starts.astype(jnp.int32), axis=1)
    return jnp.where(position >= LENGTH - padding, 0, numbers).astype(jnp.int32)


def moment_pair(key, row_count, column_count):
    first_moment = 0.5 * jax.random.normal(jax.random.fold_in(key, 11), (row_count, column_count), jnp.float32) / TOKENS ** 0.5
    second = jnp.exp(jax.random.uniform(jax.random.fold_in(key, 12), (row_count, column_count), jnp.float32, -2.3, 2.3)) / TOKENS
    return jnp.stack([first_moment, second]).astype(jnp.float32)


def draw_input_moments(key, part):
    key = jax.random.fold_in(key, 21)
    return moment_pair(key, D, HEADS * HEAD + 2 * HEAD)


def draw_output_moments(key, part):
    key = jax.random.fold_in(key, 22)
    return moment_pair(key, HEADS * HEAD, D)


def draw_gate_moments(key, part):
    key = jax.random.fold_in(key, 23)
    return moment_pair(key, D, 2 * FF)


def draw_down_moments(key, part):
    key = jax.random.fold_in(key, 24)
    return moment_pair(key, FF, D)


def draw_gain_moments(key, part):
    key = jax.random.fold_in(key, 25)
    return moment_pair(key, 2, D)


def levels(key, extent, cuts, smallest, high):
    def one(dim, blocks):
        draws = jax.random.uniform(jax.random.fold_in(jax.random.fold_in(key, 6), dim), (blocks,), jnp.float32, smallest / len(cuts), high / len(cuts))
        return jnp.repeat(jnp.exp(draws), extent[dim] // blocks).reshape((-1,) + (1,) * (len(extent) - dim - 1))

    factor_of = one(*cuts[0])
    for cut in cuts[1:]:
        factor_of = factor_of * one(*cut)
    return factor_of


def normal_values(stream_key, shape, spread, limit, cuts=(), kind=jnp.bfloat16):
    factor_of = levels(stream_key, shape, cuts, -0.22, 0.18) if cuts else 1.0
    entries = jax.random.normal(stream_key, shape, jnp.float32) * spread * factor_of
    return jnp.minimum(jnp.maximum(entries, -limit), limit).astype(kind)


def setup_inputs(seed: int = 0) -> dict:
    seeds = jax.random.split(jax.random.key(seed), 16)
    return {
        "block_in": normal_values(seeds[0], (SEQUENCES, LENGTH, D), 1.0, 6.0, ((0, 8), (1, 4))),
        "cotangent": normal_values(seeds[1], (SEQUENCES, LENGTH, D), 1.0, 6.0, ((0, 8), (1, 4))),
        "segment_ids": draw_segment_ids(jax.random.fold_in(seeds[15], 71), 0),
        "input_proj": normal_values(seeds[3], (D, QW + 2 * HEAD), (D // 2) ** -0.5, 0.21875, ((0, 4),), jnp.float32),
        "output_proj": normal_values(seeds[4], (QW, D), (QW // 8) ** -0.5, 0.4375, ((0, 4),), jnp.float32),
        "gate_up": normal_values(seeds[5], (D, 2 * FF), D ** -0.5, 0.15625, ((0, 4),), jnp.float32),
        "down_weight": normal_values(seeds[6], (FF, D), (FF // 4) ** -0.5, 0.1875, ((0, 4),), jnp.float32),
        "norm_gains": jnp.clip(1.0 + 0.1 * jax.random.normal(seeds[7], (2, D), jnp.float32), 0.5, 1.5),
        "input_moments": draw_input_moments(jax.random.fold_in(seeds[15], 71), 0),
        "output_moments": draw_output_moments(jax.random.fold_in(seeds[15], 71), 0),
        "gate_moments": draw_gate_moments(jax.random.fold_in(seeds[15], 71), 0),
        "down_moments": draw_down_moments(jax.random.fold_in(seeds[15], 71), 0),
        "gain_moments": draw_gain_moments(jax.random.fold_in(seeds[15], 71), 0),
        "update_count": jax.random.randint(seeds[13], (1,), 1, 5).astype(jnp.int32),
        "optimizer_rates": jnp.clip(jnp.exp(jax.random.uniform(seeds[14], (2,), jnp.float32, math.log(0.01), math.log(0.1))), 0.01, 0.1),
    }


norm_eps = 1e-06
adam_eps = 1e-08
beta_first = 0.9
beta_second = 0.95
highest = lax.Precision.HIGHEST

@jax.custom_vjp
def low(v):
    return lax.optimization_barrier(v.astype(jnp.bfloat16)).astype(jnp.float32)

@jax.custom_vjp
def low_back(v):
    return v

def low_keep(v):
    return (low(v), None)

def low_pass(kept, grad):
    return (grad,)

def back_keep(v):
    return (v, None)

def back_low(kept, grad):
    return (low(grad),)
low.defvjp(low_keep, low_pass)
low_back.defvjp(back_keep, back_low)

def rotate(values, positions, sign_value):
    half_width = values.shape[-1] // 2
    frequency = 10000.0 ** (-2.0 * jnp.arange(half_width).astype(jnp.float32) / values.shape[-1])
    angles = positions.astype(jnp.float32)[:, None] * frequency[None, :]
    cosine = jnp.cos(angles)
    sine_part = sign_value * jnp.sin(angles)
    if values.ndim == 3:
        cosine = cosine[:, None, :]
        sine_part = sine_part[:, None, :]
    lower_half = values[..., :half_width]
    upper_half = values[..., half_width:]
    return jnp.concatenate([lower_half * cosine - upper_half * sine_part, upper_half * cosine + lower_half * sine_part], axis=-1)

def root_norm(values, gain):
    return values * lax.rsqrt(lax.optimization_barrier(jnp.mean(values * values, axis=-1, keepdims=True)) + norm_eps) * gain

def forward(tokens, params, segments):
    input_proj, output_proj, gate_up, down_weight, norm_gains = [low(weight) for weight in params]
    length = tokens.shape[0]
    positions = jnp.arange(length).astype(jnp.int32)
    normed = low(root_norm(tokens, norm_gains[0]))
    mixed_proj = low_back(jnp.dot(normed, input_proj, precision=highest))
    queries = low(rotate(mixed_proj[:, :QW].reshape(length, HEADS, HEAD), positions, 1.0))
    key_rows = low(rotate(mixed_proj[:, QW:QW + HEAD], positions, 1.0))
    values = low(mixed_proj[:, QW + HEAD:])
    key_span = RIM * PIECE
    keys_padded = jnp.concatenate([jnp.zeros((key_span, HEAD), key_rows.dtype), key_rows])
    values_padded = jnp.concatenate([jnp.zeros((key_span, HEAD), values.dtype), values])
    ids_padded = jnp.concatenate([jnp.full((key_span,), -1, jnp.int32), segments.astype(jnp.int32)])

    def attend(block_index):
        row_start = (block_index * PIECE).astype(jnp.int32)
        query_block = lax.dynamic_slice_in_dim(queries, row_start, PIECE, 0)
        key_block = lax.dynamic_slice_in_dim(keys_padded, row_start, key_span + PIECE, 0)
        value_block = lax.dynamic_slice_in_dim(values_padded, row_start, key_span + PIECE, 0)
        query_ids = lax.dynamic_slice_in_dim(segments.astype(jnp.int32), row_start, PIECE, 0)
        key_ids = lax.dynamic_slice_in_dim(ids_padded, row_start, key_span + PIECE, 0)
        distance = jnp.arange(PIECE)[:, None] + key_span - jnp.arange(key_span + PIECE)[None, :]
        allowed = (distance >= 0) & (distance < WINDOW) & (query_ids[:, None] == key_ids[None, :])
        scores = low_back(jnp.einsum('thd,kd->htk', query_block, key_block, precision=highest)) * HEAD ** (-0.5)
        scores = jnp.where(allowed[None], scores, -1e+30)
        weights = low(jax.nn.softmax(scores, axis=-1))
        return jnp.einsum('htk,kd->thd', weights, value_block, precision=highest)
    blocks = lax.map(jax.checkpoint(attend), jnp.arange(length // PIECE).astype(jnp.int32))
    attended = blocks.reshape(length, HEADS, HEAD)
    attended = jnp.where((segments != 0)[:, None, None], attended, 0.0)
    flat_heads = low_back(low(attended.reshape(length, QW)))
    middle = tokens + low_back(jnp.dot(flat_heads, output_proj, precision=highest))
    normed_two = low(root_norm(middle, norm_gains[1]))
    gated_proj = low_back(jnp.dot(normed_two, gate_up, precision=highest))
    hidden = low(jax.nn.gelu(gated_proj[:, :FF], approximate=True) * gated_proj[:, FF:])
    return middle + low_back(jnp.dot(hidden, down_weight, precision=highest))

def adamw_step(weight, moments, grad, step_value, optimizer_rates):
    fix_first = 1.0 - beta_first ** step_value
    fix_second = 1.0 - beta_second ** step_value
    first_moment = beta_first * moments[0] + (1.0 - beta_first) * grad
    second = beta_second * moments[1] + (1.0 - beta_second) * grad * grad
    update = first_moment / fix_first / (jnp.sqrt(second / fix_second) + adam_eps) + optimizer_rates[1] * weight
    return (optimizer_rates[0] * update, jnp.stack([first_moment, second]))

def adamw_update(weight, moments, grad, step_value, optimizer_rates):
    change, new_moments = adamw_step(weight, moments, grad, step_value, optimizer_rates)
    return (weight - change, new_moments)

def reference(block_in, cotangent, segment_ids, input_proj, output_proj, gate_up, down_weight, norm_gains, input_moments, output_moments, gate_moments, down_moments, gain_moments, update_count, optimizer_rates):
    params = (input_proj, output_proj, gate_up, down_weight, norm_gains)

    def one_sequence(running, sequence_items):
        tokens, grads_out, segments = sequence_items
        outputs, pull_back = jax.vjp(lambda tokens_in, weights_in: forward(tokens_in, weights_in, segments), tokens.astype(jnp.float32), params)
        token_grad, param_grads = pull_back(grads_out.astype(jnp.float32))
        running = jax.tree.map(lambda held, added: held + added, running, param_grads)
        return (running, (outputs.astype(jnp.bfloat16), token_grad.astype(jnp.bfloat16)))
    zero_grads = jax.tree.map(jnp.zeros_like, params)
    totals, (block_out, block_in_grad) = lax.scan(one_sequence, zero_grads, (block_in, cotangent, segment_ids))
    grad_list = [total_grad / TOKENS for total_grad in totals]
    step_value = update_count[0].astype(jnp.float32)
    moment_args = (input_moments, output_moments, gate_moments, down_moments, gain_moments)
    updates = [adamw_update(params[which], moment_args[which], grad_list[which], step_value, optimizer_rates) for which in range(4)]
    gains_step, gain_moments_new = adamw_step(norm_gains, gain_moments, grad_list[4], step_value, optimizer_rates)
    return (block_out, block_in_grad, grad_list[0], grad_list[1], grad_list[2], grad_list[3], grad_list[4], updates[0][0], updates[1][0], updates[2][0], updates[3][0], gains_step, updates[0][1], updates[1][1], updates[2][1], updates[3][1], gain_moments_new)
```

```python
import jax
import jax.numpy as jnp
from jax import lax
from jax.experimental import pallas as pl
from jax.experimental.pallas import tpu as pltpu
from jax.sharding import Mesh
from jax.sharding import PartitionSpec as P

HEADS = 12
HEAD = 128
FF = 4608
WINDOW = 1024


norm_eps = 1e-06
adam_eps = 1e-08
beta_first = 0.9
beta_second = 0.95
head_group = 4
BF = jnp.bfloat16
F32 = jnp.float32
MESH_ID = pl.DeviceIdType.MESH
VMEM_BYTES = 56 * 1024 * 1024
ANY = pl.BlockSpec(memory_space=pl.ANY)


def passed_along(block, axis, distance):
    devices = range(lax.axis_size(axis))
    route = [(i - distance, i) for i in devices if i - distance in devices]
    return lax.ppermute(block, axis, route)


def swapped(block, axis):
    return lax.ppermute(block, axis, [(0, 1), (1, 0)])


def rotate(values, positions, sign_value):
    half_width = values.shape[-1] // 2
    frequency = 10000.0 ** (-2.0 * jnp.arange(half_width).astype(jnp.float32) / values.shape[-1])
    angles = positions.astype(jnp.float32)[:, None] * frequency[None, :]
    cosine = jnp.cos(angles)
    sine_part = sign_value * jnp.sin(angles)
    if values.ndim == 3:
        cosine = cosine[:, None, :]
        sine_part = sine_part[:, None, :]
    lower_half = values[..., :half_width]
    upper_half = values[..., half_width:]
    return jnp.concatenate(
        [
            lower_half * cosine - upper_half * sine_part,
            upper_half * cosine + lower_half * sine_part,
        ],
        axis=-1,
    )


def root_norm(values, gain):
    return values * lax.rsqrt(jnp.mean(values * values, axis=-1, keepdims=True) + norm_eps) * gain


def gated_unit(gate_part, up_part):
    return jax.nn.gelu(gate_part, approximate=True) * up_part


def adamw_step(weight, moments, grad, step_value, optimizer_rates):
    fix_first = 1.0 - beta_first**step_value
    fix_second = 1.0 - beta_second**step_value
    first_moment = beta_first * moments[0] + (1.0 - beta_first) * grad
    second = beta_second * moments[1] + (1.0 - beta_second) * grad * grad
    update = (
        first_moment / fix_first / (jnp.sqrt(second / fix_second) + adam_eps)
        + optimizer_rates[1] * weight
    )
    return (optimizer_rates[0] * update, jnp.stack([first_moment, second]))


def gather_kernel(shared, chunks, S, refs):
    n = len(shared)
    nc = len(chunks)
    F = S - 1
    own = refs[:n]
    full = refs[n : 2 * n]
    loc, zs, zr, xs, xr, ys, yr, cs, cr = refs[2 * n :]
    y, x, c, z = (lax.axis_index(a) for a in ("y", "x", "c", "z"))
    k = y * 2 + x
    kx = y * 2 + 1 - x
    ky = (1 - y) * 2 + x
    kxy = 3 - k
    to_x = {"x": 1 - x}
    to_y = {"y": 1 - y}
    to_c = {"c": 1 - c}
    low = z
    high = S - 1 - z
    near_count = jnp.minimum(low, high)
    above = jnp.minimum(z + 1, S - 1)
    below = jnp.maximum(z - 1, 0)
    blocks = []
    for j in range(F):
        near = j < 2 * near_count
        dist = jnp.where(near, j // 2 + 1, j - near_count + 1)
        sign = jnp.where(near, (j % 2) * 2 - 1, jnp.where(high > low, 1, -1))
        blocks.append((z + sign * dist, sign))
    barrier = pltpu.get_barrier_semaphore()
    for target in (to_x, to_y, to_c):
        pl.semaphore_signal(barrier, inc=1, device_id=target, device_id_type=MESH_ID)

    @pl.when(z + 1 < S)
    def _():
        pl.semaphore_signal(barrier, inc=1, device_id={"z": above}, device_id_type=MESH_ID)

    @pl.when(z > 0)
    def _():
        pl.semaphore_signal(barrier, inc=1, device_id={"z": below}, device_id_type=MESH_ID)

    pl.semaphore_wait(barrier, 3 + jnp.minimum(low, 1) + jnp.minimum(high, 1))

    def own_half(i):
        return own[i].at[c] if shared[i] else own[i]

    def full_half(i):
        return full[i].at[c] if shared[i] else full[i]

    def part(ref, q, zz, kk, h=None):
        _, r0, rn = chunks[q]
        if h is None:
            return ref.at[zz, kk, :, pl.ds(r0, rn)]
        return ref.at[zz, kk, h, pl.ds(r0, rn)]

    def remote(src, dst, s, r, target):
        return pltpu.make_async_remote_copy(
            src_ref=src,
            dst_ref=dst,
            send_sem=s,
            recv_sem=r,
            device_id=target,
            device_id_type=MESH_ID,
        )

    tail = []
    local = []
    for i in range(n):
        if shared[i]:
            for half in range(2):
                local.append(
                    pltpu.make_async_copy(
                        own[i].at[half], full[i].at[half, z], loc.at[len(local)]
                    )
                )
        else:
            local.append(pltpu.make_async_copy(own[i], full[i].at[z], loc.at[len(local)]))

    def z_first(q):
        i, r0, rn = chunks[q]
        src = own_half(i).at[k, :, pl.ds(r0, rn)]
        dst = part(full_half(i), q, z, k)
        for ok, target, slot in ((z + 1 < S, above, F), (z > 0, below, F + 1)):

            def make(target=target, slot=slot):
                return remote(src, dst, zs.at[q, slot], zr.at[q, z], {"z": target})

            @pl.when(ok)
            def _(make=make):
                make().start()

            def finish(ok=ok, make=make):
                @pl.when(ok)
                def _():
                    make().wait_send()

            tail.append(finish)

    def z_next(q, j):
        zz, sign = blocks[j]
        held = full_half(chunks[q][0])
        piece = part(held, q, zz, k)
        remote(piece, piece, zs.at[q, j], zr.at[q, zz], {"z": above}).wait_recv()
        onward = z - sign
        ok = (onward >= 0) & (onward < S)
        target = jnp.clip(onward, 0, S - 1)

        def make():
            return remote(piece, piece, zs.at[q, j], zr.at[q, zz], {"z": target})

        @pl.when(ok)
        def _():
            make().start()

        def finish():
            @pl.when(ok)
            def _():
                make().wait_send()

        tail.append(finish)
        for h, s, r, target in ((0, xs, xr, to_x), (1, ys, yr, to_y)):
            p = part(held, q, zz, k, h)
            copy = remote(p, p, s.at[q, j, 0], r.at[q, j, 0], target)
            copy.start()
            tail.append(copy.wait_send)
        for h, s, r, target in ((0, ys, yr, to_y), (1, xs, xr, to_x)):
            p = part(held, q, zz, k, h)
            copy = remote(p, p, s.at[q, j, 1], r.at[q, j, 1], target)
            copy.start()
            tail.append(copy.wait_send)

    def xy_next(q, j):
        zz, _ = blocks[j]
        held = full_half(chunks[q][0])
        p = part(held, q, zz, kx, 0)
        remote(p, p, xs.at[q, j, 0], xr.at[q, j, 0], to_x).wait_recv()
        copy = remote(p, p, ys.at[q, j, 2], yr.at[q, j, 2], to_y)
        copy.start()
        tail.append(copy.wait_send)
        p = part(held, q, zz, ky, 1)
        remote(p, p, ys.at[q, j, 0], yr.at[q, j, 0], to_y).wait_recv()
        copy = remote(p, p, xs.at[q, j, 2], xr.at[q, j, 2], to_x)
        copy.start()
        tail.append(copy.wait_send)

    def last(q, j):
        i, r0, rn = chunks[q]
        zz, _ = blocks[j]
        held = full_half(i)
        for kk, h, s, r, slot, target in (
            (kx, 1, xs, xr, 1, to_x),
            (ky, 0, ys, yr, 1, to_y),
            (kxy, 1, xs, xr, 2, to_x),
            (kxy, 0, ys, yr, 2, to_y),
        ):
            p = part(held, q, zz, kk, h)
            remote(p, p, s.at[q, j, slot], r.at[q, j, slot], target).wait_recv()
        if shared[i]:
            p = held.at[zz, :, :, pl.ds(r0, rn)]
            copy = remote(p, p, cs.at[q, j], cr.at[q, j], to_c)
            copy.start()
            tail.append(copy.wait_send)
            other = full[i].at[1 - c].at[zz, :, :, pl.ds(r0, rn)]

            def finish():
                remote(other, other, cs.at[q, j], cr.at[q, j], to_c).wait_recv()

            tail.append(finish)

    z_first(0)
    for copy in local:
        copy.start()
    for t in range(1, nc + F + 3):
        if t < nc:
            z_first(t)
        for j in range(F):
            if 0 <= t - 1 - j < nc:
                z_next(t - 1 - j, j)
        for j in range(F):
            if 0 <= t - 2 - j < nc:
                xy_next(t - 2 - j, j)
        for j in range(F):
            if 0 <= t - 3 - j < nc:
                last(t - 3 - j, j)
    for copy in local:
        copy.wait()
    for wait in tail:
        wait()


def gathered(own, shared, chunks, S, cid):
    n = len(own)
    nc = len(chunks)
    F = S - 1
    outs = []
    for o, s in zip(own, shared):
        outs.append(jax.ShapeDtypeStruct((2, S) + o.shape[1:] if s else (S,) + o.shape, o.dtype))
    dma = pltpu.SemaphoreType.DMA

    def body(*refs):
        gather_kernel(shared, chunks, S, refs)

    return pl.pallas_call(
        body,
        out_shape=tuple(outs),
        in_specs=[pl.BlockSpec(memory_space=pltpu.VMEM)] * n,
        out_specs=tuple([ANY] * n),
        scratch_shapes=[
            dma((2 * n,)),
            dma((nc, F + 2)),
            dma((nc, S)),
            dma((nc, F, 3)),
            dma((nc, F, 3)),
            dma((nc, F, 3)),
            dma((nc, F, 3)),
            dma((nc, F)),
            dma((nc, F)),
        ],
        compiler_params=pltpu.CompilerParams(
            collective_id=cid, has_side_effects=True, vmem_limit_bytes=VMEM_BYTES
        ),
    )(*own)


def adam_kernel(total, parts, scal_ref, rates_ref, *refs):
    grads = refs[:parts]
    w_ref, m_ref, g_out, w_out, m_out = refs[parts:]
    step_value = scal_ref[0].astype(F32)
    log_first = jnp.log(jnp.full((8, 128), beta_first, F32))
    log_second = jnp.log(jnp.full((8, 128), beta_second, F32))
    fix_first = (1.0 - jnp.exp(step_value * log_first))[:1, :1]
    fix_second = (1.0 - jnp.exp(step_value * log_second))[:1, :1]

    def update(g_ref):
        grad = g_ref[0, 0].astype(F32) / total
        w = w_ref[...]
        first = beta_first * m_ref[0] + (1.0 - beta_first) * grad
        second = beta_second * m_ref[1] + (1.0 - beta_second) * grad * grad
        step = first / fix_first / (jnp.sqrt(second / fix_second) + adam_eps) + rates_ref[1] * w
        g_out[...] = grad
        w_out[...] = w - rates_ref[0] * step
        m_out[0] = first
        m_out[1] = second

    if parts == 1:
        update(grads[0])
    else:
        for j in range(parts):

            @pl.when(pl.program_id(0) == j)
            def _(j=j):
                update(grads[j])


def adam_call(weight, moments, grads, count, rates, total, tile_rows, tile_cols, sides):
    parts = len(grads)
    K, _, rows, _ = grads[0].shape
    tiles = rows // tile_rows

    def g_spec(j):
        def index(jj, kk, cc, ss, tt, *_):
            on = jj == j
            return (
                jnp.where(on, kk, 0),
                jnp.where(on, cc, 0),
                jnp.where(on, tt, 0),
                jnp.where(on, ss, 0),
            )

        return pl.BlockSpec((1, 1, tile_rows, tile_cols), index)

    def place(jj, kk, cc, ss, tt, *_):
        return (kk * tiles + tt, (ss * 2 + cc) * parts + jj)

    def place3(jj, kk, cc, ss, tt, *_):
        return (0,) + place(jj, kk, cc, ss, tt)

    w_spec = pl.BlockSpec((tile_rows, tile_cols), place)
    m_spec = pl.BlockSpec((2, tile_rows, tile_cols), place3)
    smem = pl.BlockSpec(memory_space=pltpu.SMEM)

    def body(*refs):
        adam_kernel(total, parts, *refs)

    return pl.pallas_call(
        body,
        grid=(parts, K, 2, sides, tiles),
        in_specs=[smem, smem] + [g_spec(j) for j in range(parts)] + [w_spec, m_spec],
        out_specs=[w_spec, w_spec, m_spec],
        out_shape=[
            jax.ShapeDtypeStruct(weight.shape, F32),
            jax.ShapeDtypeStruct(weight.shape, F32),
            jax.ShapeDtypeStruct(moments.shape, F32),
        ],
        compiler_params=pltpu.CompilerParams(
            dimension_semantics=("arbitrary",) * 5, vmem_limit_bytes=VMEM_BYTES
        ),
        cost_estimate=pl.CostEstimate(
            flops=20 * weight.size, bytes_accessed=30 * weight.size, transcendentals=weight.size
        ),
    )(count, rates, *grads, weight, moments)


def dot(a, b):
    return jnp.dot(a, b, preferred_element_type=F32)


def dot_rows(a, b):
    return lax.dot_general(a, b, (((1,), (0,)), ((), ())), preferred_element_type=F32)


def dot_t(a, b):
    return lax.dot_general(a, b, (((1,), (1,)), ((), ())), preferred_element_type=F32)


def plane_sum(left, right, zb):
    y = lax.axis_index("y")
    x = lax.axis_index("x")
    T, M = left.shape
    N = right.shape[1]
    r = M // (zb * 8)
    rows = left.T.reshape(zb, 2, 2, 2, r, T).transpose(3, 1, 2, 0, 4, 5)

    def pick(h, yy, xx):
        block = lax.dynamic_index_in_dim(rows[h], yy, 0, keepdims=False)
        return lax.dynamic_index_in_dim(block, xx, 0, keepdims=False).reshape(zb * r, T)

    sent0 = jnp.concatenate([pick(0, 0, 1 - x), pick(0, 1, 1 - x)], axis=0)
    sent1 = jnp.concatenate([pick(1, 1 - y, 0), pick(1, 1 - y, 1)], axis=0)
    got0 = swapped(dot_rows(sent0, right).astype(BF), "x").reshape(2, zb * r, N)
    got1 = swapped(dot_rows(sent1, right).astype(BF), "y").reshape(2, zb * r, N)

    def at(got, i):
        return lax.dynamic_index_in_dim(got, i, 0, keepdims=False).astype(F32)

    next0 = swapped((dot_rows(pick(0, 1 - y, x), right) + at(got0, 1 - y)).astype(BF), "y")
    next1 = swapped((dot_rows(pick(1, y, 1 - x), right) + at(got1, 1 - x)).astype(BF), "x")
    last0 = dot_rows(pick(0, y, x), right) + at(got0, y) + next0.astype(F32)
    last1 = dot_rows(pick(1, y, x), right) + at(got1, x) + next1.astype(F32)
    both = [v.astype(BF).reshape(zb, 1, r, N) for v in (last0, last1)]
    return jnp.concatenate(both, axis=1)


def handed_out(share):
    S, _, r, N = share.shape
    mine = lax.psum_scatter(share.reshape(S, 2 * r, N), "z", scatter_dimension=0, tiled=False)
    return lax.all_gather(mine, ("y", "x", "c"), axis=0).reshape(4, 2, 2 * r, N)


def on_device(
    Y,
    S,
    block_in,
    cotangent,
    segment_ids,
    input_proj,
    output_proj,
    gate_up,
    down_weight,
    norm_gains,
    input_moments,
    output_moments,
    gate_moments,
    down_moments,
    gain_moments,
    update_count,
    optimizer_rates,
):
    seq_place = lax.axis_index("z")
    core = lax.axis_index("c")
    D = block_in.shape[-1]
    half_ff = FF // 2
    quarter_ff = FF // 4
    rows_d = input_proj.shape[0]
    rows_f = down_weight.shape[0]
    fast = Y == 2 and rows_d % 128 == 0
    in_half = input_proj.shape[1] // 2
    d_half = D // 2

    in_low = input_proj.astype(BF)
    out_low = output_proj.astype(BF)
    down_low = down_weight.astype(BF)

    def halves(w):
        n = w.shape[1] // 2
        return jnp.stack([w[:, :n], w[:, n:]])

    def gate_part(j):
        cols = []
        for side in range(2):
            first = side * FF + core * half_ff + j * quarter_ff
            cols.append(lax.dynamic_slice_in_dim(gate_up, first, quarter_ff, 1))
        return jnp.concatenate(cols, axis=1).astype(BF)

    if fast:
        r = rows_d // 8
        rf = rows_f // 8
        own_in = halves(in_low).reshape(2, 4, 2, r, in_half)
        own_out = halves(out_low).reshape(2, 4, 2, r, d_half)
        own_down = halves(down_low).reshape(2, 4, 2, rf, d_half)
        in_full, out_full = gathered(
            [own_in, own_out], [True, True], [(0, 0, r), (1, 0, r)], S, 0
        )
        in_full = in_full.reshape(2, D, in_half)
        out_full = out_full.reshape(2, D, d_half)
    else:
        in_full = halves(lax.all_gather(in_low, "z", axis=0, tiled=True))
        out_full = halves(lax.all_gather(out_low, "z", axis=0, tiled=True))
        down_full = halves(lax.all_gather(down_low, "z", axis=0, tiled=True))
        gate_full = [lax.all_gather(gate_part(j), "z", axis=0, tiled=True) for j in range(2)]
    gains_full = lax.all_gather(norm_gains.astype(BF), "z", axis=1, tiled=True)

    gains_wide = gains_full.astype(F32)
    tokens = block_in[0].astype(F32)
    piece_len = tokens.shape[0]
    width_q = HEADS * HEAD
    positions = seq_place * piece_len + jnp.arange(piece_len, dtype=jnp.int32)
    normed = root_norm(tokens, gains_wide[0]).astype(BF)
    mixed_proj = jnp.concatenate([dot(normed, in_full[0]), dot(normed, in_full[1])], axis=1)
    queries = rotate(
        mixed_proj[:, :width_q].reshape(piece_len, HEADS, HEAD), positions, 1.0
    ).astype(BF)
    own_keys = rotate(mixed_proj[:, width_q : width_q + HEAD], positions, 1.0)
    own_pair = jnp.concatenate([own_keys, mixed_proj[:, width_q + HEAD :]], axis=1).astype(BF)
    reach_count = (WINDOW + piece_len - 2) // piece_len
    earlier = []
    for back_step in range(reach_count, 0, -1):
        earlier.append(passed_along(own_pair, "z", back_step))
    key_pairs = jnp.concatenate(earlier + [own_pair], axis=0)
    key_rows = key_pairs[:, :HEAD]
    values = key_pairs[:, HEAD:]
    segments = segment_ids[0]
    key_span = reach_count * piece_len
    padded_ids = jnp.concatenate([jnp.full((key_span,), -1, jnp.int32), segments])
    query_ids = lax.dynamic_slice_in_dim(segments, seq_place * piece_len, piece_len)
    key_ids = lax.dynamic_slice_in_dim(padded_ids, seq_place * piece_len, key_span + piece_len)
    distance = jnp.arange(piece_len)[:, None] + key_span - jnp.arange(key_span + piece_len)[None, :]
    allowed = (distance >= 0) & (distance < WINDOW) & (query_ids[:, None] == key_ids[None, :])
    live_rows = query_ids != 0
    score_scale = HEAD ** (-0.5)

    def masked_scores(query_part):
        scores = (
            jnp.einsum("thd,kd->htk", query_part, key_rows, preferred_element_type=F32)
            * score_scale
        )
        return jnp.where(allowed[None], scores, -1e30)

    group_outputs = []
    group_totals = []
    for first_head in range(0, HEADS, head_group):
        scores = masked_scores(queries[:, first_head : first_head + head_group])
        log_totals = jax.nn.logsumexp(scores, axis=-1)
        weights = jnp.exp(scores - log_totals[..., None]).astype(BF)
        group_outputs.append(
            jnp.einsum("htk,kd->thd", weights, values, preferred_element_type=F32)
        )
        group_totals.append(log_totals)
    attended = jnp.concatenate(group_outputs, axis=1)
    attended = jnp.where(live_rows[:, None, None], attended, 0.0)
    flat_heads = attended.reshape(piece_len, width_q).astype(BF)
    middle = tokens + jnp.concatenate(
        [dot(flat_heads, out_full[0]), dot(flat_heads, out_full[1])], axis=1
    )
    normed_two = root_norm(middle, gains_wide[1]).astype(BF)

    if fast:
        gate_own = [gate_part(j).reshape(4, 2, r, 2 * quarter_ff) for j in range(2)]
        down_full, gate_a, gate_b = gathered(
            [own_down] + gate_own,
            [True, False, False],
            [(0, i * 48, 48) for i in range(rf // 48)]
            + [(1 + j, i * 16, 16) for j in range(2) for i in range(r // 16)],
            S,
            1,
        )
        down_full = down_full.reshape(2, FF, d_half)
        gate_full = [g.reshape(D, 2 * quarter_ff) for g in (gate_a, gate_b)]
    down_mine = lax.dynamic_slice_in_dim(down_full, core * half_ff, half_ff, 1)

    upstream = cotangent[0].astype(F32)

    def pair(v):
        return jnp.concatenate([v, swapped(v, "c")], axis=0)

    low_both = pair(cotangent[0])
    normed_both = pair(normed)
    two_both = pair(normed_two)
    flat_both = pair(flat_heads)

    hidden = []
    grad_gated = []
    grad_two = 0.0
    out_sum = 0.0
    for j in range(2):
        gated = dot(two_both, gate_full[j])
        down_j = lax.slice_in_dim(down_mine, j * quarter_ff, (j + 1) * quarter_ff, axis=1)
        grad_hidden = dot_t(low_both[:, :d_half], down_j[0]) + dot_t(
            low_both[:, d_half:], down_j[1]
        )
        gate, up = gated[:, :quarter_ff], gated[:, quarter_ff:]
        unit, unit_pull = jax.vjp(gated_unit, gate, up)
        grad_gate, grad_up = unit_pull(grad_hidden)
        hidden.append(unit.astype(BF))
        grad_gated.append(jnp.concatenate([grad_gate, grad_up], axis=1).astype(BF))
        grad_two = grad_two + dot_t(grad_gated[j], gate_full[j])
        out_sum = out_sum + jnp.concatenate([dot(hidden[j], down_j[i]) for i in range(2)], axis=1)

    def core_sum(v):
        return v[:piece_len] + swapped(v[piece_len:].astype(BF), "c").astype(F32)

    hidden = jnp.concatenate(hidden, axis=1)

    def summed(left, right, zb):
        if fast:
            return handed_out(plane_sum(left, right, zb))
        whole = dot_rows(left.T, right).astype(BF)
        whole = whole.reshape(S, left.shape[1] // S, right.shape[1])
        mine = lax.psum_scatter(whole, "z", scatter_dimension=0, tiled=False)
        mine = lax.psum(mine, ("y", "x"))
        return lax.all_gather(mine, "c", axis=0)[None]

    def summed_down():
        if fast:
            share = plane_sum(hidden, low_both, S // 2)
            keep = lax.dynamic_slice_in_dim(share, core * d_half, d_half, 3)
            give = lax.dynamic_slice_in_dim(share, (1 - core) * d_half, d_half, 3)
            got = swapped(give, "c")
            first = jnp.where(core == 0, keep, got)
            second = jnp.where(core == 0, got, keep)
            return handed_out(jnp.concatenate([first, second], axis=0))
        whole = dot_rows(hidden.T, low_both).astype(BF)
        mine = lax.psum(whole, ("y", "x"))
        mine = lax.all_gather(mine, "c", axis=0, tiled=True)
        mine = lax.dynamic_slice_in_dim(mine, core * d_half, d_half, 1)
        mine = lax.psum_scatter(mine, "z", scatter_dimension=0, tiled=True)
        return lax.all_gather(mine, "c", axis=0)[None]

    gate_sums = [summed(two_both, grad_gated[j], S) for j in range(2)]
    down_sum = summed_down()

    output = middle + core_sum(out_sum)
    block_out = output.astype(BF)[None]
    grad_normed_two = core_sum(grad_two)
    _, norm_pull_two = jax.vjp(root_norm, middle, gains_wide[1])
    grad_middle_norm, grad_gain_two = norm_pull_two(grad_normed_two)
    grad_middle = upstream + grad_middle_norm
    grad_branch = grad_middle.astype(BF)

    def half_pair(v):
        n = v.shape[1] // 2
        keep = lax.dynamic_slice_in_dim(v, core * n, n, 1)
        give = lax.dynamic_slice_in_dim(v, (1 - core) * n, n, 1)
        return jnp.concatenate([keep, swapped(give, "c")], axis=0)

    out_total = summed(flat_both, half_pair(grad_branch), S)
    grad_flat = dot_t(grad_branch[:, :d_half], out_full[0]) + dot_t(
        grad_branch[:, d_half:], out_full[1]
    )
    grad_attended = (
        jnp.where(live_rows[:, None], grad_flat, 0.0).astype(BF).reshape(piece_len, HEADS, HEAD)
    )
    grad_queries = []
    grad_key_sum = jnp.zeros((key_span + piece_len, HEAD), F32)
    grad_value_sum = jnp.zeros((key_span + piece_len, HEAD), F32)
    for group_index, first_head in enumerate(range(0, HEADS, head_group)):
        query_part = queries[:, first_head : first_head + head_group]
        scores = masked_scores(query_part)
        probabilities = jnp.exp(scores - group_totals[group_index][..., None])
        weights = probabilities.astype(BF)
        grad_part = grad_attended[:, first_head : first_head + head_group]
        grad_probs = jnp.einsum("thd,kd->htk", grad_part, values, preferred_element_type=F32)
        grad_scores = probabilities * (
            grad_probs - jnp.sum(probabilities * grad_probs, axis=-1, keepdims=True)
        )
        grad_raw = (grad_scores * score_scale).astype(BF)
        grad_queries.append(
            jnp.einsum("htk,kd->thd", grad_raw, key_rows, preferred_element_type=F32)
        )
        grad_key_sum = grad_key_sum + jnp.einsum(
            "htk,thd->kd", grad_raw, query_part, preferred_element_type=F32
        )
        grad_value_sum = grad_value_sum + jnp.einsum(
            "htk,thd->kd", weights, grad_part, preferred_element_type=F32
        )
    grad_pairs = jnp.concatenate([grad_key_sum, grad_value_sum], axis=1)
    own_grad = grad_pairs[key_span:]
    for back_step in range(1, reach_count + 1):
        sent_rows = grad_pairs[
            key_span - back_step * piece_len : key_span - (back_step - 1) * piece_len
        ]
        own_grad = own_grad + passed_along(sent_rows, "z", -back_step)
    grad_query_all = jnp.concatenate(grad_queries, axis=1)
    grad_query_raw = rotate(grad_query_all, positions, -1.0).reshape(piece_len, width_q)
    grad_key_raw = rotate(own_grad[:, :HEAD], positions, -1.0)
    grad_mixed = jnp.concatenate([grad_query_raw, grad_key_raw, own_grad[:, HEAD:]], axis=1).astype(
        BF
    )
    in_total = summed(normed_both, half_pair(grad_mixed), S)
    grad_normed = dot_t(grad_mixed[:, :in_half], in_full[0]) + dot_t(
        grad_mixed[:, in_half:], in_full[1]
    )
    _, norm_pull_one = jax.vjp(root_norm, tokens, gains_wide[0])
    grad_tokens_norm, grad_gain_one = norm_pull_one(grad_normed)
    block_in_grad = (grad_middle + grad_tokens_norm).astype(BF)[None]
    gains_sum = lax.psum(jnp.stack([grad_gain_one, grad_gain_two]), ("y", "x", "c", "z"))
    gains_mine = lax.dynamic_slice_in_dim(gains_sum, seq_place * rows_d, rows_d, 1)

    token_total = piece_len * S * Y * 4 * block_in.shape[0]
    step_value = update_count[0].astype(F32)
    count = update_count
    rates = optimizer_rates

    def adam(weight, moments, grads, sides):
        rows, cols = grads[0].shape[2:]
        return adam_call(
            weight, moments, grads, count, rates, float(token_total), rows, cols // sides, sides
        )

    in_grad, in_new, in_mom = adam(input_proj, input_moments, [in_total], 1)
    out_grad, out_new, out_mom = adam(output_proj, output_moments, [out_total], 1)
    gate_grad, gate_new, gate_mom = adam(gate_up, gate_moments, gate_sums, 2)
    down_grad, down_new, down_mom = adam(down_weight, down_moments, [down_sum], 1)
    gain_grad = gains_mine / token_total
    gains_step, gain_moments_new = adamw_step(norm_gains, gain_moments, gain_grad, step_value, rates)
    return (
        block_out,
        block_in_grad,
        in_grad,
        out_grad,
        gate_grad,
        down_grad,
        gain_grad,
        in_new,
        out_new,
        gate_new,
        down_new,
        gains_step,
        in_mom,
        out_mom,
        gate_mom,
        down_mom,
        gain_moments_new,
    )


def solution(mesh):
    dp, S = mesh.shape["dp"], mesh.shape["seq"]
    Y = dp // 4
    grid = Mesh(mesh.devices.reshape(Y, 2, 2, S), ("y", "x", "c", "z"))
    data = ("y", "x", "c")
    tokens = P(data, "z", None)
    rows = P("z", None)
    moments = P(None, "z", None)
    in_specs = (
        (tokens, tokens, P(data, None))
        + (rows,) * 4
        + (P(None, "z"),)
        + (moments,) * 4
        + (P(None, None, "z"), P(), P())
    )
    out_specs = (
        (tokens, tokens)
        + (rows,) * 4
        + (P(None, "z"),)
        + (rows,) * 4
        + (P(None, "z"),)
        + (moments,) * 4
        + (P(None, None, "z"),)
    )

    def device_step(*arrays):
        return on_device(Y, S, *arrays)

    return jax.shard_map(
        device_step, mesh=grid, in_specs=in_specs, out_specs=out_specs, check_vma=False
    )
```

```python
import jax
import jax.numpy as jnp
from jax import lax
from jax.experimental import pallas as pl
from jax.experimental.pallas import tpu as pltpu
from jax.sharding import Mesh
from jax.sharding import PartitionSpec as P

HEADS = 12
HEAD = 128
FF = 4608
WINDOW = 1024


norm_eps = 1e-06
adam_eps = 1e-08
beta_first = 0.9
beta_second = 0.95
BF = jnp.bfloat16
F32 = jnp.float32
MESH_ID = pl.DeviceIdType.MESH
VMEM_BYTES = 56 * 1024 * 1024
ANY = pl.BlockSpec(memory_space=pl.ANY)
VM = pl.BlockSpec(memory_space=pltpu.VMEM)
LOG2E = 1.4426950408889634


def passed_along(block, axis, distance):
    devices = range(lax.axis_size(axis))
    route = [(i - distance, i) for i in devices if i - distance in devices]
    return lax.ppermute(block, axis, route)


def swapped(block, axis):
    return lax.ppermute(block, axis, [(0, 1), (1, 0)])


def rotate(values, positions, sign_value):
    half_width = values.shape[-1] // 2
    frequency = 10000.0 ** (-2.0 * jnp.arange(half_width).astype(jnp.float32) / values.shape[-1])
    angles = positions.astype(jnp.float32)[:, None] * frequency[None, :]
    cosine = jnp.cos(angles)
    sine_part = sign_value * jnp.sin(angles)
    if values.ndim == 3:
        cosine = cosine[:, None, :]
        sine_part = sine_part[:, None, :]
    lower_half = values[..., :half_width]
    upper_half = values[..., half_width:]
    return jnp.concatenate(
        [
            lower_half * cosine - upper_half * sine_part,
            upper_half * cosine + lower_half * sine_part,
        ],
        axis=-1,
    )


def root_norm(values, gain):
    return values * lax.rsqrt(jnp.mean(values * values, axis=-1, keepdims=True) + norm_eps) * gain


def adamw_step(weight, moments, grad, step_value, optimizer_rates):
    fix_first = 1.0 - beta_first**step_value
    fix_second = 1.0 - beta_second**step_value
    first_moment = beta_first * moments[0] + (1.0 - beta_first) * grad
    second = beta_second * moments[1] + (1.0 - beta_second) * grad * grad
    update = (
        first_moment / fix_first / (jnp.sqrt(second / fix_second) + adam_eps)
        + optimizer_rates[1] * weight
    )
    return (optimizer_rates[0] * update, jnp.stack([first_moment, second]))


def gather_kernel(shared, chunks, S, refs):
    n = len(shared)
    nc = len(chunks)
    F = S - 1
    own = refs[:n]
    full = refs[n : 2 * n]
    loc, zs, zr, xs, xr, ys, yr, cs, cr = refs[2 * n :]
    y, x, c, z = (lax.axis_index(a) for a in ("y", "x", "c", "z"))
    k = y * 2 + x
    kx = y * 2 + 1 - x
    ky = (1 - y) * 2 + x
    kxy = 3 - k
    to_x = {"x": 1 - x}
    to_y = {"y": 1 - y}
    to_c = {"c": 1 - c}
    low = z
    high = S - 1 - z
    near_count = jnp.minimum(low, high)
    above = jnp.minimum(z + 1, S - 1)
    below = jnp.maximum(z - 1, 0)
    blocks = []
    for j in range(F):
        near = j < 2 * near_count
        dist = jnp.where(near, j // 2 + 1, j - near_count + 1)
        sign = jnp.where(near, (j % 2) * 2 - 1, jnp.where(high > low, 1, -1))
        blocks.append((z + sign * dist, sign))
    barrier = pltpu.get_barrier_semaphore()
    for target in (to_x, to_y, to_c):
        pl.semaphore_signal(barrier, inc=1, device_id=target, device_id_type=MESH_ID)

    @pl.when(z + 1 < S)
    def _():
        pl.semaphore_signal(barrier, inc=1, device_id={"z": above}, device_id_type=MESH_ID)

    @pl.when(z > 0)
    def _():
        pl.semaphore_signal(barrier, inc=1, device_id={"z": below}, device_id_type=MESH_ID)

    pl.semaphore_wait(barrier, 3 + jnp.minimum(low, 1) + jnp.minimum(high, 1))

    def own_half(i):
        return own[i].at[c] if shared[i] else own[i]

    def full_half(i):
        return full[i].at[c] if shared[i] else full[i]

    def part(ref, q, zz, kk, h=None):
        _, r0, rn = chunks[q]
        if h is None:
            return ref.at[zz, kk, :, pl.ds(r0, rn)]
        return ref.at[zz, kk, h, pl.ds(r0, rn)]

    def remote(src, dst, s, r, target):
        return pltpu.make_async_remote_copy(
            src_ref=src,
            dst_ref=dst,
            send_sem=s,
            recv_sem=r,
            device_id=target,
            device_id_type=MESH_ID,
        )

    tail = []
    local = []
    for i in range(n):
        if shared[i]:
            for half in range(2):
                local.append(
                    pltpu.make_async_copy(
                        own[i].at[half], full[i].at[half, z], loc.at[len(local)]
                    )
                )
        else:
            local.append(pltpu.make_async_copy(own[i], full[i].at[z], loc.at[len(local)]))

    def z_first(q):
        i, r0, rn = chunks[q]
        src = own_half(i).at[k, :, pl.ds(r0, rn)]
        dst = part(full_half(i), q, z, k)
        for ok, target, slot in ((z + 1 < S, above, F), (z > 0, below, F + 1)):

            def make(target=target, slot=slot):
                return remote(src, dst, zs.at[q, slot], zr.at[q, z], {"z": target})

            @pl.when(ok)
            def _(make=make):
                make().start()

            def finish(ok=ok, make=make):
                @pl.when(ok)
                def _():
                    make().wait_send()

            tail.append(finish)

    def z_next(q, j):
        zz, sign = blocks[j]
        held = full_half(chunks[q][0])
        piece = part(held, q, zz, k)
        remote(piece, piece, zs.at[q, j], zr.at[q, zz], {"z": above}).wait_recv()
        onward = z - sign
        ok = (onward >= 0) & (onward < S)
        target = jnp.clip(onward, 0, S - 1)

        def make():
            return remote(piece, piece, zs.at[q, j], zr.at[q, zz], {"z": target})

        @pl.when(ok)
        def _():
            make().start()

        def finish():
            @pl.when(ok)
            def _():
                make().wait_send()

        tail.append(finish)
        for h, s, r, target in ((0, xs, xr, to_x), (1, ys, yr, to_y)):
            p = part(held, q, zz, k, h)
            copy = remote(p, p, s.at[q, j, 0], r.at[q, j, 0], target)
            copy.start()
            tail.append(copy.wait_send)
        for h, s, r, target in ((0, ys, yr, to_y), (1, xs, xr, to_x)):
            p = part(held, q, zz, k, h)
            copy = remote(p, p, s.at[q, j, 1], r.at[q, j, 1], target)
            copy.start()
            tail.append(copy.wait_send)

    def xy_next(q, j):
        zz, _ = blocks[j]
        held = full_half(chunks[q][0])
        p = part(held, q, zz, kx, 0)
        remote(p, p, xs.at[q, j, 0], xr.at[q, j, 0], to_x).wait_recv()
        copy = remote(p, p, ys.at[q, j, 2], yr.at[q, j, 2], to_y)
        copy.start()
        tail.append(copy.wait_send)
        p = part(held, q, zz, ky, 1)
        remote(p, p, ys.at[q, j, 0], yr.at[q, j, 0], to_y).wait_recv()
        copy = remote(p, p, xs.at[q, j, 2], xr.at[q, j, 2], to_x)
        copy.start()
        tail.append(copy.wait_send)

    def last(q, j):
        i, r0, rn = chunks[q]
        zz, _ = blocks[j]
        held = full_half(i)
        for kk, h, s, r, slot, target in (
            (kx, 1, xs, xr, 1, to_x),
            (ky, 0, ys, yr, 1, to_y),
            (kxy, 1, xs, xr, 2, to_x),
            (kxy, 0, ys, yr, 2, to_y),
        ):
            p = part(held, q, zz, kk, h)
            remote(p, p, s.at[q, j, slot], r.at[q, j, slot], target).wait_recv()
        if shared[i]:
            p = held.at[zz, :, :, pl.ds(r0, rn)]
            copy = remote(p, p, cs.at[q, j], cr.at[q, j], to_c)
            copy.start()
            tail.append(copy.wait_send)
            other = full[i].at[1 - c].at[zz, :, :, pl.ds(r0, rn)]

            def finish():
                remote(other, other, cs.at[q, j], cr.at[q, j], to_c).wait_recv()

            tail.append(finish)

    z_first(0)
    for copy in local:
        copy.start()
    for t in range(1, nc + F + 3):
        if t < nc:
            z_first(t)
        for j in range(F):
            if 0 <= t - 1 - j < nc:
                z_next(t - 1 - j, j)
        for j in range(F):
            if 0 <= t - 2 - j < nc:
                xy_next(t - 2 - j, j)
        for j in range(F):
            if 0 <= t - 3 - j < nc:
                last(t - 3 - j, j)
    for copy in local:
        copy.wait()
    for wait in tail:
        wait()


def gathered(own, shared, chunks, S, cid):
    n = len(own)
    nc = len(chunks)
    F = S - 1
    outs = []
    for o, s in zip(own, shared):
        outs.append(jax.ShapeDtypeStruct((2, S) + o.shape[1:] if s else (S,) + o.shape, o.dtype))
    dma = pltpu.SemaphoreType.DMA

    def body(*refs):
        gather_kernel(shared, chunks, S, refs)

    return pl.pallas_call(
        body,
        out_shape=tuple(outs),
        in_specs=[pl.BlockSpec(memory_space=pltpu.VMEM)] * n,
        out_specs=tuple([ANY] * n),
        scratch_shapes=[
            dma((2 * n,)),
            dma((nc, F + 2)),
            dma((nc, S)),
            dma((nc, F, 3)),
            dma((nc, F, 3)),
            dma((nc, F, 3)),
            dma((nc, F, 3)),
            dma((nc, F)),
            dma((nc, F)),
        ],
        compiler_params=pltpu.CompilerParams(
            collective_id=cid, has_side_effects=True, vmem_limit_bytes=VMEM_BYTES
        ),
    )(*own)


def nt(a, b):
    return lax.dot_general(a, b, (((1,), (1,)), ((), ())), preferred_element_type=F32)

def nn(a, b):
    return lax.dot_general(a, b, (((1,), (0,)), ((), ())), preferred_element_type=F32)

def fill_bias(bias, q_ids, k_ids, first, rows, span):
    key = lax.broadcasted_iota(jnp.int32, (span, rows), 0)
    query = lax.broadcasted_iota(jnp.int32, (span, rows), 1)
    distance = query + WINDOW - key
    same = k_ids[pl.ds(first, span), :1] == q_ids[:1, pl.ds(first, rows)]
    allowed = (distance >= 0) & (distance < WINDOW) & same
    bias[...] = jnp.where(allowed, 0.0, -1e30)

def fwd_kernel(heads, rows, q_ids, k_ids, q_ref, k_ref, v_ref, o_ref, l_ref, bias, vt):
    piece = q_ref.shape[0]
    span = WINDOW + rows
    vt[...] = v_ref[...].T
    factor = HEAD ** -0.5 * LOG2E
    for block in range(piece // rows):
        first = block * rows
        fill_bias(bias, q_ids, k_ids, first, rows, span)
        live = q_ids[:1, pl.ds(first, rows)] != 0
        @pl.loop(0, heads)
        def _(h):
            cols = pl.ds(pl.multiple_of(h * HEAD, HEAD), HEAD)
            q = q_ref[pl.ds(first, rows), cols]
            s = nt(k_ref[pl.ds(first, span), :], q) * factor + bias[...]
            top = jnp.max(s, axis=0, keepdims=True)
            p = jnp.exp2(s - top)
            total = jnp.sum(p, axis=0, keepdims=True)
            o = nn(vt[:, pl.ds(first, span)], p.astype(BF))
            o = jnp.where(live, o * (1.0 / total), 0.0)
            o_ref[pl.ds(first, rows), cols] = o.T.astype(BF)
            l_ref[h, :, pl.ds(first, rows)] = top + jnp.log2(total)

def bwd_kernel(heads, rows, q_ids, k_ids, q_ref, k_ref, v_ref, o_ref, do_ref, l_ref, dq_ref, dk_ref, dv_ref, bias, kt):
    piece = q_ref.shape[0]
    span = WINDOW + rows
    kt[...] = k_ref[...].T
    factor = HEAD ** -0.5 * LOG2E
    dk_ref[...] = jnp.zeros_like(dk_ref)
    dv_ref[...] = jnp.zeros_like(dv_ref)
    for block in range(piece // rows):
        first = block * rows
        fill_bias(bias, q_ids, k_ids, first, rows, span)
        @pl.loop(0, heads, unroll=2)
        def _(h):
            cols = pl.ds(pl.multiple_of(h * HEAD, HEAD), HEAD)
            q = q_ref[pl.ds(first, rows), cols]
            do = do_ref[pl.ds(first, rows), cols]
            o = o_ref[pl.ds(first, rows), cols]
            delta = jnp.sum((do.astype(F32) * o.astype(F32)).T, axis=0, keepdims=True)
            s = nt(k_ref[pl.ds(first, span), :], q) * factor + bias[...]
            p = jnp.exp2(s - l_ref[h, :, pl.ds(first, rows)])
            dp = nt(v_ref[pl.ds(first, span), :], do)
            ds = (p * ((dp - delta) * HEAD ** -0.5)).astype(BF)
            dv_ref[pl.ds(first, span), :] += nn(p.astype(BF), do)
            dk_ref[pl.ds(first, span), :] += nn(ds, q)
            dq_ref[pl.ds(first, rows), cols] = nn(kt[:, pl.ds(first, span)], ds).T


def attend(q_ids, k_ids, q, k, v, heads, rows):
    def body(*refs):
        fwd_kernel(heads, rows, *refs)

    return pl.pallas_call(
        body,
        out_shape=(
            jax.ShapeDtypeStruct(q.shape, BF),
            jax.ShapeDtypeStruct((heads, 1, q.shape[0]), F32),
        ),
        in_specs=[VM] * 5,
        out_specs=(VM, VM),
        scratch_shapes=[
            pltpu.VMEM((WINDOW + rows, rows), F32),
            pltpu.VMEM((HEAD, k.shape[0]), BF),
        ],
        compiler_params=pltpu.CompilerParams(vmem_limit_bytes=VMEM_BYTES),
        cost_estimate=pl.CostEstimate(
            flops=4 * q.size * k.shape[0], bytes_accessed=4 * q.size, transcendentals=q.size * 12
        ),
    )(q_ids, k_ids, q, k, v)


def attend_back(q_ids, k_ids, q, k, v, o, do, l, heads, rows):
    def body(*refs):
        bwd_kernel(heads, rows, *refs)

    return pl.pallas_call(
        body,
        out_shape=(
            jax.ShapeDtypeStruct(q.shape, F32),
            jax.ShapeDtypeStruct(k.shape, F32),
            jax.ShapeDtypeStruct(k.shape, F32),
        ),
        in_specs=[VM] * 8,
        out_specs=(VM, VM, VM),
        scratch_shapes=[
            pltpu.VMEM((WINDOW + rows, rows), F32),
            pltpu.VMEM((HEAD, k.shape[0]), BF),
        ],
        compiler_params=pltpu.CompilerParams(vmem_limit_bytes=VMEM_BYTES),
        cost_estimate=pl.CostEstimate(
            flops=10 * q.size * k.shape[0], bytes_accessed=12 * q.size, transcendentals=q.size * 12
        ),
    )(q_ids, k_ids, q, k, v, o, do, l)


def mlp_kernel(where, two_ref, df_ref, gate_ref, up_ref, down_ref, two_t, hid_t, grads, out, back):
    step = pl.program_id(0)
    tile = gate_ref.shape[1]
    half = down_ref.shape[2]
    rows = 256

    @pl.when(step == 0)
    def _():
        out[...] = jnp.zeros_like(out)
        back[...] = jnp.zeros_like(back)

    part = two_t.shape[0]
    two_t[...] = two_ref[:, pl.ds(pl.multiple_of(step * part, part), part)].T

    @pl.loop(0, two_ref.shape[0] // rows)
    def _(i):
        at = pl.ds(pl.multiple_of(i * rows, rows), rows)
        two = two_ref[at, :]
        gate = nn(two, gate_ref[...])
        up = nn(two, up_ref[...])
        grad = nt(df_ref[at, :half], down_ref[0]) + nt(df_ref[at, half:], down_ref[1])
        slope = 0.7978845608028654
        bent = jnp.tanh(slope * (gate + 0.044715 * (gate * gate * gate)))
        upper = 0.5 * (1.0 + bent)
        act = gate * upper
        act_slope = upper + 0.5 * gate * (1.0 - bent * bent) * (
            slope * (1.0 + 3 * 0.044715 * (gate * gate))
        )
        hid = (act * up).astype(BF)
        grad_gate = (grad * up * act_slope).astype(BF)
        grad_up = (grad * act).astype(BF)
        hid_t[:, at] = hid.T
        grads[0, at, :] = grad_gate
        grads[1, at, :] = grad_up
        out[at, :half] += nn(hid, down_ref[0])
        out[at, half:] += nn(hid, down_ref[1])
        back[at, :] += nt(grad_gate, gate_ref[...]) + nt(grad_up, up_ref[...])


def mlp_call(core, two, df, gate_full, down_full):
    T, D = two.shape
    half_ff = gate_full.shape[1] // 2
    tile = 384
    tiles = half_ff // tile
    half = down_full.shape[2]
    part = D // tiles

    def body(where, *refs):
        mlp_kernel(where, *refs)

    whole = pl.BlockSpec((T, D), lambda i, w: (0, 0))
    return pl.pallas_call(
        body,
        grid_spec=pltpu.PrefetchScalarGridSpec(
            num_scalar_prefetch=1,
            grid=(tiles,),
            in_specs=[
                whole,
                whole,
                pl.BlockSpec((D, tile), lambda i, w: (0, i)),
                pl.BlockSpec((D, tile), lambda i, w: (0, tiles + i)),
                pl.BlockSpec((2, tile, half), lambda i, w: (0, w[0] * tiles + i, 0)),
            ],
            out_specs=[
                pl.BlockSpec((part, T), lambda i, w: (i, 0)),
                pl.BlockSpec((tile, T), lambda i, w: (i, 0)),
                pl.BlockSpec((2, T, tile), lambda i, w: (0, 0, i)),
                whole,
                whole,
            ],
        ),
        out_shape=[
            jax.ShapeDtypeStruct((D, T), BF),
            jax.ShapeDtypeStruct((half_ff, T), BF),
            jax.ShapeDtypeStruct((2, T, half_ff), BF),
            jax.ShapeDtypeStruct((T, D), F32),
            jax.ShapeDtypeStruct((T, D), F32),
        ],
        compiler_params=pltpu.CompilerParams(
            dimension_semantics=("arbitrary",), vmem_limit_bytes=VMEM_BYTES
        ),
        cost_estimate=pl.CostEstimate(
            flops=12 * T * D * half_ff, bytes_accessed=40 * 2**20, transcendentals=T * half_ff
        ),
    )(core, two, df, gate_full, gate_full, down_full)


def reduce_kernel(sides, parts, S, two, hid_own, hid_other, grads, df, out, *scratch):
    left, right, s1, g1, s2, g2, fz, gz, mine, *sems = scratch
    lds, rds, s1s, s1r, s2s, s2r, zs, zr, ls, xs, xr, ys, yr, cs, cr = sems
    groups, _, _, r, T = left.shape
    n = right.shape[2]
    wide = sides * parts
    nc = wide + groups - 1
    y, x, c, z = (lax.axis_index(a) for a in ("y", "x", "c", "z"))
    k = y * 2 + x
    kx = y * 2 + 1 - x
    ky = (1 - y) * 2 + x
    kxy = 3 - k
    to_x = {"x": 1 - x}
    to_y = {"y": 1 - y}
    to_c = {"c": 1 - c}
    loads = {}

    def fetch(key, src, dst, sem):
        copy = pltpu.make_async_copy(src, dst, sem)
        copy.start()
        loads.setdefault(key, []).append(copy)

    def fetch_left(g):
        for p in range(8):
            h, kk = p // 4, p % 4
            if g == 0:
                fetch(("l", 0), two.at[:, kk, h], left.at[0, p], lds.at[0, p, 0])
            else:
                for i, (src, cc) in enumerate(((hid_own, c), (hid_other, 1 - c))):
                    dst = left.at[g, p, pl.ds(cc * (S // 2), S // 2)]
                    fetch(("l", g), src.at[:, g - 1, kk, h], dst, lds.at[g, p, i])

    def slot_of(t):
        return t % 4 if t < wide else 4

    def fetch_right(t):
        if t < wide:
            src = grads.at[t // parts, :, pl.ds((t % parts) * n, n)]
            fetch(("r", t), src, right.at[t % 4], rds.at[t])
        elif t == wide:
            fetch(("r", t), df, right.at[4], rds.at[t])

    def landed(key):
        for copy in loads.pop(key, []):
            copy.wait()

    fetch_right(0)
    fetch_left(0)
    fetch_right(1)
    barrier = pltpu.get_barrier_semaphore()
    peers = [to_x, to_y, to_c] + [{"z": lax.rem(z + e, S)} for e in range(1, S)]
    for target in peers:
        pl.semaphore_signal(barrier, inc=1, device_id=target, device_id_type=MESH_ID)
    pl.semaphore_wait(barrier, len(peers))
    for g in range(1, groups):
        fetch_left(g)

    def remote(src, dst, s, r_, target):
        return pltpu.make_async_remote_copy(
            src_ref=src, dst_ref=dst, send_sem=s, recv_sem=r_, device_id=target, device_id_type=MESH_ID
        )

    def product(t, p):
        g = max(0, t - wide + 1)
        return nn(left[g, p].reshape(S * r, T), right[slot_of(t)])

    pending = {}

    def launch(key, copy):
        copy.start()
        pending.setdefault(key, []).append(copy)

    def drain(key):
        for copy in pending.pop(key, []):
            copy.wait_send()

    def first(t):
        slot = t % 2
        landed(("l", max(0, t - wide + 1)))
        landed(("r", t))
        drain(("s1", t - 2))

        for i in range(2):
            for j, p, target in ((i, i * 2 + 1 - x, to_x), (2 + i, 4 + (1 - y) * 2 + i, to_y)):
                s1[slot, j] = product(t, p).astype(BF)
                launch(("s1", t), remote(s1.at[slot, j], g1.at[t, j], s1s.at[t, j], s1r.at[t, j], target))

    def got1(t, j):
        remote(g1.at[t, j], g1.at[t, j], s1s.at[t, j], s1r.at[t, j], to_x).wait_recv()

    def second(t):
        slot = t % 2
        drain(("s2", t - 2))
        for j in range(4):
            got1(t, j)
        for h, p, j, target in ((0, (1 - y) * 2 + x, 1 - y, to_y), (1, 4 + y * 2 + 1 - x, 3 - x, to_x)):
            s2[slot, h] = (product(t, p) + g1[t, j].astype(F32)).astype(BF)
            launch(("s2", t), remote(s2.at[slot, h], g2.at[t, h], s2s.at[t, h], s2r.at[t, h], target))

    def third(t):
        slot = t % 2
        drain(("z", t - 2))
        for h, p, j in ((0, k, y), (1, 4 + k, 2 + x)):
            remote(g2.at[t, h], g2.at[t, h], s2s.at[t, h], s2r.at[t, h], to_x).wait_recv()
            total = (product(t, p) + g1[t, j].astype(F32) + g2[t, h].astype(F32)).astype(BF)
            for zz in range(S):
                fz[slot, zz, h] = total[zz * r : (zz + 1) * r]
        for e in range(1, S):
            zz = lax.rem(z + e, S)
            launch(("z", t), remote(fz.at[slot, zz], gz.at[t, S - e - 1], zs.at[t, e - 1], zr.at[t, S - e - 1], {"z": zz}))

    def fourth(t):
        slot = t % 2
        drain(("ag", t - 2))
        for copy in pending.pop(("l", t - 2), []):
            copy.wait()
        for e in range(S - 1):
            remote(gz.at[t, e], gz.at[t, e], zs.at[t, e], zr.at[t, e], to_x).wait_recv()
        for h in range(2):
            total = fz[slot, z, h].astype(F32)
            for e in range(S - 1):
                total = total + gz[t, e, h].astype(F32)
            mine[slot, h] = total.astype(BF)
        copy = pltpu.make_async_copy(mine.at[slot], out.at[t, k, c], ls.at[t])
        copy.start()
        pending[("l", t)] = [copy]
        for h, s, r_, target in ((0, xs, xr, to_x), (1, ys, yr, to_y)):
            launch(("ag", t), remote(mine.at[slot, h], out.at[t, k, c, h], s.at[t, 0], r_.at[t, 0], target))
        for h, s, r_, target in ((0, ys, yr, to_y), (1, xs, xr, to_x)):
            launch(("ag", t), remote(mine.at[slot, h], out.at[t, k, c, h], s.at[t, 1], r_.at[t, 1], target))

    def land(t, kk, h, s, r_, j, target):
        p = out.at[t, kk, c, h]
        remote(p, p, s.at[t, j], r_.at[t, j], target).wait_recv()
        return p

    def fifth(t):
        p = land(t, kx, 0, xs, xr, 0, to_x)
        launch("end", remote(p, p, ys.at[t, 2], yr.at[t, 2], to_y))
        p = land(t, ky, 1, ys, yr, 0, to_y)
        launch("end", remote(p, p, xs.at[t, 2], xr.at[t, 2], to_x))

    def sixth(t):
        land(t, kx, 1, xs, xr, 1, to_x)
        land(t, ky, 0, ys, yr, 1, to_y)
        land(t, kxy, 1, xs, xr, 2, to_x)
        land(t, kxy, 0, ys, yr, 2, to_y)
        for copy in pending.pop(("l", t), []):
            copy.wait()
        p = out.at[t, :, c]
        launch("end", remote(p, p, cs.at[t], cr.at[t], to_c))

    stages = (first, second, third, fourth, fifth, sixth)
    for t in range(nc + len(stages) - 1):
        for lag, stage in enumerate(stages):
            if 0 <= t - lag < nc:
                stage(t - lag)
        fetch_right(t + 2)
    for t in range(nc):
        p = out.at[t, :, 1 - c]
        remote(p, p, cs.at[t], cr.at[t], to_c).wait_recv()
    for key in list(pending):
        drain(key) if key[0] != "l" else [copy.wait() for copy in pending.pop(key)]


def reduced(two_t, hid_own, hid_other, grads, df, S, cid):
    D, T = two_t.shape
    sides, _, half_ff = grads.shape
    n = df.shape[1]
    r = D // (S * 8)
    parts = half_ff // n
    groups = 1 + 2 * half_ff // (S * 8 * r)
    nc = sides * parts + groups - 1
    m = S * r
    dma = pltpu.SemaphoreType.DMA
    hid_shape = (S // 2, groups - 1, 4, 2, r, T)

    def body(*refs):
        reduce_kernel(sides, parts, S, *refs)

    return pl.pallas_call(
        body,
        out_shape=jax.ShapeDtypeStruct((nc, 4, 2, 2, r, n), BF),
        in_specs=[ANY] * 5,
        out_specs=ANY,
        scratch_shapes=[
            pltpu.VMEM((groups, 8, S, r, T), BF),
            pltpu.VMEM((5, T, n), BF),
            pltpu.VMEM((2, 4, m, n), BF),
            pltpu.VMEM((nc, 4, m, n), BF),
            pltpu.VMEM((2, 2, m, n), BF),
            pltpu.VMEM((nc, 2, m, n), BF),
            pltpu.VMEM((2, S, 2, r, n), BF),
            pltpu.VMEM((nc, S - 1, 2, r, n), BF),
            pltpu.VMEM((2, 2, r, n), BF),
            dma((groups, 8, 2)),
            dma((nc,)),
            dma((nc, 4)),
            dma((nc, 4)),
            dma((nc, 2)),
            dma((nc, 2)),
            dma((nc, S)),
            dma((nc, S)),
            dma((nc,)),
            dma((nc, 3)),
            dma((nc, 3)),
            dma((nc, 3)),
            dma((nc, 3)),
            dma((nc,)),
            dma((nc,)),
        ],
        compiler_params=pltpu.CompilerParams(
            collective_id=cid, has_side_effects=True, vmem_limit_bytes=VMEM_BYTES
        ),
        cost_estimate=pl.CostEstimate(
            flops=4 * T * D * 3 * half_ff, bytes_accessed=400 * 2**20, transcendentals=0
        ),
    )(
        two_t.reshape(S, 4, 2, r, T),
        hid_own.reshape(hid_shape),
        hid_other.reshape(hid_shape),
        grads,
        df,
    )


def adam_kernel(total, count_ref, rates_ref, g_ref, w_ref, m_ref, g_out, w_out, m_out):
    step_value = count_ref[0].astype(F32)
    log_first = jnp.log(jnp.full((8, 128), beta_first, F32))
    log_second = jnp.log(jnp.full((8, 128), beta_second, F32))
    fix_first = (1.0 - jnp.exp(step_value * log_first))[:1, :1]
    fix_second = (1.0 - jnp.exp(step_value * log_second))[:1, :1]
    grad = g_ref[0, 0, 0].reshape(w_ref.shape).astype(F32) / total
    w = w_ref[...]
    first = beta_first * m_ref[0] + (1.0 - beta_first) * grad
    second = beta_second * m_ref[1] + (1.0 - beta_second) * grad * grad
    step = first / fix_first / (jnp.sqrt(second / fix_second) + adam_eps) + rates_ref[1] * w
    g_out[...] = grad
    w_out[...] = w - rates_ref[0] * step
    m_out[0] = first
    m_out[1] = second


def adam_call(weight, moments, grads, count, rates, total, base, sides, tiles, down):
    _, _, _, _, r, n = grads.shape

    def g_place(kk, cc, ss, tt):
        return (base + ss * tiles + tt, kk, cc, 0, 0, 0)

    def place(kk, cc, ss, tt):
        if down:
            return (tt * 4 + kk, cc)
        return (kk, (ss * 2 + cc) * tiles + tt)

    def m_place(*at):
        return (0,) + place(*at)

    w_spec = pl.BlockSpec((2 * r, n), place)
    m_spec = pl.BlockSpec((2, 2 * r, n), m_place)
    smem = pl.BlockSpec(memory_space=pltpu.SMEM)

    def body(*refs):
        adam_kernel(total, *refs)

    return pl.pallas_call(
        body,
        grid=(4, 2, sides, tiles),
        in_specs=[smem, smem, pl.BlockSpec((1, 1, 1, 2, r, n), g_place), w_spec, m_spec],
        out_specs=[w_spec, w_spec, m_spec],
        out_shape=[
            jax.ShapeDtypeStruct(weight.shape, F32),
            jax.ShapeDtypeStruct(weight.shape, F32),
            jax.ShapeDtypeStruct(moments.shape, F32),
        ],
        compiler_params=pltpu.CompilerParams(
            dimension_semantics=("arbitrary",) * 4, vmem_limit_bytes=VMEM_BYTES
        ),
        cost_estimate=pl.CostEstimate(
            flops=20 * weight.size, bytes_accessed=30 * weight.size, transcendentals=weight.size
        ),
    )(count, rates, grads, weight, moments)


def dot(a, b):
    return jnp.dot(a, b, preferred_element_type=F32)


def dot_rows(a, b):
    return lax.dot_general(a, b, (((1,), (0,)), ((), ())), preferred_element_type=F32)


def dot_t(a, b):
    return lax.dot_general(a, b, (((1,), (1,)), ((), ())), preferred_element_type=F32)


def plane_sum(left, right, zb):
    y = lax.axis_index("y")
    x = lax.axis_index("x")
    T, M = left.shape
    N = right.shape[1]
    r = M // (zb * 8)
    rows = left.T.reshape(zb, 2, 2, 2, r, T).transpose(3, 1, 2, 0, 4, 5)

    def pick(h, yy, xx):
        block = lax.dynamic_index_in_dim(rows[h], yy, 0, keepdims=False)
        return lax.dynamic_index_in_dim(block, xx, 0, keepdims=False).reshape(zb * r, T)

    sent0 = jnp.concatenate([pick(0, 0, 1 - x), pick(0, 1, 1 - x)], axis=0)
    sent1 = jnp.concatenate([pick(1, 1 - y, 0), pick(1, 1 - y, 1)], axis=0)
    got0 = swapped(dot_rows(sent0, right).astype(BF), "x").reshape(2, zb * r, N)
    got1 = swapped(dot_rows(sent1, right).astype(BF), "y").reshape(2, zb * r, N)

    def at(got, i):
        return lax.dynamic_index_in_dim(got, i, 0, keepdims=False).astype(F32)

    next0 = swapped((dot_rows(pick(0, 1 - y, x), right) + at(got0, 1 - y)).astype(BF), "y")
    next1 = swapped((dot_rows(pick(1, y, 1 - x), right) + at(got1, 1 - x)).astype(BF), "x")
    last0 = dot_rows(pick(0, y, x), right) + at(got0, y) + next0.astype(F32)
    last1 = dot_rows(pick(1, y, x), right) + at(got1, x) + next1.astype(F32)
    both = [v.astype(BF).reshape(zb, 1, r, N) for v in (last0, last1)]
    return jnp.concatenate(both, axis=1)


def handed_out(share):
    S, _, r, N = share.shape
    mine = lax.psum_scatter(share.reshape(S, 2 * r, N), "z", scatter_dimension=0, tiled=False)
    return lax.all_gather(mine, ("y", "x", "c"), axis=0).reshape(4, 2, 2 * r, N)


def on_device(
    Y,
    S,
    block_in,
    cotangent,
    segment_ids,
    input_proj,
    output_proj,
    gate_up,
    down_weight,
    norm_gains,
    input_moments,
    output_moments,
    gate_moments,
    down_moments,
    gain_moments,
    update_count,
    optimizer_rates,
):
    seq_place = lax.axis_index("z")
    core = lax.axis_index("c")
    first_core = core == 0
    D = block_in.shape[-1]
    half_ff = FF // 2
    rows_d = input_proj.shape[0]
    rows_f = down_weight.shape[0]
    fast = Y == 2 and rows_d % 128 == 0
    in_half = input_proj.shape[1] // 2
    d_half = D // 2
    r = rows_d // 8

    in_low = input_proj.astype(BF)
    out_low = output_proj.astype(BF)
    down_low = down_weight.astype(BF)

    def halves(w):
        n = w.shape[1] // 2
        return jnp.stack([w[:, :n], w[:, n:]])

    gate_low = jnp.concatenate(
        [
            lax.dynamic_slice_in_dim(gate_up, side * FF + core * half_ff, half_ff, 1)
            for side in range(2)
        ],
        axis=1,
    ).astype(BF)

    if fast:
        in_full, out_full = gathered(
            [
                halves(in_low).reshape(2, 4, 2, r, in_half),
                halves(out_low).reshape(2, 4, 2, r, d_half),
            ],
            [True, True],
            [(0, 0, r), (1, 0, r)],
            S,
            0,
        )
        in_full = in_full.reshape(2, D, in_half)
        out_full = out_full.reshape(2, D, d_half)
    else:
        in_full = halves(lax.all_gather(in_low, "z", axis=0, tiled=True))
        out_full = halves(lax.all_gather(out_low, "z", axis=0, tiled=True))
        down_full = halves(lax.all_gather(down_low, "z", axis=0, tiled=True))
        gate_full = lax.all_gather(gate_low, "z", axis=0, tiled=True)
    gains_full = lax.all_gather(norm_gains.astype(BF), "z", axis=1, tiled=True)

    gains_wide = gains_full.astype(F32)
    tokens = block_in[0].astype(F32)
    piece_len = tokens.shape[0]
    width_q = HEADS * HEAD
    positions = seq_place * piece_len + jnp.arange(piece_len, dtype=jnp.int32)
    normed = root_norm(tokens, gains_wide[0]).astype(BF)
    mixed_proj = jnp.concatenate([dot(normed, in_full[0]), dot(normed, in_full[1])], axis=1)
    queries = (
        rotate(mixed_proj[:, :width_q].reshape(piece_len, HEADS, HEAD), positions, 1.0)
        .astype(BF)
        .reshape(piece_len, width_q)
    )
    own_keys = rotate(mixed_proj[:, width_q : width_q + HEAD], positions, 1.0)
    own_pair = jnp.concatenate([own_keys, mixed_proj[:, width_q + HEAD :]], axis=1).astype(BF)
    reach_count = (WINDOW + piece_len - 2) // piece_len
    earlier = []
    for back_step in range(reach_count, 0, -1):
        earlier.append(passed_along(own_pair, "z", back_step))
    key_pairs = jnp.concatenate(earlier + [own_pair], axis=0)
    key_rows = key_pairs[:, :HEAD]
    values = key_pairs[:, HEAD:]
    segments = segment_ids[0]
    key_span = reach_count * piece_len
    padded_ids = jnp.concatenate([jnp.full((key_span,), -1, jnp.int32), segments])
    query_ids = lax.dynamic_slice_in_dim(segments, seq_place * piece_len, piece_len)
    key_ids = lax.dynamic_slice_in_dim(padded_ids, seq_place * piece_len, key_span + piece_len)
    live_rows = query_ids != 0
    query_row = query_ids[None, :]
    key_column = key_ids[:, None]

    flat_heads, log_totals = attend(
        query_row, key_column, queries, key_rows, values, HEADS, piece_len
    )
    middle = tokens + jnp.concatenate(
        [dot(flat_heads, out_full[0]), dot(flat_heads, out_full[1])], axis=1
    )
    normed_two = root_norm(middle, gains_wide[1]).astype(BF)

    if fast:
        down_full, gate_full = gathered(
            [
                halves(down_low).reshape(2, 4, 2, rows_f // 8, d_half),
                gate_low.reshape(4, 2, r, 2 * half_ff),
            ],
            [True, False],
            [(0, i * 48, 48) for i in range(rows_f // 8 // 48)]
            + [(1, i * 16, 16) for i in range(r // 16)],
            S,
            1,
        )
        down_full = down_full.reshape(2, FF, d_half)
        gate_full = gate_full.reshape(D, 2 * half_ff)

    upstream = cotangent[0].astype(F32)

    def ordered(mine, other):
        return jnp.concatenate(
            [jnp.where(first_core, mine, other), jnp.where(first_core, other, mine)], axis=0
        )

    def pair(v):
        return ordered(v, swapped(v, "c"))

    def half_pair(v):
        n = v.shape[1] // 2
        keep = lax.dynamic_slice_in_dim(v, core * n, n, 1)
        give = lax.dynamic_slice_in_dim(v, (1 - core) * n, n, 1)
        return ordered(keep, swapped(give, "c"))

    def core_sum(v):
        keep = lax.dynamic_slice_in_dim(v, core * piece_len, piece_len, 0)
        give = lax.dynamic_slice_in_dim(v, (1 - core) * piece_len, piece_len, 0)
        return keep + swapped(give.astype(BF), "c").astype(F32)

    df_both = pair(cotangent[0])
    normed_both = pair(normed)
    flat_both = pair(flat_heads)
    two_both = pair(normed_two)

    two_t, hid_t, grad_gated, out_sum, two_sum = mlp_call(
        core.reshape(1).astype(jnp.int32), two_both, df_both, gate_full, down_full
    )

    output = middle + core_sum(out_sum)
    block_out = output.astype(BF)[None]
    grad_normed_two = core_sum(two_sum)
    _, norm_pull_two = jax.vjp(root_norm, middle, gains_wide[1])
    grad_middle_norm, grad_gain_two = norm_pull_two(grad_normed_two)
    grad_middle = upstream + grad_middle_norm
    grad_branch = grad_middle.astype(BF)

    grad_flat = dot_t(grad_branch[:, :d_half], out_full[0]) + dot_t(
        grad_branch[:, d_half:], out_full[1]
    )
    grad_attended = jnp.where(live_rows[:, None], grad_flat, 0.0).astype(BF)

    if fast:
        df_half = lax.dynamic_slice_in_dim(df_both, core * d_half, d_half, 1)
        mlp_sums = reduced(two_t, hid_t, swapped(hid_t, "c"), grad_gated, df_half, S, 2)

    grad_query_all, grad_keys, grad_values = attend_back(
        query_row,
        key_column,
        queries,
        key_rows,
        values,
        flat_heads,
        grad_attended,
        log_totals,
        HEADS,
        piece_len // 2,
    )
    grad_pairs = jnp.concatenate([grad_keys, grad_values], axis=1)
    own_grad = grad_pairs[key_span:]
    for back_step in range(1, reach_count + 1):
        sent_rows = grad_pairs[
            key_span - back_step * piece_len : key_span - (back_step - 1) * piece_len
        ]
        own_grad = own_grad + passed_along(sent_rows, "z", -back_step)
    grad_query_raw = rotate(
        grad_query_all.reshape(piece_len, HEADS, HEAD), positions, -1.0
    ).reshape(piece_len, width_q)
    grad_key_raw = rotate(own_grad[:, :HEAD], positions, -1.0)
    grad_mixed = jnp.concatenate([grad_query_raw, grad_key_raw, own_grad[:, HEAD:]], axis=1).astype(
        BF
    )
    grad_normed = dot_t(grad_mixed[:, :in_half], in_full[0]) + dot_t(
        grad_mixed[:, in_half:], in_full[1]
    )
    _, norm_pull_one = jax.vjp(root_norm, tokens, gains_wide[0])
    grad_tokens_norm, grad_gain_one = norm_pull_one(grad_normed)
    block_in_grad = (grad_middle + grad_tokens_norm).astype(BF)[None]
    gains_sum = lax.psum(jnp.stack([grad_gain_one, grad_gain_two]), ("y", "x", "c", "z"))
    gains_mine = lax.dynamic_slice_in_dim(gains_sum, seq_place * rows_d, rows_d, 1)

    token_total = piece_len * S * Y * 4 * block_in.shape[0]
    step_value = update_count[0].astype(F32)
    rates = optimizer_rates
    grad_half = half_pair(grad_branch)
    mixed_half = half_pair(grad_mixed)

    if fast:

        def adam(weight, moments, grads, base, sides, tiles, down=False):
            return adam_call(
                weight, moments, grads, update_count, rates, float(token_total), base, sides, tiles, down
            )

        def summed(left, right):
            return handed_out(plane_sum(left, right, S)).reshape(1, 4, 2, 2, r, right.shape[1])

        tiles = half_ff // d_half
        out_grad, out_new, out_mom = adam(
            output_proj, output_moments, summed(flat_both, grad_half), 0, 1, 1
        )
        in_grad, in_new, in_mom = adam(
            input_proj, input_moments, summed(normed_both, mixed_half), 0, 1, 1
        )
        gate_grad, gate_new, gate_mom = adam(gate_up, gate_moments, mlp_sums, 0, 2, tiles)
        down_grad, down_new, down_mom = adam(
            down_weight, down_moments, mlp_sums, 2 * tiles, 1, tiles, True
        )
    else:

        def adam(weight, moments, grad):
            grad = grad.astype(F32) / token_total
            change, new = adamw_step(weight, moments, grad, step_value, rates)
            return grad, weight - change, new

        def summed(left, right):
            whole = dot_rows(left.T, right).astype(BF)
            mine = lax.psum_scatter(whole, "z", scatter_dimension=0, tiled=True)
            return lax.psum(mine, ("y", "x"))

        gate_half = [summed(two_both, grad_gated[side]) for side in range(2)]
        gate_sum = jnp.concatenate(
            [lax.all_gather(g, "c", axis=1, tiled=True) for g in gate_half], axis=1
        )
        down_part = lax.psum(dot_rows(hid_t, df_both).astype(BF), ("y", "x"))
        down_part = lax.all_gather(down_part, "c", axis=0, tiled=True)
        down_sum = lax.psum_scatter(down_part, "z", scatter_dimension=0, tiled=True)
        out_total = lax.all_gather(summed(flat_both, grad_half), "c", axis=1, tiled=True)
        in_total = lax.all_gather(summed(normed_both, mixed_half), "c", axis=1, tiled=True)
        out_grad, out_new, out_mom = adam(output_proj, output_moments, out_total)
        in_grad, in_new, in_mom = adam(input_proj, input_moments, in_total)
        gate_grad, gate_new, gate_mom = adam(gate_up, gate_moments, gate_sum)
        down_grad, down_new, down_mom = adam(down_weight, down_moments, down_sum)
    gain_grad = gains_mine / token_total
    gains_step, gain_moments_new = adamw_step(norm_gains, gain_moments, gain_grad, step_value, rates)
    return (
        block_out,
        block_in_grad,
        in_grad,
        out_grad,
        gate_grad,
        down_grad,
        gain_grad,
        in_new,
        out_new,
        gate_new,
        down_new,
        gains_step,
        in_mom,
        out_mom,
        gate_mom,
        down_mom,
        gain_moments_new,
    )


def solution(mesh):
    dp, S = mesh.shape["dp"], mesh.shape["seq"]
    Y = dp // 4
    grid = Mesh(mesh.devices.reshape(Y, 2, 2, S), ("y", "x", "c", "z"))
    data = ("y", "x", "c")
    tokens = P(data, "z", None)
    rows = P("z", None)
    moments = P(None, "z", None)
    in_specs = (
        (tokens, tokens, P(data, None))
        + (rows,) * 4
        + (P(None, "z"),)
        + (moments,) * 4
        + (P(None, None, "z"), P(), P())
    )
    out_specs = (
        (tokens, tokens)
        + (rows,) * 4
        + (P(None, "z"),)
        + (rows,) * 4
        + (P(None, "z"),)
        + (moments,) * 4
        + (P(None, None, "z"),)
    )

    def device_step(*arrays):
        return on_device(Y, S, *arrays)

    return jax.shard_map(
        device_step, mesh=grid, in_specs=in_specs, out_specs=out_specs, check_vma=False
    )
```

```python
import jax
import jax.numpy as jnp
from jax import lax
from jax.experimental import pallas as pl
from jax.experimental.pallas import tpu as pltpu
from jax.sharding import Mesh
from jax.sharding import PartitionSpec as P

HEADS = 12
HEAD = 128
FF = 4608
WINDOW = 1024


norm_eps = 1e-06
adam_eps = 1e-08
beta_first = 0.9
beta_second = 0.95
BF = jnp.bfloat16
F32 = jnp.float32
MESH_ID = pl.DeviceIdType.MESH
VMEM_BYTES = 60 * 1024 * 1024
ANY = pl.BlockSpec(memory_space=pl.ANY)
VM = pl.BlockSpec(memory_space=pltpu.VMEM)
LOG2E = 1.4426950408889634


def passed_along(block, axis, distance):
    devices = range(lax.axis_size(axis))
    route = [(i - distance, i) for i in devices if i - distance in devices]
    return lax.ppermute(block, axis, route)


def swapped(block, axis):
    return lax.ppermute(block, axis, [(0, 1), (1, 0)])


def rotate(values, positions, sign_value):
    half_width = values.shape[-1] // 2
    frequency = 10000.0 ** (-2.0 * jnp.arange(half_width).astype(jnp.float32) / values.shape[-1])
    angles = positions.astype(jnp.float32)[:, None] * frequency[None, :]
    cosine = jnp.cos(angles)
    sine_part = sign_value * jnp.sin(angles)
    if values.ndim == 3:
        cosine = cosine[:, None, :]
        sine_part = sine_part[:, None, :]
    lower_half = values[..., :half_width]
    upper_half = values[..., half_width:]
    return jnp.concatenate(
        [
            lower_half * cosine - upper_half * sine_part,
            upper_half * cosine + lower_half * sine_part,
        ],
        axis=-1,
    )


def root_norm(values, gain):
    return values * lax.rsqrt(jnp.mean(values * values, axis=-1, keepdims=True) + norm_eps) * gain


def adamw_step(weight, moments, grad, step_value, optimizer_rates):
    fix_first = 1.0 - beta_first**step_value
    fix_second = 1.0 - beta_second**step_value
    first_moment = beta_first * moments[0] + (1.0 - beta_first) * grad
    second = beta_second * moments[1] + (1.0 - beta_second) * grad * grad
    update = (
        first_moment / fix_first / (jnp.sqrt(second / fix_second) + adam_eps)
        + optimizer_rates[1] * weight
    )
    return (optimizer_rates[0] * update, jnp.stack([first_moment, second]))


def gather_kernel(shared, chunks, S, own, full, sems, small_own, small_full, work):
    n = len(shared)
    nc = len(chunks)
    F = S - 1
    loc, zs, zr, xs, xr, ys, yr, cs, cr, ss, sr = sems
    y, x, c, z = (lax.axis_index(a) for a in ("y", "x", "c", "z"))
    k = y * 2 + x
    kx = y * 2 + 1 - x
    ky = (1 - y) * 2 + x
    kxy = 3 - k
    to_x = {"x": 1 - x}
    to_y = {"y": 1 - y}
    to_c = {"c": 1 - c}
    low = z
    high = S - 1 - z
    near_count = jnp.minimum(low, high)
    above = jnp.minimum(z + 1, S - 1)
    below = jnp.maximum(z - 1, 0)
    blocks = []
    for j in range(F):
        near = j < 2 * near_count
        dist = jnp.where(near, j // 2 + 1, j - near_count + 1)
        sign = jnp.where(near, (j % 2) * 2 - 1, jnp.where(high > low, 1, -1))
        blocks.append((z + sign * dist, sign))
    barrier = pltpu.get_barrier_semaphore()
    others = [lax.rem(z + e, S) for e in range(1, S)]
    for target in [to_x, to_y, to_c] + [{"z": zz} for zz in others]:
        pl.semaphore_signal(barrier, inc=1, device_id=target, device_id_type=MESH_ID)
    pl.semaphore_wait(barrier, 3 + F)

    def own_half(i):
        return own[i].at[c] if shared[i] else own[i]

    def full_half(i):
        return full[i].at[c] if shared[i] else full[i]

    def box(q):
        _, r0, rn, c0, cn = chunks[q]
        return pl.ds(r0, rn), pl.ds(c0, cn)

    def part(ref, q, zz, kk, h=None):
        rr, cc = box(q)
        if h is None:
            return ref.at[zz, kk, :, rr, cc]
        return ref.at[zz, kk, h, rr, cc]

    def remote(src, dst, s, r, target):
        return pltpu.make_async_remote_copy(
            src_ref=src,
            dst_ref=dst,
            send_sem=s,
            recv_sem=r,
            device_id=target,
            device_id_type=MESH_ID,
        )

    tail = []
    local = []
    arriving = {i: [] for i in range(n)}
    arriving[None] = []
    finished = [0] * n
    for i in range(n):
        if shared[i]:
            for half in range(2):
                copy = pltpu.make_async_copy(
                    own[i].at[half], full[i].at[half, z], loc.at[len(local)]
                )
                local.append(copy)
                arriving[i].append(copy.wait)
        else:
            copy = pltpu.make_async_copy(own[i], full[i].at[z], loc.at[len(local)])
            local.append(copy)
            arriving[i].append(copy.wait)

    def z_first(q):
        i = chunks[q][0]
        rr, cc = box(q)
        src = own_half(i).at[k, :, rr, cc]
        dst = part(full_half(i), q, z, k)
        for ok, target, slot in ((z + 1 < S, above, F), (z > 0, below, F + 1)):

            def make(target=target, slot=slot):
                return remote(src, dst, zs.at[q, slot], zr.at[q, z], {"z": target})

            @pl.when(ok)
            def _(make=make):
                make().start()

            def finish(ok=ok, make=make):
                @pl.when(ok)
                def _():
                    make().wait_send()

            tail.append(finish)

    def z_next(q, j):
        zz, sign = blocks[j]
        held = full_half(chunks[q][0])
        piece = part(held, q, zz, k)
        remote(piece, piece, zs.at[q, j], zr.at[q, zz], {"z": above}).wait_recv()
        onward = z - sign
        ok = (onward >= 0) & (onward < S)
        target = jnp.clip(onward, 0, S - 1)

        def make():
            return remote(piece, piece, zs.at[q, j], zr.at[q, zz], {"z": target})

        @pl.when(ok)
        def _():
            make().start()

        def finish():
            @pl.when(ok)
            def _():
                make().wait_send()

        tail.append(finish)
        for h, s, r, target in ((0, xs, xr, to_x), (1, ys, yr, to_y)):
            p = part(held, q, zz, k, h)
            copy = remote(p, p, s.at[q, j, 0], r.at[q, j, 0], target)
            copy.start()
            tail.append(copy.wait_send)
        for h, s, r, target in ((0, ys, yr, to_y), (1, xs, xr, to_x)):
            p = part(held, q, zz, k, h)
            copy = remote(p, p, s.at[q, j, 1], r.at[q, j, 1], target)
            copy.start()
            tail.append(copy.wait_send)

    def xy_next(q, j):
        zz, _ = blocks[j]
        held = full_half(chunks[q][0])
        p = part(held, q, zz, kx, 0)
        remote(p, p, xs.at[q, j, 0], xr.at[q, j, 0], to_x).wait_recv()
        copy = remote(p, p, ys.at[q, j, 2], yr.at[q, j, 2], to_y)
        copy.start()
        tail.append(copy.wait_send)
        p = part(held, q, zz, ky, 1)
        remote(p, p, ys.at[q, j, 0], yr.at[q, j, 0], to_y).wait_recv()
        copy = remote(p, p, xs.at[q, j, 2], xr.at[q, j, 2], to_x)
        copy.start()
        tail.append(copy.wait_send)

    def last(q, j):
        i = chunks[q][0]
        rr, cc = box(q)
        zz, _ = blocks[j]
        held = full_half(i)
        finished[i] += 1
        for kk, h, s, r, slot, target in (
            (kx, 1, xs, xr, 1, to_x),
            (ky, 0, ys, yr, 1, to_y),
            (kxy, 1, xs, xr, 2, to_x),
            (kxy, 0, ys, yr, 2, to_y),
        ):
            p = part(held, q, zz, kk, h)
            remote(p, p, s.at[q, j, slot], r.at[q, j, slot], target).wait_recv()
        if shared[i]:
            p = held.at[zz, :, :, rr, cc]
            copy = remote(p, p, cs.at[q, j], cr.at[q, j], to_c)
            copy.start()
            tail.append(copy.wait_send)
            other = full[i].at[1 - c].at[zz, :, :, rr, cc]

            def finish():
                remote(other, other, cs.at[q, j], cr.at[q, j], to_c).wait_recv()

            arriving[i].append(finish)

    def ready(i):
        if i is not None:
            assert finished[i] == F * sum(chunk[0] == i for chunk in chunks)
        for wait in arriving.pop(i, []):
            wait()

    z_first(0)
    for copy in local:
        copy.start()
    if small_own is not None:
        place = pltpu.make_async_copy(small_own, small_full.at[z], ss.at[0])
        place.start()
        arriving[None].append(place.wait)
        for e, zz in enumerate(others, 1):
            copy = remote(small_own, small_full.at[z], ss.at[e], sr.at[S - e], {"z": zz})
            copy.start()
            tail.append(copy.wait_send)
            came = small_full.at[zz]
            arriving[None].append(remote(came, came, ss.at[e], sr.at[e], {"z": zz}).wait_recv)
    for t in range(1, nc + F + 3):
        if t < nc:
            z_first(t)
        for j in range(F):
            if 0 <= t - 1 - j < nc:
                z_next(t - 1 - j, j)
        for j in range(F):
            if 0 <= t - 2 - j < nc:
                xy_next(t - 2 - j, j)
        for j in range(F):
            if 0 <= t - 3 - j < nc:
                last(t - 3 - j, j)
        work(t, ready)
    for i in list(arriving):
        ready(i)
    for wait in tail:
        wait()


def gather_sems(n, nc, S):
    dma = pltpu.SemaphoreType.DMA
    F = S - 1
    return [
        dma((2 * n,)),
        dma((nc, F + 2)),
        dma((nc, S)),
        dma((nc, F, 3)),
        dma((nc, F, 3)),
        dma((nc, F, 3)),
        dma((nc, F, 3)),
        dma((nc, F)),
        dma((nc, F)),
        dma((S,)),
        dma((S,)),
    ]


def nt(a, b):
    return lax.dot_general(a, b, (((1,), (1,)), ((), ())), preferred_element_type=F32)

def nn(a, b):
    return lax.dot_general(a, b, (((1,), (0,)), ((), ())), preferred_element_type=F32)

def fill_bias(bias, q_ids, k_ids, first, rows, span):
    key = lax.broadcasted_iota(jnp.int32, (span, rows), 0)
    query = lax.broadcasted_iota(jnp.int32, (span, rows), 1)
    distance = query + WINDOW - key
    same = k_ids[pl.ds(first, span), :1] == q_ids[:1, pl.ds(first, rows)]
    allowed = (distance >= 0) & (distance < WINDOW) & same
    bias[...] = jnp.where(allowed, 0.0, -1e30)

def fwd_step(h, first, rows, q_ids, q_ref, k_ref, o_ref, l_ref, bias, vt):
    span = WINDOW + rows
    factor = HEAD**-0.5 * LOG2E
    cols = pl.ds(h * HEAD, HEAD)
    q = q_ref[pl.ds(first, rows), cols]
    s = nt(k_ref[pl.ds(first, span), :], q) * factor + bias[...]
    top = jnp.max(s, axis=0, keepdims=True)
    p = jnp.exp2(s - top)
    total = jnp.sum(p, axis=0, keepdims=True)
    o = nn(vt[:, pl.ds(first, span)], p.astype(BF))
    live = q_ids[:1, pl.ds(first, rows)] != 0
    o = jnp.where(live, o * (1.0 / total), 0.0)
    o_ref[pl.ds(first, rows), cols] = o.T.astype(BF)
    l_ref[h, :, pl.ds(first, rows)] = top + jnp.log2(total)


def fwd_kernel(heads, rows, q_ids, k_ids, q_ref, k_ref, v_ref, o_ref, l_ref, bias, vt):
    vt[...] = v_ref[...].T
    for first in range(0, q_ref.shape[0], rows):
        fill_bias(bias, q_ids, k_ids, first, rows, WINDOW + rows)
        for h in range(heads):
            fwd_step(h, first, rows, q_ids, q_ref, k_ref, o_ref, l_ref, bias, vt)


def norm_rows(source, gain, target):
    rows = 64

    @pl.loop(0, target.shape[0] // rows)
    def _(i):
        at = pl.ds(pl.multiple_of(i * rows, rows), rows)
        u = source[at, :].astype(F32)
        scale = lax.rsqrt(jnp.mean(u * u, axis=1, keepdims=True) + norm_eps)
        target[at, :] = (u * scale * gain).astype(target.dtype)


def turned(u, cos_ref, sin_ref):
    return u * cos_ref[...] + pltpu.roll(u, HEAD // 2, 1) * sin_ref[...]


def remote_copy(src, dst, send, receive, target):
    return pltpu.make_async_remote_copy(
        src_ref=src,
        dst_ref=dst,
        send_sem=send,
        recv_sem=receive,
        device_id=target,
        device_id_type=MESH_ID,
    )


def started(src, dst, sem):
    copy = pltpu.make_async_copy(src, dst, sem)
    copy.start()
    return copy


def forward_kernel(heads, chunks, S, *refs):
    own = refs[:4]
    small_own, x_ref, cos_ref, sin_ref, q_ids, k_ids = refs[4:10]
    full = refs[10:14]
    small_full, h1_ref, q_ref, k_out, v_out, o_ref, l_ref, mid_ref, h2_ref, h2_other = refs[14:24]
    w_in, w_out, gains, mix, kv, bias, vt, lds, hs, hr, h2_sems = refs[24:35]
    sems = refs[35:]
    z = lax.axis_index("z")
    c = lax.axis_index("c")
    piece = x_ref.shape[0]
    reach = kv.shape[0] // piece - 1
    half = w_in.shape[-1]
    D = x_ref.shape[1]
    own_rows = pl.ds(reach * piece, piece)
    kv[...] = jnp.zeros_like(kv)
    sent = []
    loads = {}

    def gain_row(i):
        return jnp.concatenate([gains[zz, i : i + 1, :] for zz in range(S)], axis=1).astype(F32)

    def start_norm(ready):
        ready(None)
        started(small_full, gains, lds.at[0]).wait()
        norm_rows(x_ref, gain_row(0), h1_ref)

    def start_project(ready):
        ready(0)
        for i in range(2):
            loads[i] = started(full[0].at[i], w_in.at[i], lds.at[1 + i])

    def project(i):
        loads.pop(i).wait()
        mix[...] = nn(h1_ref[...], w_in[i].reshape(D, half))
        for j in range(half // HEAD):
            h = i * (half // HEAD) + j
            u = mix[:, j * HEAD : (j + 1) * HEAD]
            if h < heads:
                q_ref[:, h * HEAD : (h + 1) * HEAD] = turned(u, cos_ref, sin_ref).astype(BF)
            elif h == heads:
                kv[own_rows, :HEAD] = turned(u, cos_ref, sin_ref).astype(BF)
            else:
                kv[own_rows, HEAD:] = u.astype(BF)

    def halo(d, starting):
        there = kv.at[pl.ds((reach - d) * piece, piece)]
        target = {"z": jnp.minimum(z + d, S - 1)}
        copy = remote_copy(kv.at[own_rows], there, hs.at[d - 1], hr.at[d - 1], target)

        @pl.when(z + d < S)
        def _():
            if starting:
                copy.start()
            else:
                copy.wait_send()

        if not starting:

            @pl.when(z >= d)
            def _():
                remote_copy(there, there, hs.at[d - 1], hr.at[d - 1], target).wait_recv()

    def start_attention():
        for d in range(1, reach + 1):
            halo(d, False)
        k_out[...] = kv[:, :HEAD]
        v_out[...] = kv[:, HEAD:]
        vt[...] = kv[:, HEAD:].T
        fill_bias(bias, q_ids, k_ids, 0, piece, WINDOW + piece)

    def attention(first, count):
        for h in range(first, first + count):
            fwd_step(h, 0, piece, q_ids, q_ref, k_out, o_ref, l_ref, bias, vt)

    def start_output(ready):
        ready(1)
        for i in range(2):
            loads[i] = started(full[1].at[i], w_out.at[i], lds.at[3 + i])

    def output():
        n = w_out.shape[-1]
        for i in range(2):
            loads.pop(i).wait()
            at = slice(i * n, (i + 1) * n)
            mid_ref[:, at] = x_ref[:, at].astype(F32) + nn(o_ref[...], w_out[i].reshape(D, n))

    def finish():
        norm_rows(mid_ref, gain_row(1), h2_ref)
        copy = remote_copy(h2_ref, h2_other, h2_sems.at[0], h2_sems.at[1], {"c": 1 - c})
        copy.start()
        sent.append(copy.wait)

    third = heads // 3
    plan = {
        2: lambda ready: start_norm(ready),
        5: lambda ready: start_project(ready),
        6: lambda ready: (project(0), project(1), [halo(d, True) for d in range(1, reach + 1)]),
        7: lambda ready: (start_attention(), attention(0, third), start_output(ready)),
        8: lambda ready: attention(third, third),
        9: lambda ready: attention(2 * third, third),
        10: lambda ready: output(),
        11: lambda ready: finish(),
    }

    def work(t, ready):
        if t in plan:
            plan[t](ready)

    gather_kernel(
        [True, True, True, False], chunks, S, own, full, sems, small_own, small_full, work
    )
    for wait in sent:
        wait()


def forward(own, small, x, cos, sin, q_ids, k_ids, heads, S, cid):
    piece, D = x.shape
    keys = k_ids.shape[0]
    r, gate_cols = own[3].shape[2:]
    rf = own[2].shape[3]
    half_in, half_out = own[0].shape[-1], own[1].shape[-1]
    chunks = [(0, 0, r, 0, half_in), (1, 0, r, 0, half_out)]
    chunks += [(2, i, 48, 0, half_out) for i in range(0, rf, 48)]
    chunks += [
        (3, i, 16, j, gate_cols // 2) for j in (0, gate_cols // 2) for i in range(0, r, 16)
    ]

    def body(*refs):
        forward_kernel(heads, chunks, S, *refs)

    def shape(*dims, dtype=BF):
        return jax.ShapeDtypeStruct(dims, dtype)

    outs = [shape(2, S, *o.shape[1:]) for o in own[:3]] + [shape(S, *own[3].shape)]
    outs += [
        shape(S, *small.shape),
        shape(piece, D),
        shape(piece, heads * HEAD),
        shape(keys, HEAD),
        shape(keys, HEAD),
        shape(piece, heads * HEAD),
        shape(heads, 1, piece, dtype=F32),
        shape(piece, D, dtype=F32),
        shape(piece, D),
        shape(piece, D),
    ]
    dma = pltpu.SemaphoreType.DMA
    return pl.pallas_call(
        body,
        out_shape=tuple(outs),
        in_specs=[VM] * 10,
        out_specs=tuple([ANY] * 5 + [VM] * 8 + [ANY]),
        scratch_shapes=[
            pltpu.VMEM((2, S) + own[0].shape[1:], BF),
            pltpu.VMEM((2, S) + own[1].shape[1:], BF),
            pltpu.VMEM((S,) + small.shape, BF),
            pltpu.VMEM((piece, half_in), F32),
            pltpu.VMEM((keys, 2 * HEAD), BF),
            pltpu.VMEM((keys, piece), F32),
            pltpu.VMEM((HEAD, keys), BF),
            dma((5,)),
            dma((2,)),
            dma((2,)),
            dma((2,)),
        ]
        + gather_sems(4, len(chunks), S),
        compiler_params=pltpu.CompilerParams(
            collective_id=cid, has_side_effects=True, vmem_limit_bytes=VMEM_BYTES
        ),
    )(*own, small, x, cos, sin, q_ids, k_ids)


def back_step(h, first, rows, refs, bias, kt):
    q_ref, k_ref, v_ref, o_ref, do_ref, l_ref, dq_ref, dk_ref, dv_ref = refs
    span = WINDOW + rows
    factor = HEAD**-0.5 * LOG2E
    cols = pl.ds(h * HEAD, HEAD)
    q = q_ref[pl.ds(first, rows), cols]
    do = do_ref[pl.ds(first, rows), cols]
    o = o_ref[pl.ds(first, rows), cols]
    delta = jnp.sum((do.astype(F32) * o.astype(F32)).T, axis=0, keepdims=True)
    s = nt(k_ref[pl.ds(first, span), :], q) * factor + bias[...]
    p = jnp.exp2(s - l_ref[h, :, pl.ds(first, rows)])
    dp = nt(v_ref[pl.ds(first, span), :], do)
    ds = (p * ((dp - delta) * HEAD**-0.5)).astype(BF)
    dv_ref[pl.ds(first, span), :] += nn(p.astype(BF), do)
    dk_ref[pl.ds(first, span), :] += nn(ds, q)
    dq_ref[pl.ds(first, rows), cols] = nn(kt[:, pl.ds(first, span)], ds).T


def bwd_kernel(heads, rows, q_ids, k_ids, *refs):
    *arrays, bias, kt = refs
    q_ref, k_ref = arrays[:2]
    dk_ref, dv_ref = arrays[-2:]
    kt[...] = k_ref[...].T
    dk_ref[...] = jnp.zeros_like(dk_ref)
    dv_ref[...] = jnp.zeros_like(dv_ref)
    for first in range(0, q_ref.shape[0], rows):
        fill_bias(bias, q_ids, k_ids, first, rows, WINDOW + rows)
        for h in range(heads):
            back_step(h, first, rows, arrays, bias, kt)


def attend(q_ids, k_ids, q, k, v, heads, rows):
    def body(*refs):
        fwd_kernel(heads, rows, *refs)

    return pl.pallas_call(
        body,
        out_shape=(
            jax.ShapeDtypeStruct(q.shape, BF),
            jax.ShapeDtypeStruct((heads, 1, q.shape[0]), F32),
        ),
        in_specs=[VM] * 5,
        out_specs=(VM, VM),
        scratch_shapes=[
            pltpu.VMEM((WINDOW + rows, rows), F32),
            pltpu.VMEM((HEAD, k.shape[0]), BF),
        ],
        compiler_params=pltpu.CompilerParams(vmem_limit_bytes=VMEM_BYTES),
        cost_estimate=pl.CostEstimate(
            flops=4 * q.size * k.shape[0], bytes_accessed=4 * q.size, transcendentals=q.size * 12
        ),
    )(q_ids, k_ids, q, k, v)


def attend_back(q_ids, k_ids, q, k, v, o, do, l, heads, rows):
    def body(*refs):
        bwd_kernel(heads, rows, *refs)

    return pl.pallas_call(
        body,
        out_shape=(
            jax.ShapeDtypeStruct(q.shape, F32),
            jax.ShapeDtypeStruct(k.shape, F32),
            jax.ShapeDtypeStruct(k.shape, F32),
        ),
        in_specs=[VM] * 8,
        out_specs=(VM, VM, VM),
        scratch_shapes=[
            pltpu.VMEM((WINDOW + rows, rows), F32),
            pltpu.VMEM((HEAD, k.shape[0]), BF),
        ],
        compiler_params=pltpu.CompilerParams(vmem_limit_bytes=VMEM_BYTES),
        cost_estimate=pl.CostEstimate(
            flops=10 * q.size * k.shape[0], bytes_accessed=12 * q.size, transcendentals=q.size * 12
        ),
    )(q_ids, k_ids, q, k, v, o, do, l)


def mlp_kernel(
    where, two_own, two_other, df_own, df_other, gate_ref, up_ref, down_ref, *results
):
    two_t, hid_t, grads, out, back = results
    step = pl.program_id(0)
    rows, D = two_own.shape
    half = down_ref.shape[2]
    part = two_t.shape[0]
    core = where[0]
    places = [
        pl.ds(pl.multiple_of(core * rows, rows), rows),
        pl.ds(pl.multiple_of((1 - core) * rows, rows), rows),
    ]

    @pl.when(step == 0)
    def _():
        out[...] = jnp.zeros_like(out)
        back[...] = jnp.zeros_like(back)

    @pl.when(step < D // part)
    def _():
        cols = pl.ds(pl.multiple_of(step * part, part), part)
        for two_ref, at in zip((two_own, two_other), places):
            two_t[:, at] = two_ref[:, cols].T

    for two_ref, df_ref, at in zip((two_own, two_other), (df_own, df_other), places):
        gate = nn(two_ref[...], gate_ref[...])
        up = nn(two_ref[...], up_ref[...])
        grad = nt(df_ref[:, :half], down_ref[0]) + nt(df_ref[:, half:], down_ref[1])
        slope = 0.7978845608028654
        bent = jnp.tanh(slope * (gate + 0.044715 * (gate * gate * gate)))
        upper = 0.5 * (1.0 + bent)
        act = gate * upper
        act_slope = upper + 0.5 * gate * (1.0 - bent * bent) * (
            slope * (1.0 + 3 * 0.044715 * (gate * gate))
        )
        hid = (act * up).astype(BF)
        grad_gate = (grad * up * act_slope).astype(BF)
        grad_up = (grad * act).astype(BF)
        hid_t[:, at] = hid.T
        grads[0, at, :] = grad_gate
        grads[1, at, :] = grad_up
        out[at, :half] += nn(hid, down_ref[0])
        out[at, half:] += nn(hid, down_ref[1])
        back[at, :] += nt(grad_gate, gate_ref[...]) + nt(grad_up, up_ref[...])


def mlp_call(core, two, df, gate_full, down_full):
    T, D = 2 * two[0].shape[0], two[0].shape[1]
    half_ff = gate_full.shape[1] // 2
    tile = 256
    tiles = half_ff // tile
    half = down_full.shape[2]
    last = D // tile - 1

    def body(*refs):
        mlp_kernel(*refs)

    once = pl.Buffered(1)
    piece = pl.BlockSpec((T // 2, D), lambda i, w: (0, 0), pipeline_mode=once)
    return pl.pallas_call(
        body,
        grid_spec=pltpu.PrefetchScalarGridSpec(
            num_scalar_prefetch=1,
            grid=(tiles,),
            in_specs=[
                piece,
                piece,
                piece,
                piece,
                pl.BlockSpec((D, tile), lambda i, w: (0, i)),
                pl.BlockSpec((D, tile), lambda i, w: (0, tiles + i)),
                pl.BlockSpec((2, tile, half), lambda i, w: (0, w[0] * tiles + i, 0)),
            ],
            out_specs=[
                pl.BlockSpec((tile, T), lambda i, w: (jnp.minimum(i, last), 0)),
                pl.BlockSpec((tile, T), lambda i, w: (i, 0)),
                pl.BlockSpec((2, T, tile), lambda i, w: (0, 0, i)),
                pl.BlockSpec((T, D), lambda i, w: (0, 0)),
                pl.BlockSpec((T, D), lambda i, w: (0, 0)),
            ],
        ),
        out_shape=[
            jax.ShapeDtypeStruct((D, T), BF),
            jax.ShapeDtypeStruct((half_ff, T), BF),
            jax.ShapeDtypeStruct((2, T, half_ff), BF),
            jax.ShapeDtypeStruct((T, D), F32),
            jax.ShapeDtypeStruct((T, D), F32),
        ],
        compiler_params=pltpu.CompilerParams(
            dimension_semantics=("arbitrary",), vmem_limit_bytes=VMEM_BYTES
        ),
        cost_estimate=pl.CostEstimate(
            flops=12 * T * D * half_ff, bytes_accessed=40 * 2**20, transcendentals=T * half_ff
        ),
    )(core, *two, *df, gate_full, gate_full, down_full)


def reduce_kernel(heads, sides, parts, S, two, hid_own, hid_other, flat, grads, df, da, *more):
    q_ids, k_ids, *given = more[:8]
    out, *found = more[8:12]
    left, right, tail_right, s1, g1, s2, g2, fz, gz, mine, bias, kt, *sems = more[12:]
    arrays = given + found
    rows = given[0].shape[0] // 2
    ts, lds, rds, s1s, s1r, s2s, s2r, zs, zr, ls, xs, xr, ys, yr, cs, cr = sems
    groups, _, _, r, T = left.shape
    n = right.shape[2]
    wide = sides * parts
    last = wide + groups - 1
    nc = last + 1
    slots = g1.shape[0]
    y, x, c, z = (lax.axis_index(a) for a in ("y", "x", "c", "z"))
    k = y * 2 + x
    kx = y * 2 + 1 - x
    ky = (1 - y) * 2 + x
    kxy = 3 - k
    to_x = {"x": 1 - x}
    to_y = {"y": 1 - y}
    to_c = {"c": 1 - c}
    loads = {}

    def fetch(key, src, dst, sem):
        copy = pltpu.make_async_copy(src, dst, sem)
        copy.start()
        loads.setdefault(key, []).append(copy)

    def fetch_left(g):
        for p in range(8):
            h, kk = p // 4, p % 4
            if g == 0:
                fetch(("l", 0), two.at[:, kk, h], left.at[0, p], lds.at[0, p, 0])
            elif g == groups:
                fetch(("l", g), flat.at[:, kk, h], left.at[0, p], lds.at[g, p, 0])
            else:
                for i, (src, cc) in enumerate(((hid_own, c), (hid_other, 1 - c))):
                    dst = left.at[g, p, pl.ds(cc * (S // 2), S // 2)]
                    fetch(("l", g), src.at[:, g - 1, kk, h], dst, lds.at[g, p, i])

    def slot_of(t):
        return t % 4 if t < wide else 4

    def fetch_right(t):
        if t < wide:
            src = grads.at[t // parts, :, pl.ds((t % parts) * n, n)]
            fetch(("r", t), src, right.at[t % 4], rds.at[t])
        elif t == wide:
            fetch(("r", t), df, right.at[4], rds.at[t])

    def landed(key):
        for copy in loads.pop(key, []):
            copy.wait()

    def group_of(t):
        return max(0, t - wide + 1)

    fetch_right(0)
    fetch_left(0)
    fetch_right(1)
    barrier = pltpu.get_barrier_semaphore()
    peers = [to_x, to_y, to_c] + [{"z": lax.rem(z + e, S)} for e in range(1, S)]
    for target in peers:
        pl.semaphore_signal(barrier, inc=1, device_id=target, device_id_type=MESH_ID)
    pl.semaphore_wait(barrier, len(peers))
    for g in range(1, groups):
        fetch_left(g)

    def remote(src, dst, s, r_, target):
        return pltpu.make_async_remote_copy(
            src_ref=src, dst_ref=dst, send_sem=s, recv_sem=r_, device_id=target, device_id_type=MESH_ID
        )

    def product(t, p):
        if t == last:
            return nn(left[0, p].reshape(S * r, T), tail_right[...])
        return nn(left[group_of(t), p].reshape(S * r, T), right[slot_of(t)])

    half_rows = da.shape[0]
    place = pl.ds(pl.multiple_of(c * half_rows, half_rows), half_rows)
    other_place = pl.ds(pl.multiple_of((1 - c) * half_rows, half_rows), half_rows)
    keep = pl.ds(pl.multiple_of(c * n, n), n)
    give = pl.ds(pl.multiple_of((1 - c) * n, n), n)
    fetch(("r", last), da.at[:, keep], tail_right.at[place], ts.at[0])
    given_copy = remote(da.at[:, give], tail_right.at[place], ts.at[1], ts.at[2], to_c)
    given_copy.start()
    other = tail_right.at[other_place]
    other_copy = remote(other, other, ts.at[1], ts.at[2], to_c)

    pending = {}

    def launch(key, copy):
        copy.start()
        pending.setdefault(key, []).append(copy)

    def drain(key):
        for copy in pending.pop(key, []):
            copy.wait_send()

    def first(t):
        slot = t % 2
        landed(("l", group_of(t)))
        landed(("r", t))
        if t == last:
            other_copy.wait_recv()
            given_copy.wait_send()
        drain(("s1", t - 2))

        for i in range(2):
            for j, p, target in ((i, i * 2 + 1 - x, to_x), (2 + i, 4 + (1 - y) * 2 + i, to_y)):
                s1[slot, j] = product(t, p).astype(BF)
                launch(("s1", t), remote(s1.at[slot, j], g1.at[t % slots, j], s1s.at[t, j], s1r.at[t, j], target))

    def got1(t, j):
        remote(g1.at[t % slots, j], g1.at[t % slots, j], s1s.at[t, j], s1r.at[t, j], to_x).wait_recv()

    def second(t):
        slot = t % 2
        drain(("s2", t - 2))
        for j in range(4):
            got1(t, j)
        for h, p, j, target in ((0, (1 - y) * 2 + x, 1 - y, to_y), (1, 4 + y * 2 + 1 - x, 3 - x, to_x)):
            s2[slot, h] = (product(t, p) + g1[t % slots, j].astype(F32)).astype(BF)
            launch(("s2", t), remote(s2.at[slot, h], g2.at[t % slots, h], s2s.at[t, h], s2r.at[t, h], target))

    def third(t):
        slot = t % 2
        drain(("z", t - 2))
        for h, p, j in ((0, k, y), (1, 4 + k, 2 + x)):
            remote(g2.at[t % slots, h], g2.at[t % slots, h], s2s.at[t, h], s2r.at[t, h], to_x).wait_recv()
            total = (product(t, p) + g1[t % slots, j].astype(F32) + g2[t % slots, h].astype(F32)).astype(BF)
            for zz in range(S):
                fz[slot, zz, h] = total[zz * r : (zz + 1) * r]
        for e in range(1, S):
            zz = lax.rem(z + e, S)
            launch(("z", t), remote(fz.at[slot, zz], gz.at[t, S - e - 1], zs.at[t, e - 1], zr.at[t, S - e - 1], {"z": zz}))

    def fourth(t):
        slot = t % 2
        drain(("ag", t - 2))
        for copy in pending.pop(("l", t - 2), []):
            copy.wait()
        for e in range(S - 1):
            remote(gz.at[t, e], gz.at[t, e], zs.at[t, e], zr.at[t, e], to_x).wait_recv()
        for h in range(2):
            total = fz[slot, z, h].astype(F32)
            for e in range(S - 1):
                total = total + gz[t, e, h].astype(F32)
            mine[slot, h] = total.astype(BF)
        copy = pltpu.make_async_copy(mine.at[slot], out.at[t, k, c], ls.at[t])
        copy.start()
        pending[("l", t)] = [copy]
        for h, s, r_, target in ((0, xs, xr, to_x), (1, ys, yr, to_y)):
            launch(("ag", t), remote(mine.at[slot, h], out.at[t, k, c, h], s.at[t, 0], r_.at[t, 0], target))
        for h, s, r_, target in ((0, ys, yr, to_y), (1, xs, xr, to_x)):
            launch(("ag", t), remote(mine.at[slot, h], out.at[t, k, c, h], s.at[t, 1], r_.at[t, 1], target))

    def land(t, kk, h, s, r_, j, target):
        p = out.at[t, kk, c, h]
        remote(p, p, s.at[t, j], r_.at[t, j], target).wait_recv()
        return p

    def fifth(t):
        p = land(t, kx, 0, xs, xr, 0, to_x)
        launch("end", remote(p, p, ys.at[t, 2], yr.at[t, 2], to_y))
        p = land(t, ky, 1, ys, yr, 0, to_y)
        launch("end", remote(p, p, xs.at[t, 2], xr.at[t, 2], to_x))

    def sixth(t):
        land(t, kx, 1, xs, xr, 1, to_x)
        land(t, ky, 0, ys, yr, 1, to_y)
        land(t, kxy, 1, xs, xr, 2, to_x)
        land(t, kxy, 0, ys, yr, 2, to_y)
        for copy in pending.pop(("l", t), []):
            copy.wait()
        p = out.at[t, :, c]
        launch("end", remote(p, p, cs.at[t], cr.at[t], to_c))

    steps = [(block, h) for block in range(2) for h in range(heads)]

    def attention(t):
        if t == 0:
            kt[...] = given[1][...].T
            found[1][...] = jnp.zeros_like(found[1])
            found[2][...] = jnp.zeros_like(found[2])
        for block, h in steps[2 * t : 2 * t + 2]:
            if h == 0:
                fill_bias(bias, q_ids, k_ids, block * rows, rows, WINDOW + rows)
            back_step(h, block * rows, rows, arrays, bias, kt)

    stages = (first, second, third, fourth, fifth, sixth)
    for t in range(nc + len(stages) - 1):
        for lag, stage in enumerate(stages):
            if 0 <= t - lag < nc:
                stage(t - lag)
            if lag == 0:
                attention(t)
        fetch_right(t + 2)
        if t == wide + 2:
            fetch_left(groups)
    for t in range(nc):
        p = out.at[t, :, 1 - c]
        remote(p, p, cs.at[t], cr.at[t], to_c).wait_recv()
    for key in list(pending):
        drain(key) if key[0] != "l" else [copy.wait() for copy in pending.pop(key)]


def reduced(two_t, hid_own, hid_other, flat_t, grads, df, da, attention, heads, S, cid):
    D, T = two_t.shape
    sides, _, half_ff = grads.shape
    n = df.shape[1]
    r = D // (S * 8)
    parts = half_ff // n
    groups = 1 + 2 * half_ff // (S * 8 * r)
    nc = sides * parts + groups
    slots = min(nc, 6)
    m = S * r
    queries, keys = attention[2:4]
    dma = pltpu.SemaphoreType.DMA
    hid_shape = (S // 2, groups - 1, 4, 2, r, T)

    def body(*refs):
        reduce_kernel(heads, sides, parts, S, *refs)

    return pl.pallas_call(
        body,
        out_shape=(
            jax.ShapeDtypeStruct((nc, 4, 2, 2, r, n), BF),
            jax.ShapeDtypeStruct(queries.shape, F32),
            jax.ShapeDtypeStruct(keys.shape, F32),
            jax.ShapeDtypeStruct(keys.shape, F32),
        ),
        in_specs=[ANY] * 7 + [VM] * 8,
        out_specs=(ANY, VM, VM, VM),
        scratch_shapes=[
            pltpu.VMEM((groups, 8, S, r, T), BF),
            pltpu.VMEM((5, T, n), BF),
            pltpu.VMEM((T, n), BF),
            pltpu.VMEM((2, 4, m, n), BF),
            pltpu.VMEM((slots, 4, m, n), BF),
            pltpu.VMEM((2, 2, m, n), BF),
            pltpu.VMEM((slots, 2, m, n), BF),
            pltpu.VMEM((2, S, 2, r, n), BF),
            pltpu.VMEM((nc, S - 1, 2, r, n), BF),
            pltpu.VMEM((2, 2, r, n), BF),
            pltpu.VMEM((WINDOW + queries.shape[0] // 2, queries.shape[0] // 2), F32),
            pltpu.VMEM((HEAD, keys.shape[0]), BF),
            dma((3,)),
            dma((groups + 1, 8, 2)),
            dma((nc,)),
            dma((nc, 4)),
            dma((nc, 4)),
            dma((nc, 2)),
            dma((nc, 2)),
            dma((nc, S)),
            dma((nc, S)),
            dma((nc,)),
            dma((nc, 3)),
            dma((nc, 3)),
            dma((nc, 3)),
            dma((nc, 3)),
            dma((nc,)),
            dma((nc,)),
        ],
        compiler_params=pltpu.CompilerParams(
            collective_id=cid, has_side_effects=True, vmem_limit_bytes=VMEM_BYTES
        ),
        cost_estimate=pl.CostEstimate(
            flops=4 * T * D * 3 * half_ff, bytes_accessed=400 * 2**20, transcendentals=0
        ),
    )(
        two_t.reshape(S, 4, 2, r, T),
        hid_own.reshape(hid_shape),
        hid_other.reshape(hid_shape),
        flat_t.reshape(S, 4, 2, r, T),
        grads,
        df,
        da,
        *attention,
    )


def adam_kernel(total, tiles, gains, count_ref, rates_ref, g_ref, w_ref, m_ref, g_out, w_out, m_out, *more):
    step_value = count_ref[0].astype(F32)
    log_first = jnp.log(jnp.full((8, 128), beta_first, F32))
    log_second = jnp.log(jnp.full((8, 128), beta_second, F32))
    unfix_first = (1.0 / (1.0 - jnp.exp(step_value * log_first)))[:1, :1]
    unfix_second = (1.0 / (1.0 - jnp.exp(step_value * log_second)))[:1, :1]
    rate, decay = rates_ref[0], rates_ref[1]
    rows = w_ref.shape[0]
    n = w_ref.shape[1] // tiles

    @pl.when((pl.program_id(1) == 0) & (pl.program_id(2) == 0))
    def _():
        more[0][...] = jnp.zeros_like(more[0])

    for i in range(tiles):
        at = pl.ds(i * n, n)
        grad = g_ref[i, 0, 0].reshape(rows, n).astype(F32) * (1.0 / total)
        w = w_ref[:, at]
        first = beta_first * m_ref[0, :, at] + (1.0 - beta_first) * grad
        second = beta_second * m_ref[1, :, at] + (1.0 - beta_second) * grad * grad
        step = first * unfix_first / (jnp.sqrt(second * unfix_second) + adam_eps) + decay * w
        g_out[:, at] = grad
        w_out[:, at] = w - rate * step
        m_out[0, :, at] = first
        m_out[1, :, at] = second
        if gains:
            both = w.astype(BF).astype(F32) * grad
            for j in range(0, n, 128):
                more[0][...] += both[:, j : j + 128]


def adam_call(
    weight, moments, grads, count, rates, total, base, sides, tiles, down=False, gains=False, cores=(0, 1), held=None
):
    _, _, _, _, r, n = grads.shape
    wide = 1 if down else tiles

    def g_place(kk, cc, ss, tt):
        return (base // wide + ss + tt, kk, cores[0] + cc, 0, 0, 0)

    def place(kk, cc, ss, tt):
        return (tt * 4 + kk, ss * 2 + cores[0] + cc)

    def m_place(*at):
        return (0,) + place(*at)

    w_spec = pl.BlockSpec((2 * r, wide * n), place)
    m_spec = pl.BlockSpec((2, 2 * r, wide * n), m_place)
    smem = pl.BlockSpec(memory_space=pltpu.SMEM)
    like = jax.ShapeDtypeStruct(weight.shape, F32)
    out_specs = [w_spec, w_spec, m_spec]
    out_shape = [like, like, jax.ShapeDtypeStruct(moments.shape, F32)]
    if gains:
        out_specs.append(pl.BlockSpec((2 * r, 128), lambda kk, cc, ss, tt: (kk, 0)))
        out_shape.append(jax.ShapeDtypeStruct((weight.shape[0], 128), F32))
    else:
        out_specs.append(pl.BlockSpec((8, 128), lambda *at: (0, 0)))
        out_shape.append(jax.ShapeDtypeStruct((8, 128), F32))
    before = [] if held is None else list(held[:3])

    def body(*refs):
        five, results = refs[:5], refs[5 + len(before) :]
        adam_kernel(total, wide, gains, *five, *results)

    return pl.pallas_call(
        body,
        grid=(4, len(cores), sides, tiles // wide),
        in_specs=[smem, smem, pl.BlockSpec((wide, 1, 1, 2, r, n), g_place), w_spec, m_spec]
        + [ANY] * len(before),
        out_specs=out_specs,
        out_shape=out_shape,
        input_output_aliases={5 + i: i for i in range(len(before))},
        compiler_params=pltpu.CompilerParams(
            dimension_semantics=("arbitrary",) * 4, vmem_limit_bytes=VMEM_BYTES
        ),
        cost_estimate=pl.CostEstimate(
            flops=10 * len(cores) * weight.size,
            bytes_accessed=15 * len(cores) * weight.size,
            transcendentals=weight.size,
        ),
    )(count, rates, grads, weight, moments, *before)


def dot(a, b):
    return jnp.dot(a, b, preferred_element_type=F32)


def dot_rows(a, b):
    return lax.dot_general(a, b, (((1,), (0,)), ((), ())), preferred_element_type=F32)


def dot_t(a, b):
    return lax.dot_general(a, b, (((1,), (1,)), ((), ())), preferred_element_type=F32)


def arranged(left, S):
    T, D = left.shape
    r = D // (S * 8)
    return left.T.reshape(S, 2, 2, 2, r, T).transpose(3, 1, 2, 0, 4, 5)


def plane_sum(rows, right, between, S):
    y = lax.axis_index("y")
    x = lax.axis_index("x")
    r, T = rows.shape[4:]
    N = right.shape[1]

    def pick(h, yy, xx):
        block = lax.dynamic_index_in_dim(rows[h], yy, 0, keepdims=False)
        return lax.dynamic_index_in_dim(block, xx, 0, keepdims=False).reshape(S * r, T)

    first0 = jnp.concatenate([pick(0, 0, 1 - x), pick(0, 1, 1 - x)], axis=0)
    first1 = jnp.concatenate([pick(1, 1 - y, 0), pick(1, 1 - y, 1)], axis=0)
    sent = (dot_rows(first0, right).astype(BF), dot_rows(first1, right).astype(BF))
    sent = between(0, sent)
    got0 = swapped(sent[0], "x")
    got1 = swapped(sent[1], "y")
    got0, got1 = between(1, (got0, got1))
    got0 = got0.reshape(2, S * r, N)
    got1 = got1.reshape(2, S * r, N)

    def at(got, i):
        return lax.dynamic_index_in_dim(got, i, 0, keepdims=False).astype(F32)

    sent = (
        (dot_rows(pick(0, 1 - y, x), right) + at(got0, 1 - y)).astype(BF),
        (dot_rows(pick(1, y, 1 - x), right) + at(got1, 1 - x)).astype(BF),
    )
    sent = between(2, sent)
    next0 = swapped(sent[0], "y")
    next1 = swapped(sent[1], "x")
    next0, next1 = between(3, (next0, next1))
    last0 = dot_rows(pick(0, y, x), right) + at(got0, y) + next0.astype(F32)
    last1 = dot_rows(pick(1, y, x), right) + at(got1, x) + next1.astype(F32)
    both = [v.astype(BF).reshape(S, 1, r, N) for v in (last0, last1)]
    return jnp.concatenate(both, axis=1).reshape(S, 2 * r, N)


def on_device(
    Y,
    S,
    block_in,
    cotangent,
    segment_ids,
    input_proj,
    output_proj,
    gate_up,
    down_weight,
    norm_gains,
    input_moments,
    output_moments,
    gate_moments,
    down_moments,
    gain_moments,
    update_count,
    optimizer_rates,
):
    seq_place = lax.axis_index("z")
    core = lax.axis_index("c")
    first_core = core == 0
    D = block_in.shape[-1]
    half_ff = FF // 2
    rows_d = input_proj.shape[0]
    rows_f = down_weight.shape[0]
    fast = Y == 2 and rows_d % 128 == 0
    in_half = input_proj.shape[1] // 2
    d_half = D // 2
    r = rows_d // 8

    in_low = input_proj.astype(BF)
    out_low = output_proj.astype(BF)
    down_low = down_weight.astype(BF)

    def halves(w):
        n = w.shape[1] // 2
        return jnp.stack([w[:, :n], w[:, n:]])

    gate_low = jnp.concatenate(
        [
            lax.dynamic_slice_in_dim(gate_up, side * FF + core * half_ff, half_ff, 1)
            for side in range(2)
        ],
        axis=1,
    ).astype(BF)

    gains_low = norm_gains.astype(BF)
    tokens = block_in[0].astype(F32)
    piece_len = tokens.shape[0]
    width_q = HEADS * HEAD
    positions = seq_place * piece_len + jnp.arange(piece_len, dtype=jnp.int32)
    reach_count = (WINDOW + piece_len - 2) // piece_len
    key_span = reach_count * piece_len
    segments = segment_ids[0]
    padded_ids = jnp.concatenate([jnp.full((key_span,), -1, jnp.int32), segments])
    query_ids = lax.dynamic_slice_in_dim(segments, seq_place * piece_len, piece_len)
    key_ids = lax.dynamic_slice_in_dim(padded_ids, seq_place * piece_len, key_span + piece_len)
    live_rows = query_ids != 0
    query_row = query_ids[None, :]
    key_column = key_ids[:, None]

    if fast:
        frequency = 10000.0 ** (-2.0 * jnp.arange(HEAD // 2).astype(F32) / HEAD)
        angles = positions.astype(F32)[:, None] * jnp.concatenate([frequency, frequency])[None, :]
        side = jnp.where(jnp.arange(HEAD) < HEAD // 2, -1.0, 1.0)
        cos_table, sin_table = jnp.cos(angles), jnp.sin(angles) * side
        (
            in_full,
            out_full,
            down_full,
            gate_full,
            gains_full,
            normed,
            queries,
            key_rows,
            values,
            flat_heads,
            log_totals,
            middle,
            normed_two,
            two_other,
        ) = forward(
            [
                halves(in_low).reshape(2, 4, 2, r, in_half),
                halves(out_low).reshape(2, 4, 2, r, d_half),
                halves(down_low).reshape(2, 4, 2, rows_f // 8, d_half),
                gate_low.reshape(4, 2, r, 2 * half_ff),
            ],
            jnp.concatenate([gains_low] * 8, axis=0),
            block_in[0],
            cos_table,
            sin_table,
            query_row,
            key_column,
            HEADS,
            S,
            0,
        )
        in_full = in_full.reshape(2, D, in_half)
        out_full = out_full.reshape(2, D, d_half)
        gains_full = gains_full[:, :2].transpose(1, 0, 2).reshape(2, D)
        down_full = down_full.reshape(2, FF, d_half)
        gate_full = gate_full.reshape(D, 2 * half_ff)
        gains_wide = gains_full.astype(F32)
    else:
        in_full = halves(lax.all_gather(in_low, "z", axis=0, tiled=True))
        out_full = halves(lax.all_gather(out_low, "z", axis=0, tiled=True))
        down_full = halves(lax.all_gather(down_low, "z", axis=0, tiled=True))
        gate_full = lax.all_gather(gate_low, "z", axis=0, tiled=True)
        gains_full = lax.all_gather(gains_low, "z", axis=1, tiled=True)
        gains_wide = gains_full.astype(F32)
        normed = root_norm(tokens, gains_wide[0]).astype(BF)
        mixed_proj = jnp.concatenate([dot(normed, in_full[0]), dot(normed, in_full[1])], axis=1)
        queries = (
            rotate(mixed_proj[:, :width_q].reshape(piece_len, HEADS, HEAD), positions, 1.0)
            .astype(BF)
            .reshape(piece_len, width_q)
        )
        own_keys = rotate(mixed_proj[:, width_q : width_q + HEAD], positions, 1.0)
        own_pair = jnp.concatenate([own_keys, mixed_proj[:, width_q + HEAD :]], axis=1).astype(BF)
        earlier = []
        for back_step in range(reach_count, 0, -1):
            earlier.append(passed_along(own_pair, "z", back_step))
        key_pairs = jnp.concatenate(earlier + [own_pair], axis=0)
        key_rows = key_pairs[:, :HEAD]
        values = key_pairs[:, HEAD:]
        flat_heads, log_totals = attend(
            query_row, key_column, queries, key_rows, values, HEADS, piece_len
        )
        middle = tokens + jnp.concatenate(
            [dot(flat_heads, out_full[0]), dot(flat_heads, out_full[1])], axis=1
        )
        normed_two = root_norm(middle, gains_wide[1]).astype(BF)
        two_other = swapped(normed_two, "c")

    upstream = cotangent[0].astype(F32)

    def ordered(mine, other):
        return jnp.concatenate(
            [jnp.where(first_core, mine, other), jnp.where(first_core, other, mine)], axis=0
        )

    def pair(v):
        return ordered(v, swapped(v, "c"))

    def half_pair(v):
        n = v.shape[1] // 2
        keep = lax.dynamic_slice_in_dim(v, core * n, n, 1)
        give = lax.dynamic_slice_in_dim(v, (1 - core) * n, n, 1)
        return ordered(keep, swapped(give, "c"))

    def core_sum(v):
        keep = lax.dynamic_slice_in_dim(v, core * piece_len, piece_len, 0)
        give = lax.dynamic_slice_in_dim(v, (1 - core) * piece_len, piece_len, 0)
        return keep + swapped(give.astype(BF), "c").astype(F32)

    df_other = swapped(cotangent[0], "c")
    df_both = ordered(cotangent[0], df_other)
    normed_both = pair(normed)
    flat_both = pair(flat_heads)

    two_t, hid_t, grad_gated, out_sum, two_sum = mlp_call(
        core.reshape(1).astype(jnp.int32),
        (normed_two, two_other),
        (cotangent[0], df_other),
        gate_full,
        down_full,
    )

    output = middle + core_sum(out_sum)
    block_out = output.astype(BF)[None]
    grad_normed_two = core_sum(two_sum)
    _, norm_pull_two = jax.vjp(root_norm, middle, gains_wide[1])
    grad_middle_norm, grad_gain_two = norm_pull_two(grad_normed_two)
    grad_middle = upstream + grad_middle_norm
    grad_branch = grad_middle.astype(BF)

    grad_flat = dot_t(grad_branch[:, :d_half], out_full[0]) + dot_t(
        grad_branch[:, d_half:], out_full[1]
    )
    grad_attended = jnp.where(live_rows[:, None], grad_flat, 0.0).astype(BF)

    attention = (
        query_row,
        key_column,
        queries,
        key_rows,
        values,
        flat_heads,
        grad_attended,
        log_totals,
    )
    if fast:
        df_half = lax.dynamic_slice_in_dim(df_both, core * d_half, d_half, 1)
        mlp_sums, grad_query_all, grad_keys, grad_values = reduced(
            two_t,
            hid_t,
            swapped(hid_t, "c"),
            flat_both.T,
            grad_gated,
            df_half,
            grad_branch,
            attention,
            HEADS,
            S,
            2,
        )
    else:
        grad_query_all, grad_keys, grad_values = attend_back(*attention, HEADS, piece_len // 2)
    grad_pairs = jnp.concatenate([grad_keys, grad_values], axis=1)
    own_grad = grad_pairs[key_span:]
    grad_pairs = grad_pairs.astype(BF)
    sent_rows = [
        grad_pairs[key_span - back_step * piece_len : key_span - (back_step - 1) * piece_len]
        for back_step in range(1, reach_count + 1)
    ]
    token_total = piece_len * S * Y * 4 * block_in.shape[0]
    rates = optimizer_rates
    done = {}

    def update(name, *arguments):
        wait, weight, moments, grads, *rest = arguments
        count, wait = lax.optimization_barrier((update_count, wait))
        done[name] = adam_call(
            weight, moments, grads, count, rates, float(token_total), *rest, held=done.get(name)
        )
        return wait

    def behind(name, arrays):
        arrays, token = lax.optimization_barrier((arrays, done[name][3]))
        done[name] = tuple(done[name][:3]) + (token,)
        return arrays

    tiles = half_ff // d_half
    chunk_out = 3 * tiles
    if fast:
        sent_rows = update(
            "out", sent_rows, output_proj, output_moments, mlp_sums, chunk_out, 1, 1
        )
    got_rows = [passed_along(rows, "z", -i - 1) for i, rows in enumerate(sent_rows)]
    if fast:
        got_rows = behind("out", got_rows)
    for rows in got_rows:
        own_grad = own_grad + rows.astype(F32)
    grad_query_raw = rotate(
        grad_query_all.reshape(piece_len, HEADS, HEAD), positions, -1.0
    ).reshape(piece_len, width_q)
    grad_key_raw = rotate(own_grad[:, :HEAD], positions, -1.0)
    grad_mixed = jnp.concatenate([grad_query_raw, grad_key_raw, own_grad[:, HEAD:]], axis=1).astype(
        BF
    )
    grad_normed = dot_t(grad_mixed[:, :in_half], in_full[0]) + dot_t(
        grad_mixed[:, in_half:], in_full[1]
    )
    _, norm_pull_one = jax.vjp(root_norm, tokens, gains_wide[0])
    grad_tokens_norm, grad_gain_one = norm_pull_one(grad_normed)
    block_in_grad = (grad_middle + grad_tokens_norm).astype(BF)[None]
    step_value = update_count[0].astype(F32)
    mixed_half = half_pair(grad_mixed)

    if fast:
        gains_two = []

        def gate_update(wait, which):
            wait = update(
                "gate", wait, gate_up, gate_moments, mlp_sums, 0, 2, tiles, False, True, (which,)
            )
            gains_two.append(done["gate"][3])
            return wait

        def between(i, arrays):
            if i == 0:
                return gate_update(arrays, 0)
            if i == 1:
                return behind("gate", arrays)
            return arrays

        share = plane_sum(arranged(normed_both, S), mixed_half, between, S)
        share = update(
            "down", share, down_weight, down_moments, mlp_sums, 2 * tiles, 1, tiles, True
        )
        mine = lax.psum_scatter(share, "z", scatter_dimension=0, tiled=False)
        mine = behind("down", mine)
        mine = gate_update(mine, 1)
        in_sum = lax.all_gather(mine, ("y", "x", "c"), axis=0)
        in_sum = behind("gate", in_sum).reshape(1, 4, 2, 2, r, in_half)
        update("in", in_sum, input_proj, input_moments, in_sum, 0, 1, 1, False, True)
        in_grad, in_new, in_mom, gain_one = done["in"]
        out_grad, out_new, out_mom, _ = done["out"]
        gate_grad, gate_new, gate_mom, _ = done["gate"]
        down_grad, down_new, down_mom, _ = done["down"]
        gain_grad = jnp.stack(
            [jnp.sum(v, axis=1) for v in (gain_one, gains_two[0] + gains_two[1])]
        ) / gains_low.astype(F32)
    else:

        def adam(weight, moments, grad):
            grad = grad.astype(F32) / token_total
            change, new = adamw_step(weight, moments, grad, step_value, rates)
            return grad, weight - change, new

        def summed(left, right):
            whole = dot_rows(left.T, right).astype(BF)
            mine = lax.psum_scatter(whole, "z", scatter_dimension=0, tiled=True)
            return lax.psum(mine, ("y", "x"))

        two_both = ordered(normed_two, two_other)
        grad_half = half_pair(grad_branch)
        gate_half = [summed(two_both, grad_gated[side]) for side in range(2)]
        gate_sum = jnp.concatenate(
            [lax.all_gather(g, "c", axis=1, tiled=True) for g in gate_half], axis=1
        )
        down_part = lax.psum(dot_rows(hid_t, df_both).astype(BF), ("y", "x"))
        down_part = lax.all_gather(down_part, "c", axis=0, tiled=True)
        down_sum = lax.psum_scatter(down_part, "z", scatter_dimension=0, tiled=True)
        out_total = lax.all_gather(summed(flat_both, grad_half), "c", axis=1, tiled=True)
        in_total = lax.all_gather(summed(normed_both, mixed_half), "c", axis=1, tiled=True)
        out_grad, out_new, out_mom = adam(output_proj, output_moments, out_total)
        in_grad, in_new, in_mom = adam(input_proj, input_moments, in_total)
        gate_grad, gate_new, gate_mom = adam(gate_up, gate_moments, gate_sum)
        down_grad, down_new, down_mom = adam(down_weight, down_moments, down_sum)
        gains_sum = lax.psum(jnp.stack([grad_gain_one, grad_gain_two]), ("y", "x", "c", "z"))
        gain_grad = lax.dynamic_slice_in_dim(gains_sum, seq_place * rows_d, rows_d, 1) / token_total
    gains_step, gain_moments_new = adamw_step(norm_gains, gain_moments, gain_grad, step_value, rates)
    return (
        block_out,
        block_in_grad,
        in_grad,
        out_grad,
        gate_grad,
        down_grad,
        gain_grad,
        in_new,
        out_new,
        gate_new,
        down_new,
        gains_step,
        in_mom,
        out_mom,
        gate_mom,
        down_mom,
        gain_moments_new,
    )


def solution(mesh):
    dp, S = mesh.shape["dp"], mesh.shape["seq"]
    Y = dp // 4
    grid = Mesh(mesh.devices.reshape(Y, 2, 2, S), ("y", "x", "c", "z"))
    data = ("y", "x", "c")
    tokens = P(data, "z", None)
    rows = P("z", None)
    moments = P(None, "z", None)
    in_specs = (
        (tokens, tokens, P(data, None))
        + (rows,) * 4
        + (P(None, "z"),)
        + (moments,) * 4
        + (P(None, None, "z"), P(), P())
    )
    out_specs = (
        (tokens, tokens)
        + (rows,) * 4
        + (P(None, "z"),)
        + (rows,) * 4
        + (P(None, "z"),)
        + (moments,) * 4
        + (P(None, None, "z"),)
    )

    def device_step(*arrays):
        return on_device(Y, S, *arrays)

    return jax.shard_map(
        device_step, mesh=grid, in_specs=in_specs, out_specs=out_specs, check_vma=False
    )
```

```python
import jax
import jax.numpy as jnp
from jax import lax
from jax.experimental import pallas as pl
from jax.experimental.pallas import tpu as pltpu
from jax.sharding import Mesh
from jax.sharding import PartitionSpec as P

HEADS = 12
HEAD = 128
FF = 4608
WINDOW = 1024


norm_eps = 1e-06
adam_eps = 1e-08
beta_first = 0.9
beta_second = 0.95
BF = jnp.bfloat16
F32 = jnp.float32
MESH_ID = pl.DeviceIdType.MESH
VMEM_BYTES = 60 * 1024 * 1024
BACKWARD_VMEM = 127 * 512 * 1024
ANY = pl.BlockSpec(memory_space=pl.ANY)
VM = pl.BlockSpec(memory_space=pltpu.VMEM)
LOG2E = 1.4426950408889634


def passed_along(block, axis, distance):
    devices = range(lax.axis_size(axis))
    route = [(i - distance, i) for i in devices if i - distance in devices]
    return lax.ppermute(block, axis, route)


def swapped(block, axis):
    return lax.ppermute(block, axis, [(0, 1), (1, 0)])


def rotate(values, positions, sign_value):
    half_width = values.shape[-1] // 2
    frequency = 10000.0 ** (-2.0 * jnp.arange(half_width).astype(jnp.float32) / values.shape[-1])
    angles = positions.astype(jnp.float32)[:, None] * frequency[None, :]
    cosine = jnp.cos(angles)
    sine_part = sign_value * jnp.sin(angles)
    if values.ndim == 3:
        cosine = cosine[:, None, :]
        sine_part = sine_part[:, None, :]
    lower_half = values[..., :half_width]
    upper_half = values[..., half_width:]
    return jnp.concatenate(
        [
            lower_half * cosine - upper_half * sine_part,
            upper_half * cosine + lower_half * sine_part,
        ],
        axis=-1,
    )


def root_norm(values, gain):
    return values * lax.rsqrt(jnp.mean(values * values, axis=-1, keepdims=True) + norm_eps) * gain


def adamw_step(weight, moments, grad, step_value, optimizer_rates):
    fix_first = 1.0 - beta_first**step_value
    fix_second = 1.0 - beta_second**step_value
    first_moment = beta_first * moments[0] + (1.0 - beta_first) * grad
    second = beta_second * moments[1] + (1.0 - beta_second) * grad * grad
    update = (
        first_moment / fix_first / (jnp.sqrt(second / fix_second) + adam_eps)
        + optimizer_rates[1] * weight
    )
    return (optimizer_rates[0] * update, jnp.stack([first_moment, second]))


def gather_kernel(shared, chunks, S, own, full, sems, small_own, small_full, work):
    n = len(shared)
    nc = len(chunks)
    F = S - 1
    loc, zs, zr, xs, xr, ys, yr, cs, cr, ss, sr = sems
    y, x, c, z = (lax.axis_index(a) for a in ("y", "x", "c", "z"))
    k = y * 2 + x
    kx = y * 2 + 1 - x
    ky = (1 - y) * 2 + x
    kxy = 3 - k
    to_x = {"x": 1 - x}
    to_y = {"y": 1 - y}
    to_c = {"c": 1 - c}
    low = z
    high = S - 1 - z
    near_count = jnp.minimum(low, high)
    above = jnp.minimum(z + 1, S - 1)
    below = jnp.maximum(z - 1, 0)
    blocks = []
    for j in range(F):
        near = j < 2 * near_count
        dist = jnp.where(near, j // 2 + 1, j - near_count + 1)
        sign = jnp.where(near, (j % 2) * 2 - 1, jnp.where(high > low, 1, -1))
        blocks.append((z + sign * dist, sign))
    barrier = pltpu.get_barrier_semaphore()
    others = [lax.rem(z + e, S) for e in range(1, S)]
    for target in [to_x, to_y, to_c] + [{"z": zz} for zz in others]:
        pl.semaphore_signal(barrier, inc=1, device_id=target, device_id_type=MESH_ID)
    pl.semaphore_wait(barrier, 3 + F)

    def own_half(i):
        return own[i].at[c] if shared[i] else own[i]

    def full_half(i):
        return full[i].at[c] if shared[i] else full[i]

    def box(q):
        _, r0, rn, c0, cn = chunks[q]
        return pl.ds(r0, rn), pl.ds(c0, cn)

    def part(ref, q, zz, kk, h=None):
        rr, cc = box(q)
        if h is None:
            return ref.at[zz, kk, :, rr, cc]
        return ref.at[zz, kk, h, rr, cc]

    def remote(src, dst, s, r, target):
        return pltpu.make_async_remote_copy(
            src_ref=src,
            dst_ref=dst,
            send_sem=s,
            recv_sem=r,
            device_id=target,
            device_id_type=MESH_ID,
        )

    tail = []
    local = []
    arriving = {i: [] for i in range(n)}
    arriving[None] = []
    finished = [0] * n
    for i in range(n):
        if shared[i]:
            for half in range(2):
                copy = pltpu.make_async_copy(
                    own[i].at[half], full[i].at[half, z], loc.at[len(local)]
                )
                local.append(copy)
                arriving[i].append(copy.wait)
        else:
            copy = pltpu.make_async_copy(own[i], full[i].at[z], loc.at[len(local)])
            local.append(copy)
            arriving[i].append(copy.wait)

    def z_first(q):
        i = chunks[q][0]
        rr, cc = box(q)
        src = own_half(i).at[k, :, rr, cc]
        dst = part(full_half(i), q, z, k)
        for ok, target, slot in ((z + 1 < S, above, F), (z > 0, below, F + 1)):

            def make(target=target, slot=slot):
                return remote(src, dst, zs.at[q, slot], zr.at[q, z], {"z": target})

            @pl.when(ok)
            def _(make=make):
                make().start()

            def finish(ok=ok, make=make):
                @pl.when(ok)
                def _():
                    make().wait_send()

            tail.append(finish)

    def z_next(q, j):
        zz, sign = blocks[j]
        held = full_half(chunks[q][0])
        piece = part(held, q, zz, k)
        remote(piece, piece, zs.at[q, j], zr.at[q, zz], {"z": above}).wait_recv()
        onward = z - sign
        ok = (onward >= 0) & (onward < S)
        target = jnp.clip(onward, 0, S - 1)

        def make():
            return remote(piece, piece, zs.at[q, j], zr.at[q, zz], {"z": target})

        @pl.when(ok)
        def _():
            make().start()

        def finish():
            @pl.when(ok)
            def _():
                make().wait_send()

        tail.append(finish)
        for h, s, r, target in ((0, xs, xr, to_x), (1, ys, yr, to_y)):
            p = part(held, q, zz, k, h)
            copy = remote(p, p, s.at[q, j, 0], r.at[q, j, 0], target)
            copy.start()
            tail.append(copy.wait_send)
        for h, s, r, target in ((0, ys, yr, to_y), (1, xs, xr, to_x)):
            p = part(held, q, zz, k, h)
            copy = remote(p, p, s.at[q, j, 1], r.at[q, j, 1], target)
            copy.start()
            tail.append(copy.wait_send)

    def xy_next(q, j):
        zz, _ = blocks[j]
        held = full_half(chunks[q][0])
        p = part(held, q, zz, kx, 0)
        remote(p, p, xs.at[q, j, 0], xr.at[q, j, 0], to_x).wait_recv()
        copy = remote(p, p, ys.at[q, j, 2], yr.at[q, j, 2], to_y)
        copy.start()
        tail.append(copy.wait_send)
        p = part(held, q, zz, ky, 1)
        remote(p, p, ys.at[q, j, 0], yr.at[q, j, 0], to_y).wait_recv()
        copy = remote(p, p, xs.at[q, j, 2], xr.at[q, j, 2], to_x)
        copy.start()
        tail.append(copy.wait_send)

    def last(q, j):
        i = chunks[q][0]
        rr, cc = box(q)
        zz, _ = blocks[j]
        held = full_half(i)
        finished[i] += 1
        for kk, h, s, r, slot, target in (
            (kx, 1, xs, xr, 1, to_x),
            (ky, 0, ys, yr, 1, to_y),
            (kxy, 1, xs, xr, 2, to_x),
            (kxy, 0, ys, yr, 2, to_y),
        ):
            p = part(held, q, zz, kk, h)
            remote(p, p, s.at[q, j, slot], r.at[q, j, slot], target).wait_recv()
        if shared[i]:
            p = held.at[zz, :, :, rr, cc]
            copy = remote(p, p, cs.at[q, j], cr.at[q, j], to_c)
            copy.start()
            tail.append(copy.wait_send)
            other = full[i].at[1 - c].at[zz, :, :, rr, cc]

            def finish():
                remote(other, other, cs.at[q, j], cr.at[q, j], to_c).wait_recv()

            arriving[i].append(finish)

    def ready(i):
        if i is not None:
            assert finished[i] == F * sum(chunk[0] == i for chunk in chunks)
        for wait in arriving.pop(i, []):
            wait()

    z_first(0)
    for copy in local:
        copy.start()
    if small_own is not None:
        place = pltpu.make_async_copy(small_own, small_full.at[z], ss.at[0])
        place.start()
        arriving[None].append(place.wait)
        for e, zz in enumerate(others, 1):
            copy = remote(small_own, small_full.at[z], ss.at[e], sr.at[S - e], {"z": zz})
            copy.start()
            tail.append(copy.wait_send)
            came = small_full.at[zz]
            arriving[None].append(remote(came, came, ss.at[e], sr.at[e], {"z": zz}).wait_recv)
    for t in range(1, nc + F + 3):
        if t < nc:
            z_first(t)
        for j in range(F):
            if 0 <= t - 1 - j < nc:
                z_next(t - 1 - j, j)
        for j in range(F):
            if 0 <= t - 2 - j < nc:
                xy_next(t - 2 - j, j)
        for j in range(F):
            if 0 <= t - 3 - j < nc:
                last(t - 3 - j, j)
        work(t, ready)
    for i in list(arriving):
        ready(i)
    for wait in tail:
        wait()


def gather_sems(n, nc, S):
    dma = pltpu.SemaphoreType.DMA
    F = S - 1
    return [
        dma((2 * n,)),
        dma((nc, F + 2)),
        dma((nc, S)),
        dma((nc, F, 3)),
        dma((nc, F, 3)),
        dma((nc, F, 3)),
        dma((nc, F, 3)),
        dma((nc, F)),
        dma((nc, F)),
        dma((S,)),
        dma((S,)),
    ]


def nt(a, b):
    return lax.dot_general(a, b, (((1,), (1,)), ((), ())), preferred_element_type=F32)

def nn(a, b):
    return lax.dot_general(a, b, (((1,), (0,)), ((), ())), preferred_element_type=F32)

def fill_bias(bias, q_ids, k_ids, first, rows, span):
    key = lax.broadcasted_iota(jnp.int32, (span, rows), 0)
    query = lax.broadcasted_iota(jnp.int32, (span, rows), 1)
    distance = query + WINDOW - key
    same = k_ids[pl.ds(first, span), :1] == q_ids[:1, pl.ds(first, rows)]
    allowed = (distance >= 0) & (distance < WINDOW) & same
    bias[...] = jnp.where(allowed, 0.0, -1e30)

def fwd_step(h, first, rows, q_ids, q_ref, k_ref, o_ref, l_ref, bias, vt):
    span = WINDOW + rows
    factor = HEAD**-0.5 * LOG2E
    cols = pl.ds(h * HEAD, HEAD)
    q = q_ref[pl.ds(first, rows), cols]
    s = nt(k_ref[pl.ds(first, span), :], q) * factor + bias[...]
    top = jnp.max(s, axis=0, keepdims=True)
    p = jnp.exp2(s - top)
    total = jnp.sum(p, axis=0, keepdims=True)
    o = nn(vt[:, pl.ds(first, span)], p.astype(BF))
    live = q_ids[:1, pl.ds(first, rows)] != 0
    o = jnp.where(live, o * (1.0 / total), 0.0)
    o_ref[pl.ds(first, rows), cols] = o.T.astype(BF)
    l_ref[h, :, pl.ds(first, rows)] = top + jnp.log2(total)


def fwd_kernel(heads, rows, q_ids, k_ids, q_ref, k_ref, v_ref, o_ref, l_ref, bias, vt):
    vt[...] = v_ref[...].T
    for first in range(0, q_ref.shape[0], rows):
        fill_bias(bias, q_ids, k_ids, first, rows, WINDOW + rows)
        for h in range(heads):
            fwd_step(h, first, rows, q_ids, q_ref, k_ref, o_ref, l_ref, bias, vt)


def norm_rows(source, gain, target):
    rows = 64

    @pl.loop(0, target.shape[0] // rows)
    def _(i):
        at = pl.ds(pl.multiple_of(i * rows, rows), rows)
        u = source[at, :].astype(F32)
        scale = lax.rsqrt(jnp.mean(u * u, axis=1, keepdims=True) + norm_eps)
        target[at, :] = (u * scale * gain).astype(target.dtype)


def turned(u, cos_ref, sin_ref):
    return u * cos_ref[...] + pltpu.roll(u, HEAD // 2, 1) * sin_ref[...]


def remote_copy(src, dst, send, receive, target):
    return pltpu.make_async_remote_copy(
        src_ref=src,
        dst_ref=dst,
        send_sem=send,
        recv_sem=receive,
        device_id=target,
        device_id_type=MESH_ID,
    )


def started(src, dst, sem):
    copy = pltpu.make_async_copy(src, dst, sem)
    copy.start()
    return copy


def forward_kernel(heads, chunks, S, *refs):
    own = refs[:4]
    small_own, x_ref, cos_ref, sin_ref, q_ids, k_ids = refs[4:10]
    full = refs[10:14]
    small_full, h1_ref, q_ref, k_out, v_out, o_ref, l_ref, mid_ref, h2_ref, h2_other = refs[14:24]
    h1_t, h1_t_other, o_t, o_t_other = refs[24:28]
    w_in, w_out, gains, mix, kv, bias, vt, lds, hs, hr, h2_sems = refs[28:39]
    sems = refs[39:]
    z = lax.axis_index("z")
    c = lax.axis_index("c")
    piece = x_ref.shape[0]
    reach = kv.shape[0] // piece - 1
    half = w_in.shape[-1]
    D = x_ref.shape[1]
    own_rows = pl.ds(reach * piece, piece)
    kv[...] = jnp.zeros_like(kv)
    sent = []
    loads = {}

    def gain_row(i):
        return jnp.concatenate([gains[zz, i : i + 1, :] for zz in range(S)], axis=1).astype(F32)

    def start_norm(ready):
        ready(None)
        started(small_full, gains, lds.at[0]).wait()
        norm_rows(x_ref, gain_row(0), h1_ref)

    def start_project(ready):
        ready(0)
        for i in range(2):
            loads[i] = started(full[0].at[i], w_in.at[i], lds.at[1 + i])

    def project(i):
        loads.pop(i).wait()
        mix[...] = nn(h1_ref[...], w_in[i].reshape(D, half))
        for j in range(half // HEAD):
            h = i * (half // HEAD) + j
            u = mix[:, j * HEAD : (j + 1) * HEAD]
            if h < heads:
                q_ref[:, h * HEAD : (h + 1) * HEAD] = turned(u, cos_ref, sin_ref).astype(BF)
            elif h == heads:
                kv[own_rows, :HEAD] = turned(u, cos_ref, sin_ref).astype(BF)
            else:
                kv[own_rows, HEAD:] = u.astype(BF)

    def halo(d, starting):
        there = kv.at[pl.ds((reach - d) * piece, piece)]
        target = {"z": jnp.minimum(z + d, S - 1)}
        copy = remote_copy(kv.at[own_rows], there, hs.at[d - 1], hr.at[d - 1], target)

        @pl.when(z + d < S)
        def _():
            if starting:
                copy.start()
            else:
                copy.wait_send()

        if not starting:

            @pl.when(z >= d)
            def _():
                remote_copy(there, there, hs.at[d - 1], hr.at[d - 1], target).wait_recv()

    def start_attention():
        for d in range(1, reach + 1):
            halo(d, False)
        k_out[...] = kv[:, :HEAD]
        v_out[...] = kv[:, HEAD:]
        vt[...] = kv[:, HEAD:].T
        fill_bias(bias, q_ids, k_ids, 0, piece, WINDOW + piece)

    def attention(first, count):
        for h in range(first, first + count):
            fwd_step(h, 0, piece, q_ids, q_ref, k_out, o_ref, l_ref, bias, vt)

    def start_output(ready):
        ready(1)
        for i in range(2):
            loads[i] = started(full[1].at[i], w_out.at[i], lds.at[3 + i])

    def output():
        n = w_out.shape[-1]
        for i in range(2):
            loads.pop(i).wait()
            at = slice(i * n, (i + 1) * n)
            mid_ref[:, at] = x_ref[:, at].astype(F32) + nn(o_ref[...], w_out[i].reshape(D, n))

    def finish():
        norm_rows(mid_ref, gain_row(1), h2_ref)
        to_partner(h2_ref, h2_other, 0)

    def to_partner(src, dst, i):
        copy = remote_copy(src, dst, h2_sems.at[2 * i], h2_sems.at[2 * i + 1], {"c": 1 - c})
        copy.start()
        sent.append(copy.wait)

    def transpose(src, dst, there, i):
        for j in range(0, D, HEAD):
            dst[j : j + HEAD, :] = src[:, j : j + HEAD].T
        to_partner(dst, there, i)

    third = heads // 3
    plan = {
        2: lambda ready: start_norm(ready),
        5: lambda ready: start_project(ready),
        6: lambda ready: (project(0), project(1), [halo(d, True) for d in range(1, reach + 1)]),
        7: lambda ready: (start_attention(), attention(0, third), start_output(ready)),
        8: lambda ready: attention(third, third),
        9: lambda ready: attention(2 * third, third),
        10: lambda ready: output(),
        11: lambda ready: (finish(), transpose(h1_ref, h1_t, h1_t_other, 1)),
        12: lambda ready: transpose(o_ref, o_t, o_t_other, 2),
    }

    def work(t, ready):
        if t in plan:
            plan[t](ready)

    gather_kernel(
        [True, True, True, False], chunks, S, own, full, sems, small_own, small_full, work
    )
    for wait in sent:
        wait()


def forward(own, small, x, cos, sin, q_ids, k_ids, heads, S, cid):
    piece, D = x.shape
    keys = k_ids.shape[0]
    r, gate_cols = own[3].shape[2:]
    rf = own[2].shape[3]
    half_in, half_out = own[0].shape[-1], own[1].shape[-1]
    chunks = [(0, 0, r, 0, half_in), (1, 0, r, 0, half_out)]
    chunks += [(2, i, 48, 0, half_out) for i in range(0, rf, 48)]
    chunks += [
        (3, i, 16, j, gate_cols // 2) for j in (0, gate_cols // 2) for i in range(0, r, 16)
    ]

    def body(*refs):
        forward_kernel(heads, chunks, S, *refs)

    def shape(*dims, dtype=BF):
        return jax.ShapeDtypeStruct(dims, dtype)

    outs = [shape(2, S, *o.shape[1:]) for o in own[:3]] + [shape(S, *own[3].shape)]
    outs += [
        shape(S, *small.shape),
        shape(piece, D),
        shape(piece, heads * HEAD),
        shape(keys, HEAD),
        shape(keys, HEAD),
        shape(piece, heads * HEAD),
        shape(heads, 1, piece, dtype=F32),
        shape(piece, D, dtype=F32),
        shape(piece, D),
        shape(piece, D),
        shape(D, piece),
        shape(D, piece),
        shape(D, piece),
        shape(D, piece),
    ]
    dma = pltpu.SemaphoreType.DMA
    return pl.pallas_call(
        body,
        out_shape=tuple(outs),
        in_specs=[VM] * 10,
        out_specs=tuple([ANY] * 5 + [VM] * 8 + [ANY] + [VM, ANY] * 2),
        scratch_shapes=[
            pltpu.VMEM((2, S) + own[0].shape[1:], BF),
            pltpu.VMEM((2, S) + own[1].shape[1:], BF),
            pltpu.VMEM((S,) + small.shape, BF),
            pltpu.VMEM((piece, half_in), F32),
            pltpu.VMEM((keys, 2 * HEAD), BF),
            pltpu.VMEM((keys, piece), F32),
            pltpu.VMEM((HEAD, keys), BF),
            dma((5,)),
            dma((2,)),
            dma((2,)),
            dma((6,)),
        ]
        + gather_sems(4, len(chunks), S),
        compiler_params=pltpu.CompilerParams(
            collective_id=cid, has_side_effects=True, vmem_limit_bytes=VMEM_BYTES
        ),
    )(*own, small, x, cos, sin, q_ids, k_ids)


def back_step(h, first, rows, refs, bias, kt, finish):
    q_ref, k_ref, v_ref, o_ref, do_ref, l_ref, dq_ref, dk_ref, dv_ref = refs
    span = WINDOW + rows
    factor = HEAD**-0.5 * LOG2E
    cols = pl.ds(h * HEAD, HEAD)
    q = q_ref[pl.ds(first, rows), cols]
    do = do_ref[pl.ds(first, rows), cols]
    o = o_ref[pl.ds(first, rows), cols]
    delta = jnp.sum((do.astype(F32) * o.astype(F32)).T, axis=0, keepdims=True)
    s = nt(k_ref[pl.ds(first, span), :], q) * factor + bias[...]
    p = jnp.exp2(s - l_ref[h, :, pl.ds(first, rows)])
    dp = nt(v_ref[pl.ds(first, span), :], do)
    ds = (p * ((dp - delta) * HEAD**-0.5)).astype(BF)
    dv_ref[pl.ds(first, span), :] += nn(p.astype(BF), do)
    dk_ref[pl.ds(first, span), :] += nn(ds, q)
    dq = nn(kt[:, pl.ds(first, span)], ds).T
    dq_ref[pl.ds(first, rows), cols] = finish(dq, first).astype(dq_ref.dtype)


def bwd_kernel(heads, rows, q_ids, k_ids, *refs):
    *arrays, bias, kt = refs
    q_ref, k_ref = arrays[:2]
    dk_ref, dv_ref = arrays[-2:]
    kt[...] = k_ref[...].T
    dk_ref[...] = jnp.zeros_like(dk_ref)
    dv_ref[...] = jnp.zeros_like(dv_ref)
    for first in range(0, q_ref.shape[0], rows):
        fill_bias(bias, q_ids, k_ids, first, rows, WINDOW + rows)
        for h in range(heads):
            back_step(h, first, rows, arrays, bias, kt, lambda dq, first: dq)


def attend(q_ids, k_ids, q, k, v, heads, rows):
    def body(*refs):
        fwd_kernel(heads, rows, *refs)

    return pl.pallas_call(
        body,
        out_shape=(
            jax.ShapeDtypeStruct(q.shape, BF),
            jax.ShapeDtypeStruct((heads, 1, q.shape[0]), F32),
        ),
        in_specs=[VM] * 5,
        out_specs=(VM, VM),
        scratch_shapes=[
            pltpu.VMEM((WINDOW + rows, rows), F32),
            pltpu.VMEM((HEAD, k.shape[0]), BF),
        ],
        compiler_params=pltpu.CompilerParams(vmem_limit_bytes=VMEM_BYTES),
        cost_estimate=pl.CostEstimate(
            flops=4 * q.size * k.shape[0], bytes_accessed=4 * q.size, transcendentals=q.size * 12
        ),
    )(q_ids, k_ids, q, k, v)


def attend_back(q_ids, k_ids, q, k, v, o, do, l, heads, rows):
    def body(*refs):
        bwd_kernel(heads, rows, *refs)

    return pl.pallas_call(
        body,
        out_shape=(
            jax.ShapeDtypeStruct(q.shape, F32),
            jax.ShapeDtypeStruct(k.shape, F32),
            jax.ShapeDtypeStruct(k.shape, F32),
        ),
        in_specs=[VM] * 8,
        out_specs=(VM, VM, VM),
        scratch_shapes=[
            pltpu.VMEM((WINDOW + rows, rows), F32),
            pltpu.VMEM((HEAD, k.shape[0]), BF),
        ],
        compiler_params=pltpu.CompilerParams(vmem_limit_bytes=VMEM_BYTES),
        cost_estimate=pl.CostEstimate(
            flops=10 * q.size * k.shape[0], bytes_accessed=12 * q.size, transcendentals=q.size * 12
        ),
    )(q_ids, k_ids, q, k, v, o, do, l)


def mlp_kernel(
    where, two_own, two_other, df_own, df_other, gate_ref, up_ref, down_ref, *results
):
    two_t, hid_t, grads, out_low, back_low, out, back = results
    step = pl.program_id(0)
    rows, D = two_own.shape
    half = down_ref.shape[2]
    part = two_t.shape[0]
    core = where[0]
    places = [
        pl.ds(pl.multiple_of(core * rows, rows), rows),
        pl.ds(pl.multiple_of((1 - core) * rows, rows), rows),
    ]

    @pl.when(step == 0)
    def _():
        out[...] = jnp.zeros_like(out)
        back[...] = jnp.zeros_like(back)

    @pl.when(step < D // part)
    def _():
        cols = pl.ds(pl.multiple_of(step * part, part), part)
        for two_ref, at in zip((two_own, two_other), places):
            two_t[:, at] = two_ref[:, cols].T

    for two_ref, df_ref, at in zip((two_own, two_other), (df_own, df_other), places):
        gate = nn(two_ref[...], gate_ref[...])
        up = nn(two_ref[...], up_ref[...])
        grad = nt(df_ref[:, :half], down_ref[0]) + nt(df_ref[:, half:], down_ref[1])
        slope = 0.7978845608028654
        bent = jnp.tanh(slope * (gate + 0.044715 * (gate * gate * gate)))
        upper = 0.5 * (1.0 + bent)
        act = gate * upper
        act_slope = upper + 0.5 * gate * (1.0 - bent * bent) * (
            slope * (1.0 + 3 * 0.044715 * (gate * gate))
        )
        hid = (act * up).astype(BF)
        grad_gate = (grad * up * act_slope).astype(BF)
        grad_up = (grad * act).astype(BF)
        hid_t[:, at] = hid.T
        grads[0, at, :] = grad_gate
        grads[1, at, :] = grad_up
        out[at, :half] += nn(hid, down_ref[0])
        out[at, half:] += nn(hid, down_ref[1])
        back[at, :] += nt(grad_gate, gate_ref[...]) + nt(grad_up, up_ref[...])

    @pl.when(step == pl.num_programs(0) - 1)
    def _():
        out_low[...] = out[...].astype(BF)
        back_low[...] = back[...].astype(BF)


def mlp_call(core, two, df, gate_full, down_full):
    T, D = 2 * two[0].shape[0], two[0].shape[1]
    half_ff = gate_full.shape[1] // 2
    tile = 256
    tiles = half_ff // tile
    half = down_full.shape[2]
    last = D // tile - 1

    def body(*refs):
        mlp_kernel(*refs)

    once = pl.Buffered(1)
    piece = pl.BlockSpec((T // 2, D), lambda i, w: (0, 0), pipeline_mode=once)
    return pl.pallas_call(
        body,
        grid_spec=pltpu.PrefetchScalarGridSpec(
            num_scalar_prefetch=1,
            grid=(tiles,),
            in_specs=[
                piece,
                piece,
                piece,
                piece,
                pl.BlockSpec((D, tile), lambda i, w: (0, i)),
                pl.BlockSpec((D, tile), lambda i, w: (0, tiles + i)),
                pl.BlockSpec((2, tile, half), lambda i, w: (0, w[0] * tiles + i, 0)),
            ],
            out_specs=[
                pl.BlockSpec((tile, T), lambda i, w: (jnp.minimum(i, last), 0)),
                pl.BlockSpec((tile, T), lambda i, w: (i, 0)),
                pl.BlockSpec((2, T, tile), lambda i, w: (0, 0, i)),
                pl.BlockSpec((T, D), lambda i, w: (0, 0)),
                pl.BlockSpec((T, D), lambda i, w: (0, 0)),
            ],
            scratch_shapes=[pltpu.VMEM((T, D), F32), pltpu.VMEM((T, D), F32)],
        ),
        out_shape=[
            jax.ShapeDtypeStruct((D, T), BF),
            jax.ShapeDtypeStruct((half_ff, T), BF),
            jax.ShapeDtypeStruct((2, T, half_ff), BF),
            jax.ShapeDtypeStruct((T, D), BF),
            jax.ShapeDtypeStruct((T, D), BF),
        ],
        compiler_params=pltpu.CompilerParams(
            dimension_semantics=("arbitrary",), vmem_limit_bytes=VMEM_BYTES
        ),
        cost_estimate=pl.CostEstimate(
            flops=12 * T * D * half_ff, bytes_accessed=40 * 2**20, transcendentals=T * half_ff
        ),
    )(core, *two, *df, gate_full, gate_full, down_full)


def split_widths(total, most):
    first = -(-total // 256) * 128
    assert first <= most
    return (first, total - first)


def backward_kernel(heads, sides, parts, S, *refs):
    two, hid, *flats = refs[:6]
    flat_own, flat_other, norm_own, norm_other = flats[2], flats[3], flats[0], flats[1]
    grads, dy_own, dy_other, back, middle, w_out, gains_ref = refs[6:13]
    q_ids, k_ids, q_ref, k_ref, v_ref, o_ref, l_ref, cos_ref, sin_ref = refs[13:22]
    out, hid_land, dx_out, mixed = refs[22:26]
    left, right, out_right, mix_right, s1, g1, s2, g2, fz, gz, mine, da, do, got, tails, landed_tails, gains = refs[26:43]
    x1, dk, dv, bias, kt = refs[43:48]
    lds, rds, fs, cs_in, hs, hr, s1s, s1r, s2s, s2r, zs, zr, ls, xs, xr, ys, yr, cs, cr = refs[48:]
    _, _, _, r, T = left.shape
    n = right.shape[2]
    piece, D = da.shape
    reach = tails.shape[0]
    wide = sides * parts
    rows_groups = hid.shape[1]
    chunk_out = wide + rows_groups
    mix_half = mix_right.shape[1]
    widths = [n] * (chunk_out + 1) + list(split_widths(mix_half, n))
    nc = len(widths)
    left_slots = left.shape[0]
    right_slots = right.shape[0]
    slots = g1.shape[0]
    y, x, c, z = (lax.axis_index(a) for a in ("y", "x", "c", "z"))
    k = y * 2 + x
    kx = y * 2 + 1 - x
    ky = (1 - y) * 2 + x
    kxy = 3 - k
    to_x = {"x": 1 - x}
    to_y = {"y": 1 - y}
    to_c = {"c": 1 - c}
    place = pl.ds(pl.multiple_of(c * piece, piece), piece)
    other_place = pl.ds(pl.multiple_of((1 - c) * piece, piece), piece)
    loads = {}
    pending = {}

    def fetch(key, src, dst, sem):
        loads.setdefault(key, []).append(started(src, dst, sem))

    def landed(key):
        for copy in loads.pop(key, []):
            copy.wait()

    def launch(key, copy):
        copy.start()
        pending.setdefault(key, []).append(copy)

    def drain(key):
        for copy in pending.pop(key, []):
            copy.wait_send()

    groups = 3 + rows_groups

    def group_of(t):
        if t < wide:
            return 0
        return min(t - wide + 1, groups - 1)

    def fetch_left(g):
        slot = g % left_slots
        for p in range(8):
            h, kk = p // 4, p % 4
            if g == 0:
                fetch(("l", g), two.at[:, kk, h], left.at[slot, p], lds.at[g, p, 0])
                continue
            if g <= rows_groups:
                if g == 1 and p == 0:
                    landed_hid.wait_recv()
                half = left.shape[2] // 2
                pairs = [
                    (hid.at[:, g - 1, kk, h], left.at[slot, p, pl.ds(c * half, half)]),
                    (hid_land.at[:, g - 1, kk, h], left.at[slot, p, pl.ds((1 - c) * half, half)]),
                ]
            else:
                own, other = (flat_own, flat_other) if g == groups - 2 else (norm_own, norm_other)
                pairs = [
                    (own.at[:, kk, h], left.at[slot, p, :, :, place]),
                    (other.at[:, kk, h], left.at[slot, p, :, :, other_place]),
                ]
            for i, (src, dst) in enumerate(pairs):
                fetch(("l", g), src, dst, lds.at[g, p, i])

    def fetch_right(t):
        slot = t % right_slots
        if t < wide:
            src = grads.at[t // parts, :, pl.ds((t % parts) * n, n)]
            fetch(("r", t), src, right.at[slot], rds.at[t, 0])
        elif t == wide:
            keep = pl.ds(pl.multiple_of(c * n, n), n)
            fetch(("r", t), dy_own.at[:, keep], right.at[slot, place], rds.at[t, 0])
            fetch(("r", t), dy_other.at[:, keep], right.at[slot, other_place], rds.at[t, 1])

    fetch_right(0)
    fetch_left(0)
    fetch_right(1)
    landed_tails[...] = jnp.zeros_like(landed_tails)
    barrier = pltpu.get_barrier_semaphore()
    peers = [to_x, to_y, to_c] + [{"z": lax.rem(z + e, S)} for e in range(1, S)]
    for target in peers:
        pl.semaphore_signal(barrier, inc=1, device_id=target, device_id_type=MESH_ID)
    pl.semaphore_wait(barrier, len(peers))
    launch("end", remote_copy(back.at[other_place], got, cs_in.at[0], cs_in.at[1], to_c))
    launch("end", remote_copy(hid, hid_land, cs_in.at[2], cs_in.at[3], to_c))
    landed_hid = remote_copy(hid, hid_land, cs_in.at[2], cs_in.at[3], to_c)
    landed_back = remote_copy(got, got, cs_in.at[0], cs_in.at[1], to_c)

    def product(t, p):
        lhs = left[group_of(t) % left_slots, p].reshape(S * r, T)
        if t <= chunk_out - 1:
            return nn(lhs, right[min(t, wide) % right_slots])
        if t == chunk_out:
            return nn(lhs, out_right[...])
        first = sum(widths[chunk_out + 1 : t])
        return nn(lhs, mix_right[:, first : first + widths[t]])

    def cut(ref, t):
        return ref if widths[t] == n else ref.at[:, pl.ds(0, widths[t])]

    def first(t):
        slot = t % 2
        landed(("l", group_of(t)))
        landed(("r", t))
        drain(("s1", t - 2))
        for i in range(2):
            for j, p, target in ((i, i * 2 + 1 - x, to_x), (2 + i, 4 + (1 - y) * 2 + i, to_y)):
                src, dst = cut(s1.at[slot, j], t), cut(g1.at[t % slots, j], t)
                src[...] = product(t, p).astype(BF)
                launch(("s1", t), remote_copy(src, dst, s1s.at[t, j], s1r.at[t, j], target))

    def second(t):
        slot = t % 2
        drain(("s2", t - 2))
        for j in range(4):
            dst = cut(g1.at[t % slots, j], t)
            remote_copy(dst, dst, s1s.at[t, j], s1r.at[t, j], to_x).wait_recv()
        for h, p, j, target in ((0, (1 - y) * 2 + x, 1 - y, to_y), (1, 4 + y * 2 + 1 - x, 3 - x, to_x)):
            src, dst = cut(s2.at[slot, h], t), cut(g2.at[t % slots, h], t)
            came = cut(g1.at[t % slots, j], t)
            src[...] = (product(t, p) + came[...].astype(F32)).astype(BF)
            launch(("s2", t), remote_copy(src, dst, s2s.at[t, h], s2r.at[t, h], target))

    def third(t):
        slot = t % 2
        w = widths[t]
        drain(("z", t - 2))
        for h, p, j in ((0, k, y), (1, 4 + k, 2 + x)):
            dst = cut(g2.at[t % slots, h], t)
            remote_copy(dst, dst, s2s.at[t, h], s2r.at[t, h], to_x).wait_recv()
            came = cut(g1.at[t % slots, j], t)
            total = (product(t, p) + came[...].astype(F32) + dst[...].astype(F32)).astype(BF)
            for zz in range(S):
                fz[slot, zz, h, :, :w] = total[zz * r : (zz + 1) * r]
        for e in range(1, S):
            src = fz.at[slot, lax.rem(z + e, S), :, :, pl.ds(0, w)]
            dst = gz.at[t, S - e - 1, :, :, pl.ds(0, w)]
            target = {"z": lax.rem(z + e, S)}
            launch(("z", t), remote_copy(src, dst, zs.at[t, e - 1], zr.at[t, S - e - 1], target))

    def fourth(t):
        slot = t % 2
        w = widths[t]
        drain(("ag", t - 2))
        landed(("o", t - 2))
        for e in range(S - 1):
            dst = gz.at[t, e, :, :, pl.ds(0, w)]
            remote_copy(dst, dst, zs.at[t, e], zr.at[t, e], to_x).wait_recv()
        for h in range(2):
            total = fz[slot, z, h, :, :w].astype(F32)
            for e in range(S - 1):
                total = total + gz[t, e, h, :, :w].astype(F32)
            mine[slot, h, :, :w] = total.astype(BF)
        cols = pl.ds(0, w)
        fetch(("o", t), mine.at[slot, :, :, cols], out.at[t, k, c, :, :, cols], ls.at[t])
        for i, hs_ in enumerate(((0, 1), (1, 0))):
            for h, s, r_, target in ((hs_[0], xs, xr, to_x), (hs_[1], ys, yr, to_y)):
                src, dst = mine.at[slot, h, :, cols], out.at[t, k, c, h, :, cols]
                launch(("ag", t), remote_copy(src, dst, s.at[t, i], r_.at[t, i], target))

    def land(t, kk, h, s, r_, j, target):
        p = out.at[t, kk, c, h, :, pl.ds(0, widths[t])]
        remote_copy(p, p, s.at[t, j], r_.at[t, j], target).wait_recv()
        return p

    def fifth(t):
        p = land(t, kx, 0, xs, xr, 0, to_x)
        launch("end", remote_copy(p, p, ys.at[t, 2], yr.at[t, 2], to_y))
        p = land(t, ky, 1, ys, yr, 0, to_y)
        launch("end", remote_copy(p, p, xs.at[t, 2], xr.at[t, 2], to_x))

    def sixth(t):
        land(t, kx, 1, xs, xr, 1, to_x)
        land(t, ky, 0, ys, yr, 1, to_y)
        land(t, kxy, 1, xs, xr, 2, to_x)
        land(t, kxy, 0, ys, yr, 2, to_y)
        landed(("o", t))
        p = out.at[t, :, c, :, :, pl.ds(0, widths[t])]
        launch("end", remote_copy(p, p, cs.at[t], cr.at[t], to_c))


    def norm_back():
        for key in ("near", "x1", "dy", "gains"):
            landed(key)
        landed_back.wait_recv()
        gain = jnp.concatenate([gains[zz, 1:2, :] for zz in range(S)], axis=1).astype(F32)
        step = 64

        @pl.loop(0, piece // step)
        def _(i):
            at = pl.ds(pl.multiple_of(i * step, step), step)
            u = x1[at, :]
            scale = lax.rsqrt(jnp.mean(u * u, axis=1, keepdims=True) + norm_eps)
            hat = u * scale
            e = (do[at, :].astype(F32) + got[at, :].astype(F32)) * gain
            inner = jnp.mean(e * hat, axis=1, keepdims=True)
            dx = mixed[at, :D].astype(F32) + scale * (e - hat * inner)
            x1[at, :] = dx
            da[at, :] = dx.astype(BF)

        fetch("dx", x1, dx_out, fs.at[4])
        launch("end", remote_copy(give_of(da, n), out_right.at[place], cs_in.at[4], cs_in.at[5], to_c))
        out_right[place, :] = keep_of(da, n)[...]
        for i in range(2):
            fetch("w", w_out.at[i, pl.ds(T, piece)], got.at[:, pl.ds(i * n, n)], fs.at[7 + i])

    def give_of(ref, width):
        return ref.at[:, pl.ds(pl.multiple_of((1 - c) * width, width), width)]

    def keep_of(ref, width):
        return ref.at[:, pl.ds(pl.multiple_of(c * width, width), width)]

    def heads_back():
        landed("w")
        live = k_ids[pl.ds(reach * piece, piece), :1] != 0
        for j in range(0, D, piece):
            if j < T:
                low, high = right[2, j : j + piece, :], right[3, j : j + piece, :]
            else:
                low, high = got[:, :n], got[:, n:]
            part = nt(da[:, :n], low) + nt(da[:, n:], high)
            do[:, j : j + piece] = jnp.where(live, part, 0.0).astype(BF)

    half_rows = piece // 2
    steps = [(block, h) for block in range(2) for h in range(heads)]

    def turn_back(dq, first):
        at = pl.ds(first, half_rows)
        return dq * cos_ref[at, :] - pltpu.roll(dq, HEAD // 2, 1) * sin_ref[at, :]

    def attention(first_step, count):
        arrays = (q_ref, k_ref, v_ref, o_ref, do, l_ref, mixed, dk, dv)
        if first_step == 0:
            kt[...] = k_ref[...].T
            dk[...] = jnp.zeros_like(dk)
            dv[...] = jnp.zeros_like(dv)
        for block, h in steps[first_step : first_step + count]:
            if h == 0:
                fill_bias(bias, q_ids, k_ids, block * half_rows, half_rows, WINDOW + half_rows)
            back_step(h, block * half_rows, half_rows, arrays, bias, kt, turn_back)

    def tail(d):
        target = {"z": jnp.maximum(z - d, 0)}
        return remote_copy(tails.at[d - 1], landed_tails.at[d - 1], hs.at[d - 1], hr.at[d - 1], target)

    def send_tails():
        for d in range(1, reach + 1):
            at = pl.ds((reach - d) * piece, piece)
            tails[d - 1, :, :HEAD] = dk[at, :].astype(BF)
            tails[d - 1, :, HEAD:] = dv[at, :].astype(BF)

            @pl.when(z >= d)
            def _(d=d):
                tail(d).start()

    def mix_back():
        for d in range(1, reach + 1):

            @pl.when(z >= d)
            def _(d=d):
                tail(d).wait_send()

            @pl.when(z + d < S)
            def _(d=d):
                tail(d).wait_recv()

        at = pl.ds(reach * piece, piece)
        keys, values = dk[at, :], dv[at, :]
        for d in range(1, reach + 1):
            keys = keys + landed_tails[d - 1, :, :HEAD].astype(F32)
            values = values + landed_tails[d - 1, :, HEAD:].astype(F32)
        keys = keys * cos_ref[...] - pltpu.roll(keys, HEAD // 2, 1) * sin_ref[...]
        width = heads * HEAD
        mixed[:, width : width + HEAD] = keys.astype(BF)
        mixed[:, width + HEAD :] = values.astype(BF)
        launch("end", remote_copy(give_of(mixed, mix_half), mix_right.at[place], cs_in.at[6], cs_in.at[7], to_c))
        mix_right[place, :] = keep_of(mixed, mix_half)[...]

    def came(ref, i):
        ref = ref.at[other_place]
        remote_copy(ref, ref, cs_in.at[i], cs_in.at[i + 1], to_c).wait_recv()

    stages = (first, second, third, fourth, fifth, sixth)

    fetch("near", back.at[place], do, fs.at[0])
    fetch("x1", middle, x1, fs.at[1])
    fetch("dy", dy_own, mixed.at[:, pl.ds(0, D)], fs.at[2])
    fetch("gains", gains_ref, gains, fs.at[3])
    for i in range(2):
        fetch("w", w_out.at[i, pl.ds(0, T)], right.at[2 + i], fs.at[5 + i])
    each = 5

    def work(t):
        if t == 0:
            norm_back()
        if t == 1:
            heads_back()
        if t >= 2 and (t - 2) * each < len(steps):
            attention((t - 2) * each, each)
        if t == 7:
            send_tails()
        if t == 8:
            mix_back()

    for t in range(nc + len(stages) - 1):
        for lag, stage in enumerate(stages):
            if lag == 0 and t == chunk_out:
                came(out_right, 4)
            if lag == 0 and t == chunk_out + 1:
                came(mix_right, 6)
            if 0 <= t - lag < nc:
                stage(t - lag)
            if lag == 0:
                work(t)
        if t == 1:
            fetch_right(2)
        if t >= 1:
            fetch_right(t + 2)
        for g in range(1, groups):
            if t == wide + g - (3 if g < left_slots else 2):
                fetch_left(g)
    for t in range(nc):
        p = out.at[t, :, 1 - c, :, :, pl.ds(0, widths[t])]
        remote_copy(p, p, cs.at[t], cr.at[t], to_c).wait_recv()
    for key in list(pending):
        drain(key)
    for key in list(loads):
        landed(key)


def backward(two_t, hid_t, transposed, grads, dy, back, middle, w_out, gains, attention, tables, heads, S, cid):
    D, T = two_t.shape
    sides, _, half_ff = grads.shape
    piece = middle.shape[0]
    n = w_out.shape[2]
    r = D // (S * 8)
    parts = half_ff // n
    rows_groups = 2 * half_ff // (S * 8 * r)
    mixed = attention[2].shape[1] + 2 * HEAD
    nc = sides * parts + rows_groups + 3
    m = S * r
    slots = 5
    keys = attention[3].shape[0]
    reach = keys // piece - 1
    dma = pltpu.SemaphoreType.DMA
    hid_shape = (S // 2, rows_groups, 4, 2, r, T)

    def body(*refs):
        backward_kernel(heads, sides, parts, S, *refs)

    def vmem(*shape):
        return pltpu.VMEM(shape, BF)

    results = pl.pallas_call(
        body,
        out_shape=(
            jax.ShapeDtypeStruct((nc, 4, 2, 2, r, n), BF),
            jax.ShapeDtypeStruct(hid_shape, BF),
            jax.ShapeDtypeStruct((piece, D), F32),
            jax.ShapeDtypeStruct((piece, mixed), BF),
        ),
        in_specs=[ANY] * 13 + [VM] * 9,
        out_specs=(ANY, ANY, ANY, VM),
        scratch_shapes=[
            vmem(3, 8, S, r, T),
            vmem(4, T, n),
            vmem(T, n),
            vmem(T, mixed // 2),
            vmem(2, 4, m, n),
            vmem(slots, 4, m, n),
            vmem(2, 2, m, n),
            vmem(slots, 2, m, n),
            vmem(2, S, 2, r, n),
            vmem(nc, S - 1, 2, r, n),
            vmem(2, 2, r, n),
            vmem(piece, D),
            vmem(piece, D),
            vmem(piece, D),
            vmem(reach, piece, 2 * HEAD),
            vmem(reach, piece, 2 * HEAD),
            vmem(*gains.shape),
            pltpu.VMEM((piece, D), F32),
            pltpu.VMEM((keys, HEAD), F32),
            pltpu.VMEM((keys, HEAD), F32),
            pltpu.VMEM((WINDOW + piece // 2, piece // 2), F32),
            pltpu.VMEM((HEAD, keys), BF),
            dma((rows_groups + 3, 8, 2)),
            dma((nc, 2)),
            dma((9,)),
            dma((8,)),
            dma((reach,)),
            dma((reach,)),
            dma((nc, 4)),
            dma((nc, 4)),
            dma((nc, 2)),
            dma((nc, 2)),
            dma((nc, S)),
            dma((nc, S)),
            dma((nc,)),
            dma((nc, 3)),
            dma((nc, 3)),
            dma((nc, 3)),
            dma((nc, 3)),
            dma((nc,)),
            dma((nc,)),
        ],
        compiler_params=pltpu.CompilerParams(
            collective_id=cid, has_side_effects=True, vmem_limit_bytes=BACKWARD_VMEM
        ),
    )(
        two_t.reshape(S, 4, 2, r, T),
        hid_t.reshape(hid_shape),
        *[v.reshape(S, 4, 2, r, piece) for v in transposed],
        grads,
        *dy,
        back,
        middle,
        w_out,
        gains,
        *attention,
        *tables,
    )
    return results[0], results[2], results[3]


def adam_kernel(total, widths, gains, count_ref, rates_ref, g_ref, w_ref, m_ref, g_out, w_out, m_out, *more):
    step_value = count_ref[0].astype(F32)
    log_first = jnp.log(jnp.full((8, 128), beta_first, F32))
    log_second = jnp.log(jnp.full((8, 128), beta_second, F32))
    unfix_first = (1.0 / (1.0 - jnp.exp(step_value * log_first)))[:1, :1]
    unfix_second = (1.0 / (1.0 - jnp.exp(step_value * log_second)))[:1, :1]
    rate, decay = rates_ref[0], rates_ref[1]
    rows = w_ref.shape[0]

    if gains:

        @pl.when((pl.program_id(1) == 0) & (pl.program_id(2) == 0))
        def _():
            more[0][...] = jnp.zeros_like(more[0])

    for i, n in enumerate(widths):
        at = pl.ds(sum(widths[:i]), n)
        grad = g_ref[i, :, 0, :, :, :n].reshape(rows, n).astype(F32) * (1.0 / total)
        w = w_ref[:, at]
        first = beta_first * m_ref[0, :, at] + (1.0 - beta_first) * grad
        second = beta_second * m_ref[1, :, at] + (1.0 - beta_second) * grad * grad
        step = first * unfix_first / (jnp.sqrt(second * unfix_second) + adam_eps) + decay * w
        g_out[:, at] = grad
        w_out[:, at] = w - rate * step
        m_out[0, :, at] = first
        m_out[1, :, at] = second
        if gains:
            both = w.astype(BF).astype(F32) * grad
            for j in range(0, n, 128):
                more[0][...] += both[:, j : j + 128]


def adam_call(
    weight, moments, grads, count, rates, total, base, widths, sides=1, tiles=1, gains=False, chips=4
):
    _, _, _, _, r, n = grads.shape
    wide = len(widths)

    def g_place(kk, cc, ss, tt):
        return (base // wide + ss + tt, kk, cc, 0, 0, 0)

    def place(kk, cc, ss, tt):
        return (tt * (4 // chips) + kk, ss * 2 + cc)

    def m_place(*at):
        return (0,) + place(*at)

    rows = chips * 2 * r
    w_spec = pl.BlockSpec((rows, sum(widths)), place)
    m_spec = pl.BlockSpec((2, rows, sum(widths)), m_place)
    smem = pl.BlockSpec(memory_space=pltpu.SMEM)
    like = jax.ShapeDtypeStruct(weight.shape, F32)
    out_specs = [w_spec, w_spec, m_spec]
    out_shape = [like, like, jax.ShapeDtypeStruct(moments.shape, F32)]
    if gains:
        out_specs.append(pl.BlockSpec((rows, 128), lambda kk, cc, ss, tt: (kk, 0)))
        out_shape.append(jax.ShapeDtypeStruct((weight.shape[0], 128), F32))

    def body(*refs):
        adam_kernel(total, widths, gains, *refs)

    return pl.pallas_call(
        body,
        grid=(4 // chips, 2, sides, tiles),
        in_specs=[smem, smem, pl.BlockSpec((wide, chips, 1, 2, r, n), g_place), w_spec, m_spec],
        out_specs=out_specs,
        out_shape=out_shape,
        compiler_params=pltpu.CompilerParams(
            dimension_semantics=("arbitrary",) * 4, vmem_limit_bytes=VMEM_BYTES
        ),
        cost_estimate=pl.CostEstimate(
            flops=20 * weight.size,
            bytes_accessed=30 * weight.size,
            transcendentals=weight.size,
        ),
    )(count, rates, grads, weight, moments)


def dot(a, b):
    return jnp.dot(a, b, preferred_element_type=F32)


def dot_rows(a, b):
    return lax.dot_general(a, b, (((1,), (0,)), ((), ())), preferred_element_type=F32)


def dot_t(a, b):
    return lax.dot_general(a, b, (((1,), (1,)), ((), ())), preferred_element_type=F32)


def on_device(
    Y,
    S,
    block_in,
    cotangent,
    segment_ids,
    input_proj,
    output_proj,
    gate_up,
    down_weight,
    norm_gains,
    input_moments,
    output_moments,
    gate_moments,
    down_moments,
    gain_moments,
    update_count,
    optimizer_rates,
):
    seq_place = lax.axis_index("z")
    core = lax.axis_index("c")
    first_core = core == 0
    D = block_in.shape[-1]
    half_ff = FF // 2
    rows_d = input_proj.shape[0]
    rows_f = down_weight.shape[0]
    fast = Y == 2 and rows_d % 128 == 0
    in_half = input_proj.shape[1] // 2
    d_half = D // 2
    r = rows_d // 8

    in_low = input_proj.astype(BF)
    out_low = output_proj.astype(BF)
    down_low = down_weight.astype(BF)

    def halves(w):
        n = w.shape[1] // 2
        return jnp.stack([w[:, :n], w[:, n:]])

    gate_low = jnp.concatenate(
        [
            lax.dynamic_slice_in_dim(gate_up, side * FF + core * half_ff, half_ff, 1)
            for side in range(2)
        ],
        axis=1,
    ).astype(BF)

    gains_low = norm_gains.astype(BF)
    tokens = block_in[0].astype(F32)
    piece_len = tokens.shape[0]
    width_q = HEADS * HEAD
    positions = seq_place * piece_len + jnp.arange(piece_len, dtype=jnp.int32)
    reach_count = (WINDOW + piece_len - 2) // piece_len
    key_span = reach_count * piece_len
    segments = segment_ids[0]
    padded_ids = jnp.concatenate([jnp.full((key_span,), -1, jnp.int32), segments])
    query_ids = lax.dynamic_slice_in_dim(segments, seq_place * piece_len, piece_len)
    key_ids = lax.dynamic_slice_in_dim(padded_ids, seq_place * piece_len, key_span + piece_len)
    live_rows = query_ids != 0
    query_row = query_ids[None, :]
    key_column = key_ids[:, None]

    if fast:
        frequency = 10000.0 ** (-2.0 * jnp.arange(HEAD // 2).astype(F32) / HEAD)
        angles = positions.astype(F32)[:, None] * jnp.concatenate([frequency, frequency])[None, :]
        side = jnp.where(jnp.arange(HEAD) < HEAD // 2, -1.0, 1.0)
        cos_table, sin_table = jnp.cos(angles), jnp.sin(angles) * side
        (
            in_full,
            out_full,
            down_full,
            gate_full,
            gains_full,
            normed,
            queries,
            key_rows,
            values,
            flat_heads,
            log_totals,
            middle,
            normed_two,
            two_other,
            *transposed,
        ) = forward(
            [
                halves(in_low).reshape(2, 4, 2, r, in_half),
                halves(out_low).reshape(2, 4, 2, r, d_half),
                halves(down_low).reshape(2, 4, 2, rows_f // 8, d_half),
                gate_low.reshape(4, 2, r, 2 * half_ff),
            ],
            jnp.concatenate([gains_low] * 8, axis=0),
            block_in[0],
            cos_table,
            sin_table,
            query_row,
            key_column,
            HEADS,
            S,
            0,
        )
        in_full = in_full.reshape(2, D, in_half)
        out_full = out_full.reshape(2, D, d_half)
        gains_small = gains_full
        gains_full = gains_full[:, :2].transpose(1, 0, 2).reshape(2, D)
        down_full = down_full.reshape(2, FF, d_half)
        gate_full = gate_full.reshape(D, 2 * half_ff)
        gains_wide = gains_full.astype(F32)
    else:
        in_full = halves(lax.all_gather(in_low, "z", axis=0, tiled=True))
        out_full = halves(lax.all_gather(out_low, "z", axis=0, tiled=True))
        down_full = halves(lax.all_gather(down_low, "z", axis=0, tiled=True))
        gate_full = lax.all_gather(gate_low, "z", axis=0, tiled=True)
        gains_full = lax.all_gather(gains_low, "z", axis=1, tiled=True)
        gains_wide = gains_full.astype(F32)
        normed = root_norm(tokens, gains_wide[0]).astype(BF)
        mixed_proj = jnp.concatenate([dot(normed, in_full[0]), dot(normed, in_full[1])], axis=1)
        queries = (
            rotate(mixed_proj[:, :width_q].reshape(piece_len, HEADS, HEAD), positions, 1.0)
            .astype(BF)
            .reshape(piece_len, width_q)
        )
        own_keys = rotate(mixed_proj[:, width_q : width_q + HEAD], positions, 1.0)
        own_pair = jnp.concatenate([own_keys, mixed_proj[:, width_q + HEAD :]], axis=1).astype(BF)
        earlier = []
        for back_step in range(reach_count, 0, -1):
            earlier.append(passed_along(own_pair, "z", back_step))
        key_pairs = jnp.concatenate(earlier + [own_pair], axis=0)
        key_rows = key_pairs[:, :HEAD]
        values = key_pairs[:, HEAD:]
        flat_heads, log_totals = attend(
            query_row, key_column, queries, key_rows, values, HEADS, piece_len
        )
        middle = tokens + jnp.concatenate(
            [dot(flat_heads, out_full[0]), dot(flat_heads, out_full[1])], axis=1
        )
        normed_two = root_norm(middle, gains_wide[1]).astype(BF)
        two_other = swapped(normed_two, "c")

    upstream = cotangent[0].astype(F32)

    def ordered(mine, other):
        return jnp.concatenate(
            [jnp.where(first_core, mine, other), jnp.where(first_core, other, mine)], axis=0
        )

    def pair(v):
        return ordered(v, swapped(v, "c"))

    def half_pair(v):
        n = v.shape[1] // 2
        keep = lax.dynamic_slice_in_dim(v, core * n, n, 1)
        give = lax.dynamic_slice_in_dim(v, (1 - core) * n, n, 1)
        return ordered(keep, swapped(give, "c"))

    def core_sum(v):
        keep = lax.dynamic_slice_in_dim(v, core * piece_len, piece_len, 0)
        give = lax.dynamic_slice_in_dim(v, (1 - core) * piece_len, piece_len, 0)
        return keep.astype(F32) + swapped(give, "c").astype(F32)

    df_other = swapped(cotangent[0], "c")
    two_t, hid_t, grad_gated, out_sum, two_sum = mlp_call(
        core.reshape(1).astype(jnp.int32),
        (normed_two, two_other),
        (cotangent[0], df_other),
        gate_full,
        down_full,
    )
    output = middle + core_sum(out_sum)
    block_out = output.astype(BF)[None]
    token_total = piece_len * S * Y * 4 * block_in.shape[0]
    step_value = update_count[0].astype(F32)
    rates = optimizer_rates

    if fast:
        sums, grad_middle, grad_mixed = backward(
            two_t,
            hid_t,
            transposed,
            grad_gated,
            (cotangent[0], df_other),
            two_sum,
            middle,
            out_full,
            gains_small,
            (query_row, key_column, queries, key_rows, values, flat_heads, log_totals),
            (cos_table, sin_table),
            HEADS,
            S,
            2,
        )
    else:
        grad_normed_two = core_sum(two_sum)
        _, norm_pull_two = jax.vjp(root_norm, middle, gains_wide[1])
        grad_middle_norm, grad_gain_two = norm_pull_two(grad_normed_two)
        grad_middle = upstream + grad_middle_norm
        grad_branch = grad_middle.astype(BF)
        grad_flat = dot_t(grad_branch[:, :d_half], out_full[0]) + dot_t(
            grad_branch[:, d_half:], out_full[1]
        )
        grad_attended = jnp.where(live_rows[:, None], grad_flat, 0.0).astype(BF)
        grad_query_all, grad_keys, grad_values = attend_back(
            query_row,
            key_column,
            queries,
            key_rows,
            values,
            flat_heads,
            grad_attended,
            log_totals,
            HEADS,
            piece_len // 2,
        )
        grad_pairs = jnp.concatenate([grad_keys, grad_values], axis=1)
        own_grad = grad_pairs[key_span:]
        for back_step in range(1, reach_count + 1):
            sent_rows = grad_pairs[
                key_span - back_step * piece_len : key_span - (back_step - 1) * piece_len
            ]
            own_grad = own_grad + passed_along(sent_rows, "z", -back_step)
        grad_query_raw = rotate(
            grad_query_all.reshape(piece_len, HEADS, HEAD), positions, -1.0
        ).reshape(piece_len, width_q)
        grad_key_raw = rotate(own_grad[:, :HEAD], positions, -1.0)
        grad_mixed = jnp.concatenate(
            [grad_query_raw, grad_key_raw, own_grad[:, HEAD:]], axis=1
        ).astype(BF)
    grad_normed = dot_t(grad_mixed[:, :in_half], in_full[0]) + dot_t(
        grad_mixed[:, in_half:], in_full[1]
    )
    _, norm_pull_one = jax.vjp(root_norm, tokens, gains_wide[0])
    grad_tokens_norm, grad_gain_one = norm_pull_one(grad_normed)
    block_in_grad = (grad_middle + grad_tokens_norm).astype(BF)[None]

    if fast:

        def adam(weight, moments, *rest, **more):
            return adam_call(
                weight, moments, sums, update_count, rates, float(token_total), *rest, **more
            )

        tiles = half_ff // d_half
        same = (d_half,) * tiles
        gate_grad, gate_new, gate_mom, gain_two = adam(
            gate_up, gate_moments, 0, same, sides=2, gains=True, chips=2
        )
        down_grad, down_new, down_mom = adam(
            down_weight, down_moments, 2 * tiles, (d_half,), tiles=tiles
        )
        out_grad, out_new, out_mom = adam(output_proj, output_moments, 3 * tiles, (d_half,))
        in_grad, in_new, in_mom, gain_one = adam(
            input_proj, input_moments, 3 * tiles + 1, split_widths(in_half, d_half), gains=True
        )
        gain_grad = jnp.stack(
            [jnp.sum(v, axis=1) for v in (gain_one, gain_two)]
        ) / gains_low.astype(F32)
    else:

        def adam(weight, moments, grad):
            grad = grad.astype(F32) / token_total
            change, new = adamw_step(weight, moments, grad, step_value, rates)
            return grad, weight - change, new

        def summed(left, right):
            whole = dot_rows(left.T, right).astype(BF)
            mine = lax.psum_scatter(whole, "z", scatter_dimension=0, tiled=True)
            return lax.psum(mine, ("y", "x"))

        two_both = ordered(normed_two, two_other)
        grad_half = half_pair(grad_branch)
        mixed_half = half_pair(grad_mixed)
        normed_both = pair(normed)
        flat_both = pair(flat_heads)
        df_both = pair(cotangent[0])
        gate_half = [summed(two_both, grad_gated[side]) for side in range(2)]
        gate_sum = jnp.concatenate(
            [lax.all_gather(g, "c", axis=1, tiled=True) for g in gate_half], axis=1
        )
        down_part = lax.psum(dot_rows(hid_t, df_both).astype(BF), ("y", "x"))
        down_part = lax.all_gather(down_part, "c", axis=0, tiled=True)
        down_sum = lax.psum_scatter(down_part, "z", scatter_dimension=0, tiled=True)
        out_total = lax.all_gather(summed(flat_both, grad_half), "c", axis=1, tiled=True)
        in_total = lax.all_gather(summed(normed_both, mixed_half), "c", axis=1, tiled=True)
        out_grad, out_new, out_mom = adam(output_proj, output_moments, out_total)
        in_grad, in_new, in_mom = adam(input_proj, input_moments, in_total)
        gate_grad, gate_new, gate_mom = adam(gate_up, gate_moments, gate_sum)
        down_grad, down_new, down_mom = adam(down_weight, down_moments, down_sum)
        gains_sum = lax.psum(jnp.stack([grad_gain_one, grad_gain_two]), ("y", "x", "c", "z"))
        gain_grad = lax.dynamic_slice_in_dim(gains_sum, seq_place * rows_d, rows_d, 1) / token_total
    gains_step, gain_moments_new = adamw_step(norm_gains, gain_moments, gain_grad, step_value, rates)
    return (
        block_out,
        block_in_grad,
        in_grad,
        out_grad,
        gate_grad,
        down_grad,
        gain_grad,
        in_new,
        out_new,
        gate_new,
        down_new,
        gains_step,
        in_mom,
        out_mom,
        gate_mom,
        down_mom,
        gain_moments_new,
    )


def solution(mesh):
    dp, S = mesh.shape["dp"], mesh.shape["seq"]
    Y = dp // 4
    grid = Mesh(mesh.devices.reshape(Y, 2, 2, S), ("y", "x", "c", "z"))
    data = ("y", "x", "c")
    tokens = P(data, "z", None)
    rows = P("z", None)
    moments = P(None, "z", None)
    in_specs = (
        (tokens, tokens, P(data, None))
        + (rows,) * 4
        + (P(None, "z"),)
        + (moments,) * 4
        + (P(None, None, "z"), P(), P())
    )
    out_specs = (
        (tokens, tokens)
        + (rows,) * 4
        + (P(None, "z"),)
        + (rows,) * 4
        + (P(None, "z"),)
        + (moments,) * 4
        + (P(None, None, "z"),)
    )

    def device_step(*arrays):
        return on_device(Y, S, *arrays)

    return jax.shard_map(
        device_step, mesh=grid, in_specs=in_specs, out_specs=out_specs, check_vma=False
    )
```

```python
import jax
import jax.numpy as jnp
from jax import lax
from jax.experimental import pallas as pl
from jax.experimental.pallas import tpu as pltpu
from jax.sharding import Mesh
from jax.sharding import PartitionSpec as P

HEADS = 12
HEAD = 128
FF = 4608
WINDOW = 1024


norm_eps = 1e-06
adam_eps = 1e-08
beta_first = 0.9
beta_second = 0.95
BF = jnp.bfloat16
F32 = jnp.float32
MESH_ID = pl.DeviceIdType.MESH
VMEM_BYTES = 60 * 1024 * 1024
BACKWARD_VMEM = 127 * 512 * 1024
ANY = pl.BlockSpec(memory_space=pl.ANY)
VM = pl.BlockSpec(memory_space=pltpu.VMEM)
LOG2E = 1.4426950408889634


def passed_along(block, axis, distance):
    devices = range(lax.axis_size(axis))
    route = [(i - distance, i) for i in devices if i - distance in devices]
    return lax.ppermute(block, axis, route)


def swapped(block, axis):
    return lax.ppermute(block, axis, [(0, 1), (1, 0)])


def rotate(values, positions, sign_value):
    half_width = values.shape[-1] // 2
    frequency = 10000.0 ** (-2.0 * jnp.arange(half_width).astype(jnp.float32) / values.shape[-1])
    angles = positions.astype(jnp.float32)[:, None] * frequency[None, :]
    cosine = jnp.cos(angles)
    sine_part = sign_value * jnp.sin(angles)
    if values.ndim == 3:
        cosine = cosine[:, None, :]
        sine_part = sine_part[:, None, :]
    lower_half = values[..., :half_width]
    upper_half = values[..., half_width:]
    return jnp.concatenate(
        [
            lower_half * cosine - upper_half * sine_part,
            upper_half * cosine + lower_half * sine_part,
        ],
        axis=-1,
    )


def root_norm(values, gain):
    return values * lax.rsqrt(jnp.mean(values * values, axis=-1, keepdims=True) + norm_eps) * gain


def adamw_step(weight, moments, grad, step_value, optimizer_rates):
    fix_first = 1.0 - beta_first**step_value
    fix_second = 1.0 - beta_second**step_value
    first_moment = beta_first * moments[0] + (1.0 - beta_first) * grad
    second = beta_second * moments[1] + (1.0 - beta_second) * grad * grad
    update = (
        first_moment / fix_first / (jnp.sqrt(second / fix_second) + adam_eps)
        + optimizer_rates[1] * weight
    )
    return (optimizer_rates[0] * update, jnp.stack([first_moment, second]))


def gather_kernel(shared, groups, S, own, full, sems, small_own, small_full, prepare, work):
    n = len(shared)
    chunks = [chunk for group in groups for chunk in group]
    members = []
    for group in groups:
        first = members[-1][-1] + 1 if members else 0
        members.append(range(first, first + len(group)))
    ng = len(groups)
    F = S - 1
    loc, zs, zr, xs, xr, ys, yr, cs, cr, ss, sr = sems
    y, x, c, z = (lax.axis_index(a) for a in ("y", "x", "c", "z"))
    k = y * 2 + x
    kx = y * 2 + 1 - x
    ky = (1 - y) * 2 + x
    kxy = 3 - k
    to_x = {"x": 1 - x}
    to_y = {"y": 1 - y}
    to_c = {"c": 1 - c}
    low = z
    high = S - 1 - z
    near_count = jnp.minimum(low, high)
    above = jnp.minimum(z + 1, S - 1)
    below = jnp.maximum(z - 1, 0)
    blocks = []
    for j in range(F):
        near = j < 2 * near_count
        dist = jnp.where(near, j // 2 + 1, j - near_count + 1)
        sign = jnp.where(near, (j % 2) * 2 - 1, jnp.where(high > low, 1, -1))
        blocks.append((z + sign * dist, sign))
    barrier = pltpu.get_barrier_semaphore()
    others = [lax.rem(z + e, S) for e in range(1, S)]
    for target in [to_x, to_y, to_c] + [{"z": zz} for zz in others]:
        pl.semaphore_signal(barrier, inc=1, device_id=target, device_id_type=MESH_ID)
    pl.semaphore_wait(barrier, 3 + F)

    def box(q, half):
        i, r0, rn, c0, cn, _ = chunks[q]
        if shared[i]:
            columns = full[i].shape[-1] // 2
            c0 = pl.multiple_of(half * columns + c0, 128)
        return pl.ds(r0, rn), pl.ds(c0, cn)

    def part(q, zz, kk, h=None, half=c):
        rr, cc = box(q, half)
        held = full[chunks[q][0]]
        if h is None:
            return held.at[zz, kk, :, rr, cc]
        return held.at[zz, kk, h, rr, cc]

    def carried(q):
        route = chunks[q][5]
        if route == "xy":
            return (k,)
        return (x, 2 + x) if route == "x" else (2 * y, 2 * y + 1)

    def exchanged(q):
        if chunks[q][5] == "x":
            return xs, xr, to_x, (1 - x, 3 - x)
        return ys, yr, to_y, (2 - 2 * y, 3 - 2 * y)

    def remote(src, dst, s, r, target):
        return pltpu.make_async_remote_copy(
            src_ref=src,
            dst_ref=dst,
            send_sem=s,
            recv_sem=r,
            device_id=target,
            device_id_type=MESH_ID,
        )

    tail = []
    arriving = {i: [] for i in range(n)}
    arriving[None] = []
    finished = [0] * n

    def begin(g):
        i, r0, rn, c0 = groups[g][0][:4]
        prepare(g)
        rows = pl.ds(r0, rn)
        if shared[i]:
            src, dst = own[i].at[:, :, rows], full[i].at[z, :, :, rows]
        else:
            cc = pl.ds(c0, sum(chunk[4] for chunk in groups[g]))
            src, dst = own[i].at[:, :, rows, cc], full[i].at[z, :, :, rows, cc]
        for q in members[g]:
            z_first(q)
        copy = pltpu.make_async_copy(src, dst, loc.at[g])
        copy.start()
        arriving[i].append(copy.wait)

    def z_first(q):
        i = chunks[q][0]
        rr, cc = box(q, c)
        for m, kk in enumerate(carried(q)):
            for ok, target, slot in ((z + 1 < S, above, F), (z > 0, below, F + 1)):

                def make(target=target, slot=slot, m=m, kk=kk):
                    return remote(
                        own[i].at[kk, :, rr, cc],
                        part(q, z, kk),
                        zs.at[q, slot, m],
                        zr.at[q, z, m],
                        {"z": target},
                    )

                @pl.when(ok)
                def _(make=make):
                    make().start()

                def finish(ok=ok, make=make):
                    @pl.when(ok)
                    def _():
                        make().wait_send()

                tail.append(finish)

    def send(p, s, r, q, j, slot, target):
        copy = remote(p, p, s.at[q, j, slot], r.at[q, j, slot], target)
        copy.start()
        tail.append(copy.wait_send)

    def z_next(q, j):
        zz, sign = blocks[j]
        onward = z - sign
        ok = (onward >= 0) & (onward < S)
        target = jnp.clip(onward, 0, S - 1)
        for m, kk in enumerate(carried(q)):
            piece = part(q, zz, kk)
            remote(piece, piece, zs.at[q, j, m], zr.at[q, zz, m], {"z": above}).wait_recv()

            def make(piece=piece, m=m):
                return remote(piece, piece, zs.at[q, j, m], zr.at[q, zz, m], {"z": target})

            @pl.when(ok)
            def _(make=make):
                make().start()

            def finish(make=make):
                @pl.when(ok)
                def _():
                    make().wait_send()

            tail.append(finish)
            if chunks[q][5] != "xy":
                s, r, neighbour, _ = exchanged(q)
                send(piece, s, r, q, j, m, neighbour)
        if chunks[q][5] == "xy":
            send(part(q, zz, k, 0), xs, xr, q, j, 0, to_x)
            send(part(q, zz, k, 1), ys, yr, q, j, 0, to_y)
            send(part(q, zz, k, 0), ys, yr, q, j, 1, to_y)
            send(part(q, zz, k, 1), xs, xr, q, j, 1, to_x)

    def xy_next(q, j):
        if chunks[q][5] != "xy":
            return
        zz, _ = blocks[j]
        p = part(q, zz, kx, 0)
        remote(p, p, xs.at[q, j, 0], xr.at[q, j, 0], to_x).wait_recv()
        send(p, ys, yr, q, j, 2, to_y)
        p = part(q, zz, ky, 1)
        remote(p, p, ys.at[q, j, 0], yr.at[q, j, 0], to_y).wait_recv()
        send(p, xs, xr, q, j, 2, to_x)

    def last(q, j):
        i = chunks[q][0]
        zz, _ = blocks[j]
        finished[i] += 1
        if chunks[q][5] == "xy":
            for kk, h, s, r, slot, target in (
                (kx, 1, xs, xr, 1, to_x),
                (ky, 0, ys, yr, 1, to_y),
                (kxy, 1, xs, xr, 2, to_x),
                (kxy, 0, ys, yr, 2, to_y),
            ):
                p = part(q, zz, kk, h)
                remote(p, p, s.at[q, j, slot], r.at[q, j, slot], target).wait_recv()
        else:
            s, r, neighbour, theirs = exchanged(q)
            for m, kk in enumerate(theirs):
                p = part(q, zz, kk)
                remote(p, p, s.at[q, j, m], r.at[q, j, m], neighbour).wait_recv()
        if shared[i]:
            rr, cc = box(q, c)
            p = full[i].at[zz, :, :, rr, cc]
            copy = remote(p, p, cs.at[q, j], cr.at[q, j], to_c)
            copy.start()
            tail.append(copy.wait_send)
            rr, cc = box(q, 1 - c)
            other = full[i].at[zz, :, :, rr, cc]

            def finish():
                remote(other, other, cs.at[q, j], cr.at[q, j], to_c).wait_recv()

            arriving[i].append(finish)

    def ready(i):
        if i is not None:
            assert finished[i] == F * sum(chunk[0] == i for chunk in chunks)
        for wait in arriving.pop(i, []):
            wait()

    begin(0)
    if small_own is not None:
        place = pltpu.make_async_copy(small_own, small_full.at[z], ss.at[0])
        place.start()
        arriving[None].append(place.wait)
        for e, zz in enumerate(others, 1):
            copy = remote(small_own, small_full.at[z], ss.at[e], sr.at[S - e], {"z": zz})
            copy.start()
            tail.append(copy.wait_send)
            came = small_full.at[zz]
            arriving[None].append(remote(came, came, ss.at[e], sr.at[e], {"z": zz}).wait_recv)
    for t in range(1, ng + F + 3):
        if t < ng:
            begin(t)
        for lag, stage in ((1, z_next), (2, xy_next), (3, last)):
            for j in reversed(range(F)):
                if 0 <= t - lag - j < ng:
                    for q in members[t - lag - j]:
                        stage(q, j)
        work(t, ready)
    for i in list(arriving):
        ready(i)
    for wait in tail:
        wait()


def gather_sems(ng, nc, S):
    dma = pltpu.SemaphoreType.DMA
    F = S - 1
    return [
        dma((ng,)),
        dma((nc, F + 2, 2)),
        dma((nc, S, 2)),
        dma((nc, F, 3)),
        dma((nc, F, 3)),
        dma((nc, F, 3)),
        dma((nc, F, 3)),
        dma((nc, F)),
        dma((nc, F)),
        dma((S,)),
        dma((S,)),
    ]


def nt(a, b):
    return lax.dot_general(a, b, (((1,), (1,)), ((), ())), preferred_element_type=F32)

def nn(a, b):
    return lax.dot_general(a, b, (((1,), (0,)), ((), ())), preferred_element_type=F32)

def fill_bias(bias, q_ids, k_ids, first, rows, span):
    key = lax.broadcasted_iota(jnp.int32, (span, rows), 0)
    query = lax.broadcasted_iota(jnp.int32, (span, rows), 1)
    distance = query + WINDOW - key
    same = k_ids[pl.ds(first, span), :1] == q_ids[:1, pl.ds(first, rows)]
    allowed = (distance >= 0) & (distance < WINDOW) & same
    bias[...] = jnp.where(allowed, 0.0, -1e30)

def fwd_step(h, first, rows, q_ids, q_ref, k_ref, o_ref, l_ref, bias, vt):
    span = WINDOW + rows
    factor = HEAD**-0.5 * LOG2E
    cols = pl.ds(h * HEAD, HEAD)
    q = q_ref[pl.ds(first, rows), cols]
    s = nt(k_ref[pl.ds(first, span), :], q) * factor + bias[...]
    top = jnp.max(s, axis=0, keepdims=True)
    p = jnp.exp2(s - top)
    total = jnp.sum(p, axis=0, keepdims=True)
    o = nn(vt[:, pl.ds(first, span)], p.astype(BF))
    live = q_ids[:1, pl.ds(first, rows)] != 0
    o = jnp.where(live, o * (1.0 / total), 0.0)
    o_ref[pl.ds(first, rows), cols] = o.T.astype(BF)
    l_ref[h, :, pl.ds(first, rows)] = top + jnp.log2(total)


def fwd_kernel(heads, rows, q_ids, k_ids, q_ref, k_ref, v_ref, o_ref, l_ref, bias, vt):
    vt[...] = v_ref[...].T
    for first in range(0, q_ref.shape[0], rows):
        fill_bias(bias, q_ids, k_ids, first, rows, WINDOW + rows)
        for h in range(heads):
            fwd_step(h, first, rows, q_ids, q_ref, k_ref, o_ref, l_ref, bias, vt)


def norm_rows(source, gain, target):
    rows = 64

    @pl.loop(0, target.shape[0] // rows)
    def _(i):
        at = pl.ds(pl.multiple_of(i * rows, rows), rows)
        u = source[at, :].astype(F32)
        scale = lax.rsqrt(jnp.mean(u * u, axis=1, keepdims=True) + norm_eps)
        target[at, :] = (u * scale * gain).astype(target.dtype)


def turned(u, cos_ref, sin_ref):
    return u * cos_ref[...] + pltpu.roll(u, HEAD // 2, 1) * sin_ref[...]


def remote_copy(src, dst, send, receive, target):
    return pltpu.make_async_remote_copy(
        src_ref=src,
        dst_ref=dst,
        send_sem=send,
        recv_sem=receive,
        device_id=target,
        device_id_type=MESH_ID,
    )


def started(src, dst, sem):
    copy = pltpu.make_async_copy(src, dst, sem)
    copy.start()
    return copy


def forward_kernel(heads, groups, S, *refs):
    masters = refs[:4]
    small_own, x_ref, cos_ref, sin_ref, q_ids, k_ids = refs[4:10]
    full = refs[10:14]
    small_full, h1_ref, q_ref, k_out, v_out, o_ref, l_ref, mid_ref, h2_ref, h2_other = refs[14:24]
    h1_t, h1_t_other, o_t, o_t_other = refs[24:28]
    w_in, w_out, gains, mix, kv, bias, vt, lds, hs, hr, h2_sems = refs[28:39]
    own = refs[39:43]
    stages = refs[43:47]
    stage_sems = refs[47]
    sems = refs[48:]
    z = lax.axis_index("z")
    c = lax.axis_index("c")
    piece = x_ref.shape[0]
    reach = kv.shape[0] // piece - 1
    half = w_in.shape[-1] // 2
    D = x_ref.shape[1]
    half_ff = own[3].shape[-1] // 2
    own_rows = pl.ds(reach * piece, piece)
    kv[...] = jnp.zeros_like(kv)
    sent = []
    loads = {}

    def gain_row(i):
        return jnp.concatenate([gains[zz, i : i + 1, :] for zz in range(S)], axis=1).astype(F32)

    def start_norm(ready):
        ready(None)
        started(small_full, gains, lds.at[0]).wait()
        norm_rows(x_ref, gain_row(0), h1_ref)


    def of_weight(g):
        return sum(group[0][0] == groups[g][0][0] for group in groups[:g])

    def stage(g):
        i, r0, rn, c0 = groups[g][0][:4]
        slot = of_weight(g) % stages[i].shape[0]
        cols = pl.ds(0, masters[i].shape[-1])
        if i == 3:
            first = c0 // half_ff * 2 * half_ff + c * half_ff
            cols = pl.ds(pl.multiple_of(first, 128), half_ff)
        src = masters[i].at[:, :, pl.ds(r0, rn), cols]
        loads["stage", g] = started(src, stages[i].at[slot], stage_sems.at[g])

    for g in range(len(groups)):
        if of_weight(g) < stages[groups[g][0][0]].shape[0]:
            stage(g)

    def prepare(g):
        i, r0, rn, c0 = groups[g][0][:4]
        slot = of_weight(g) % stages[i].shape[0]
        loads.pop(("stage", g)).wait()
        cols = pl.ds(c0, half_ff) if i == 3 else pl.ds(0, own[i].shape[-1])

        @pl.loop(0, 8)
        def _(p):
            kk, h = p // 2, p % 2
            own[i][kk, h, pl.ds(r0, rn), cols] = stages[i][slot, kk, h].astype(BF)

        later = g + stages[i].shape[0]
        if later < len(groups) and groups[later][0][0] == i:
            stage(later)

    def start_project(ready):
        ready(0)
        for i in range(2):
            at = pl.ds(i * half, half)
            loads[i] = started(full[0].at[:, :, :, :, at], w_in.at[:, :, :, :, at], lds.at[1 + i])

    def project(i):
        loads.pop(i).wait()
        weight = w_in[:, :, :, :, i * half : (i + 1) * half].reshape(D, half)
        mix[...] = nn(h1_ref[...], weight)
        for j in range(half // HEAD):
            h = i * (half // HEAD) + j
            u = mix[:, j * HEAD : (j + 1) * HEAD]
            if h < heads:
                q_ref[:, h * HEAD : (h + 1) * HEAD] = turned(u, cos_ref, sin_ref).astype(BF)
            elif h == heads:
                kv[own_rows, :HEAD] = turned(u, cos_ref, sin_ref).astype(BF)
            else:
                kv[own_rows, HEAD:] = u.astype(BF)

    def halo(d, starting):
        there = kv.at[pl.ds((reach - d) * piece, piece)]
        target = {"z": jnp.minimum(z + d, S - 1)}
        copy = remote_copy(kv.at[own_rows], there, hs.at[d - 1], hr.at[d - 1], target)

        @pl.when(z + d < S)
        def _():
            if starting:
                copy.start()
            else:
                copy.wait_send()

        if not starting:

            @pl.when(z >= d)
            def _():
                remote_copy(there, there, hs.at[d - 1], hr.at[d - 1], target).wait_recv()

    def start_attention():
        for d in range(1, reach + 1):
            halo(d, False)
        k_out[...] = kv[:, :HEAD]
        v_out[...] = kv[:, HEAD:]
        vt[...] = kv[:, HEAD:].T
        fill_bias(bias, q_ids, k_ids, 0, piece, WINDOW + piece)

    def attention(first, count):
        for h in range(first, first + count):
            fwd_step(h, 0, piece, q_ids, q_ref, k_out, o_ref, l_ref, bias, vt)

    def start_output(ready):
        ready(1)
        for i in range(2):
            at = pl.ds(i * (D // 2), D // 2)
            loads[i] = started(full[1].at[:, :, :, :, at], w_out.at[:, :, :, :, at], lds.at[3 + i])

    def output():
        n = D // 2
        for i in range(2):
            loads.pop(i).wait()
            at = slice(i * n, (i + 1) * n)
            weight = w_out[:, :, :, :, at].reshape(D, n)
            mid_ref[:, at] = x_ref[:, at].astype(F32) + nn(o_ref[...], weight)

    def finish():
        norm_rows(mid_ref, gain_row(1), h2_ref)
        to_partner(h2_ref, h2_other, 0)

    def to_partner(src, dst, i):
        copy = remote_copy(src, dst, h2_sems.at[2 * i], h2_sems.at[2 * i + 1], {"c": 1 - c})
        copy.start()
        sent.append(copy.wait)

    def transpose(src, dst, there, i):
        for j in range(0, D, HEAD):
            dst[j : j + HEAD, :] = src[:, j : j + HEAD].T
        to_partner(dst, there, i)

    third = heads // 3
    plan = {
        2: lambda ready: start_norm(ready),
        5: lambda ready: start_project(ready),
        6: lambda ready: (project(0), project(1), [halo(d, True) for d in range(1, reach + 1)]),
        7: lambda ready: (start_attention(), attention(0, third), start_output(ready)),
        8: lambda ready: attention(third, third),
        9: lambda ready: attention(2 * third, third),
        10: lambda ready: output(),
        11: lambda ready: (finish(), transpose(h1_ref, h1_t, h1_t_other, 1)),
        12: lambda ready: transpose(o_ref, o_t, o_t_other, 2),
    }

    def work(t, ready):
        if t in plan:
            plan[t](ready)

    gather_kernel(
        [True, True, True, False], groups, S, own, full, sems, small_own, small_full, prepare, work
    )
    for wait in sent:
        wait()


def forward(masters, small, x, cos, sin, q_ids, k_ids, heads, S, cid):
    piece, D = x.shape
    keys = k_ids.shape[0]
    r = masters[0].shape[2]
    rf = masters[2].shape[2]
    all_in, all_out, all_gate = (masters[i].shape[-1] for i in (0, 1, 3))
    half_in, half_out, half_ff = all_in // 2, all_out // 2, all_gate // 4

    def routed(i, r0, rn, c0, cn):
        return [(i, r0, rn, c0, cn, "xy")]

    groups = [routed(0, 0, r, 0, half_in), routed(1, 0, r, 0, half_out)]
    groups += [routed(2, i, 48, 0, half_out) for i in range(0, rf, 48)]
    groups += [routed(3, i, 16, j * half_ff, half_ff) for j in range(2) for i in range(0, r, 16)]

    def body(*refs):
        forward_kernel(heads, groups, S, *refs)

    def shape(*dims, dtype=BF):
        return jax.ShapeDtypeStruct(dims, dtype)

    own = [(4, 2) + masters[i].shape[2:] for i in range(3)] + [(4, 2, r, 2 * half_ff)]
    outs = [shape(S, *o) for o in own]
    outs += [
        shape(S, *small.shape),
        shape(piece, D),
        shape(piece, heads * HEAD),
        shape(keys, HEAD),
        shape(keys, HEAD),
        shape(piece, heads * HEAD),
        shape(heads, 1, piece, dtype=F32),
        shape(piece, D, dtype=F32),
        shape(piece, D),
        shape(piece, D),
        shape(D, piece),
        shape(D, piece),
        shape(D, piece),
        shape(D, piece),
    ]
    dma = pltpu.SemaphoreType.DMA
    return pl.pallas_call(
        body,
        out_shape=tuple(outs),
        in_specs=[ANY] * 4 + [VM] * 6,
        out_specs=tuple([ANY] * 5 + [VM] * 8 + [ANY] + [VM, ANY] * 2),
        scratch_shapes=[
            pltpu.VMEM((S,) + own[0], BF),
            pltpu.VMEM((S,) + own[1], BF),
            pltpu.VMEM((S,) + small.shape, BF),
            pltpu.VMEM((piece, half_in), F32),
            pltpu.VMEM((keys, 2 * HEAD), BF),
            pltpu.VMEM((keys, piece), F32),
            pltpu.VMEM((HEAD, keys), BF),
            dma((5,)),
            dma((2,)),
            dma((2,)),
            dma((6,)),
        ]
        + [pltpu.VMEM(o, BF) for o in own]
        + [
            pltpu.VMEM((1, 4, 2, r, all_in), F32),
            pltpu.VMEM((1, 4, 2, r, all_out), F32),
            pltpu.VMEM((2, 4, 2, 48, all_out), F32),
            pltpu.VMEM((2, 4, 2, 16, half_ff), F32),
            dma((len(groups),)),
        ]
        + gather_sems(len(groups), sum(map(len, groups)), S),
        compiler_params=pltpu.CompilerParams(
            collective_id=cid, has_side_effects=True, vmem_limit_bytes=VMEM_BYTES
        ),
    )(*masters, small, x, cos, sin, q_ids, k_ids)


def back_step(h, first, rows, refs, bias, kt, finish):
    q_ref, k_ref, v_ref, o_ref, do_ref, l_ref, dq_ref, dk_ref, dv_ref = refs
    span = WINDOW + rows
    factor = HEAD**-0.5 * LOG2E
    cols = pl.ds(h * HEAD, HEAD)
    q = q_ref[pl.ds(first, rows), cols]
    do = do_ref[pl.ds(first, rows), cols]
    o = o_ref[pl.ds(first, rows), cols]
    delta = jnp.sum((do.astype(F32) * o.astype(F32)).T, axis=0, keepdims=True)
    s = nt(k_ref[pl.ds(first, span), :], q) * factor + bias[...]
    p = jnp.exp2(s - l_ref[h, :, pl.ds(first, rows)])
    dp = nt(v_ref[pl.ds(first, span), :], do)
    ds = (p * ((dp - delta) * HEAD**-0.5)).astype(BF)
    dv_ref[pl.ds(first, span), :] += nn(p.astype(BF), do)
    dk_ref[pl.ds(first, span), :] += nn(ds, q)
    dq = nn(kt[:, pl.ds(first, span)], ds).T
    dq_ref[pl.ds(first, rows), cols] = finish(dq, first).astype(dq_ref.dtype)


def bwd_kernel(heads, rows, q_ids, k_ids, *refs):
    *arrays, bias, kt = refs
    q_ref, k_ref = arrays[:2]
    dk_ref, dv_ref = arrays[-2:]
    kt[...] = k_ref[...].T
    dk_ref[...] = jnp.zeros_like(dk_ref)
    dv_ref[...] = jnp.zeros_like(dv_ref)
    for first in range(0, q_ref.shape[0], rows):
        fill_bias(bias, q_ids, k_ids, first, rows, WINDOW + rows)
        for h in range(heads):
            back_step(h, first, rows, arrays, bias, kt, lambda dq, first: dq)


def attend(q_ids, k_ids, q, k, v, heads, rows):
    def body(*refs):
        fwd_kernel(heads, rows, *refs)

    return pl.pallas_call(
        body,
        out_shape=(
            jax.ShapeDtypeStruct(q.shape, BF),
            jax.ShapeDtypeStruct((heads, 1, q.shape[0]), F32),
        ),
        in_specs=[VM] * 5,
        out_specs=(VM, VM),
        scratch_shapes=[
            pltpu.VMEM((WINDOW + rows, rows), F32),
            pltpu.VMEM((HEAD, k.shape[0]), BF),
        ],
        compiler_params=pltpu.CompilerParams(vmem_limit_bytes=VMEM_BYTES),
        cost_estimate=pl.CostEstimate(
            flops=4 * q.size * k.shape[0], bytes_accessed=4 * q.size, transcendentals=q.size * 12
        ),
    )(q_ids, k_ids, q, k, v)


def attend_back(q_ids, k_ids, q, k, v, o, do, l, heads, rows):
    def body(*refs):
        bwd_kernel(heads, rows, *refs)

    return pl.pallas_call(
        body,
        out_shape=(
            jax.ShapeDtypeStruct(q.shape, F32),
            jax.ShapeDtypeStruct(k.shape, F32),
            jax.ShapeDtypeStruct(k.shape, F32),
        ),
        in_specs=[VM] * 8,
        out_specs=(VM, VM, VM),
        scratch_shapes=[
            pltpu.VMEM((WINDOW + rows, rows), F32),
            pltpu.VMEM((HEAD, k.shape[0]), BF),
        ],
        compiler_params=pltpu.CompilerParams(vmem_limit_bytes=VMEM_BYTES),
        cost_estimate=pl.CostEstimate(
            flops=10 * q.size * k.shape[0], bytes_accessed=12 * q.size, transcendentals=q.size * 12
        ),
    )(q_ids, k_ids, q, k, v, o, do, l)


def mlp_kernel(
    where, two_own, two_other, df_own, df_other, gate_ref, up_ref, down_ref, *results
):
    two_t, hid_t, grads, out_low, back_low, out, back = results
    step = pl.program_id(0)
    rows, D = two_own.shape
    part = two_t.shape[0]
    core = where[0]
    block = 512

    @pl.when(step == 0)
    def _():
        out[...] = jnp.zeros_like(out)
        back[...] = jnp.zeros_like(back)

    @pl.when(step < D // part)
    def _():
        cols = pl.ds(pl.multiple_of(step * part, part), part)
        for two_ref, owner in ((two_own, core), (two_other, 1 - core)):
            at = pl.ds(pl.multiple_of(owner * rows, rows), rows)
            two_t[:, at] = two_ref[:, cols].T

    def tokens(two_ref, df_ref, owner, first):
        here = pl.ds(first, block)
        at = pl.ds(pl.multiple_of(owner * rows + first, block), block)
        two = two_ref[here, :]
        gate = nn(two, gate_ref[...])
        up = nn(two, up_ref[...])
        grad = nt(df_ref[here, :], down_ref[...])
        slope = 0.7978845608028654
        bent = jnp.tanh(slope * (gate + 0.044715 * (gate * gate * gate)))
        upper = 0.5 * (1.0 + bent)
        act = gate * upper
        act_slope = upper + 0.5 * gate * (1.0 - bent * bent) * (
            slope * (1.0 + 3 * 0.044715 * (gate * gate))
        )
        hid = (act * up).astype(BF)
        grad_gate = (grad * up * act_slope).astype(BF)
        grad_up = (grad * act).astype(BF)
        hid_t[:, at] = hid.T
        grads[0, at, :] = grad_gate
        grads[1, at, :] = grad_up
        out[at, :] += nn(hid, down_ref[...])
        back[at, :] += nt(grad_gate, gate_ref[...]) + nt(grad_up, up_ref[...])

    for two_ref, df_ref, owner in ((two_own, df_own, core), (two_other, df_other, 1 - core)):
        for first in range(0, rows, block):
            tokens(two_ref, df_ref, owner, first)

    @pl.when(step == pl.num_programs(0) - 1)
    def _():
        out_low[...] = out[...].astype(BF)
        back_low[...] = back[...].astype(BF)


def mlp_call(core, two, df, gate_full, down_full):
    T, D = 2 * two[0].shape[0], two[0].shape[1]
    half_ff = gate_full.shape[1] // 2
    tile = 256
    tiles = half_ff // tile
    part = max(D // tiles // 128 * 128, 256)
    last = D // part - 1

    def body(*refs):
        mlp_kernel(*refs)

    once = pl.Buffered(1)
    piece = pl.BlockSpec((T // 2, D), lambda i, w: (0, 0), pipeline_mode=once)
    return pl.pallas_call(
        body,
        grid_spec=pltpu.PrefetchScalarGridSpec(
            num_scalar_prefetch=1,
            grid=(tiles,),
            in_specs=[
                piece,
                piece,
                piece,
                piece,
                pl.BlockSpec((D, tile), lambda i, w: (0, i)),
                pl.BlockSpec((D, tile), lambda i, w: (0, tiles + i)),
                pl.BlockSpec((tile, D), lambda i, w: (w[0] * tiles + i, 0)),
            ],
            out_specs=[
                pl.BlockSpec((part, T), lambda i, w: (jnp.minimum(i, last), 0)),
                pl.BlockSpec((tile, T), lambda i, w: (i, 0)),
                pl.BlockSpec((2, T, tile), lambda i, w: (0, 0, i)),
                pl.BlockSpec((T, D), lambda i, w: (0, 0), pipeline_mode=once),
                pl.BlockSpec((T, D), lambda i, w: (0, 0), pipeline_mode=once),
            ],
            scratch_shapes=[pltpu.VMEM((T, D), F32), pltpu.VMEM((T, D), F32)],
        ),
        out_shape=[
            jax.ShapeDtypeStruct((D, T), BF),
            jax.ShapeDtypeStruct((half_ff, T), BF),
            jax.ShapeDtypeStruct((2, T, half_ff), BF),
            jax.ShapeDtypeStruct((T, D), BF),
            jax.ShapeDtypeStruct((T, D), BF),
        ],
        compiler_params=pltpu.CompilerParams(
            dimension_semantics=("arbitrary",), vmem_limit_bytes=BACKWARD_VMEM
        ),
        cost_estimate=pl.CostEstimate(
            flops=12 * T * D * half_ff, bytes_accessed=40 * 2**20, transcendentals=T * half_ff
        ),
    )(core, *two, *df, gate_full, gate_full, down_full)


def split_widths(total, most):
    first = -(-total // 256) * 128
    assert first <= most
    return (first, total - first)


def backward_kernel(heads, sides, parts, S, *refs):
    two, hid, *flats = refs[:6]
    flat_own, flat_other, norm_own, norm_other = flats[2], flats[3], flats[0], flats[1]
    grads, dy_own, dy_other, back, middle, w_out, gains_ref, x_ref, w_in = refs[6:15]
    q_ids, k_ids, q_ref, k_ref, v_ref, o_ref, l_ref, cos_ref, sin_ref = refs[15:24]
    out, hid_land, x_grad = refs[24:27]
    left, right, out_right, mix_right, s1, g1, s2, g2, fz, gz, mine, da, do, got = refs[27:41]
    tails, landed_tails, gains, x1, dk, dv, bias, kt, mixed, w_rows = refs[41:51]
    lds, rds, fs, cs_in, hs, hr, s1s, s1r, s2s, s2r, zs, zr, ls, xs, xr, ys, yr, cs, cr = refs[51:]
    _, _, _, r, T = left.shape
    n = right.shape[2]
    piece, D = da.shape
    reach = tails.shape[0]
    wide = sides * parts
    rows_groups = hid.shape[1]
    chunk_out = wide + rows_groups
    mix_half = mix_right.shape[1]
    widths = [n] * (chunk_out + 1) + list(split_widths(mix_half, n))
    nc = len(widths)
    left_slots = left.shape[0]
    right_slots = right.shape[0]
    slots = g1.shape[0]
    y, x, c, z = (lax.axis_index(a) for a in ("y", "x", "c", "z"))
    k = y * 2 + x
    kx = y * 2 + 1 - x
    ky = (1 - y) * 2 + x
    kxy = 3 - k
    to_x = {"x": 1 - x}
    to_y = {"y": 1 - y}
    to_c = {"c": 1 - c}
    place = pl.ds(pl.multiple_of(c * piece, piece), piece)
    other_place = pl.ds(pl.multiple_of((1 - c) * piece, piece), piece)
    loads = {}
    pending = {}

    def fetch(key, src, dst, sem):
        loads.setdefault(key, []).append(started(src, dst, sem))

    def landed(key):
        for copy in loads.pop(key, []):
            copy.wait()

    def launch(key, copy):
        copy.start()
        pending.setdefault(key, []).append(copy)

    def drain(key):
        for copy in pending.pop(key, []):
            copy.wait_send()

    groups = 3 + rows_groups

    def group_of(t):
        if t < wide:
            return 0
        return min(t - wide + 1, groups - 1)

    def fetch_left(g):
        slot = g % left_slots
        for p in range(8):
            h, kk = p // 4, p % 4
            if g == 0:
                fetch(("l", g), two.at[:, kk, h], left.at[slot, p], lds.at[g, p, 0])
                continue
            if g <= rows_groups:
                if g == 1 and p == 0:
                    landed_hid.wait_recv()
                half = left.shape[2] // 2
                pairs = [
                    (hid.at[:, g - 1, kk, h], left.at[slot, p, pl.ds(c * half, half)]),
                    (hid_land.at[:, g - 1, kk, h], left.at[slot, p, pl.ds((1 - c) * half, half)]),
                ]
            else:
                own, other = (flat_own, flat_other) if g == groups - 2 else (norm_own, norm_other)
                pairs = [
                    (own.at[:, kk, h], left.at[slot, p, :, :, place]),
                    (other.at[:, kk, h], left.at[slot, p, :, :, other_place]),
                ]
            for i, (src, dst) in enumerate(pairs):
                fetch(("l", g), src, dst, lds.at[g, p, i])

    def fetch_right(t):
        slot = t % right_slots
        if t < wide:
            src = grads.at[t // parts, :, pl.ds((t % parts) * n, n)]
            fetch(("r", t), src, right.at[slot], rds.at[t, 0])
        elif t == wide:
            keep = pl.ds(pl.multiple_of(c * n, n), n)
            fetch(("r", t), dy_own.at[:, keep], right.at[slot, place], rds.at[t, 0])
            fetch(("r", t), dy_other.at[:, keep], right.at[slot, other_place], rds.at[t, 1])

    fetch_right(0)
    fetch_left(0)
    fetch_right(1)
    landed_tails[...] = jnp.zeros_like(landed_tails)
    barrier = pltpu.get_barrier_semaphore()
    peers = [to_x, to_y, to_c] + [{"z": lax.rem(z + e, S)} for e in range(1, S)]
    for target in peers:
        pl.semaphore_signal(barrier, inc=1, device_id=target, device_id_type=MESH_ID)
    pl.semaphore_wait(barrier, len(peers))
    launch("end", remote_copy(back.at[other_place], got, cs_in.at[0], cs_in.at[1], to_c))
    launch("end", remote_copy(hid, hid_land, cs_in.at[2], cs_in.at[3], to_c))
    landed_hid = remote_copy(hid, hid_land, cs_in.at[2], cs_in.at[3], to_c)
    landed_back = remote_copy(got, got, cs_in.at[0], cs_in.at[1], to_c)

    def product(t, p):
        lhs = left[group_of(t) % left_slots, p].reshape(S * r, T)
        if t <= chunk_out - 1:
            return nn(lhs, right[min(t, wide) % right_slots])
        if t == chunk_out:
            return nn(lhs, out_right[...])
        first = sum(widths[chunk_out + 1 : t])
        return nn(lhs, mix_right[:, first : first + widths[t]])

    def cut(ref, t):
        return ref if widths[t] == n else ref.at[:, pl.ds(0, widths[t])]

    def first(t):
        slot = t % 2
        landed(("l", group_of(t)))
        landed(("r", t))
        drain(("s1", t - 2))
        for i in range(2):
            for j, p, target in ((i, i * 2 + 1 - x, to_x), (2 + i, 4 + (1 - y) * 2 + i, to_y)):
                src, dst = cut(s1.at[slot, j], t), cut(g1.at[t % slots, j], t)
                src[...] = product(t, p).astype(BF)
                launch(("s1", t), remote_copy(src, dst, s1s.at[t, j], s1r.at[t, j], target))

    def second(t):
        slot = t % 2
        drain(("s2", t - 2))
        for j in range(4):
            dst = cut(g1.at[t % slots, j], t)
            remote_copy(dst, dst, s1s.at[t, j], s1r.at[t, j], to_x).wait_recv()
        for h, p, j, target in ((0, (1 - y) * 2 + x, 1 - y, to_y), (1, 4 + y * 2 + 1 - x, 3 - x, to_x)):
            src, dst = cut(s2.at[slot, h], t), cut(g2.at[t % slots, h], t)
            came = cut(g1.at[t % slots, j], t)
            src[...] = (product(t, p) + came[...].astype(F32)).astype(BF)
            launch(("s2", t), remote_copy(src, dst, s2s.at[t, h], s2r.at[t, h], target))

    def third(t):
        slot = t % 2
        w = widths[t]
        drain(("z", t - 2))
        for h, p, j in ((0, k, y), (1, 4 + k, 2 + x)):
            dst = cut(g2.at[t % slots, h], t)
            remote_copy(dst, dst, s2s.at[t, h], s2r.at[t, h], to_x).wait_recv()
            came = cut(g1.at[t % slots, j], t)
            total = (product(t, p) + came[...].astype(F32) + dst[...].astype(F32)).astype(BF)
            for zz in range(S):
                fz[slot, zz, h, :, :w] = total[zz * r : (zz + 1) * r]
        for e in range(1, S):
            src = fz.at[slot, lax.rem(z + e, S), :, :, pl.ds(0, w)]
            dst = gz.at[t, S - e - 1, :, :, pl.ds(0, w)]
            target = {"z": lax.rem(z + e, S)}
            launch(("z", t), remote_copy(src, dst, zs.at[t, e - 1], zr.at[t, S - e - 1], target))

    def fourth(t):
        slot = t % 2
        w = widths[t]
        drain(("ag", t - 2))
        landed(("o", t - 2))
        for e in range(S - 1):
            dst = gz.at[t, e, :, :, pl.ds(0, w)]
            remote_copy(dst, dst, zs.at[t, e], zr.at[t, e], to_x).wait_recv()
        for h in range(2):
            total = fz[slot, z, h, :, :w].astype(F32)
            for e in range(S - 1):
                total = total + gz[t, e, h, :, :w].astype(F32)
            mine[slot, h, :, :w] = total.astype(BF)
        cols = pl.ds(0, w)
        fetch(("o", t), mine.at[slot, :, :, cols], out.at[t, k, c, :, :, cols], ls.at[t])
        for i, hs_ in enumerate(((0, 1), (1, 0))):
            for h, s, r_, target in ((hs_[0], xs, xr, to_x), (hs_[1], ys, yr, to_y)):
                src, dst = mine.at[slot, h, :, cols], out.at[t, k, c, h, :, cols]
                launch(("ag", t), remote_copy(src, dst, s.at[t, i], r_.at[t, i], target))

    def land(t, kk, h, s, r_, j, target):
        p = out.at[t, kk, c, h, :, pl.ds(0, widths[t])]
        remote_copy(p, p, s.at[t, j], r_.at[t, j], target).wait_recv()
        return p

    def fifth(t):
        p = land(t, kx, 0, xs, xr, 0, to_x)
        launch("end", remote_copy(p, p, ys.at[t, 2], yr.at[t, 2], to_y))
        p = land(t, ky, 1, ys, yr, 0, to_y)
        launch("end", remote_copy(p, p, xs.at[t, 2], xr.at[t, 2], to_x))

    def sixth(t):
        land(t, kx, 1, xs, xr, 1, to_x)
        land(t, ky, 0, ys, yr, 1, to_y)
        land(t, kxy, 1, xs, xr, 2, to_x)
        land(t, kxy, 0, ys, yr, 2, to_y)
        landed(("o", t))
        p = out.at[t, :, c, :, :, pl.ds(0, widths[t])]
        launch("end", remote_copy(p, p, cs.at[t], cr.at[t], to_c))


    def norm_back():
        for key in ("near", "x1", "dy", "gains"):
            landed(key)
        landed_back.wait_recv()
        gain = jnp.concatenate([gains[zz, 1:2, :] for zz in range(S)], axis=1).astype(F32)
        step = 64

        @pl.loop(0, piece // step)
        def _(i):
            at = pl.ds(pl.multiple_of(i * step, step), step)
            u = x1[at, :]
            scale = lax.rsqrt(jnp.mean(u * u, axis=1, keepdims=True) + norm_eps)
            hat = u * scale
            e = (do[at, :].astype(F32) + got[at, :].astype(F32)) * gain
            inner = jnp.mean(e * hat, axis=1, keepdims=True)
            dx = mixed[at, :D].astype(F32) + scale * (e - hat * inner)
            x1[at, :] = dx
            da[at, :] = dx.astype(BF)

        launch("da", remote_copy(give_of(da, n), out_right.at[place], cs_in.at[4], cs_in.at[5], to_c))
        out_right[place, :] = keep_of(da, n)[...]
        for i in range(2):
            fetch("w", w_out.at[pl.ds(T, piece), pl.ds(i * n, n)], got.at[:, pl.ds(i * n, n)], fs.at[7 + i])

    def give_of(ref, width):
        return ref.at[:, pl.ds(pl.multiple_of((1 - c) * width, width), width)]

    def keep_of(ref, width):
        return ref.at[:, pl.ds(pl.multiple_of(c * width, width), width)]

    def heads_back():
        landed("w")
        live = k_ids[pl.ds(reach * piece, piece), :1] != 0
        for j in range(0, D, piece):
            if j < T:
                low, high = right[2, j : j + piece, :], right[3, j : j + piece, :]
            else:
                low, high = got[:, :n], got[:, n:]
            part = nt(da[:, :n], low) + nt(da[:, n:], high)
            do[:, j : j + piece] = jnp.where(live, part, 0.0).astype(BF)

    half_rows = piece // 2
    steps = [(block, h) for block in range(2) for h in range(heads)]

    def turn_back(dq, first):
        at = pl.ds(first, half_rows)
        return dq * cos_ref[at, :] - pltpu.roll(dq, HEAD // 2, 1) * sin_ref[at, :]

    def attention(first_step, count):
        arrays = (q_ref, k_ref, v_ref, o_ref, do, l_ref, mixed, dk, dv)
        if first_step == 0:
            kt[...] = k_ref[...].T
            dk[...] = jnp.zeros_like(dk)
            dv[...] = jnp.zeros_like(dv)
        for block, h in steps[first_step : first_step + count]:
            if h == 0:
                fill_bias(bias, q_ids, k_ids, block * half_rows, half_rows, WINDOW + half_rows)
            back_step(h, block * half_rows, half_rows, arrays, bias, kt, turn_back)

    def tail(d):
        target = {"z": jnp.maximum(z - d, 0)}
        return remote_copy(tails.at[d - 1], landed_tails.at[d - 1], hs.at[d - 1], hr.at[d - 1], target)

    def send_tails():
        for d in range(1, reach + 1):
            at = pl.ds((reach - d) * piece, piece)
            tails[d - 1, :, :HEAD] = dk[at, :].astype(BF)
            tails[d - 1, :, HEAD:] = dv[at, :].astype(BF)

            @pl.when(z >= d)
            def _(d=d):
                tail(d).start()

    def mix_back():
        for d in range(1, reach + 1):

            @pl.when(z >= d)
            def _(d=d):
                tail(d).wait_send()

            @pl.when(z + d < S)
            def _(d=d):
                tail(d).wait_recv()

        at = pl.ds(reach * piece, piece)
        keys, values = dk[at, :], dv[at, :]
        for d in range(1, reach + 1):
            keys = keys + landed_tails[d - 1, :, :HEAD].astype(F32)
            values = values + landed_tails[d - 1, :, HEAD:].astype(F32)
        keys = keys * cos_ref[...] - pltpu.roll(keys, HEAD // 2, 1) * sin_ref[...]
        width = heads * HEAD
        mixed[:, width : width + HEAD] = keys.astype(BF)
        mixed[:, width + HEAD :] = values.astype(BF)
        launch("end", remote_copy(give_of(mixed, mix_half), mix_right.at[place], cs_in.at[6], cs_in.at[7], to_c))
        mix_right[place, :] = keep_of(mixed, mix_half)[...]

    step_rows = w_rows.shape[1]

    def fetch_rows(j):
        if j * step_rows < D:
            fetch(("q", j), w_in.at[pl.ds(j * step_rows, step_rows)], w_rows.at[j % 2], fs.at[9 + j % 2])

    def start_input():
        drain("da")
        fetch_rows(0)
        fetch_rows(1)
        fetch("x0", x_ref, got, fs.at[4])

    def project_back(j):
        landed(("q", j))
        da[:, j * step_rows : (j + 1) * step_rows] = nt(mixed[...], w_rows[j % 2]).astype(BF)
        fetch_rows(j + 2)

    def input_back():
        landed("x0")
        gain = jnp.concatenate([gains[zz, 0:1, :] for zz in range(S)], axis=1).astype(F32)
        step = 64

        @pl.loop(0, piece // step)
        def _(i):
            at = pl.ds(pl.multiple_of(i * step, step), step)
            u = got[at, :].astype(F32)
            scale = lax.rsqrt(jnp.mean(u * u, axis=1, keepdims=True) + norm_eps)
            hat = u * scale
            e = da[at, :].astype(F32) * gain
            inner = jnp.mean(e * hat, axis=1, keepdims=True)
            do[at, :] = (x1[at, :] + scale * (e - hat * inner)).astype(BF)

        fetch("x_grad", do, x_grad, fs.at[0])

    def came(ref, i):
        ref = ref.at[other_place]
        remote_copy(ref, ref, cs_in.at[i], cs_in.at[i + 1], to_c).wait_recv()

    stages = (first, second, third, fourth, fifth, sixth)

    fetch("near", back.at[place], do, fs.at[0])
    fetch("x1", middle, x1, fs.at[1])
    fetch("dy", dy_own, mixed.at[:, pl.ds(0, D)], fs.at[2])
    fetch("gains", gains_ref, gains, fs.at[3])
    for i in range(2):
        fetch("w", w_out.at[pl.ds(0, T), pl.ds(i * n, n)], right.at[2 + i], fs.at[5 + i])
    each = 5

    def work(t):
        if t == 0:
            norm_back()
        if t == 1:
            heads_back()
        if t >= 2 and (t - 2) * each < len(steps):
            attention((t - 2) * each, each)
        if t == 7:
            send_tails()
        if t == 8:
            mix_back()
            start_input()
        if t >= 9 and (t - 9) * step_rows < D:
            project_back(t - 9)
        if t == 15:
            input_back()

    for t in range(nc + len(stages) - 1):
        for lag, stage in enumerate(stages):
            if lag == 0 and t == chunk_out:
                came(out_right, 4)
            if lag == 0 and t == chunk_out + 1:
                came(mix_right, 6)
            if 0 <= t - lag < nc:
                stage(t - lag)
            if lag == 0:
                work(t)
        if t == 1:
            fetch_right(2)
        if t >= 1:
            fetch_right(t + 2)
        for g in range(1, groups):
            if t == wide + g - (3 if g < left_slots else 2):
                fetch_left(g)
    for t in range(nc):
        p = out.at[t, :, 1 - c, :, :, pl.ds(0, widths[t])]
        remote_copy(p, p, cs.at[t], cr.at[t], to_c).wait_recv()
    for key in list(pending):
        drain(key)
    for key in list(loads):
        landed(key)


def backward(
    two_t, hid_t, transposed, grads, dy, back, middle, w_out, gains, x, w_in, attention, tables, heads, S, cid
):
    D, T = two_t.shape
    sides, _, half_ff = grads.shape
    piece = middle.shape[0]
    n = D // 2
    r = D // (S * 8)
    parts = half_ff // n
    rows_groups = 2 * half_ff // (S * 8 * r)
    mixed = attention[2].shape[1] + 2 * HEAD
    nc = sides * parts + rows_groups + 3
    m = S * r
    slots = 5
    keys = attention[3].shape[0]
    reach = keys // piece - 1
    dma = pltpu.SemaphoreType.DMA
    hid_shape = (S // 2, rows_groups, 4, 2, r, T)

    def body(*refs):
        backward_kernel(heads, sides, parts, S, *refs)

    def vmem(*shape):
        return pltpu.VMEM(shape, BF)

    results = pl.pallas_call(
        body,
        out_shape=(
            jax.ShapeDtypeStruct((nc, 4, 2, 2, r, n), BF),
            jax.ShapeDtypeStruct(hid_shape, BF),
            jax.ShapeDtypeStruct((piece, D), BF),
        ),
        in_specs=[ANY] * 15 + [VM] * 9,
        out_specs=(ANY, ANY, ANY),
        scratch_shapes=[
            vmem(3, 8, S, r, T),
            vmem(4, T, n),
            vmem(T, n),
            vmem(T, mixed // 2),
            vmem(2, 4, m, n),
            vmem(slots, 4, m, n),
            vmem(2, 2, m, n),
            vmem(slots, 2, m, n),
            vmem(2, S, 2, r, n),
            vmem(nc, S - 1, 2, r, n),
            vmem(2, 2, r, n),
            vmem(piece, D),
            vmem(piece, D),
            vmem(piece, D),
            vmem(reach, piece, 2 * HEAD),
            vmem(reach, piece, 2 * HEAD),
            vmem(*gains.shape),
            pltpu.VMEM((piece, D), F32),
            pltpu.VMEM((keys, HEAD), F32),
            pltpu.VMEM((keys, HEAD), F32),
            pltpu.VMEM((WINDOW + piece // 2, piece // 2), F32),
            pltpu.VMEM((HEAD, keys), BF),
            vmem(piece, mixed),
            vmem(2, 256, mixed),
            dma((rows_groups + 3, 8, 2)),
            dma((nc, 2)),
            dma((11,)),
            dma((8,)),
            dma((reach,)),
            dma((reach,)),
            dma((nc, 4)),
            dma((nc, 4)),
            dma((nc, 2)),
            dma((nc, 2)),
            dma((nc, S)),
            dma((nc, S)),
            dma((nc,)),
            dma((nc, 3)),
            dma((nc, 3)),
            dma((nc, 3)),
            dma((nc, 3)),
            dma((nc,)),
            dma((nc,)),
        ],
        compiler_params=pltpu.CompilerParams(
            collective_id=cid, has_side_effects=True, vmem_limit_bytes=BACKWARD_VMEM
        ),
    )(
        two_t.reshape(S, 4, 2, r, T),
        hid_t.reshape(hid_shape),
        *[v.reshape(S, 4, 2, r, piece) for v in transposed],
        grads,
        *dy,
        back,
        middle,
        w_out,
        gains,
        x,
        w_in,
        *attention,
        *tables,
    )
    return results[0], results[2]


def adam_kernel(total, widths, gains, count_ref, rates_ref, g_ref, w_ref, m_ref, g_out, w_out, m_out, *more):
    step_value = count_ref[0].astype(F32)
    log_first = jnp.log(jnp.full((8, 128), beta_first, F32))
    log_second = jnp.log(jnp.full((8, 128), beta_second, F32))
    unfix_first = (1.0 / (1.0 - jnp.exp(step_value * log_first)))[:1, :1]
    unfix_second = (1.0 / (1.0 - jnp.exp(step_value * log_second)))[:1, :1]
    rate, decay = rates_ref[0], rates_ref[1]
    rows = w_ref.shape[0]

    if gains:

        @pl.when((pl.program_id(1) == 0) & (pl.program_id(2) == 0))
        def _():
            more[0][...] = jnp.zeros_like(more[0])

    for i, n in enumerate(widths):
        at = pl.ds(sum(widths[:i]), n)
        grad = g_ref[i, :, 0, :, :, :n].reshape(rows, n).astype(F32) * (1.0 / total)
        w = w_ref[:, at]
        first = beta_first * m_ref[0, :, at] + (1.0 - beta_first) * grad
        second = beta_second * m_ref[1, :, at] + (1.0 - beta_second) * grad * grad
        step = first * unfix_first / (jnp.sqrt(second * unfix_second) + adam_eps) + decay * w
        g_out[:, at] = grad
        w_out[:, at] = w - rate * step
        m_out[0, :, at] = first
        m_out[1, :, at] = second
        if gains:
            both = w.astype(BF).astype(F32) * grad
            for j in range(0, n, 128):
                more[0][...] += both[:, j : j + 128]


def adam_call(
    weight, moments, grads, count, rates, total, base, widths, sides=1, tiles=1, gains=False, chips=4
):
    _, _, _, _, r, n = grads.shape
    wide = len(widths)

    def g_place(kk, cc, ss, tt):
        return (base // wide + ss + tt, kk, cc, 0, 0, 0)

    def place(kk, cc, ss, tt):
        return (tt * (4 // chips) + kk, ss * 2 + cc)

    def m_place(*at):
        return (0,) + place(*at)

    rows = chips * 2 * r
    w_spec = pl.BlockSpec((rows, sum(widths)), place)
    m_spec = pl.BlockSpec((2, rows, sum(widths)), m_place)
    smem = pl.BlockSpec(memory_space=pltpu.SMEM)
    like = jax.ShapeDtypeStruct(weight.shape, F32)
    out_specs = [w_spec, w_spec, m_spec]
    out_shape = [like, like, jax.ShapeDtypeStruct(moments.shape, F32)]
    if gains:
        out_specs.append(pl.BlockSpec((rows, 128), lambda kk, cc, ss, tt: (kk, 0)))
        out_shape.append(jax.ShapeDtypeStruct((weight.shape[0], 128), F32))

    def body(*refs):
        adam_kernel(total, widths, gains, *refs)

    return pl.pallas_call(
        body,
        grid=(4 // chips, 2, sides, tiles),
        in_specs=[smem, smem, pl.BlockSpec((wide, chips, 1, 2, r, n), g_place), w_spec, m_spec],
        out_specs=out_specs,
        out_shape=out_shape,
        compiler_params=pltpu.CompilerParams(
            dimension_semantics=("arbitrary",) * 4, vmem_limit_bytes=VMEM_BYTES
        ),
        cost_estimate=pl.CostEstimate(
            flops=20 * weight.size,
            bytes_accessed=30 * weight.size,
            transcendentals=weight.size,
        ),
    )(count, rates, grads, weight, moments)


def dot(a, b):
    return jnp.dot(a, b, preferred_element_type=F32)


def dot_rows(a, b):
    return lax.dot_general(a, b, (((1,), (0,)), ((), ())), preferred_element_type=F32)


def dot_t(a, b):
    return lax.dot_general(a, b, (((1,), (1,)), ((), ())), preferred_element_type=F32)


def on_device(
    Y,
    S,
    block_in,
    cotangent,
    segment_ids,
    input_proj,
    output_proj,
    gate_up,
    down_weight,
    norm_gains,
    input_moments,
    output_moments,
    gate_moments,
    down_moments,
    gain_moments,
    update_count,
    optimizer_rates,
):
    seq_place = lax.axis_index("z")
    core = lax.axis_index("c")
    first_core = core == 0
    D = block_in.shape[-1]
    half_ff = FF // 2
    rows_d = input_proj.shape[0]
    rows_f = down_weight.shape[0]
    fast = Y == 2 and rows_d % 128 == 0
    in_half = input_proj.shape[1] // 2
    d_half = D // 2
    r = rows_d // 8

    gains_low = norm_gains.astype(BF)
    tokens = block_in[0].astype(F32)
    piece_len = tokens.shape[0]
    width_q = HEADS * HEAD
    positions = seq_place * piece_len + jnp.arange(piece_len, dtype=jnp.int32)
    reach_count = (WINDOW + piece_len - 2) // piece_len
    key_span = reach_count * piece_len
    segments = segment_ids[0]
    padded_ids = jnp.concatenate([jnp.full((key_span,), -1, jnp.int32), segments])
    query_ids = lax.dynamic_slice_in_dim(segments, seq_place * piece_len, piece_len)
    key_ids = lax.dynamic_slice_in_dim(padded_ids, seq_place * piece_len, key_span + piece_len)
    live_rows = query_ids != 0
    query_row = query_ids[None, :]
    key_column = key_ids[:, None]

    if fast:
        frequency = 10000.0 ** (-2.0 * jnp.arange(HEAD // 2).astype(F32) / HEAD)
        angles = positions.astype(F32)[:, None] * jnp.concatenate([frequency, frequency])[None, :]
        side = jnp.where(jnp.arange(HEAD) < HEAD // 2, -1.0, 1.0)
        cos_table, sin_table = jnp.cos(angles), jnp.sin(angles) * side
        (
            in_full,
            out_full,
            down_full,
            gate_full,
            gains_full,
            normed,
            queries,
            key_rows,
            values,
            flat_heads,
            log_totals,
            middle,
            normed_two,
            two_other,
            *transposed,
        ) = forward(
            [
                w.reshape(4, 2, w.shape[0] // 8, w.shape[1])
                for w in (input_proj, output_proj, down_weight, gate_up)
            ],
            jnp.concatenate([gains_low] * 8, axis=0),
            block_in[0],
            cos_table,
            sin_table,
            query_row,
            key_column,
            HEADS,
            S,
            0,
        )
        in_full = in_full.reshape(D, 2 * in_half)
        out_full = out_full.reshape(D, D)
        gains_small = gains_full
        gains_full = gains_full[:, :2].transpose(1, 0, 2).reshape(2, D)
        down_full = down_full.reshape(FF, D)
        gate_full = gate_full.reshape(D, 2 * half_ff)
        gains_wide = gains_full.astype(F32)
    else:
        gate_low = jnp.concatenate(
            [
                lax.dynamic_slice_in_dim(gate_up, side * FF + core * half_ff, half_ff, 1)
                for side in range(2)
            ],
            axis=1,
        )
        in_full, out_full, down_full, gate_full = (
            lax.all_gather(w.astype(BF), "z", axis=0, tiled=True)
            for w in (input_proj, output_proj, down_weight, gate_low)
        )
        gains_full = lax.all_gather(gains_low, "z", axis=1, tiled=True)
        gains_wide = gains_full.astype(F32)
        normed = root_norm(tokens, gains_wide[0]).astype(BF)
        mixed_proj = dot(normed, in_full)
        queries = (
            rotate(mixed_proj[:, :width_q].reshape(piece_len, HEADS, HEAD), positions, 1.0)
            .astype(BF)
            .reshape(piece_len, width_q)
        )
        own_keys = rotate(mixed_proj[:, width_q : width_q + HEAD], positions, 1.0)
        own_pair = jnp.concatenate([own_keys, mixed_proj[:, width_q + HEAD :]], axis=1).astype(BF)
        earlier = []
        for back_step in range(reach_count, 0, -1):
            earlier.append(passed_along(own_pair, "z", back_step))
        key_pairs = jnp.concatenate(earlier + [own_pair], axis=0)
        key_rows = key_pairs[:, :HEAD]
        values = key_pairs[:, HEAD:]
        flat_heads, log_totals = attend(
            query_row, key_column, queries, key_rows, values, HEADS, piece_len
        )
        middle = tokens + dot(flat_heads, out_full)
        normed_two = root_norm(middle, gains_wide[1]).astype(BF)
        two_other = swapped(normed_two, "c")

    upstream = cotangent[0].astype(F32)

    def ordered(mine, other):
        return jnp.concatenate(
            [jnp.where(first_core, mine, other), jnp.where(first_core, other, mine)], axis=0
        )

    def pair(v):
        return ordered(v, swapped(v, "c"))

    def half_pair(v):
        n = v.shape[1] // 2
        keep = lax.dynamic_slice_in_dim(v, core * n, n, 1)
        give = lax.dynamic_slice_in_dim(v, (1 - core) * n, n, 1)
        return ordered(keep, swapped(give, "c"))

    def core_sum(v):
        keep = lax.dynamic_slice_in_dim(v, core * piece_len, piece_len, 0)
        give = lax.dynamic_slice_in_dim(v, (1 - core) * piece_len, piece_len, 0)
        return keep.astype(F32) + swapped(give, "c").astype(F32)

    df_other = swapped(cotangent[0], "c")
    two_t, hid_t, grad_gated, out_sum, two_sum = mlp_call(
        core.reshape(1).astype(jnp.int32),
        (normed_two, two_other),
        (cotangent[0], df_other),
        gate_full,
        down_full,
    )
    output = middle + core_sum(out_sum)
    block_out = output.astype(BF)[None]
    token_total = piece_len * S * Y * 4 * block_in.shape[0]
    step_value = update_count[0].astype(F32)
    rates = optimizer_rates

    if fast:
        sums, block_in_grad = backward(
            two_t,
            hid_t,
            transposed,
            grad_gated,
            (cotangent[0], df_other),
            two_sum,
            middle,
            out_full,
            gains_small,
            block_in[0],
            in_full,
            (query_row, key_column, queries, key_rows, values, flat_heads, log_totals),
            (cos_table, sin_table),
            HEADS,
            S,
            2,
        )
    else:
        grad_normed_two = core_sum(two_sum)
        _, norm_pull_two = jax.vjp(root_norm, middle, gains_wide[1])
        grad_middle_norm, grad_gain_two = norm_pull_two(grad_normed_two)
        grad_middle = upstream + grad_middle_norm
        grad_branch = grad_middle.astype(BF)
        grad_flat = dot_t(grad_branch, out_full)
        grad_attended = jnp.where(live_rows[:, None], grad_flat, 0.0).astype(BF)
        grad_query_all, grad_keys, grad_values = attend_back(
            query_row,
            key_column,
            queries,
            key_rows,
            values,
            flat_heads,
            grad_attended,
            log_totals,
            HEADS,
            piece_len // 2,
        )
        grad_pairs = jnp.concatenate([grad_keys, grad_values], axis=1)
        own_grad = grad_pairs[key_span:]
        for back_step in range(1, reach_count + 1):
            sent_rows = grad_pairs[
                key_span - back_step * piece_len : key_span - (back_step - 1) * piece_len
            ]
            own_grad = own_grad + passed_along(sent_rows, "z", -back_step)
        grad_query_raw = rotate(
            grad_query_all.reshape(piece_len, HEADS, HEAD), positions, -1.0
        ).reshape(piece_len, width_q)
        grad_key_raw = rotate(own_grad[:, :HEAD], positions, -1.0)
        grad_mixed = jnp.concatenate(
            [grad_query_raw, grad_key_raw, own_grad[:, HEAD:]], axis=1
        ).astype(BF)
        grad_normed = dot_t(grad_mixed, in_full)
        _, norm_pull_one = jax.vjp(root_norm, tokens, gains_wide[0])
        grad_tokens_norm, grad_gain_one = norm_pull_one(grad_normed)
        block_in_grad = (grad_middle + grad_tokens_norm).astype(BF)

    if fast:

        def adam(weight, moments, *rest, **more):
            return adam_call(
                weight, moments, sums, update_count, rates, float(token_total), *rest, **more
            )

        tiles = half_ff // d_half
        same = (d_half,) * tiles
        gate_grad, gate_new, gate_mom, gain_two = adam(
            gate_up, gate_moments, 0, same, sides=2, gains=True, chips=2
        )
        down_grad, down_new, down_mom = adam(
            down_weight, down_moments, 2 * tiles, (d_half,), tiles=tiles
        )
        out_grad, out_new, out_mom = adam(output_proj, output_moments, 3 * tiles, (d_half,))
        in_grad, in_new, in_mom, gain_one = adam(
            input_proj, input_moments, 3 * tiles + 1, split_widths(in_half, d_half), gains=True
        )
        gain_grad = jnp.stack(
            [jnp.sum(v, axis=1) for v in (gain_one, gain_two)]
        ) / gains_low.astype(F32)
    else:

        def adam(weight, moments, grad):
            grad = grad.astype(F32) / token_total
            change, new = adamw_step(weight, moments, grad, step_value, rates)
            return grad, weight - change, new

        def summed(left, right):
            whole = dot_rows(left.T, right).astype(BF)
            mine = lax.psum_scatter(whole, "z", scatter_dimension=0, tiled=True)
            return lax.psum(mine, ("y", "x"))

        two_both = ordered(normed_two, two_other)
        grad_half = half_pair(grad_branch)
        mixed_half = half_pair(grad_mixed)
        normed_both = pair(normed)
        flat_both = pair(flat_heads)
        df_both = pair(cotangent[0])
        gate_half = [summed(two_both, grad_gated[side]) for side in range(2)]
        gate_sum = jnp.concatenate(
            [lax.all_gather(g, "c", axis=1, tiled=True) for g in gate_half], axis=1
        )
        down_part = lax.psum(dot_rows(hid_t, df_both).astype(BF), ("y", "x"))
        down_part = lax.all_gather(down_part, "c", axis=0, tiled=True)
        down_sum = lax.psum_scatter(down_part, "z", scatter_dimension=0, tiled=True)
        out_total = lax.all_gather(summed(flat_both, grad_half), "c", axis=1, tiled=True)
        in_total = lax.all_gather(summed(normed_both, mixed_half), "c", axis=1, tiled=True)
        out_grad, out_new, out_mom = adam(output_proj, output_moments, out_total)
        in_grad, in_new, in_mom = adam(input_proj, input_moments, in_total)
        gate_grad, gate_new, gate_mom = adam(gate_up, gate_moments, gate_sum)
        down_grad, down_new, down_mom = adam(down_weight, down_moments, down_sum)
        gains_sum = lax.psum(jnp.stack([grad_gain_one, grad_gain_two]), ("y", "x", "c", "z"))
        gain_grad = lax.dynamic_slice_in_dim(gains_sum, seq_place * rows_d, rows_d, 1) / token_total
    gains_step, gain_moments_new = adamw_step(norm_gains, gain_moments, gain_grad, step_value, rates)
    return (
        block_out,
        block_in_grad[None],
        in_grad,
        out_grad,
        gate_grad,
        down_grad,
        gain_grad,
        in_new,
        out_new,
        gate_new,
        down_new,
        gains_step,
        in_mom,
        out_mom,
        gate_mom,
        down_mom,
        gain_moments_new,
    )


def solution(mesh):
    dp, S = mesh.shape["dp"], mesh.shape["seq"]
    Y = dp // 4
    grid = Mesh(mesh.devices.reshape(Y, 2, 2, S), ("y", "x", "c", "z"))
    data = ("y", "x", "c")
    tokens = P(data, "z", None)
    rows = P("z", None)
    moments = P(None, "z", None)
    in_specs = (
        (tokens, tokens, P(data, None))
        + (rows,) * 4
        + (P(None, "z"),)
        + (moments,) * 4
        + (P(None, None, "z"), P(), P())
    )
    out_specs = (
        (tokens, tokens)
        + (rows,) * 4
        + (P(None, "z"),)
        + (rows,) * 4
        + (P(None, "z"),)
        + (moments,) * 4
        + (P(None, None, "z"),)
    )

    def device_step(*arrays):
        return on_device(Y, S, *arrays)

    return jax.shard_map(
        device_step, mesh=grid, in_specs=in_specs, out_specs=out_specs, check_vma=False
    )
```

```python
import jax
import jax.numpy as jnp
from jax import lax
from jax.experimental import pallas as pl
from jax.experimental.pallas import tpu as pltpu
from jax.sharding import Mesh
from jax.sharding import PartitionSpec as P

HEADS = 12
HEAD = 128
FF = 4608
WINDOW = 1024


norm_eps = 1e-06
adam_eps = 1e-08
beta_first = 0.9
beta_second = 0.95
BF = jnp.bfloat16
F32 = jnp.float32
MESH_ID = pl.DeviceIdType.MESH
VMEM_BYTES = 60 * 1024 * 1024
BACKWARD_VMEM = 127 * 512 * 1024
ANY = pl.BlockSpec(memory_space=pl.ANY)
VM = pl.BlockSpec(memory_space=pltpu.VMEM)
LOG2E = 1.4426950408889634


def passed_along(block, axis, distance):
    devices = range(lax.axis_size(axis))
    route = [(i - distance, i) for i in devices if i - distance in devices]
    return lax.ppermute(block, axis, route)


def swapped(block, axis):
    return lax.ppermute(block, axis, [(0, 1), (1, 0)])


def rotate(values, positions, sign_value):
    half_width = values.shape[-1] // 2
    frequency = 10000.0 ** (-2.0 * jnp.arange(half_width).astype(jnp.float32) / values.shape[-1])
    angles = positions.astype(jnp.float32)[:, None] * frequency[None, :]
    cosine = jnp.cos(angles)
    sine_part = sign_value * jnp.sin(angles)
    if values.ndim == 3:
        cosine = cosine[:, None, :]
        sine_part = sine_part[:, None, :]
    lower_half = values[..., :half_width]
    upper_half = values[..., half_width:]
    return jnp.concatenate(
        [
            lower_half * cosine - upper_half * sine_part,
            upper_half * cosine + lower_half * sine_part,
        ],
        axis=-1,
    )


def root_norm(values, gain):
    return values * lax.rsqrt(jnp.mean(values * values, axis=-1, keepdims=True) + norm_eps) * gain


def adamw_step(weight, moments, grad, step_value, optimizer_rates):
    fix_first = 1.0 - beta_first**step_value
    fix_second = 1.0 - beta_second**step_value
    first_moment = beta_first * moments[0] + (1.0 - beta_first) * grad
    second = beta_second * moments[1] + (1.0 - beta_second) * grad * grad
    update = (
        first_moment / fix_first / (jnp.sqrt(second / fix_second) + adam_eps)
        + optimizer_rates[1] * weight
    )
    return (optimizer_rates[0] * update, jnp.stack([first_moment, second]))


def gather_kernel(shared, groups, S, own, full, sems, small_own, small_full, prepare, work):
    n = len(shared)
    chunks = [chunk for group in groups for chunk in group]
    members = []
    for group in groups:
        first = members[-1][-1] + 1 if members else 0
        members.append(range(first, first + len(group)))
    ng = len(groups)
    F = S - 1
    loc, zs, zr, xs, xr, ys, yr, cs, cr, ss, sr = sems
    y, x, c, z = (lax.axis_index(a) for a in ("y", "x", "c", "z"))
    k = y * 2 + x
    kx = y * 2 + 1 - x
    ky = (1 - y) * 2 + x
    kxy = 3 - k
    to_x = {"x": 1 - x}
    to_y = {"y": 1 - y}
    to_c = {"c": 1 - c}
    low = z
    high = S - 1 - z
    near_count = jnp.minimum(low, high)
    above = jnp.minimum(z + 1, S - 1)
    below = jnp.maximum(z - 1, 0)
    blocks = []
    for j in range(F):
        near = j < 2 * near_count
        dist = jnp.where(near, j // 2 + 1, j - near_count + 1)
        sign = jnp.where(near, (j % 2) * 2 - 1, jnp.where(high > low, 1, -1))
        blocks.append((z + sign * dist, sign))
    barrier = pltpu.get_barrier_semaphore()
    others = [lax.rem(z + e, S) for e in range(1, S)]
    for target in [to_x, to_y, to_c] + [{"z": zz} for zz in others]:
        pl.semaphore_signal(barrier, inc=1, device_id=target, device_id_type=MESH_ID)
    pl.semaphore_wait(barrier, 3 + F)

    def box(q, half):
        i, r0, rn, c0, cn, _ = chunks[q]
        if shared[i]:
            columns = full[i].shape[-1] // 2
            c0 = pl.multiple_of(half * columns + c0, 128)
        return pl.ds(r0, rn), pl.ds(c0, cn)

    def part(q, zz, kk, h=None, half=c):
        rr, cc = box(q, half)
        held = full[chunks[q][0]]
        if h is None:
            return held.at[zz, kk, :, rr, cc]
        return held.at[zz, kk, h, rr, cc]

    def carried(q):
        route = chunks[q][5]
        if route == "xy":
            return (k,)
        return (x, 2 + x) if route == "x" else (2 * y, 2 * y + 1)

    def exchanged(q):
        if chunks[q][5] == "x":
            return xs, xr, to_x, (1 - x, 3 - x)
        return ys, yr, to_y, (2 - 2 * y, 3 - 2 * y)

    def remote(src, dst, s, r, target):
        return pltpu.make_async_remote_copy(
            src_ref=src,
            dst_ref=dst,
            send_sem=s,
            recv_sem=r,
            device_id=target,
            device_id_type=MESH_ID,
        )

    tail = []
    arriving = {i: [] for i in range(n)}
    arriving[None] = []
    finished = [0] * n

    def begin(g):
        i, r0, rn, c0 = groups[g][0][:4]
        prepare(g)
        rows = pl.ds(r0, rn)
        if shared[i]:
            src, dst = own[i].at[:, :, rows], full[i].at[z, :, :, rows]
        else:
            cc = pl.ds(c0, sum(chunk[4] for chunk in groups[g]))
            src, dst = own[i].at[:, :, rows, cc], full[i].at[z, :, :, rows, cc]
        for q in members[g]:
            z_first(q)
        copy = pltpu.make_async_copy(src, dst, loc.at[g])
        copy.start()
        arriving[i].append(copy.wait)

    def z_first(q):
        i = chunks[q][0]
        rr, cc = box(q, c)
        for m, kk in enumerate(carried(q)):
            for ok, target, slot in ((z + 1 < S, above, F), (z > 0, below, F + 1)):

                def make(target=target, slot=slot, m=m, kk=kk):
                    return remote(
                        own[i].at[kk, :, rr, cc],
                        part(q, z, kk),
                        zs.at[q, slot, m],
                        zr.at[q, z, m],
                        {"z": target},
                    )

                @pl.when(ok)
                def _(make=make):
                    make().start()

                def finish(ok=ok, make=make):
                    @pl.when(ok)
                    def _():
                        make().wait_send()

                tail.append(finish)

    def send(p, s, r, q, j, slot, target):
        copy = remote(p, p, s.at[q, j, slot], r.at[q, j, slot], target)
        copy.start()
        tail.append(copy.wait_send)

    def z_next(q, j):
        zz, sign = blocks[j]
        onward = z - sign
        ok = (onward >= 0) & (onward < S)
        target = jnp.clip(onward, 0, S - 1)
        for m, kk in enumerate(carried(q)):
            piece = part(q, zz, kk)
            remote(piece, piece, zs.at[q, j, m], zr.at[q, zz, m], {"z": above}).wait_recv()

            def make(piece=piece, m=m):
                return remote(piece, piece, zs.at[q, j, m], zr.at[q, zz, m], {"z": target})

            @pl.when(ok)
            def _(make=make):
                make().start()

            def finish(make=make):
                @pl.when(ok)
                def _():
                    make().wait_send()

            tail.append(finish)
            if chunks[q][5] != "xy":
                s, r, neighbour, _ = exchanged(q)
                send(piece, s, r, q, j, m, neighbour)
        if chunks[q][5] == "xy":
            send(part(q, zz, k, 0), xs, xr, q, j, 0, to_x)
            send(part(q, zz, k, 1), ys, yr, q, j, 0, to_y)
            send(part(q, zz, k, 0), ys, yr, q, j, 1, to_y)
            send(part(q, zz, k, 1), xs, xr, q, j, 1, to_x)

    def xy_next(q, j):
        if chunks[q][5] != "xy":
            return
        zz, _ = blocks[j]
        p = part(q, zz, kx, 0)
        remote(p, p, xs.at[q, j, 0], xr.at[q, j, 0], to_x).wait_recv()
        send(p, ys, yr, q, j, 2, to_y)
        p = part(q, zz, ky, 1)
        remote(p, p, ys.at[q, j, 0], yr.at[q, j, 0], to_y).wait_recv()
        send(p, xs, xr, q, j, 2, to_x)

    def last(q, j):
        i = chunks[q][0]
        zz, _ = blocks[j]
        finished[i] += 1
        if chunks[q][5] == "xy":
            for kk, h, s, r, slot, target in (
                (kx, 1, xs, xr, 1, to_x),
                (ky, 0, ys, yr, 1, to_y),
                (kxy, 1, xs, xr, 2, to_x),
                (kxy, 0, ys, yr, 2, to_y),
            ):
                p = part(q, zz, kk, h)
                remote(p, p, s.at[q, j, slot], r.at[q, j, slot], target).wait_recv()
        else:
            s, r, neighbour, theirs = exchanged(q)
            for m, kk in enumerate(theirs):
                p = part(q, zz, kk)
                remote(p, p, s.at[q, j, m], r.at[q, j, m], neighbour).wait_recv()
        if shared[i]:
            rr, cc = box(q, c)
            p = full[i].at[zz, :, :, rr, cc]
            copy = remote(p, p, cs.at[q, j], cr.at[q, j], to_c)
            copy.start()
            tail.append(copy.wait_send)
            rr, cc = box(q, 1 - c)
            other = full[i].at[zz, :, :, rr, cc]

            def finish():
                remote(other, other, cs.at[q, j], cr.at[q, j], to_c).wait_recv()

            arriving[i].append(finish)

    def ready(i):
        if i is not None:
            assert finished[i] == F * sum(chunk[0] == i for chunk in chunks)
        for wait in arriving.pop(i, []):
            wait()

    begin(0)
    if small_own is not None:
        place = pltpu.make_async_copy(small_own, small_full.at[z], ss.at[0])
        place.start()
        arriving[None].append(place.wait)
        for e, zz in enumerate(others, 1):
            copy = remote(small_own, small_full.at[z], ss.at[e], sr.at[S - e], {"z": zz})
            copy.start()
            tail.append(copy.wait_send)
            came = small_full.at[zz]
            arriving[None].append(remote(came, came, ss.at[e], sr.at[e], {"z": zz}).wait_recv)
    for t in range(1, ng + F + 3):
        if t < ng:
            begin(t)
        for lag, stage in ((1, z_next), (2, xy_next), (3, last)):
            for j in reversed(range(F)):
                if 0 <= t - lag - j < ng:
                    for q in members[t - lag - j]:
                        stage(q, j)
        work(t, ready)
    for i in list(arriving):
        ready(i)
    for wait in tail:
        wait()


def gather_sems(ng, nc, S):
    dma = pltpu.SemaphoreType.DMA
    F = S - 1
    return [
        dma((ng,)),
        dma((nc, F + 2, 2)),
        dma((nc, S, 2)),
        dma((nc, F, 3)),
        dma((nc, F, 3)),
        dma((nc, F, 3)),
        dma((nc, F, 3)),
        dma((nc, F)),
        dma((nc, F)),
        dma((S,)),
        dma((S,)),
    ]


def nt(a, b):
    return lax.dot_general(a, b, (((1,), (1,)), ((), ())), preferred_element_type=F32)

def nn(a, b):
    return lax.dot_general(a, b, (((1,), (0,)), ((), ())), preferred_element_type=F32)

def fill_bias(bias, q_ids, k_ids, first, rows, span):
    key = lax.broadcasted_iota(jnp.int32, (span, rows), 0)
    query = lax.broadcasted_iota(jnp.int32, (span, rows), 1)
    distance = query + WINDOW - key
    same = k_ids[pl.ds(first, span), :1] == q_ids[:1, pl.ds(first, rows)]
    allowed = (distance >= 0) & (distance < WINDOW) & same
    bias[...] = jnp.where(allowed, 0.0, -1e30)

def fwd_step(h, first, rows, q_ids, q_ref, k_ref, o_ref, l_ref, bias, vt):
    span = WINDOW + rows
    factor = HEAD**-0.5 * LOG2E
    cols = pl.ds(h * HEAD, HEAD)
    q = q_ref[pl.ds(first, rows), cols]
    s = nt(k_ref[pl.ds(first, span), :], q) * factor + bias[...]
    top = jnp.max(s, axis=0, keepdims=True)
    p = jnp.exp2(s - top)
    total = jnp.sum(p, axis=0, keepdims=True)
    o = nn(vt[:, pl.ds(first, span)], p.astype(BF))
    live = q_ids[:1, pl.ds(first, rows)] != 0
    o = jnp.where(live, o * (1.0 / total), 0.0)
    o_ref[pl.ds(first, rows), cols] = o.T.astype(BF)
    l_ref[h, :, pl.ds(first, rows)] = top + jnp.log2(total)


def fwd_kernel(heads, rows, q_ids, k_ids, q_ref, k_ref, v_ref, o_ref, l_ref, bias, vt):
    vt[...] = v_ref[...].T
    for first in range(0, q_ref.shape[0], rows):
        fill_bias(bias, q_ids, k_ids, first, rows, WINDOW + rows)
        for h in range(heads):
            fwd_step(h, first, rows, q_ids, q_ref, k_ref, o_ref, l_ref, bias, vt)


def norm_rows(source, gain, target):
    rows = 64

    @pl.loop(0, target.shape[0] // rows)
    def _(i):
        at = pl.ds(pl.multiple_of(i * rows, rows), rows)
        u = source[at, :].astype(F32)
        scale = lax.rsqrt(jnp.mean(u * u, axis=1, keepdims=True) + norm_eps)
        target[at, :] = (u * scale * gain).astype(target.dtype)


def turned(u, cos_ref, sin_ref):
    return u * cos_ref[...] + pltpu.roll(u, HEAD // 2, 1) * sin_ref[...]


def remote_copy(src, dst, send, receive, target):
    return pltpu.make_async_remote_copy(
        src_ref=src,
        dst_ref=dst,
        send_sem=send,
        recv_sem=receive,
        device_id=target,
        device_id_type=MESH_ID,
    )


def started(src, dst, sem):
    copy = pltpu.make_async_copy(src, dst, sem)
    copy.start()
    return copy


def forward_kernel(heads, groups, S, *refs):
    masters = refs[:4]
    small_own, x_ref, cos_ref, sin_ref, q_ids, k_ids = refs[4:10]
    full = refs[10:14]
    small_full, h1_ref, q_ref, k_out, v_out, o_ref, l_ref, mid_ref, h2_ref, h2_other = refs[14:24]
    h1_t, h1_t_other, o_t, o_t_other = refs[24:28]
    w_in, w_out, gains, mix, kv, bias, vt, lds, hs, hr, h2_sems = refs[28:39]
    own = refs[39:43]
    stages = refs[43:47]
    stage_sems = refs[47]
    sems = refs[48:]
    z = lax.axis_index("z")
    c = lax.axis_index("c")
    piece = x_ref.shape[0]
    reach = kv.shape[0] // piece - 1
    half = w_in.shape[-1] // 2
    D = x_ref.shape[1]
    half_ff = own[3].shape[-1] // 2
    own_rows = pl.ds(reach * piece, piece)
    kv[...] = jnp.zeros_like(kv)
    sent = []
    loads = {}

    def gain_row(i):
        return jnp.concatenate([gains[zz, i : i + 1, :] for zz in range(S)], axis=1).astype(F32)

    def start_norm(ready):
        ready(None)
        started(small_full, gains, lds.at[0]).wait()
        norm_rows(x_ref, gain_row(0), h1_ref)


    def of_weight(g):
        return sum(group[0][0] == groups[g][0][0] for group in groups[:g])

    def stage(g):
        i, r0, rn, c0 = groups[g][0][:4]
        slot = of_weight(g) % stages[i].shape[0]
        cols = pl.ds(0, masters[i].shape[-1])
        if i == 3:
            first = c0 // half_ff * 2 * half_ff + c * half_ff
            cols = pl.ds(pl.multiple_of(first, 128), half_ff)
        src = masters[i].at[:, :, pl.ds(r0, rn), cols]
        loads["stage", g] = started(src, stages[i].at[slot], stage_sems.at[g])

    for g in range(len(groups)):
        if of_weight(g) < stages[groups[g][0][0]].shape[0]:
            stage(g)

    def prepare(g):
        i, r0, rn, c0 = groups[g][0][:4]
        slot = of_weight(g) % stages[i].shape[0]
        loads.pop(("stage", g)).wait()
        cols = pl.ds(c0, half_ff) if i == 3 else pl.ds(0, own[i].shape[-1])

        @pl.loop(0, 8)
        def _(p):
            kk, h = p // 2, p % 2
            own[i][kk, h, pl.ds(r0, rn), cols] = stages[i][slot, kk, h].astype(BF)

        later = g + stages[i].shape[0]
        if later < len(groups) and groups[later][0][0] == i:
            stage(later)

    def start_project(ready):
        ready(0)
        for i in range(2):
            at = pl.ds(i * half, half)
            loads[i] = started(full[0].at[:, :, :, :, at], w_in.at[:, :, :, :, at], lds.at[1 + i])

    def project(i):
        loads.pop(i).wait()
        weight = w_in[:, :, :, :, i * half : (i + 1) * half].reshape(D, half)
        mix[...] = nn(h1_ref[...], weight)
        for j in range(half // HEAD):
            h = i * (half // HEAD) + j
            u = mix[:, j * HEAD : (j + 1) * HEAD]
            if h < heads:
                q_ref[:, h * HEAD : (h + 1) * HEAD] = turned(u, cos_ref, sin_ref).astype(BF)
            elif h == heads:
                kv[own_rows, :HEAD] = turned(u, cos_ref, sin_ref).astype(BF)
            else:
                kv[own_rows, HEAD:] = u.astype(BF)

    def halo(d, starting):
        there = kv.at[pl.ds((reach - d) * piece, piece)]
        target = {"z": jnp.minimum(z + d, S - 1)}
        copy = remote_copy(kv.at[own_rows], there, hs.at[d - 1], hr.at[d - 1], target)

        @pl.when(z + d < S)
        def _():
            if starting:
                copy.start()
            else:
                copy.wait_send()

        if not starting:

            @pl.when(z >= d)
            def _():
                remote_copy(there, there, hs.at[d - 1], hr.at[d - 1], target).wait_recv()

    def start_attention():
        for d in range(1, reach + 1):
            halo(d, False)
        k_out[...] = kv[:, :HEAD]
        v_out[...] = kv[:, HEAD:]
        vt[...] = kv[:, HEAD:].T
        fill_bias(bias, q_ids, k_ids, 0, piece, WINDOW + piece)

    def attention(first, count):
        for h in range(first, first + count):
            fwd_step(h, 0, piece, q_ids, q_ref, k_out, o_ref, l_ref, bias, vt)

    def start_output(ready):
        ready(1)
        for i in range(2):
            at = pl.ds(i * (D // 2), D // 2)
            loads[i] = started(full[1].at[:, :, :, :, at], w_out.at[:, :, :, :, at], lds.at[3 + i])

    def output():
        n = D // 2
        for i in range(2):
            loads.pop(i).wait()
            at = slice(i * n, (i + 1) * n)
            weight = w_out[:, :, :, :, at].reshape(D, n)
            mid_ref[:, at] = x_ref[:, at].astype(F32) + nn(o_ref[...], weight)

    def finish():
        norm_rows(mid_ref, gain_row(1), h2_ref)
        to_partner(h2_ref, h2_other, 0)

    def to_partner(src, dst, i):
        copy = remote_copy(src, dst, h2_sems.at[2 * i], h2_sems.at[2 * i + 1], {"c": 1 - c})
        copy.start()
        sent.append(copy.wait)

    def transpose(src, dst, there, i):
        for j in range(0, D, HEAD):
            dst[j : j + HEAD, :] = src[:, j : j + HEAD].T
        to_partner(dst, there, i)

    third = heads // 3
    plan = {
        2: lambda ready: start_norm(ready),
        5: lambda ready: start_project(ready),
        6: lambda ready: (project(0), project(1), [halo(d, True) for d in range(1, reach + 1)]),
        7: lambda ready: (start_attention(), attention(0, third), start_output(ready)),
        8: lambda ready: attention(third, third),
        9: lambda ready: attention(2 * third, third),
        10: lambda ready: output(),
        11: lambda ready: (finish(), transpose(h1_ref, h1_t, h1_t_other, 1)),
        12: lambda ready: transpose(o_ref, o_t, o_t_other, 2),
    }

    def work(t, ready):
        if t in plan:
            plan[t](ready)

    gather_kernel(
        [True, True, True, False], groups, S, own, full, sems, small_own, small_full, prepare, work
    )
    for wait in sent:
        wait()


def forward(masters, small, x, cos, sin, q_ids, k_ids, heads, S, cid):
    piece, D = x.shape
    keys = k_ids.shape[0]
    r = masters[0].shape[2]
    rf = masters[2].shape[2]
    all_in, all_out, all_gate = (masters[i].shape[-1] for i in (0, 1, 3))
    half_in, half_out, half_ff = all_in // 2, all_out // 2, all_gate // 4

    def routed(i, r0, rn, c0, cn):
        return [(i, r0, rn, c0, cn, "xy")]

    groups = [routed(0, 0, r, 0, half_in), routed(1, 0, r, 0, half_out)]
    groups += [routed(2, i, 48, 0, half_out) for i in range(0, rf, 48)]
    groups += [routed(3, i, 16, j * half_ff, half_ff) for j in range(2) for i in range(0, r, 16)]

    def body(*refs):
        forward_kernel(heads, groups, S, *refs)

    def shape(*dims, dtype=BF):
        return jax.ShapeDtypeStruct(dims, dtype)

    own = [(4, 2) + masters[i].shape[2:] for i in range(3)] + [(4, 2, r, 2 * half_ff)]
    outs = [shape(S, *o) for o in own]
    outs += [
        shape(S, *small.shape),
        shape(piece, D),
        shape(piece, heads * HEAD),
        shape(keys, HEAD),
        shape(keys, HEAD),
        shape(piece, heads * HEAD),
        shape(heads, 1, piece, dtype=F32),
        shape(piece, D, dtype=F32),
        shape(piece, D),
        shape(piece, D),
        shape(D, piece),
        shape(D, piece),
        shape(D, piece),
        shape(D, piece),
    ]
    dma = pltpu.SemaphoreType.DMA
    return pl.pallas_call(
        body,
        out_shape=tuple(outs),
        in_specs=[ANY] * 4 + [VM] * 6,
        out_specs=tuple([ANY] * 5 + [VM] * 8 + [ANY] + [VM, ANY] * 2),
        scratch_shapes=[
            pltpu.VMEM((S,) + own[0], BF),
            pltpu.VMEM((S,) + own[1], BF),
            pltpu.VMEM((S,) + small.shape, BF),
            pltpu.VMEM((piece, half_in), F32),
            pltpu.VMEM((keys, 2 * HEAD), BF),
            pltpu.VMEM((keys, piece), F32),
            pltpu.VMEM((HEAD, keys), BF),
            dma((5,)),
            dma((2,)),
            dma((2,)),
            dma((6,)),
        ]
        + [pltpu.VMEM(o, BF) for o in own]
        + [
            pltpu.VMEM((1, 4, 2, r, all_in), F32),
            pltpu.VMEM((1, 4, 2, r, all_out), F32),
            pltpu.VMEM((2, 4, 2, 48, all_out), F32),
            pltpu.VMEM((2, 4, 2, 16, half_ff), F32),
            dma((len(groups),)),
        ]
        + gather_sems(len(groups), sum(map(len, groups)), S),
        compiler_params=pltpu.CompilerParams(
            collective_id=cid, has_side_effects=True, vmem_limit_bytes=VMEM_BYTES
        ),
    )(*masters, small, x, cos, sin, q_ids, k_ids)


def back_step(h, first, rows, refs, bias, kt, finish):
    q_ref, k_ref, v_ref, o_ref, do_ref, l_ref, dq_ref, dk_ref, dv_ref = refs
    span = WINDOW + rows
    factor = HEAD**-0.5 * LOG2E
    cols = pl.ds(h * HEAD, HEAD)
    q = q_ref[pl.ds(first, rows), cols]
    do = do_ref[pl.ds(first, rows), cols]
    o = o_ref[pl.ds(first, rows), cols]
    delta = jnp.sum((do.astype(F32) * o.astype(F32)).T, axis=0, keepdims=True)
    s = nt(k_ref[pl.ds(first, span), :], q) * factor + bias[...]
    p = jnp.exp2(s - l_ref[h, :, pl.ds(first, rows)])
    dp = nt(v_ref[pl.ds(first, span), :], do)
    ds = (p * ((dp - delta) * HEAD**-0.5)).astype(BF)
    dv_ref[pl.ds(first, span), :] += nn(p.astype(BF), do)
    dk_ref[pl.ds(first, span), :] += nn(ds, q)
    dq = nn(kt[:, pl.ds(first, span)], ds).T
    dq_ref[pl.ds(first, rows), cols] = finish(dq, first).astype(dq_ref.dtype)


def bwd_kernel(heads, rows, q_ids, k_ids, *refs):
    *arrays, bias, kt = refs
    q_ref, k_ref = arrays[:2]
    dk_ref, dv_ref = arrays[-2:]
    kt[...] = k_ref[...].T
    dk_ref[...] = jnp.zeros_like(dk_ref)
    dv_ref[...] = jnp.zeros_like(dv_ref)
    for first in range(0, q_ref.shape[0], rows):
        fill_bias(bias, q_ids, k_ids, first, rows, WINDOW + rows)
        for h in range(heads):
            back_step(h, first, rows, arrays, bias, kt, lambda dq, first: dq)


def attend(q_ids, k_ids, q, k, v, heads, rows):
    def body(*refs):
        fwd_kernel(heads, rows, *refs)

    return pl.pallas_call(
        body,
        out_shape=(
            jax.ShapeDtypeStruct(q.shape, BF),
            jax.ShapeDtypeStruct((heads, 1, q.shape[0]), F32),
        ),
        in_specs=[VM] * 5,
        out_specs=(VM, VM),
        scratch_shapes=[
            pltpu.VMEM((WINDOW + rows, rows), F32),
            pltpu.VMEM((HEAD, k.shape[0]), BF),
        ],
        compiler_params=pltpu.CompilerParams(vmem_limit_bytes=VMEM_BYTES),
        cost_estimate=pl.CostEstimate(
            flops=4 * q.size * k.shape[0], bytes_accessed=4 * q.size, transcendentals=q.size * 12
        ),
    )(q_ids, k_ids, q, k, v)


def attend_back(q_ids, k_ids, q, k, v, o, do, l, heads, rows):
    def body(*refs):
        bwd_kernel(heads, rows, *refs)

    return pl.pallas_call(
        body,
        out_shape=(
            jax.ShapeDtypeStruct(q.shape, F32),
            jax.ShapeDtypeStruct(k.shape, F32),
            jax.ShapeDtypeStruct(k.shape, F32),
        ),
        in_specs=[VM] * 8,
        out_specs=(VM, VM, VM),
        scratch_shapes=[
            pltpu.VMEM((WINDOW + rows, rows), F32),
            pltpu.VMEM((HEAD, k.shape[0]), BF),
        ],
        compiler_params=pltpu.CompilerParams(vmem_limit_bytes=VMEM_BYTES),
        cost_estimate=pl.CostEstimate(
            flops=10 * q.size * k.shape[0], bytes_accessed=12 * q.size, transcendentals=q.size * 12
        ),
    )(q_ids, k_ids, q, k, v, o, do, l)


def mlp_kernel(
    where, two_own, two_other, df_own, df_other, gate_ref, up_ref, down_ref, *results
):
    two_t, hid_t, grads, back_low, back = results
    step = pl.program_id(0)
    rows, D = two_own.shape
    part = two_t.shape[0]
    core = where[0]
    block = 512

    @pl.when(step == 0)
    def _():
        back[...] = jnp.zeros_like(back)

    @pl.when(step < D // part)
    def _():
        cols = pl.ds(pl.multiple_of(step * part, part), part)
        for two_ref, owner in ((two_own, core), (two_other, 1 - core)):
            at = pl.ds(pl.multiple_of(owner * rows, rows), rows)
            two_t[:, at] = two_ref[:, cols].T

    def tokens(two_ref, df_ref, owner, first):
        here = pl.ds(first, block)
        at = pl.ds(pl.multiple_of(owner * rows + first, block), block)
        two = two_ref[here, :]
        gate = nn(two, gate_ref[...])
        up = nn(two, up_ref[...])
        grad = nt(df_ref[here, :], down_ref[...])
        slope = 0.7978845608028654
        bent = jnp.tanh(slope * (gate + 0.044715 * (gate * gate * gate)))
        upper = 0.5 * (1.0 + bent)
        act = gate * upper
        act_slope = upper + 0.5 * gate * (1.0 - bent * bent) * (
            slope * (1.0 + 3 * 0.044715 * (gate * gate))
        )
        hid = (act * up).astype(BF)
        grad_gate = (grad * up * act_slope).astype(BF)
        grad_up = (grad * act).astype(BF)
        hid_t[:, at] = hid.T
        grads[0, at, :] = grad_gate
        grads[1, at, :] = grad_up
        back[at, :] += nt(grad_gate, gate_ref[...]) + nt(grad_up, up_ref[...])

    for two_ref, df_ref, owner in ((two_own, df_own, core), (two_other, df_other, 1 - core)):
        for first in range(0, rows, block):
            tokens(two_ref, df_ref, owner, first)

    @pl.when(step == pl.num_programs(0) - 1)
    def _():
        back_low[...] = back[...].astype(BF)


def mlp_call(core, two, df, gate_full, down_full):
    T, D = 2 * two[0].shape[0], two[0].shape[1]
    half_ff = gate_full.shape[1] // 2
    tile = 256
    tiles = half_ff // tile
    part = max(D // tiles // 128 * 128, 256)
    last = D // part - 1

    def body(*refs):
        mlp_kernel(*refs)

    once = pl.Buffered(1)
    piece = pl.BlockSpec((T // 2, D), lambda i, w: (0, 0), pipeline_mode=once)
    return pl.pallas_call(
        body,
        grid_spec=pltpu.PrefetchScalarGridSpec(
            num_scalar_prefetch=1,
            grid=(tiles,),
            in_specs=[
                piece,
                piece,
                piece,
                piece,
                pl.BlockSpec((D, tile), lambda i, w: (0, i)),
                pl.BlockSpec((D, tile), lambda i, w: (0, tiles + i)),
                pl.BlockSpec((tile, D), lambda i, w: (w[0] * tiles + i, 0)),
            ],
            out_specs=[
                pl.BlockSpec((part, T), lambda i, w: (jnp.minimum(i, last), 0)),
                pl.BlockSpec((tile, T), lambda i, w: (i, 0)),
                pl.BlockSpec((2, T, tile), lambda i, w: (0, 0, i)),
                pl.BlockSpec((T, D), lambda i, w: (0, 0), pipeline_mode=once),
            ],
            scratch_shapes=[pltpu.VMEM((T, D), F32)],
        ),
        out_shape=[
            jax.ShapeDtypeStruct((D, T), BF),
            jax.ShapeDtypeStruct((half_ff, T), BF),
            jax.ShapeDtypeStruct((2, T, half_ff), BF),
            jax.ShapeDtypeStruct((T, D), BF),
        ],
        compiler_params=pltpu.CompilerParams(
            dimension_semantics=("arbitrary",), vmem_limit_bytes=BACKWARD_VMEM
        ),
        cost_estimate=pl.CostEstimate(
            flops=10 * T * D * half_ff, bytes_accessed=40 * 2**20, transcendentals=T * half_ff
        ),
    )(core, *two, *df, gate_full, gate_full, down_full)


def split_widths(total, most):
    first = -(-total // 256) * 128
    assert first <= most
    return (first, total - first)


def backward_kernel(heads, sides, parts, S, *refs):
    two, hid, *flats = refs[:6]
    flat_own, flat_other, norm_own, norm_other = flats[2], flats[3], flats[0], flats[1]
    grads, dy_own, dy_other, back, middle, w_out, gains_ref, x_ref, w_in, w_down = refs[6:16]
    q_ids, k_ids, q_ref, k_ref, v_ref, o_ref, l_ref, cos_ref, sin_ref = refs[16:25]
    out, hid_land, x_grad, y_out, dx_land = refs[25:30]
    left, right, out_right, mix_right, s1, g1, s2, g2, fz, gz, mine, da, do, got = refs[30:44]
    tails, landed_tails, gains, x1, dk, dv, bias, kt, mixed, w_rows, w_tiles = refs[44:55]
    lds, rds, fs, cs_in, hs, hr, s1s, s1r, s2s, s2r, zs, zr, ls, xs, xr, ys, yr, cs, cr = refs[55:]
    _, _, _, r, T = left.shape
    n = right.shape[2]
    piece, D = da.shape
    reach = tails.shape[0]
    wide = sides * parts
    rows_groups = hid.shape[1]
    chunk_out = wide + rows_groups
    mix_half = mix_right.shape[1]
    widths = [n] * (chunk_out + 1) + list(split_widths(mix_half, n))
    nc = len(widths)
    left_slots = left.shape[0]
    right_slots = right.shape[0]
    slots = g1.shape[0]
    y, x, c, z = (lax.axis_index(a) for a in ("y", "x", "c", "z"))
    k = y * 2 + x
    kx = y * 2 + 1 - x
    ky = (1 - y) * 2 + x
    kxy = 3 - k
    to_x = {"x": 1 - x}
    to_y = {"y": 1 - y}
    to_c = {"c": 1 - c}
    place = pl.ds(pl.multiple_of(c * piece, piece), piece)
    other_place = pl.ds(pl.multiple_of((1 - c) * piece, piece), piece)
    loads = {}
    pending = {}

    def fetch(key, src, dst, sem):
        loads.setdefault(key, []).append(started(src, dst, sem))

    def landed(key):
        for copy in loads.pop(key, []):
            copy.wait()

    def launch(key, copy):
        copy.start()
        pending.setdefault(key, []).append(copy)

    def drain(key):
        for copy in pending.pop(key, []):
            copy.wait_send()

    groups = 3 + rows_groups

    def group_of(t):
        if t < wide:
            return 0
        return min(t - wide + 1, groups - 1)

    def fetch_left(g):
        slot = g % left_slots
        for p in range(8):
            h, kk = p // 4, p % 4
            if g == 0:
                fetch(("l", g), two.at[:, kk, h], left.at[slot, p], lds.at[g, p, 0])
                continue
            if g <= rows_groups:
                if g == 1 and p == 0:
                    landed_hid.wait_recv()
                half = left.shape[2] // 2
                pairs = [
                    (hid.at[:, g - 1, kk, h], left.at[slot, p, pl.ds(c * half, half)]),
                    (hid_land.at[:, g - 1, kk, h], left.at[slot, p, pl.ds((1 - c) * half, half)]),
                ]
            else:
                own, other = (flat_own, flat_other) if g == groups - 2 else (norm_own, norm_other)
                pairs = [
                    (own.at[:, kk, h], left.at[slot, p, :, :, place]),
                    (other.at[:, kk, h], left.at[slot, p, :, :, other_place]),
                ]
            for i, (src, dst) in enumerate(pairs):
                fetch(("l", g), src, dst, lds.at[g, p, i])

    def fetch_right(t):
        slot = t % right_slots
        if t < wide:
            src = grads.at[t // parts, :, pl.ds((t % parts) * n, n)]
            fetch(("r", t), src, right.at[slot], rds.at[t, 0])
        elif t == wide:
            keep = pl.ds(pl.multiple_of(c * n, n), n)
            fetch(("r", t), dy_own.at[:, keep], right.at[slot, place], rds.at[t, 0])
            fetch(("r", t), dy_other.at[:, keep], right.at[slot, other_place], rds.at[t, 1])

    fetch_right(0)
    fetch_left(0)
    fetch_right(1)
    landed_tails[...] = jnp.zeros_like(landed_tails)
    barrier = pltpu.get_barrier_semaphore()
    peers = [to_x, to_y, to_c] + [{"z": lax.rem(z + e, S)} for e in range(1, S)]
    for target in peers:
        pl.semaphore_signal(barrier, inc=1, device_id=target, device_id_type=MESH_ID)
    pl.semaphore_wait(barrier, len(peers))
    launch("end", remote_copy(back.at[other_place], got, cs_in.at[0], cs_in.at[1], to_c))
    launch("end", remote_copy(hid, hid_land, cs_in.at[2], cs_in.at[3], to_c))
    landed_hid = remote_copy(hid, hid_land, cs_in.at[2], cs_in.at[3], to_c)
    landed_back = remote_copy(got, got, cs_in.at[0], cs_in.at[1], to_c)

    def product(t, p):
        lhs = left[group_of(t) % left_slots, p].reshape(S * r, T)
        if t <= chunk_out - 1:
            return nn(lhs, right[min(t, wide) % right_slots])
        if t == chunk_out:
            return nn(lhs, out_right[...])
        first = sum(widths[chunk_out + 1 : t])
        return nn(lhs, mix_right[:, first : first + widths[t]])

    def cut(ref, t):
        return ref if widths[t] == n else ref.at[:, pl.ds(0, widths[t])]

    def first(t):
        slot = t % 2
        landed(("l", group_of(t)))
        landed(("r", t))
        drain(("s1", t - 2))
        for i in range(2):
            for j, p, target in ((i, i * 2 + 1 - x, to_x), (2 + i, 4 + (1 - y) * 2 + i, to_y)):
                src, dst = cut(s1.at[slot, j], t), cut(g1.at[t % slots, j], t)
                src[...] = product(t, p).astype(BF)
                launch(("s1", t), remote_copy(src, dst, s1s.at[t, j], s1r.at[t, j], target))

    def second(t):
        slot = t % 2
        drain(("s2", t - 2))
        for j in range(4):
            dst = cut(g1.at[t % slots, j], t)
            remote_copy(dst, dst, s1s.at[t, j], s1r.at[t, j], to_x).wait_recv()
        for h, p, j, target in ((0, (1 - y) * 2 + x, 1 - y, to_y), (1, 4 + y * 2 + 1 - x, 3 - x, to_x)):
            src, dst = cut(s2.at[slot, h], t), cut(g2.at[t % slots, h], t)
            came = cut(g1.at[t % slots, j], t)
            src[...] = (product(t, p) + came[...].astype(F32)).astype(BF)
            launch(("s2", t), remote_copy(src, dst, s2s.at[t, h], s2r.at[t, h], target))

    def third(t):
        slot = t % 2
        w = widths[t]
        drain(("z", t - 2))
        for h, p, j in ((0, k, y), (1, 4 + k, 2 + x)):
            dst = cut(g2.at[t % slots, h], t)
            remote_copy(dst, dst, s2s.at[t, h], s2r.at[t, h], to_x).wait_recv()
            came = cut(g1.at[t % slots, j], t)
            total = (product(t, p) + came[...].astype(F32) + dst[...].astype(F32)).astype(BF)
            for zz in range(S):
                fz[slot, zz, h, :, :w] = total[zz * r : (zz + 1) * r]
        for e in range(1, S):
            src = fz.at[slot, lax.rem(z + e, S), :, :, pl.ds(0, w)]
            dst = gz.at[t, S - e - 1, :, :, pl.ds(0, w)]
            target = {"z": lax.rem(z + e, S)}
            launch(("z", t), remote_copy(src, dst, zs.at[t, e - 1], zr.at[t, S - e - 1], target))

    def fourth(t):
        slot = t % 2
        w = widths[t]
        drain(("ag", t - 2))
        landed(("o", t - 2))
        for e in range(S - 1):
            dst = gz.at[t, e, :, :, pl.ds(0, w)]
            remote_copy(dst, dst, zs.at[t, e], zr.at[t, e], to_x).wait_recv()
        for h in range(2):
            total = fz[slot, z, h, :, :w].astype(F32)
            for e in range(S - 1):
                total = total + gz[t, e, h, :, :w].astype(F32)
            mine[slot, h, :, :w] = total.astype(BF)
        cols = pl.ds(0, w)
        fetch(("o", t), mine.at[slot, :, :, cols], out.at[t, k, c, :, :, cols], ls.at[t])
        for i, hs_ in enumerate(((0, 1), (1, 0))):
            for h, s, r_, target in ((hs_[0], xs, xr, to_x), (hs_[1], ys, yr, to_y)):
                src, dst = mine.at[slot, h, :, cols], out.at[t, k, c, h, :, cols]
                launch(("ag", t), remote_copy(src, dst, s.at[t, i], r_.at[t, i], target))

    def land(t, kk, h, s, r_, j, target):
        p = out.at[t, kk, c, h, :, pl.ds(0, widths[t])]
        remote_copy(p, p, s.at[t, j], r_.at[t, j], target).wait_recv()
        return p

    def fifth(t):
        p = land(t, kx, 0, xs, xr, 0, to_x)
        launch("end", remote_copy(p, p, ys.at[t, 2], yr.at[t, 2], to_y))
        p = land(t, ky, 1, ys, yr, 0, to_y)
        launch("end", remote_copy(p, p, xs.at[t, 2], xr.at[t, 2], to_x))

    def sixth(t):
        land(t, kx, 1, xs, xr, 1, to_x)
        land(t, ky, 0, ys, yr, 1, to_y)
        land(t, kxy, 1, xs, xr, 2, to_x)
        land(t, kxy, 0, ys, yr, 2, to_y)
        landed(("o", t))
        p = out.at[t, :, c, :, :, pl.ds(0, widths[t])]
        launch("end", remote_copy(p, p, cs.at[t], cr.at[t], to_c))


    def norm_back():
        for key in ("near", "x1", "dy", "gains"):
            landed(key)
        landed_back.wait_recv()
        gain = jnp.concatenate([gains[zz, 1:2, :] for zz in range(S)], axis=1).astype(F32)
        step = 64

        @pl.loop(0, piece // step)
        def _(i):
            at = pl.ds(pl.multiple_of(i * step, step), step)
            u = x1[at, :]
            scale = lax.rsqrt(jnp.mean(u * u, axis=1, keepdims=True) + norm_eps)
            hat = u * scale
            e = (do[at, :].astype(F32) + got[at, :].astype(F32)) * gain
            inner = jnp.mean(e * hat, axis=1, keepdims=True)
            dx = mixed[at, :D].astype(F32) + scale * (e - hat * inner)
            x1[at, :] = dx
            da[at, :] = dx.astype(BF)

        fetch("dx", x1, dx_land, fs.at[11])
        launch("da", remote_copy(give_of(da, n), out_right.at[place], cs_in.at[4], cs_in.at[5], to_c))
        out_right[place, :] = keep_of(da, n)[...]
        for i in range(2):
            fetch("w", w_out.at[pl.ds(T, piece), pl.ds(i * n, n)], got.at[:, pl.ds(i * n, n)], fs.at[7 + i])

    def give_of(ref, width):
        return ref.at[:, pl.ds(pl.multiple_of((1 - c) * width, width), width)]

    def keep_of(ref, width):
        return ref.at[:, pl.ds(pl.multiple_of(c * width, width), width)]

    def heads_back():
        landed("w")
        live = k_ids[pl.ds(reach * piece, piece), :1] != 0
        for j in range(0, D, piece):
            if j < T:
                low, high = right[2, j : j + piece, :], right[3, j : j + piece, :]
            else:
                low, high = got[:, :n], got[:, n:]
            part = nt(da[:, :n], low) + nt(da[:, n:], high)
            do[:, j : j + piece] = jnp.where(live, part, 0.0).astype(BF)

    half_rows = piece // 2
    steps = [(block, h) for block in range(2) for h in range(heads)]

    def turn_back(dq, first):
        at = pl.ds(first, half_rows)
        return dq * cos_ref[at, :] - pltpu.roll(dq, HEAD // 2, 1) * sin_ref[at, :]

    def attention(first_step, count):
        arrays = (q_ref, k_ref, v_ref, o_ref, do, l_ref, mixed, dk, dv)
        if first_step == 0:
            kt[...] = k_ref[...].T
            dk[...] = jnp.zeros_like(dk)
            dv[...] = jnp.zeros_like(dv)
        for block, h in steps[first_step : first_step + count]:
            if h == 0:
                fill_bias(bias, q_ids, k_ids, block * half_rows, half_rows, WINDOW + half_rows)
            back_step(h, block * half_rows, half_rows, arrays, bias, kt, turn_back)

    def tail(d):
        target = {"z": jnp.maximum(z - d, 0)}
        return remote_copy(tails.at[d - 1], landed_tails.at[d - 1], hs.at[d - 1], hr.at[d - 1], target)

    def send_tails():
        for d in range(1, reach + 1):
            at = pl.ds((reach - d) * piece, piece)
            tails[d - 1, :, :HEAD] = dk[at, :].astype(BF)
            tails[d - 1, :, HEAD:] = dv[at, :].astype(BF)

            @pl.when(z >= d)
            def _(d=d):
                tail(d).start()

    def mix_back():
        for d in range(1, reach + 1):

            @pl.when(z >= d)
            def _(d=d):
                tail(d).wait_send()

            @pl.when(z + d < S)
            def _(d=d):
                tail(d).wait_recv()

        at = pl.ds(reach * piece, piece)
        keys, values = dk[at, :], dv[at, :]
        for d in range(1, reach + 1):
            keys = keys + landed_tails[d - 1, :, :HEAD].astype(F32)
            values = values + landed_tails[d - 1, :, HEAD:].astype(F32)
        keys = keys * cos_ref[...] - pltpu.roll(keys, HEAD // 2, 1) * sin_ref[...]
        width = heads * HEAD
        mixed[:, width : width + HEAD] = keys.astype(BF)
        mixed[:, width + HEAD :] = values.astype(BF)
        launch("end", remote_copy(give_of(mixed, mix_half), mix_right.at[place], cs_in.at[6], cs_in.at[7], to_c))
        mix_right[place, :] = keep_of(mixed, mix_half)[...]

    step_rows = w_rows.shape[1]

    def fetch_rows(j):
        if j * step_rows < D:
            fetch(("q", j), w_in.at[pl.ds(j * step_rows, step_rows)], w_rows.at[j % 2], fs.at[9 + j % 2])

    def start_input():
        drain("da")
        fetch_rows(0)
        fetch_rows(1)
        fetch("x0", x_ref, got, fs.at[4])

    def project_back(j):
        landed(("q", j))
        da[:, j * step_rows : (j + 1) * step_rows] = nt(mixed[...], w_rows[j % 2]).astype(BF)
        fetch_rows(j + 2)

    def input_back():
        landed("x0")
        landed("dx")
        gain = jnp.concatenate([gains[zz, 0:1, :] for zz in range(S)], axis=1).astype(F32)
        step = 64

        @pl.loop(0, piece // step)
        def _(i):
            at = pl.ds(pl.multiple_of(i * step, step), step)
            u = got[at, :].astype(F32)
            scale = lax.rsqrt(jnp.mean(u * u, axis=1, keepdims=True) + norm_eps)
            hat = u * scale
            e = da[at, :].astype(F32) * gain
            inner = jnp.mean(e * hat, axis=1, keepdims=True)
            do[at, :] = (x1[at, :] + scale * (e - hat * inner)).astype(BF)

        fetch("x_grad", do, x_grad, fs.at[0])

    spread = {6: ((1, 0, 3),), 7: ((1, 3, 6), (2, 0, 3)), 8: ((1, 6, 8), (2, 3, 6), (3, 0, 3))}
    spread.update({9: ((2, 6, 8), (3, 3, 6)), 10: ((3, 6, 8),)})
    out_steps = [(g, p) for t in sorted(spread) for g, a, b in spread[t] for p in range(a, b)]
    out_count = {t: sum(b - a for _, a, b in spread[t]) for t in spread}
    assert rows_groups == 3 and wide == 6

    def fetch_tile(i):
        if i < len(out_steps):
            g, p = out_steps[i]
            fetch(("d", i), w_down.at[:, g - 1, p % 4, p // 4], w_tiles.at[i % 2], fs.at[12 + i % 2])

    def output_step(i):
        g, p = out_steps[i]
        landed(("d", i))
        fetch_tile(i + 1)
        lhs = left[g % left_slots, p, :, :, place].reshape(S * r, piece)
        for j in range(0, D, piece):
            rhs = w_tiles[i % 2, :, :, j : j + piece].reshape(S * r, piece)
            x1[:, j : j + piece] += lax.dot_general(
                lhs, rhs, (((0,), (0,)), ((), ())), preferred_element_type=F32
            )

    def output_work(t):
        if t == 2:
            landed("dx")
            fetch("x1", middle, x1, fs.at[1])
        if t == 5:
            landed("x1")
            fetch_tile(0)
        if t in out_count:
            done = sum(out_count[u] for u in out_count if u < t)
            for i in range(done, done + out_count[t]):
                output_step(i)
        if t == 11:
            do[...] = x1[...].astype(BF)
            fetch("y", do, y_out, fs.at[2])
        if t == 13:
            landed("y")
            fetch("dx", dx_land, x1, fs.at[11])

    def came(ref, i):
        ref = ref.at[other_place]
        remote_copy(ref, ref, cs_in.at[i], cs_in.at[i + 1], to_c).wait_recv()

    stages = (first, second, third, fourth, fifth, sixth)

    fetch("near", back.at[place], do, fs.at[0])
    fetch("x1", middle, x1, fs.at[1])
    fetch("dy", dy_own, mixed.at[:, pl.ds(0, D)], fs.at[2])
    fetch("gains", gains_ref, gains, fs.at[3])
    for i in range(2):
        fetch("w", w_out.at[pl.ds(0, T), pl.ds(i * n, n)], right.at[2 + i], fs.at[5 + i])
    each = 5

    def work(t):
        if t == 0:
            norm_back()
        if t == 1:
            heads_back()
        if t >= 2 and (t - 2) * each < len(steps):
            attention((t - 2) * each, each)
        if t == 7:
            send_tails()
        if t == 8:
            mix_back()
            start_input()
        if t >= 9 and (t - 9) * step_rows < D:
            project_back(t - 9)
        output_work(t)
        if t == 15:
            input_back()

    for t in range(nc + len(stages) - 1):
        for lag, stage in enumerate(stages):
            if lag == 0 and t == chunk_out:
                came(out_right, 4)
            if lag == 0 and t == chunk_out + 1:
                came(mix_right, 6)
            if 0 <= t - lag < nc:
                stage(t - lag)
            if lag == 0:
                work(t)
        if t == 1:
            fetch_right(2)
        if t >= 1:
            fetch_right(t + 2)
        for g in range(1, groups):
            if t == wide + g - (3 if g < left_slots else 2):
                fetch_left(g)
    for t in range(nc):
        p = out.at[t, :, 1 - c, :, :, pl.ds(0, widths[t])]
        remote_copy(p, p, cs.at[t], cr.at[t], to_c).wait_recv()
    for key in list(pending):
        drain(key)
    for key in list(loads):
        landed(key)


def backward(
    two_t, hid_t, transposed, grads, dy, back, middle, w_out, gains, x, w_in, w_down, attention, tables, heads, S, cid
):
    D, T = two_t.shape
    sides, _, half_ff = grads.shape
    piece = middle.shape[0]
    n = D // 2
    r = D // (S * 8)
    parts = half_ff // n
    rows_groups = 2 * half_ff // (S * 8 * r)
    mixed = attention[2].shape[1] + 2 * HEAD
    nc = sides * parts + rows_groups + 3
    m = S * r
    slots = 5
    keys = attention[3].shape[0]
    reach = keys // piece - 1
    dma = pltpu.SemaphoreType.DMA
    hid_shape = (S // 2, rows_groups, 4, 2, r, T)

    def body(*refs):
        backward_kernel(heads, sides, parts, S, *refs)

    def vmem(*shape):
        return pltpu.VMEM(shape, BF)

    results = pl.pallas_call(
        body,
        out_shape=(
            jax.ShapeDtypeStruct((nc, 4, 2, 2, r, n), BF),
            jax.ShapeDtypeStruct(hid_shape, BF),
            jax.ShapeDtypeStruct((piece, D), BF),
            jax.ShapeDtypeStruct((piece, D), BF),
            jax.ShapeDtypeStruct((piece, D), F32),
        ),
        in_specs=[ANY] * 16 + [VM] * 9,
        out_specs=(ANY,) * 5,
        scratch_shapes=[
            vmem(3, 8, S, r, T),
            vmem(4, T, n),
            vmem(T, n),
            vmem(T, mixed // 2),
            vmem(2, 4, m, n),
            vmem(slots, 4, m, n),
            vmem(2, 2, m, n),
            vmem(slots, 2, m, n),
            vmem(2, S, 2, r, n),
            vmem(nc, S - 1, 2, r, n),
            vmem(2, 2, r, n),
            vmem(piece, D),
            vmem(piece, D),
            vmem(piece, D),
            vmem(reach, piece, 2 * HEAD),
            vmem(reach, piece, 2 * HEAD),
            vmem(*gains.shape),
            pltpu.VMEM((piece, D), F32),
            pltpu.VMEM((keys, HEAD), F32),
            pltpu.VMEM((keys, HEAD), F32),
            pltpu.VMEM((WINDOW + piece // 2, piece // 2), F32),
            pltpu.VMEM((HEAD, keys), BF),
            vmem(piece, mixed),
            vmem(2, 256, mixed),
            vmem(2, S, r, D),
            dma((rows_groups + 3, 8, 2)),
            dma((nc, 2)),
            dma((14,)),
            dma((8,)),
            dma((reach,)),
            dma((reach,)),
            dma((nc, 4)),
            dma((nc, 4)),
            dma((nc, 2)),
            dma((nc, 2)),
            dma((nc, S)),
            dma((nc, S)),
            dma((nc,)),
            dma((nc, 3)),
            dma((nc, 3)),
            dma((nc, 3)),
            dma((nc, 3)),
            dma((nc,)),
            dma((nc,)),
        ],
        compiler_params=pltpu.CompilerParams(
            collective_id=cid, has_side_effects=True, vmem_limit_bytes=BACKWARD_VMEM
        ),
    )(
        two_t.reshape(S, 4, 2, r, T),
        hid_t.reshape(hid_shape),
        *[v.reshape(S, 4, 2, r, piece) for v in transposed],
        grads,
        *dy,
        back,
        middle,
        w_out,
        gains,
        x,
        w_in,
        w_down.reshape(S, rows_groups, 4, 2, r, D),
        *attention,
        *tables,
    )
    return results[0], results[2], results[3]


def adam_kernel(total, widths, gains, count_ref, rates_ref, g_ref, w_ref, m_ref, g_out, w_out, m_out, *more):
    step_value = count_ref[0].astype(F32)
    log_first = jnp.log(jnp.full((8, 128), beta_first, F32))
    log_second = jnp.log(jnp.full((8, 128), beta_second, F32))
    unfix_first = (1.0 / (1.0 - jnp.exp(step_value * log_first)))[:1, :1]
    unfix_second = (1.0 / (1.0 - jnp.exp(step_value * log_second)))[:1, :1]
    rate, decay = rates_ref[0], rates_ref[1]
    rows = w_ref.shape[0]

    if gains:

        @pl.when((pl.program_id(1) == 0) & (pl.program_id(2) == 0))
        def _():
            more[0][...] = jnp.zeros_like(more[0])

    for i, n in enumerate(widths):
        at = pl.ds(sum(widths[:i]), n)
        grad = g_ref[i, :, 0, :, :, :n].reshape(rows, n).astype(F32) * (1.0 / total)
        w = w_ref[:, at]
        first = beta_first * m_ref[0, :, at] + (1.0 - beta_first) * grad
        second = beta_second * m_ref[1, :, at] + (1.0 - beta_second) * grad * grad
        step = first * unfix_first / (jnp.sqrt(second * unfix_second) + adam_eps) + decay * w
        g_out[:, at] = grad
        w_out[:, at] = w - rate * step
        m_out[0, :, at] = first
        m_out[1, :, at] = second
        if gains:
            both = w.astype(BF).astype(F32) * grad
            for j in range(0, n, 128):
                more[0][...] += both[:, j : j + 128]


def adam_call(
    weight, moments, grads, count, rates, total, base, widths, sides=1, tiles=1, gains=False, chips=4
):
    _, _, _, _, r, n = grads.shape
    wide = len(widths)

    def g_place(kk, cc, ss, tt):
        return (base // wide + ss + tt, kk, cc, 0, 0, 0)

    def place(kk, cc, ss, tt):
        return (tt * (4 // chips) + kk, ss * 2 + cc)

    def m_place(*at):
        return (0,) + place(*at)

    rows = chips * 2 * r
    w_spec = pl.BlockSpec((rows, sum(widths)), place)
    m_spec = pl.BlockSpec((2, rows, sum(widths)), m_place)
    smem = pl.BlockSpec(memory_space=pltpu.SMEM)
    like = jax.ShapeDtypeStruct(weight.shape, F32)
    out_specs = [w_spec, w_spec, m_spec]
    out_shape = [like, like, jax.ShapeDtypeStruct(moments.shape, F32)]
    if gains:
        out_specs.append(pl.BlockSpec((rows, 128), lambda kk, cc, ss, tt: (kk, 0)))
        out_shape.append(jax.ShapeDtypeStruct((weight.shape[0], 128), F32))

    def body(*refs):
        adam_kernel(total, widths, gains, *refs)

    return pl.pallas_call(
        body,
        grid=(4 // chips, 2, sides, tiles),
        in_specs=[smem, smem, pl.BlockSpec((wide, chips, 1, 2, r, n), g_place), w_spec, m_spec],
        out_specs=out_specs,
        out_shape=out_shape,
        compiler_params=pltpu.CompilerParams(
            dimension_semantics=("arbitrary",) * 4, vmem_limit_bytes=VMEM_BYTES
        ),
        cost_estimate=pl.CostEstimate(
            flops=20 * weight.size,
            bytes_accessed=30 * weight.size,
            transcendentals=weight.size,
        ),
    )(count, rates, grads, weight, moments)


def dot(a, b):
    return jnp.dot(a, b, preferred_element_type=F32)


def dot_rows(a, b):
    return lax.dot_general(a, b, (((1,), (0,)), ((), ())), preferred_element_type=F32)


def dot_t(a, b):
    return lax.dot_general(a, b, (((1,), (1,)), ((), ())), preferred_element_type=F32)


def on_device(
    Y,
    S,
    block_in,
    cotangent,
    segment_ids,
    input_proj,
    output_proj,
    gate_up,
    down_weight,
    norm_gains,
    input_moments,
    output_moments,
    gate_moments,
    down_moments,
    gain_moments,
    update_count,
    optimizer_rates,
):
    seq_place = lax.axis_index("z")
    core = lax.axis_index("c")
    first_core = core == 0
    D = block_in.shape[-1]
    half_ff = FF // 2
    rows_d = input_proj.shape[0]
    rows_f = down_weight.shape[0]
    fast = Y == 2 and rows_d % 128 == 0
    in_half = input_proj.shape[1] // 2
    d_half = D // 2
    r = rows_d // 8

    gains_low = norm_gains.astype(BF)
    tokens = block_in[0].astype(F32)
    piece_len = tokens.shape[0]
    width_q = HEADS * HEAD
    positions = seq_place * piece_len + jnp.arange(piece_len, dtype=jnp.int32)
    reach_count = (WINDOW + piece_len - 2) // piece_len
    key_span = reach_count * piece_len
    segments = segment_ids[0]
    padded_ids = jnp.concatenate([jnp.full((key_span,), -1, jnp.int32), segments])
    query_ids = lax.dynamic_slice_in_dim(segments, seq_place * piece_len, piece_len)
    key_ids = lax.dynamic_slice_in_dim(padded_ids, seq_place * piece_len, key_span + piece_len)
    live_rows = query_ids != 0
    query_row = query_ids[None, :]
    key_column = key_ids[:, None]

    if fast:
        frequency = 10000.0 ** (-2.0 * jnp.arange(HEAD // 2).astype(F32) / HEAD)
        angles = positions.astype(F32)[:, None] * jnp.concatenate([frequency, frequency])[None, :]
        side = jnp.where(jnp.arange(HEAD) < HEAD // 2, -1.0, 1.0)
        cos_table, sin_table = jnp.cos(angles), jnp.sin(angles) * side
        (
            in_full,
            out_full,
            down_full,
            gate_full,
            gains_full,
            normed,
            queries,
            key_rows,
            values,
            flat_heads,
            log_totals,
            middle,
            normed_two,
            two_other,
            *transposed,
        ) = forward(
            [
                w.reshape(4, 2, w.shape[0] // 8, w.shape[1])
                for w in (input_proj, output_proj, down_weight, gate_up)
            ],
            jnp.concatenate([gains_low] * 8, axis=0),
            block_in[0],
            cos_table,
            sin_table,
            query_row,
            key_column,
            HEADS,
            S,
            0,
        )
        in_full = in_full.reshape(D, 2 * in_half)
        out_full = out_full.reshape(D, D)
        gains_small = gains_full
        gains_full = gains_full[:, :2].transpose(1, 0, 2).reshape(2, D)
        down_full = down_full.reshape(FF, D)
        gate_full = gate_full.reshape(D, 2 * half_ff)
        gains_wide = gains_full.astype(F32)
    else:
        gate_low = jnp.concatenate(
            [
                lax.dynamic_slice_in_dim(gate_up, side * FF + core * half_ff, half_ff, 1)
                for side in range(2)
            ],
            axis=1,
        )
        in_full, out_full, down_full, gate_full = (
            lax.all_gather(w.astype(BF), "z", axis=0, tiled=True)
            for w in (input_proj, output_proj, down_weight, gate_low)
        )
        gains_full = lax.all_gather(gains_low, "z", axis=1, tiled=True)
        gains_wide = gains_full.astype(F32)
        normed = root_norm(tokens, gains_wide[0]).astype(BF)
        mixed_proj = dot(normed, in_full)
        queries = (
            rotate(mixed_proj[:, :width_q].reshape(piece_len, HEADS, HEAD), positions, 1.0)
            .astype(BF)
            .reshape(piece_len, width_q)
        )
        own_keys = rotate(mixed_proj[:, width_q : width_q + HEAD], positions, 1.0)
        own_pair = jnp.concatenate([own_keys, mixed_proj[:, width_q + HEAD :]], axis=1).astype(BF)
        earlier = []
        for back_step in range(reach_count, 0, -1):
            earlier.append(passed_along(own_pair, "z", back_step))
        key_pairs = jnp.concatenate(earlier + [own_pair], axis=0)
        key_rows = key_pairs[:, :HEAD]
        values = key_pairs[:, HEAD:]
        flat_heads, log_totals = attend(
            query_row, key_column, queries, key_rows, values, HEADS, piece_len
        )
        middle = tokens + dot(flat_heads, out_full)
        normed_two = root_norm(middle, gains_wide[1]).astype(BF)
        two_other = swapped(normed_two, "c")

    upstream = cotangent[0].astype(F32)

    def ordered(mine, other):
        return jnp.concatenate(
            [jnp.where(first_core, mine, other), jnp.where(first_core, other, mine)], axis=0
        )

    def pair(v):
        return ordered(v, swapped(v, "c"))

    def half_pair(v):
        n = v.shape[1] // 2
        keep = lax.dynamic_slice_in_dim(v, core * n, n, 1)
        give = lax.dynamic_slice_in_dim(v, (1 - core) * n, n, 1)
        return ordered(keep, swapped(give, "c"))

    def core_sum(v):
        keep = lax.dynamic_slice_in_dim(v, core * piece_len, piece_len, 0)
        give = lax.dynamic_slice_in_dim(v, (1 - core) * piece_len, piece_len, 0)
        return keep.astype(F32) + swapped(give, "c").astype(F32)

    df_other = swapped(cotangent[0], "c")
    two_t, hid_t, grad_gated, two_sum = mlp_call(
        core.reshape(1).astype(jnp.int32),
        (normed_two, two_other),
        (cotangent[0], df_other),
        gate_full,
        down_full,
    )
    token_total = piece_len * S * Y * 4 * block_in.shape[0]
    step_value = update_count[0].astype(F32)
    rates = optimizer_rates

    if fast:
        sums, block_in_grad, block_out = backward(
            two_t,
            hid_t,
            transposed,
            grad_gated,
            (cotangent[0], df_other),
            two_sum,
            middle,
            out_full,
            gains_small,
            block_in[0],
            in_full,
            down_full,
            (query_row, key_column, queries, key_rows, values, flat_heads, log_totals),
            (cos_table, sin_table),
            HEADS,
            S,
            2,
        )
    else:
        down_mine = lax.dynamic_slice_in_dim(down_full, core * half_ff, half_ff, 0)
        block_out = (middle + core_sum(dot(hid_t.T, down_mine).astype(BF))).astype(BF)
        grad_normed_two = core_sum(two_sum)
        _, norm_pull_two = jax.vjp(root_norm, middle, gains_wide[1])
        grad_middle_norm, grad_gain_two = norm_pull_two(grad_normed_two)
        grad_middle = upstream + grad_middle_norm
        grad_branch = grad_middle.astype(BF)
        grad_flat = dot_t(grad_branch, out_full)
        grad_attended = jnp.where(live_rows[:, None], grad_flat, 0.0).astype(BF)
        grad_query_all, grad_keys, grad_values = attend_back(
            query_row,
            key_column,
            queries,
            key_rows,
            values,
            flat_heads,
            grad_attended,
            log_totals,
            HEADS,
            piece_len // 2,
        )
        grad_pairs = jnp.concatenate([grad_keys, grad_values], axis=1)
        own_grad = grad_pairs[key_span:]
        for back_step in range(1, reach_count + 1):
            sent_rows = grad_pairs[
                key_span - back_step * piece_len : key_span - (back_step - 1) * piece_len
            ]
            own_grad = own_grad + passed_along(sent_rows, "z", -back_step)
        grad_query_raw = rotate(
            grad_query_all.reshape(piece_len, HEADS, HEAD), positions, -1.0
        ).reshape(piece_len, width_q)
        grad_key_raw = rotate(own_grad[:, :HEAD], positions, -1.0)
        grad_mixed = jnp.concatenate(
            [grad_query_raw, grad_key_raw, own_grad[:, HEAD:]], axis=1
        ).astype(BF)
        grad_normed = dot_t(grad_mixed, in_full)
        _, norm_pull_one = jax.vjp(root_norm, tokens, gains_wide[0])
        grad_tokens_norm, grad_gain_one = norm_pull_one(grad_normed)
        block_in_grad = (grad_middle + grad_tokens_norm).astype(BF)

    if fast:

        def adam(weight, moments, *rest, **more):
            return adam_call(
                weight, moments, sums, update_count, rates, float(token_total), *rest, **more
            )

        tiles = half_ff // d_half
        same = (d_half,) * tiles
        gate_grad, gate_new, gate_mom, gain_two = adam(
            gate_up, gate_moments, 0, same, sides=2, gains=True, chips=2
        )
        down_grad, down_new, down_mom = adam(
            down_weight, down_moments, 2 * tiles, (d_half,), tiles=tiles
        )
        out_grad, out_new, out_mom = adam(output_proj, output_moments, 3 * tiles, (d_half,))
        in_grad, in_new, in_mom, gain_one = adam(
            input_proj, input_moments, 3 * tiles + 1, split_widths(in_half, d_half), gains=True
        )
        gain_grad = jnp.stack(
            [jnp.sum(v, axis=1) for v in (gain_one, gain_two)]
        ) / gains_low.astype(F32)
    else:

        def adam(weight, moments, grad):
            grad = grad.astype(F32) / token_total
            change, new = adamw_step(weight, moments, grad, step_value, rates)
            return grad, weight - change, new

        def summed(left, right):
            whole = dot_rows(left.T, right).astype(BF)
            mine = lax.psum_scatter(whole, "z", scatter_dimension=0, tiled=True)
            return lax.psum(mine, ("y", "x"))

        two_both = ordered(normed_two, two_other)
        grad_half = half_pair(grad_branch)
        mixed_half = half_pair(grad_mixed)
        normed_both = pair(normed)
        flat_both = pair(flat_heads)
        df_both = pair(cotangent[0])
        gate_half = [summed(two_both, grad_gated[side]) for side in range(2)]
        gate_sum = jnp.concatenate(
            [lax.all_gather(g, "c", axis=1, tiled=True) for g in gate_half], axis=1
        )
        down_part = lax.psum(dot_rows(hid_t, df_both).astype(BF), ("y", "x"))
        down_part = lax.all_gather(down_part, "c", axis=0, tiled=True)
        down_sum = lax.psum_scatter(down_part, "z", scatter_dimension=0, tiled=True)
        out_total = lax.all_gather(summed(flat_both, grad_half), "c", axis=1, tiled=True)
        in_total = lax.all_gather(summed(normed_both, mixed_half), "c", axis=1, tiled=True)
        out_grad, out_new, out_mom = adam(output_proj, output_moments, out_total)
        in_grad, in_new, in_mom = adam(input_proj, input_moments, in_total)
        gate_grad, gate_new, gate_mom = adam(gate_up, gate_moments, gate_sum)
        down_grad, down_new, down_mom = adam(down_weight, down_moments, down_sum)
        gains_sum = lax.psum(jnp.stack([grad_gain_one, grad_gain_two]), ("y", "x", "c", "z"))
        gain_grad = lax.dynamic_slice_in_dim(gains_sum, seq_place * rows_d, rows_d, 1) / token_total
    gains_step, gain_moments_new = adamw_step(norm_gains, gain_moments, gain_grad, step_value, rates)
    return (
        block_out[None],
        block_in_grad[None],
        in_grad,
        out_grad,
        gate_grad,
        down_grad,
        gain_grad,
        in_new,
        out_new,
        gate_new,
        down_new,
        gains_step,
        in_mom,
        out_mom,
        gate_mom,
        down_mom,
        gain_moments_new,
    )


def solution(mesh):
    dp, S = mesh.shape["dp"], mesh.shape["seq"]
    Y = dp // 4
    grid = Mesh(mesh.devices.reshape(Y, 2, 2, S), ("y", "x", "c", "z"))
    data = ("y", "x", "c")
    tokens = P(data, "z", None)
    rows = P("z", None)
    moments = P(None, "z", None)
    in_specs = (
        (tokens, tokens, P(data, None))
        + (rows,) * 4
        + (P(None, "z"),)
        + (moments,) * 4
        + (P(None, None, "z"), P(), P())
    )
    out_specs = (
        (tokens, tokens)
        + (rows,) * 4
        + (P(None, "z"),)
        + (rows,) * 4
        + (P(None, "z"),)
        + (moments,) * 4
        + (P(None, None, "z"),)
    )

    def device_step(*arrays):
        return on_device(Y, S, *arrays)

    return jax.shard_map(
        device_step, mesh=grid, in_specs=in_specs, out_specs=out_specs, check_vma=False
    )
```

```python
import jax
import jax.numpy as jnp
from jax import lax
from jax.experimental import pallas as pl
from jax.experimental.pallas import tpu as pltpu
from jax.sharding import Mesh
from jax.sharding import PartitionSpec as P

HEADS = 12
HEAD = 128
FF = 4608
WINDOW = 1024


norm_eps = 1e-06
adam_eps = 1e-08
beta_first = 0.9
beta_second = 0.95
BF = jnp.bfloat16
F32 = jnp.float32
MESH_ID = pl.DeviceIdType.MESH
VMEM_BYTES = 60 * 1024 * 1024
BACKWARD_VMEM = 127 * 512 * 1024
ANY = pl.BlockSpec(memory_space=pl.ANY)
VM = pl.BlockSpec(memory_space=pltpu.VMEM)
LOG2E = 1.4426950408889634


def passed_along(block, axis, distance):
    devices = range(lax.axis_size(axis))
    route = [(i - distance, i) for i in devices if i - distance in devices]
    return lax.ppermute(block, axis, route)


def swapped(block, axis):
    return lax.ppermute(block, axis, [(0, 1), (1, 0)])


def rotate(values, positions, sign_value):
    half_width = values.shape[-1] // 2
    frequency = 10000.0 ** (-2.0 * jnp.arange(half_width).astype(jnp.float32) / values.shape[-1])
    angles = positions.astype(jnp.float32)[:, None] * frequency[None, :]
    cosine = jnp.cos(angles)
    sine_part = sign_value * jnp.sin(angles)
    if values.ndim == 3:
        cosine = cosine[:, None, :]
        sine_part = sine_part[:, None, :]
    lower_half = values[..., :half_width]
    upper_half = values[..., half_width:]
    return jnp.concatenate(
        [
            lower_half * cosine - upper_half * sine_part,
            upper_half * cosine + lower_half * sine_part,
        ],
        axis=-1,
    )


def root_norm(values, gain):
    return values * lax.rsqrt(jnp.mean(values * values, axis=-1, keepdims=True) + norm_eps) * gain


def adamw_step(weight, moments, grad, step_value, optimizer_rates):
    fix_first = 1.0 - beta_first**step_value
    fix_second = 1.0 - beta_second**step_value
    first_moment = beta_first * moments[0] + (1.0 - beta_first) * grad
    second = beta_second * moments[1] + (1.0 - beta_second) * grad * grad
    update = (
        first_moment / fix_first / (jnp.sqrt(second / fix_second) + adam_eps)
        + optimizer_rates[1] * weight
    )
    return (optimizer_rates[0] * update, jnp.stack([first_moment, second]))


def gather_kernel(shared, groups, S, own, full, sems, small_own, small_full, prepare, work):
    n = len(shared)
    chunks = [chunk for group in groups for chunk in group]
    members = []
    for group in groups:
        first = members[-1][-1] + 1 if members else 0
        members.append(range(first, first + len(group)))
    ng = len(groups)
    F = S - 1
    loc, zs, zr, xs, xr, ys, yr, cs, cr, ss, sr = sems
    y, x, c, z = (lax.axis_index(a) for a in ("y", "x", "c", "z"))
    k = y * 2 + x
    kx = y * 2 + 1 - x
    ky = (1 - y) * 2 + x
    kxy = 3 - k
    to_x = {"x": 1 - x}
    to_y = {"y": 1 - y}
    to_c = {"c": 1 - c}
    low = z
    high = S - 1 - z
    near_count = jnp.minimum(low, high)
    above = jnp.minimum(z + 1, S - 1)
    below = jnp.maximum(z - 1, 0)
    blocks = []
    for j in range(F):
        near = j < 2 * near_count
        dist = jnp.where(near, j // 2 + 1, j - near_count + 1)
        sign = jnp.where(near, (j % 2) * 2 - 1, jnp.where(high > low, 1, -1))
        blocks.append((z + sign * dist, sign))
    barrier = pltpu.get_barrier_semaphore()
    others = [lax.rem(z + e, S) for e in range(1, S)]
    for target in [to_x, to_y, to_c] + [{"z": zz} for zz in others]:
        pl.semaphore_signal(barrier, inc=1, device_id=target, device_id_type=MESH_ID)
    pl.semaphore_wait(barrier, 3 + F)

    def box(q, half):
        i, r0, rn, c0, cn, _ = chunks[q]
        if shared[i]:
            columns = full[i].shape[-1] // 2
            c0 = pl.multiple_of(half * columns + c0, 128)
        return pl.ds(r0, rn), pl.ds(c0, cn)

    def part(q, zz, kk, h=None, half=c):
        rr, cc = box(q, half)
        held = full[chunks[q][0]]
        if h is None:
            return held.at[zz, kk, :, rr, cc]
        return held.at[zz, kk, h, rr, cc]

    def carried(q):
        route = chunks[q][5]
        if route == "xy":
            return (k,)
        return (x, 2 + x) if route == "x" else (2 * y, 2 * y + 1)

    def exchanged(q):
        if chunks[q][5] == "x":
            return xs, xr, to_x, (1 - x, 3 - x)
        return ys, yr, to_y, (2 - 2 * y, 3 - 2 * y)

    def remote(src, dst, s, r, target):
        return pltpu.make_async_remote_copy(
            src_ref=src,
            dst_ref=dst,
            send_sem=s,
            recv_sem=r,
            device_id=target,
            device_id_type=MESH_ID,
        )

    tail = []
    arriving = {i: [] for i in range(n)}
    arriving[None] = []
    finished = [0] * n

    def begin(g):
        i, r0, rn, c0 = groups[g][0][:4]
        prepare(g)
        rows = pl.ds(r0, rn)
        if shared[i]:
            src, dst = own[i].at[:, :, rows], full[i].at[z, :, :, rows]
        else:
            cc = pl.ds(c0, sum(chunk[4] for chunk in groups[g]))
            src, dst = own[i].at[:, :, rows, cc], full[i].at[z, :, :, rows, cc]
        for q in members[g]:
            z_first(q)
        copy = pltpu.make_async_copy(src, dst, loc.at[g])
        copy.start()
        arriving[i].append(copy.wait)

    def z_first(q):
        i = chunks[q][0]
        rr, cc = box(q, c)
        for m, kk in enumerate(carried(q)):
            for ok, target, slot in ((z + 1 < S, above, F), (z > 0, below, F + 1)):

                def make(target=target, slot=slot, m=m, kk=kk):
                    return remote(
                        own[i].at[kk, :, rr, cc],
                        part(q, z, kk),
                        zs.at[q, slot, m],
                        zr.at[q, z, m],
                        {"z": target},
                    )

                @pl.when(ok)
                def _(make=make):
                    make().start()

                def finish(ok=ok, make=make):
                    @pl.when(ok)
                    def _():
                        make().wait_send()

                tail.append(finish)

    def send(p, s, r, q, j, slot, target):
        copy = remote(p, p, s.at[q, j, slot], r.at[q, j, slot], target)
        copy.start()
        tail.append(copy.wait_send)

    def z_next(q, j):
        zz, sign = blocks[j]
        onward = z - sign
        ok = (onward >= 0) & (onward < S)
        target = jnp.clip(onward, 0, S - 1)
        for m, kk in enumerate(carried(q)):
            piece = part(q, zz, kk)
            remote(piece, piece, zs.at[q, j, m], zr.at[q, zz, m], {"z": above}).wait_recv()

            def make(piece=piece, m=m):
                return remote(piece, piece, zs.at[q, j, m], zr.at[q, zz, m], {"z": target})

            @pl.when(ok)
            def _(make=make):
                make().start()

            def finish(make=make):
                @pl.when(ok)
                def _():
                    make().wait_send()

            tail.append(finish)
            if chunks[q][5] != "xy":
                s, r, neighbour, _ = exchanged(q)
                send(piece, s, r, q, j, m, neighbour)
        if chunks[q][5] == "xy":
            send(part(q, zz, k, 0), xs, xr, q, j, 0, to_x)
            send(part(q, zz, k, 1), ys, yr, q, j, 0, to_y)
            send(part(q, zz, k, 0), ys, yr, q, j, 1, to_y)
            send(part(q, zz, k, 1), xs, xr, q, j, 1, to_x)

    def xy_next(q, j):
        if chunks[q][5] != "xy":
            return
        zz, _ = blocks[j]
        p = part(q, zz, kx, 0)
        remote(p, p, xs.at[q, j, 0], xr.at[q, j, 0], to_x).wait_recv()
        send(p, ys, yr, q, j, 2, to_y)
        p = part(q, zz, ky, 1)
        remote(p, p, ys.at[q, j, 0], yr.at[q, j, 0], to_y).wait_recv()
        send(p, xs, xr, q, j, 2, to_x)

    def last(q, j):
        i = chunks[q][0]
        zz, _ = blocks[j]
        finished[i] += 1
        if chunks[q][5] == "xy":
            for kk, h, s, r, slot, target in (
                (kx, 1, xs, xr, 1, to_x),
                (ky, 0, ys, yr, 1, to_y),
                (kxy, 1, xs, xr, 2, to_x),
                (kxy, 0, ys, yr, 2, to_y),
            ):
                p = part(q, zz, kk, h)
                remote(p, p, s.at[q, j, slot], r.at[q, j, slot], target).wait_recv()
        else:
            s, r, neighbour, theirs = exchanged(q)
            for m, kk in enumerate(theirs):
                p = part(q, zz, kk)
                remote(p, p, s.at[q, j, m], r.at[q, j, m], neighbour).wait_recv()
        if shared[i]:
            rr, cc = box(q, c)
            p = full[i].at[zz, :, :, rr, cc]
            copy = remote(p, p, cs.at[q, j], cr.at[q, j], to_c)
            copy.start()
            tail.append(copy.wait_send)
            rr, cc = box(q, 1 - c)
            other = full[i].at[zz, :, :, rr, cc]

            def finish():
                remote(other, other, cs.at[q, j], cr.at[q, j], to_c).wait_recv()

            arriving[i].append(finish)

    def ready(i):
        if i is not None:
            assert finished[i] == F * sum(chunk[0] == i for chunk in chunks)
        for wait in arriving.pop(i, []):
            wait()

    begin(0)
    if small_own is not None:
        place = pltpu.make_async_copy(small_own, small_full.at[z], ss.at[0])
        place.start()
        arriving[None].append(place.wait)
        for e, zz in enumerate(others, 1):
            copy = remote(small_own, small_full.at[z], ss.at[e], sr.at[S - e], {"z": zz})
            copy.start()
            tail.append(copy.wait_send)
            came = small_full.at[zz]
            arriving[None].append(remote(came, came, ss.at[e], sr.at[e], {"z": zz}).wait_recv)
    for t in range(1, ng + F + 3):
        if t < ng:
            begin(t)
        for lag, stage in ((1, z_next), (2, xy_next), (3, last)):
            for j in reversed(range(F)):
                if 0 <= t - lag - j < ng:
                    for q in members[t - lag - j]:
                        stage(q, j)
        work(t, ready)
    for i in list(arriving):
        ready(i)
    for wait in tail:
        wait()


def gather_sems(ng, nc, S):
    dma = pltpu.SemaphoreType.DMA
    F = S - 1
    return [
        dma((ng,)),
        dma((nc, F + 2, 2)),
        dma((nc, S, 2)),
        dma((nc, F, 3)),
        dma((nc, F, 3)),
        dma((nc, F, 3)),
        dma((nc, F, 3)),
        dma((nc, F)),
        dma((nc, F)),
        dma((S,)),
        dma((S,)),
    ]


def nt(a, b):
    return lax.dot_general(a, b, (((1,), (1,)), ((), ())), preferred_element_type=F32)

def nn(a, b):
    return lax.dot_general(a, b, (((1,), (0,)), ((), ())), preferred_element_type=F32)

def fill_bias(bias, q_ids, k_ids, first, rows, span):
    key = lax.broadcasted_iota(jnp.int32, (span, rows), 0)
    query = lax.broadcasted_iota(jnp.int32, (span, rows), 1)
    distance = query + WINDOW - key
    same = k_ids[pl.ds(first, span), :1] == q_ids[:1, pl.ds(first, rows)]
    allowed = (distance >= 0) & (distance < WINDOW) & same
    bias[...] = jnp.where(allowed, 0.0, -1e30)

def fwd_step(h, first, rows, q_ids, q_ref, k_ref, o_ref, l_ref, bias, vt):
    span = WINDOW + rows
    factor = HEAD**-0.5 * LOG2E
    cols = pl.ds(h * HEAD, HEAD)
    q = q_ref[pl.ds(first, rows), cols]
    s = nt(k_ref[pl.ds(first, span), :], q) * factor + bias[...]
    top = jnp.max(s, axis=0, keepdims=True)
    p = jnp.exp2(s - top)
    total = jnp.sum(p, axis=0, keepdims=True)
    o = nn(vt[:, pl.ds(first, span)], p.astype(BF))
    live = q_ids[:1, pl.ds(first, rows)] != 0
    o = jnp.where(live, o * (1.0 / total), 0.0)
    o_ref[pl.ds(first, rows), cols] = o.T.astype(BF)
    l_ref[h, :, pl.ds(first, rows)] = top + jnp.log2(total)


def fwd_kernel(heads, rows, q_ids, k_ids, q_ref, k_ref, v_ref, o_ref, l_ref, bias, vt):
    vt[...] = v_ref[...].T
    for first in range(0, q_ref.shape[0], rows):
        fill_bias(bias, q_ids, k_ids, first, rows, WINDOW + rows)
        for h in range(heads):
            fwd_step(h, first, rows, q_ids, q_ref, k_ref, o_ref, l_ref, bias, vt)


def norm_rows(source, gain, target):
    rows = 64

    @pl.loop(0, target.shape[0] // rows)
    def _(i):
        at = pl.ds(pl.multiple_of(i * rows, rows), rows)
        u = source[at, :].astype(F32)
        scale = lax.rsqrt(jnp.mean(u * u, axis=1, keepdims=True) + norm_eps)
        target[at, :] = (u * scale * gain).astype(target.dtype)


def turned(u, cos_ref, sin_ref):
    return u * cos_ref[...] + pltpu.roll(u, HEAD // 2, 1) * sin_ref[...]


def remote_copy(src, dst, send, receive, target):
    return pltpu.make_async_remote_copy(
        src_ref=src,
        dst_ref=dst,
        send_sem=send,
        recv_sem=receive,
        device_id=target,
        device_id_type=MESH_ID,
    )


def started(src, dst, sem):
    copy = pltpu.make_async_copy(src, dst, sem)
    copy.start()
    return copy


def forward_kernel(heads, groups, S, *refs):
    masters = refs[:4]
    small_own, x_ref, cos_ref, sin_ref, q_ids, k_ids = refs[4:10]
    full = refs[10:14]
    small_full, h1_ref, q_ref, k_out, v_out, o_ref, l_ref, mid_ref, h2_ref, h2_other = refs[14:24]
    h1_t, h1_t_other, o_t, o_t_other = refs[24:28]
    w_in, w_out, gains, mix, kv, bias, vt, lds, hs, hr, h2_sems = refs[28:39]
    own = refs[39:43]
    stages = refs[43:47]
    stage_sems = refs[47]
    sems = refs[48:]
    z = lax.axis_index("z")
    c = lax.axis_index("c")
    piece = x_ref.shape[0]
    reach = kv.shape[0] // piece - 1
    half = w_in.shape[-1] // 2
    D = x_ref.shape[1]
    half_ff = own[3].shape[-1] // 2
    own_rows = pl.ds(reach * piece, piece)
    kv[...] = jnp.zeros_like(kv)
    sent = []
    loads = {}

    def gain_row(i):
        return jnp.concatenate([gains[zz, i : i + 1, :] for zz in range(S)], axis=1).astype(F32)

    def start_norm(ready):
        ready(None)
        started(small_full, gains, lds.at[0]).wait()
        norm_rows(x_ref, gain_row(0), h1_ref)


    def of_weight(g):
        return sum(group[0][0] == groups[g][0][0] for group in groups[:g])

    def stage(g):
        i, r0, rn, c0 = groups[g][0][:4]
        slot = of_weight(g) % stages[i].shape[0]
        cols = pl.ds(0, masters[i].shape[-1])
        if i == 3:
            first = c0 // half_ff * 2 * half_ff + c * half_ff
            cols = pl.ds(pl.multiple_of(first, 128), half_ff)
        src = masters[i].at[:, :, pl.ds(r0, rn), cols]
        loads["stage", g] = started(src, stages[i].at[slot], stage_sems.at[g])

    for g in range(len(groups)):
        if of_weight(g) < stages[groups[g][0][0]].shape[0]:
            stage(g)

    def prepare(g):
        i, r0, rn, c0 = groups[g][0][:4]
        slot = of_weight(g) % stages[i].shape[0]
        loads.pop(("stage", g)).wait()
        cols = pl.ds(c0, half_ff) if i == 3 else pl.ds(0, own[i].shape[-1])

        @pl.loop(0, 8)
        def _(p):
            kk, h = p // 2, p % 2
            own[i][kk, h, pl.ds(r0, rn), cols] = stages[i][slot, kk, h].astype(BF)

        later = g + stages[i].shape[0]
        if later < len(groups) and groups[later][0][0] == i:
            stage(later)

    def start_project(ready):
        ready(0)
        for i in range(2):
            at = pl.ds(i * half, half)
            loads[i] = started(full[0].at[:, :, :, :, at], w_in.at[:, :, :, :, at], lds.at[1 + i])

    def project(i):
        loads.pop(i).wait()
        weight = w_in[:, :, :, :, i * half : (i + 1) * half].reshape(D, half)
        mix[...] = nn(h1_ref[...], weight)
        for j in range(half // HEAD):
            h = i * (half // HEAD) + j
            u = mix[:, j * HEAD : (j + 1) * HEAD]
            if h < heads:
                q_ref[:, h * HEAD : (h + 1) * HEAD] = turned(u, cos_ref, sin_ref).astype(BF)
            elif h == heads:
                kv[own_rows, :HEAD] = turned(u, cos_ref, sin_ref).astype(BF)
            else:
                kv[own_rows, HEAD:] = u.astype(BF)

    def halo(d, starting):
        there = kv.at[pl.ds((reach - d) * piece, piece)]
        target = {"z": jnp.minimum(z + d, S - 1)}
        copy = remote_copy(kv.at[own_rows], there, hs.at[d - 1], hr.at[d - 1], target)

        @pl.when(z + d < S)
        def _():
            if starting:
                copy.start()
            else:
                copy.wait_send()

        if not starting:

            @pl.when(z >= d)
            def _():
                remote_copy(there, there, hs.at[d - 1], hr.at[d - 1], target).wait_recv()

    def start_attention():
        for d in range(1, reach + 1):
            halo(d, False)
        k_out[...] = kv[:, :HEAD]
        v_out[...] = kv[:, HEAD:]
        vt[...] = kv[:, HEAD:].T
        fill_bias(bias, q_ids, k_ids, 0, piece, WINDOW + piece)

    def attention(first, count):
        for h in range(first, first + count):
            fwd_step(h, 0, piece, q_ids, q_ref, k_out, o_ref, l_ref, bias, vt)

    def start_output(ready):
        ready(1)
        for i in range(2):
            at = pl.ds(i * (D // 2), D // 2)
            loads[i] = started(full[1].at[:, :, :, :, at], w_out.at[:, :, :, :, at], lds.at[3 + i])

    def output():
        n = D // 2
        for i in range(2):
            loads.pop(i).wait()
            at = slice(i * n, (i + 1) * n)
            weight = w_out[:, :, :, :, at].reshape(D, n)
            mid_ref[:, at] = x_ref[:, at].astype(F32) + nn(o_ref[...], weight)

    def finish():
        norm_rows(mid_ref, gain_row(1), h2_ref)
        to_partner(h2_ref, h2_other, 0)

    def to_partner(src, dst, i):
        copy = remote_copy(src, dst, h2_sems.at[2 * i], h2_sems.at[2 * i + 1], {"c": 1 - c})
        copy.start()
        sent.append(copy.wait)

    def transpose(src, dst, there, i):
        for j in range(0, D, HEAD):
            dst[j : j + HEAD, :] = src[:, j : j + HEAD].T
        to_partner(dst, there, i)

    third = heads // 3
    plan = {
        2: lambda ready: start_norm(ready),
        5: lambda ready: start_project(ready),
        6: lambda ready: (project(0), project(1), [halo(d, True) for d in range(1, reach + 1)]),
        7: lambda ready: (start_attention(), attention(0, third), start_output(ready)),
        8: lambda ready: attention(third, third),
        9: lambda ready: attention(2 * third, third),
        10: lambda ready: output(),
        11: lambda ready: (finish(), transpose(h1_ref, h1_t, h1_t_other, 1)),
        12: lambda ready: transpose(o_ref, o_t, o_t_other, 2),
    }

    def work(t, ready):
        if t in plan:
            plan[t](ready)

    gather_kernel(
        [True, True, True, False], groups, S, own, full, sems, small_own, small_full, prepare, work
    )
    for wait in sent:
        wait()


def forward(masters, small, x, cos, sin, q_ids, k_ids, heads, S, cid):
    piece, D = x.shape
    keys = k_ids.shape[0]
    r = masters[0].shape[2]
    rf = masters[2].shape[2]
    all_in, all_out, all_gate = (masters[i].shape[-1] for i in (0, 1, 3))
    half_in, half_out, half_ff = all_in // 2, all_out // 2, all_gate // 4

    def routed(i, r0, rn, c0, cn):
        return [(i, r0, rn, c0, cn, "xy")]

    groups = [routed(0, 0, r, 0, half_in), routed(1, 0, r, 0, half_out)]
    groups += [routed(2, i, 48, 0, half_out) for i in range(0, rf, 48)]
    groups += [routed(3, i, 16, j * half_ff, half_ff) for j in range(2) for i in range(0, r, 16)]

    def body(*refs):
        forward_kernel(heads, groups, S, *refs)

    def shape(*dims, dtype=BF):
        return jax.ShapeDtypeStruct(dims, dtype)

    own = [(4, 2) + masters[i].shape[2:] for i in range(3)] + [(4, 2, r, 2 * half_ff)]
    outs = [shape(S, *o) for o in own]
    outs += [
        shape(S, *small.shape),
        shape(piece, D),
        shape(piece, heads * HEAD),
        shape(keys, HEAD),
        shape(keys, HEAD),
        shape(piece, heads * HEAD),
        shape(heads, 1, piece, dtype=F32),
        shape(piece, D, dtype=F32),
        shape(piece, D),
        shape(piece, D),
        shape(D, piece),
        shape(D, piece),
        shape(D, piece),
        shape(D, piece),
    ]
    dma = pltpu.SemaphoreType.DMA
    return pl.pallas_call(
        body,
        out_shape=tuple(outs),
        in_specs=[ANY] * 4 + [VM] * 6,
        out_specs=tuple([ANY] * 5 + [VM] * 8 + [ANY] + [VM, ANY] * 2),
        scratch_shapes=[
            pltpu.VMEM((S,) + own[0], BF),
            pltpu.VMEM((S,) + own[1], BF),
            pltpu.VMEM((S,) + small.shape, BF),
            pltpu.VMEM((piece, half_in), F32),
            pltpu.VMEM((keys, 2 * HEAD), BF),
            pltpu.VMEM((keys, piece), F32),
            pltpu.VMEM((HEAD, keys), BF),
            dma((5,)),
            dma((2,)),
            dma((2,)),
            dma((6,)),
        ]
        + [pltpu.VMEM(o, BF) for o in own]
        + [
            pltpu.VMEM((1, 4, 2, r, all_in), F32),
            pltpu.VMEM((1, 4, 2, r, all_out), F32),
            pltpu.VMEM((2, 4, 2, 48, all_out), F32),
            pltpu.VMEM((2, 4, 2, 16, half_ff), F32),
            dma((len(groups),)),
        ]
        + gather_sems(len(groups), sum(map(len, groups)), S),
        compiler_params=pltpu.CompilerParams(
            collective_id=cid, has_side_effects=True, vmem_limit_bytes=VMEM_BYTES
        ),
    )(*masters, small, x, cos, sin, q_ids, k_ids)


def back_step(h, first, rows, refs, bias, kt, finish):
    q_ref, k_ref, v_ref, o_ref, do_ref, l_ref, dq_ref, dk_ref, dv_ref = refs
    span = WINDOW + rows
    factor = HEAD**-0.5 * LOG2E
    cols = pl.ds(h * HEAD, HEAD)
    q = q_ref[pl.ds(first, rows), cols]
    do = do_ref[pl.ds(first, rows), cols]
    o = o_ref[pl.ds(first, rows), cols]
    delta = jnp.sum((do.astype(F32) * o.astype(F32)).T, axis=0, keepdims=True)
    s = nt(k_ref[pl.ds(first, span), :], q) * factor + bias[...]
    p = jnp.exp2(s - l_ref[h, :, pl.ds(first, rows)])
    dp = nt(v_ref[pl.ds(first, span), :], do)
    ds = (p * ((dp - delta) * HEAD**-0.5)).astype(BF)
    dv_ref[pl.ds(first, span), :] += nn(p.astype(BF), do)
    dk_ref[pl.ds(first, span), :] += nn(ds, q)
    dq = nn(kt[:, pl.ds(first, span)], ds).T
    dq_ref[pl.ds(first, rows), cols] = finish(dq, first).astype(dq_ref.dtype)


def bwd_kernel(heads, rows, q_ids, k_ids, *refs):
    *arrays, bias, kt = refs
    q_ref, k_ref = arrays[:2]
    dk_ref, dv_ref = arrays[-2:]
    kt[...] = k_ref[...].T
    dk_ref[...] = jnp.zeros_like(dk_ref)
    dv_ref[...] = jnp.zeros_like(dv_ref)
    for first in range(0, q_ref.shape[0], rows):
        fill_bias(bias, q_ids, k_ids, first, rows, WINDOW + rows)
        for h in range(heads):
            back_step(h, first, rows, arrays, bias, kt, lambda dq, first: dq)


def attend(q_ids, k_ids, q, k, v, heads, rows):
    def body(*refs):
        fwd_kernel(heads, rows, *refs)

    return pl.pallas_call(
        body,
        out_shape=(
            jax.ShapeDtypeStruct(q.shape, BF),
            jax.ShapeDtypeStruct((heads, 1, q.shape[0]), F32),
        ),
        in_specs=[VM] * 5,
        out_specs=(VM, VM),
        scratch_shapes=[
            pltpu.VMEM((WINDOW + rows, rows), F32),
            pltpu.VMEM((HEAD, k.shape[0]), BF),
        ],
        compiler_params=pltpu.CompilerParams(vmem_limit_bytes=VMEM_BYTES),
        cost_estimate=pl.CostEstimate(
            flops=4 * q.size * k.shape[0], bytes_accessed=4 * q.size, transcendentals=q.size * 12
        ),
    )(q_ids, k_ids, q, k, v)


def attend_back(q_ids, k_ids, q, k, v, o, do, l, heads, rows):
    def body(*refs):
        bwd_kernel(heads, rows, *refs)

    return pl.pallas_call(
        body,
        out_shape=(
            jax.ShapeDtypeStruct(q.shape, F32),
            jax.ShapeDtypeStruct(k.shape, F32),
            jax.ShapeDtypeStruct(k.shape, F32),
        ),
        in_specs=[VM] * 8,
        out_specs=(VM, VM, VM),
        scratch_shapes=[
            pltpu.VMEM((WINDOW + rows, rows), F32),
            pltpu.VMEM((HEAD, k.shape[0]), BF),
        ],
        compiler_params=pltpu.CompilerParams(vmem_limit_bytes=VMEM_BYTES),
        cost_estimate=pl.CostEstimate(
            flops=10 * q.size * k.shape[0], bytes_accessed=12 * q.size, transcendentals=q.size * 12
        ),
    )(q_ids, k_ids, q, k, v, o, do, l)


def mlp_kernel(
    where, two_own, two_other, df_own, df_other, gate_ref, up_ref, down_ref, *results
):
    two_t, hid_t, grads, back_low, back = results
    step = pl.program_id(0)
    rows, D = two_own.shape
    part = two_t.shape[0]
    core = where[0]
    block = 256

    @pl.when(step == 0)
    def _():
        back[...] = jnp.zeros_like(back)

    @pl.when(step < D // part)
    def _():
        cols = pl.ds(pl.multiple_of(step * part, part), part)
        for two_ref, owner in ((two_own, core), (two_other, 1 - core)):
            at = pl.ds(pl.multiple_of(owner * rows, rows), rows)
            two_t[:, at] = two_ref[:, cols].T

    def tokens(two_ref, df_ref, owner, first):
        here = pl.ds(first, block)
        at = pl.ds(pl.multiple_of(owner * rows + first, block), block)
        two = two_ref[here, :]
        gate = nn(two, gate_ref[...])
        up = nn(two, up_ref[...])
        grad = nt(df_ref[here, :], down_ref[...])
        slope = 0.7978845608028654
        cube = slope * 0.044715
        square = gate * gate
        upper = 0.5 + 0.5 * jnp.tanh(gate * (slope + cube * square))
        act = gate * upper
        act_slope = upper + act * (1.0 - upper) * (2.0 * slope + 6.0 * cube * square)
        hid = (act * up).astype(BF)
        grad_gate = (grad * up * act_slope).astype(BF)
        grad_up = (grad * act).astype(BF)
        hid_t[:, at] = hid.T
        grads[0, at, :] = grad_gate
        grads[1, at, :] = grad_up
        back[at, :] += nt(grad_gate, gate_ref[...]) + nt(grad_up, up_ref[...])

    for two_ref, df_ref, owner in ((two_own, df_own, core), (two_other, df_other, 1 - core)):
        for first in range(0, rows, block):
            tokens(two_ref, df_ref, owner, first)

    @pl.when(step == pl.num_programs(0) - 1)
    def _():
        back_low[...] = back[...].astype(BF)


def mlp_call(core, two, df, gate_full, down_full):
    T, D = 2 * two[0].shape[0], two[0].shape[1]
    half_ff = gate_full.shape[1] // 2
    tile = 768
    tiles = half_ff // tile
    part = max(D // tiles // 128 * 128, 256)
    last = D // part - 1

    def body(*refs):
        mlp_kernel(*refs)

    once = pl.Buffered(1)
    piece = pl.BlockSpec((T // 2, D), lambda i, w: (0, 0), pipeline_mode=once)
    return pl.pallas_call(
        body,
        grid_spec=pltpu.PrefetchScalarGridSpec(
            num_scalar_prefetch=1,
            grid=(tiles,),
            in_specs=[
                piece,
                piece,
                piece,
                piece,
                pl.BlockSpec((D, tile), lambda i, w: (0, i)),
                pl.BlockSpec((D, tile), lambda i, w: (0, tiles + i)),
                pl.BlockSpec((tile, D), lambda i, w: (w[0] * tiles + i, 0)),
            ],
            out_specs=[
                pl.BlockSpec((part, T), lambda i, w: (jnp.minimum(i, last), 0)),
                pl.BlockSpec((tile, T), lambda i, w: (i, 0)),
                pl.BlockSpec((2, T, tile), lambda i, w: (0, 0, i)),
                pl.BlockSpec((T, D), lambda i, w: (0, 0), pipeline_mode=once),
            ],
            scratch_shapes=[pltpu.VMEM((T, D), F32)],
        ),
        out_shape=[
            jax.ShapeDtypeStruct((D, T), BF),
            jax.ShapeDtypeStruct((half_ff, T), BF),
            jax.ShapeDtypeStruct((2, T, half_ff), BF),
            jax.ShapeDtypeStruct((T, D), BF),
        ],
        compiler_params=pltpu.CompilerParams(
            dimension_semantics=("arbitrary",), vmem_limit_bytes=BACKWARD_VMEM
        ),
        cost_estimate=pl.CostEstimate(
            flops=10 * T * D * half_ff, bytes_accessed=40 * 2**20, transcendentals=T * half_ff
        ),
    )(core, *two, *df, gate_full, gate_full, down_full)


def split_widths(total, most):
    first = -(-total // 256) * 128
    assert first <= most
    return (first, total - first)


def backward_kernel(heads, sides, parts, S, *refs):
    two, hid, *flats = refs[:6]
    flat_own, flat_other, norm_own, norm_other = flats[2], flats[3], flats[0], flats[1]
    grads, dy_own, dy_other, back, middle, w_out, gains_ref, x_ref, w_in, w_down = refs[6:16]
    q_ids, k_ids, q_ref, k_ref, v_ref, o_ref, l_ref, cos_ref, sin_ref = refs[16:25]
    out, hid_land, x_grad, y_out, dx_land = refs[25:30]
    left, right, out_right, mix_right, s1, g1, s2, g2, fz, gz, mine, da, do, got = refs[30:44]
    tails, landed_tails, gains, x1, dk, dv, bias, kt, mixed, w_rows, w_tiles = refs[44:55]
    lds, rds, fs, cs_in, hs, hr, s1s, s1r, s2s, s2r, zs, zr, ls, xs, xr, ys, yr, cs, cr = refs[55:]
    _, _, _, r, T = left.shape
    n = right.shape[2]
    piece, D = da.shape
    reach = tails.shape[0]
    wide = sides * parts
    rows_groups = hid.shape[1]
    chunk_out = wide + rows_groups
    mix_half = mix_right.shape[1]
    widths = [n] * (chunk_out + 1) + list(split_widths(mix_half, n))
    nc = len(widths)
    left_slots = left.shape[0]
    right_slots = right.shape[0]
    slots = g1.shape[0]
    y, x, c, z = (lax.axis_index(a) for a in ("y", "x", "c", "z"))
    k = y * 2 + x
    kx = y * 2 + 1 - x
    ky = (1 - y) * 2 + x
    kxy = 3 - k
    to_x = {"x": 1 - x}
    to_y = {"y": 1 - y}
    to_c = {"c": 1 - c}
    place = pl.ds(pl.multiple_of(c * piece, piece), piece)
    other_place = pl.ds(pl.multiple_of((1 - c) * piece, piece), piece)
    loads = {}
    pending = {}

    def fetch(key, src, dst, sem):
        loads.setdefault(key, []).append(started(src, dst, sem))

    def landed(key):
        for copy in loads.pop(key, []):
            copy.wait()

    def launch(key, copy):
        copy.start()
        pending.setdefault(key, []).append(copy)

    def drain(key):
        for copy in pending.pop(key, []):
            copy.wait_send()

    groups = 3 + rows_groups

    def group_of(t):
        if t < wide:
            return 0
        return min(t - wide + 1, groups - 1)

    def fetch_left(g):
        slot = g % left_slots
        for p in range(8):
            h, kk = p // 4, p % 4
            if g == 0:
                fetch(("l", g), two.at[:, kk, h], left.at[slot, p], lds.at[g, p, 0])
                continue
            if g <= rows_groups:
                if g == 1 and p == 0:
                    landed_hid.wait_recv()
                half = left.shape[2] // 2
                pairs = [
                    (hid.at[:, g - 1, kk, h], left.at[slot, p, pl.ds(c * half, half)]),
                    (hid_land.at[:, g - 1, kk, h], left.at[slot, p, pl.ds((1 - c) * half, half)]),
                ]
            else:
                own, other = (flat_own, flat_other) if g == groups - 2 else (norm_own, norm_other)
                pairs = [
                    (own.at[:, kk, h], left.at[slot, p, :, :, place]),
                    (other.at[:, kk, h], left.at[slot, p, :, :, other_place]),
                ]
            for i, (src, dst) in enumerate(pairs):
                fetch(("l", g), src, dst, lds.at[g, p, i])

    def fetch_right(t):
        slot = t % right_slots
        if t < wide:
            src = grads.at[t // parts, :, pl.ds((t % parts) * n, n)]
            fetch(("r", t), src, right.at[slot], rds.at[t, 0])
        elif t == wide:
            keep = pl.ds(pl.multiple_of(c * n, n), n)
            fetch(("r", t), dy_own.at[:, keep], right.at[slot, place], rds.at[t, 0])
            fetch(("r", t), dy_other.at[:, keep], right.at[slot, other_place], rds.at[t, 1])

    fetch_right(0)
    fetch_left(0)
    fetch_right(1)
    landed_tails[...] = jnp.zeros_like(landed_tails)
    barrier = pltpu.get_barrier_semaphore()
    peers = [to_x, to_y, to_c] + [{"z": lax.rem(z + e, S)} for e in range(1, S)]
    for target in peers:
        pl.semaphore_signal(barrier, inc=1, device_id=target, device_id_type=MESH_ID)
    pl.semaphore_wait(barrier, len(peers))
    launch("end", remote_copy(back.at[other_place], got, cs_in.at[0], cs_in.at[1], to_c))
    launch("end", remote_copy(hid, hid_land, cs_in.at[2], cs_in.at[3], to_c))
    landed_hid = remote_copy(hid, hid_land, cs_in.at[2], cs_in.at[3], to_c)
    landed_back = remote_copy(got, got, cs_in.at[0], cs_in.at[1], to_c)

    def product(t, p):
        lhs = left[group_of(t) % left_slots, p].reshape(S * r, T)
        if t <= chunk_out - 1:
            return nn(lhs, right[min(t, wide) % right_slots])
        if t == chunk_out:
            return nn(lhs, out_right[...])
        first = sum(widths[chunk_out + 1 : t])
        return nn(lhs, mix_right[:, first : first + widths[t]])

    def cut(ref, t):
        return ref if widths[t] == n else ref.at[:, pl.ds(0, widths[t])]

    def first(t):
        slot = t % 2
        landed(("l", group_of(t)))
        landed(("r", t))
        drain(("s1", t - 2))
        for i in range(2):
            for j, p, target in ((i, i * 2 + 1 - x, to_x), (2 + i, 4 + (1 - y) * 2 + i, to_y)):
                src, dst = cut(s1.at[slot, j], t), cut(g1.at[t % slots, j], t)
                src[...] = product(t, p).astype(BF)
                launch(("s1", t), remote_copy(src, dst, s1s.at[t, j], s1r.at[t, j], target))

    def second(t):
        slot = t % 2
        drain(("s2", t - 2))
        for j in range(4):
            dst = cut(g1.at[t % slots, j], t)
            remote_copy(dst, dst, s1s.at[t, j], s1r.at[t, j], to_x).wait_recv()
        for h, p, j, target in ((0, (1 - y) * 2 + x, 1 - y, to_y), (1, 4 + y * 2 + 1 - x, 3 - x, to_x)):
            src, dst = cut(s2.at[slot, h], t), cut(g2.at[t % slots, h], t)
            came = cut(g1.at[t % slots, j], t)
            src[...] = (product(t, p) + came[...].astype(F32)).astype(BF)
            launch(("s2", t), remote_copy(src, dst, s2s.at[t, h], s2r.at[t, h], target))

    def third(t):
        slot = t % 2
        w = widths[t]
        drain(("z", t - 2))
        for h, p, j in ((0, k, y), (1, 4 + k, 2 + x)):
            dst = cut(g2.at[t % slots, h], t)
            remote_copy(dst, dst, s2s.at[t, h], s2r.at[t, h], to_x).wait_recv()
            came = cut(g1.at[t % slots, j], t)
            total = (product(t, p) + came[...].astype(F32) + dst[...].astype(F32)).astype(BF)
            for zz in range(S):
                fz[slot, zz, h, :, :w] = total[zz * r : (zz + 1) * r]
        for e in range(1, S):
            src = fz.at[slot, lax.rem(z + e, S), :, :, pl.ds(0, w)]
            dst = gz.at[t, S - e - 1, :, :, pl.ds(0, w)]
            target = {"z": lax.rem(z + e, S)}
            launch(("z", t), remote_copy(src, dst, zs.at[t, e - 1], zr.at[t, S - e - 1], target))

    def fourth(t):
        slot = t % 2
        w = widths[t]
        drain(("ag", t - 2))
        landed(("o", t - 2))
        for e in range(S - 1):
            dst = gz.at[t, e, :, :, pl.ds(0, w)]
            remote_copy(dst, dst, zs.at[t, e], zr.at[t, e], to_x).wait_recv()
        for h in range(2):
            total = fz[slot, z, h, :, :w].astype(F32)
            for e in range(S - 1):
                total = total + gz[t, e, h, :, :w].astype(F32)
            mine[slot, h, :, :w] = total.astype(BF)
        cols = pl.ds(0, w)
        fetch(("o", t), mine.at[slot, :, :, cols], out.at[t, k, c, :, :, cols], ls.at[t])
        for i, hs_ in enumerate(((0, 1), (1, 0))):
            for h, s, r_, target in ((hs_[0], xs, xr, to_x), (hs_[1], ys, yr, to_y)):
                src, dst = mine.at[slot, h, :, cols], out.at[t, k, c, h, :, cols]
                launch(("ag", t), remote_copy(src, dst, s.at[t, i], r_.at[t, i], target))

    def land(t, kk, h, s, r_, j, target):
        p = out.at[t, kk, c, h, :, pl.ds(0, widths[t])]
        remote_copy(p, p, s.at[t, j], r_.at[t, j], target).wait_recv()
        return p

    def fifth(t):
        p = land(t, kx, 0, xs, xr, 0, to_x)
        launch("end", remote_copy(p, p, ys.at[t, 2], yr.at[t, 2], to_y))
        p = land(t, ky, 1, ys, yr, 0, to_y)
        launch("end", remote_copy(p, p, xs.at[t, 2], xr.at[t, 2], to_x))

    def sixth(t):
        land(t, kx, 1, xs, xr, 1, to_x)
        land(t, ky, 0, ys, yr, 1, to_y)
        land(t, kxy, 1, xs, xr, 2, to_x)
        land(t, kxy, 0, ys, yr, 2, to_y)
        landed(("o", t))
        p = out.at[t, :, c, :, :, pl.ds(0, widths[t])]
        launch("end", remote_copy(p, p, cs.at[t], cr.at[t], to_c))


    def norm_back():
        for key in ("near", "x1", "dy", "gains"):
            landed(key)
        landed_back.wait_recv()
        gain = jnp.concatenate([gains[zz, 1:2, :] for zz in range(S)], axis=1).astype(F32)
        step = 64

        @pl.loop(0, piece // step)
        def _(i):
            at = pl.ds(pl.multiple_of(i * step, step), step)
            u = x1[at, :]
            scale = lax.rsqrt(jnp.mean(u * u, axis=1, keepdims=True) + norm_eps)
            hat = u * scale
            e = (do[at, :].astype(F32) + got[at, :].astype(F32)) * gain
            inner = jnp.mean(e * hat, axis=1, keepdims=True)
            dx = mixed[at, :D].astype(F32) + scale * (e - hat * inner)
            x1[at, :] = dx
            da[at, :] = dx.astype(BF)

        fetch("dx", x1, dx_land, fs.at[11])
        launch("da", remote_copy(give_of(da, n), out_right.at[place], cs_in.at[4], cs_in.at[5], to_c))
        out_right[place, :] = keep_of(da, n)[...]
        for i in range(2):
            fetch("w", w_out.at[pl.ds(T, piece), pl.ds(i * n, n)], got.at[:, pl.ds(i * n, n)], fs.at[7 + i])

    def give_of(ref, width):
        return ref.at[:, pl.ds(pl.multiple_of((1 - c) * width, width), width)]

    def keep_of(ref, width):
        return ref.at[:, pl.ds(pl.multiple_of(c * width, width), width)]

    def heads_back():
        landed("w")
        live = k_ids[pl.ds(reach * piece, piece), :1] != 0
        for j in range(0, D, piece):
            if j < T:
                low, high = right[2, j : j + piece, :], right[3, j : j + piece, :]
            else:
                low, high = got[:, :n], got[:, n:]
            part = nt(da[:, :n], low) + nt(da[:, n:], high)
            do[:, j : j + piece] = jnp.where(live, part, 0.0).astype(BF)

    half_rows = piece // 2
    steps = [(block, h) for block in range(2) for h in range(heads)]

    def turn_back(dq, first):
        at = pl.ds(first, half_rows)
        return dq * cos_ref[at, :] - pltpu.roll(dq, HEAD // 2, 1) * sin_ref[at, :]

    def attention(first_step, count):
        arrays = (q_ref, k_ref, v_ref, o_ref, do, l_ref, mixed, dk, dv)
        if first_step == 0:
            kt[...] = k_ref[...].T
            dk[...] = jnp.zeros_like(dk)
            dv[...] = jnp.zeros_like(dv)
        for block, h in steps[first_step : first_step + count]:
            if h == 0:
                fill_bias(bias, q_ids, k_ids, block * half_rows, half_rows, WINDOW + half_rows)
            back_step(h, block * half_rows, half_rows, arrays, bias, kt, turn_back)

    def tail(d):
        target = {"z": jnp.maximum(z - d, 0)}
        return remote_copy(tails.at[d - 1], landed_tails.at[d - 1], hs.at[d - 1], hr.at[d - 1], target)

    def send_tails():
        for d in range(1, reach + 1):
            at = pl.ds((reach - d) * piece, piece)
            tails[d - 1, :, :HEAD] = dk[at, :].astype(BF)
            tails[d - 1, :, HEAD:] = dv[at, :].astype(BF)

            @pl.when(z >= d)
            def _(d=d):
                tail(d).start()

    def mix_back():
        for d in range(1, reach + 1):

            @pl.when(z >= d)
            def _(d=d):
                tail(d).wait_send()

            @pl.when(z + d < S)
            def _(d=d):
                tail(d).wait_recv()

        at = pl.ds(reach * piece, piece)
        keys, values = dk[at, :], dv[at, :]
        for d in range(1, reach + 1):
            keys = keys + landed_tails[d - 1, :, :HEAD].astype(F32)
            values = values + landed_tails[d - 1, :, HEAD:].astype(F32)
        keys = keys * cos_ref[...] - pltpu.roll(keys, HEAD // 2, 1) * sin_ref[...]
        width = heads * HEAD
        mixed[:, width : width + HEAD] = keys.astype(BF)
        mixed[:, width + HEAD :] = values.astype(BF)
        launch("end", remote_copy(give_of(mixed, mix_half), mix_right.at[place], cs_in.at[6], cs_in.at[7], to_c))
        mix_right[place, :] = keep_of(mixed, mix_half)[...]

    step_rows = w_rows.shape[1]

    def fetch_rows(j):
        if j * step_rows < D:
            fetch(("q", j), w_in.at[pl.ds(j * step_rows, step_rows)], w_rows.at[j % 2], fs.at[9 + j % 2])

    def start_input():
        drain("da")
        fetch_rows(0)
        fetch_rows(1)
        fetch("x0", x_ref, got, fs.at[4])

    def project_back(j):
        landed(("q", j))
        da[:, j * step_rows : (j + 1) * step_rows] = nt(mixed[...], w_rows[j % 2]).astype(BF)
        fetch_rows(j + 2)

    def input_back():
        landed("x0")
        landed("dx")
        gain = jnp.concatenate([gains[zz, 0:1, :] for zz in range(S)], axis=1).astype(F32)
        step = 64

        @pl.loop(0, piece // step)
        def _(i):
            at = pl.ds(pl.multiple_of(i * step, step), step)
            u = got[at, :].astype(F32)
            scale = lax.rsqrt(jnp.mean(u * u, axis=1, keepdims=True) + norm_eps)
            hat = u * scale
            e = da[at, :].astype(F32) * gain
            inner = jnp.mean(e * hat, axis=1, keepdims=True)
            do[at, :] = (x1[at, :] + scale * (e - hat * inner)).astype(BF)

        fetch("x_grad", do, x_grad, fs.at[0])

    spread = {6: ((1, 0, 3),), 7: ((1, 3, 6), (2, 0, 3)), 8: ((1, 6, 8), (2, 3, 6), (3, 0, 3))}
    spread.update({9: ((2, 6, 8), (3, 3, 6)), 10: ((3, 6, 8),)})
    out_steps = [(g, p) for t in sorted(spread) for g, a, b in spread[t] for p in range(a, b)]
    out_count = {t: sum(b - a for _, a, b in spread[t]) for t in spread}
    assert rows_groups == 3 and wide == 6

    def fetch_tile(i):
        if i < len(out_steps):
            g, p = out_steps[i]
            fetch(("d", i), w_down.at[:, g - 1, p % 4, p // 4], w_tiles.at[i % 2], fs.at[12 + i % 2])

    def output_step(i):
        g, p = out_steps[i]
        landed(("d", i))
        fetch_tile(i + 1)
        lhs = left[g % left_slots, p, :, :, place].reshape(S * r, piece)
        for j in range(0, D, piece):
            rhs = w_tiles[i % 2, :, :, j : j + piece].reshape(S * r, piece)
            x1[:, j : j + piece] += lax.dot_general(
                lhs, rhs, (((0,), (0,)), ((), ())), preferred_element_type=F32
            )

    def output_work(t):
        if t == 2:
            landed("dx")
            fetch("x1", middle, x1, fs.at[1])
        if t == 5:
            landed("x1")
            fetch_tile(0)
        if t in out_count:
            done = sum(out_count[u] for u in out_count if u < t)
            for i in range(done, done + out_count[t]):
                output_step(i)
        if t == 11:
            do[...] = x1[...].astype(BF)
            fetch("y", do, y_out, fs.at[2])
        if t == 13:
            landed("y")
            fetch("dx", dx_land, x1, fs.at[11])

    def came(ref, i):
        ref = ref.at[other_place]
        remote_copy(ref, ref, cs_in.at[i], cs_in.at[i + 1], to_c).wait_recv()

    stages = (first, second, third, fourth, fifth, sixth)

    fetch("near", back.at[place], do, fs.at[0])
    fetch("x1", middle, x1, fs.at[1])
    fetch("dy", dy_own, mixed.at[:, pl.ds(0, D)], fs.at[2])
    fetch("gains", gains_ref, gains, fs.at[3])
    for i in range(2):
        fetch("w", w_out.at[pl.ds(0, T), pl.ds(i * n, n)], right.at[2 + i], fs.at[5 + i])
    each = 5

    def work(t):
        if t == 0:
            norm_back()
        if t == 1:
            heads_back()
        if t >= 2 and (t - 2) * each < len(steps):
            attention((t - 2) * each, each)
        if t == 7:
            send_tails()
        if t == 8:
            mix_back()
            start_input()
        if t >= 9 and (t - 9) * step_rows < D:
            project_back(t - 9)
        output_work(t)
        if t == 15:
            input_back()

    for t in range(nc + len(stages) - 1):
        for lag, stage in enumerate(stages):
            if lag == 0 and t == chunk_out:
                came(out_right, 4)
            if lag == 0 and t == chunk_out + 1:
                came(mix_right, 6)
            if 0 <= t - lag < nc:
                stage(t - lag)
            if lag == 0:
                work(t)
        if t == 1:
            fetch_right(2)
        if t >= 1:
            fetch_right(t + 2)
        for g in range(1, groups):
            if t == wide + g - (3 if g < left_slots else 2):
                fetch_left(g)
    for t in range(nc):
        p = out.at[t, :, 1 - c, :, :, pl.ds(0, widths[t])]
        remote_copy(p, p, cs.at[t], cr.at[t], to_c).wait_recv()
    for key in list(pending):
        drain(key)
    for key in list(loads):
        landed(key)


def backward(
    two_t, hid_t, transposed, grads, dy, back, middle, w_out, gains, x, w_in, w_down, attention, tables, heads, S, cid
):
    D, T = two_t.shape
    sides, _, half_ff = grads.shape
    piece = middle.shape[0]
    n = D // 2
    r = D // (S * 8)
    parts = half_ff // n
    rows_groups = 2 * half_ff // (S * 8 * r)
    mixed = attention[2].shape[1] + 2 * HEAD
    nc = sides * parts + rows_groups + 3
    m = S * r
    slots = 5
    keys = attention[3].shape[0]
    reach = keys // piece - 1
    dma = pltpu.SemaphoreType.DMA
    hid_shape = (S // 2, rows_groups, 4, 2, r, T)

    def body(*refs):
        backward_kernel(heads, sides, parts, S, *refs)

    def vmem(*shape):
        return pltpu.VMEM(shape, BF)

    results = pl.pallas_call(
        body,
        out_shape=(
            jax.ShapeDtypeStruct((nc, 4, 2, 2, r, n), BF),
            jax.ShapeDtypeStruct(hid_shape, BF),
            jax.ShapeDtypeStruct((piece, D), BF),
            jax.ShapeDtypeStruct((piece, D), BF),
            jax.ShapeDtypeStruct((piece, D), F32),
        ),
        in_specs=[ANY] * 16 + [VM] * 9,
        out_specs=(ANY,) * 5,
        scratch_shapes=[
            vmem(3, 8, S, r, T),
            vmem(4, T, n),
            vmem(T, n),
            vmem(T, mixed // 2),
            vmem(2, 4, m, n),
            vmem(slots, 4, m, n),
            vmem(2, 2, m, n),
            vmem(slots, 2, m, n),
            vmem(2, S, 2, r, n),
            vmem(nc, S - 1, 2, r, n),
            vmem(2, 2, r, n),
            vmem(piece, D),
            vmem(piece, D),
            vmem(piece, D),
            vmem(reach, piece, 2 * HEAD),
            vmem(reach, piece, 2 * HEAD),
            vmem(*gains.shape),
            pltpu.VMEM((piece, D), F32),
            pltpu.VMEM((keys, HEAD), F32),
            pltpu.VMEM((keys, HEAD), F32),
            pltpu.VMEM((WINDOW + piece // 2, piece // 2), F32),
            pltpu.VMEM((HEAD, keys), BF),
            vmem(piece, mixed),
            vmem(2, 256, mixed),
            vmem(2, S, r, D),
            dma((rows_groups + 3, 8, 2)),
            dma((nc, 2)),
            dma((14,)),
            dma((8,)),
            dma((reach,)),
            dma((reach,)),
            dma((nc, 4)),
            dma((nc, 4)),
            dma((nc, 2)),
            dma((nc, 2)),
            dma((nc, S)),
            dma((nc, S)),
            dma((nc,)),
            dma((nc, 3)),
            dma((nc, 3)),
            dma((nc, 3)),
            dma((nc, 3)),
            dma((nc,)),
            dma((nc,)),
        ],
        compiler_params=pltpu.CompilerParams(
            collective_id=cid, has_side_effects=True, vmem_limit_bytes=BACKWARD_VMEM
        ),
    )(
        two_t.reshape(S, 4, 2, r, T),
        hid_t.reshape(hid_shape),
        *[v.reshape(S, 4, 2, r, piece) for v in transposed],
        grads,
        *dy,
        back,
        middle,
        w_out,
        gains,
        x,
        w_in,
        w_down.reshape(S, rows_groups, 4, 2, r, D),
        *attention,
        *tables,
    )
    return results[0], results[2], results[3]


def adam_kernel(total, widths, gains, count_ref, rates_ref, g_ref, w_ref, m_ref, g_out, w_out, m_out, *more):
    step_value = count_ref[0].astype(F32)
    log_first = jnp.log(jnp.full((8, 128), beta_first, F32))
    log_second = jnp.log(jnp.full((8, 128), beta_second, F32))
    unfix_first = (1.0 / (1.0 - jnp.exp(step_value * log_first)))[:1, :1]
    unfix_second = (1.0 / (1.0 - jnp.exp(step_value * log_second)))[:1, :1]
    rate, decay = rates_ref[0], rates_ref[1]
    rows = w_ref.shape[0]

    if gains:

        @pl.when((pl.program_id(1) == 0) & (pl.program_id(2) == 0))
        def _():
            more[0][...] = jnp.zeros_like(more[0])

    for i, n in enumerate(widths):
        at = pl.ds(sum(widths[:i]), n)
        grad = g_ref[i, :, 0, :, :, :n].reshape(rows, n).astype(F32) * (1.0 / total)
        w = w_ref[:, at]
        first = beta_first * m_ref[0, :, at] + (1.0 - beta_first) * grad
        second = beta_second * m_ref[1, :, at] + (1.0 - beta_second) * grad * grad
        step = first * unfix_first / (jnp.sqrt(second * unfix_second) + adam_eps) + decay * w
        g_out[:, at] = grad
        w_out[:, at] = w - rate * step
        m_out[0, :, at] = first
        m_out[1, :, at] = second
        if gains:
            both = w.astype(BF).astype(F32) * grad
            for j in range(0, n, 128):
                more[0][...] += both[:, j : j + 128]


def adam_call(
    weight, moments, grads, count, rates, total, base, widths, sides=1, tiles=1, gains=False, chips=4
):
    _, _, _, _, r, n = grads.shape
    wide = len(widths)

    def g_place(kk, cc, ss, tt):
        return (base // wide + ss + tt, kk, cc, 0, 0, 0)

    def place(kk, cc, ss, tt):
        return (tt * (4 // chips) + kk, ss * 2 + cc)

    def m_place(*at):
        return (0,) + place(*at)

    rows = chips * 2 * r
    w_spec = pl.BlockSpec((rows, sum(widths)), place)
    m_spec = pl.BlockSpec((2, rows, sum(widths)), m_place)
    smem = pl.BlockSpec(memory_space=pltpu.SMEM)
    like = jax.ShapeDtypeStruct(weight.shape, F32)
    out_specs = [w_spec, w_spec, m_spec]
    out_shape = [like, like, jax.ShapeDtypeStruct(moments.shape, F32)]
    if gains:
        out_specs.append(pl.BlockSpec((rows, 128), lambda kk, cc, ss, tt: (kk, 0)))
        out_shape.append(jax.ShapeDtypeStruct((weight.shape[0], 128), F32))

    def body(*refs):
        adam_kernel(total, widths, gains, *refs)

    return pl.pallas_call(
        body,
        grid=(4 // chips, 2, sides, tiles),
        in_specs=[smem, smem, pl.BlockSpec((wide, chips, 1, 2, r, n), g_place), w_spec, m_spec],
        out_specs=out_specs,
        out_shape=out_shape,
        compiler_params=pltpu.CompilerParams(
            dimension_semantics=("arbitrary",) * 4, vmem_limit_bytes=VMEM_BYTES
        ),
        cost_estimate=pl.CostEstimate(
            flops=20 * weight.size,
            bytes_accessed=30 * weight.size,
            transcendentals=weight.size,
        ),
    )(count, rates, grads, weight, moments)


def dot(a, b):
    return jnp.dot(a, b, preferred_element_type=F32)


def dot_rows(a, b):
    return lax.dot_general(a, b, (((1,), (0,)), ((), ())), preferred_element_type=F32)


def dot_t(a, b):
    return lax.dot_general(a, b, (((1,), (1,)), ((), ())), preferred_element_type=F32)


def on_device(
    Y,
    S,
    block_in,
    cotangent,
    segment_ids,
    input_proj,
    output_proj,
    gate_up,
    down_weight,
    norm_gains,
    input_moments,
    output_moments,
    gate_moments,
    down_moments,
    gain_moments,
    update_count,
    optimizer_rates,
):
    seq_place = lax.axis_index("z")
    core = lax.axis_index("c")
    first_core = core == 0
    D = block_in.shape[-1]
    half_ff = FF // 2
    rows_d = input_proj.shape[0]
    rows_f = down_weight.shape[0]
    fast = Y == 2 and rows_d % 128 == 0
    in_half = input_proj.shape[1] // 2
    d_half = D // 2
    r = rows_d // 8

    gains_low = norm_gains.astype(BF)
    tokens = block_in[0].astype(F32)
    piece_len = tokens.shape[0]
    width_q = HEADS * HEAD
    positions = seq_place * piece_len + jnp.arange(piece_len, dtype=jnp.int32)
    reach_count = (WINDOW + piece_len - 2) // piece_len
    key_span = reach_count * piece_len
    segments = segment_ids[0]
    padded_ids = jnp.concatenate([jnp.full((key_span,), -1, jnp.int32), segments])
    query_ids = lax.dynamic_slice_in_dim(segments, seq_place * piece_len, piece_len)
    key_ids = lax.dynamic_slice_in_dim(padded_ids, seq_place * piece_len, key_span + piece_len)
    live_rows = query_ids != 0
    query_row = query_ids[None, :]
    key_column = key_ids[:, None]

    if fast:
        frequency = 10000.0 ** (-2.0 * jnp.arange(HEAD // 2).astype(F32) / HEAD)
        angles = positions.astype(F32)[:, None] * jnp.concatenate([frequency, frequency])[None, :]
        side = jnp.where(jnp.arange(HEAD) < HEAD // 2, -1.0, 1.0)
        cos_table, sin_table = jnp.cos(angles), jnp.sin(angles) * side
        (
            in_full,
            out_full,
            down_full,
            gate_full,
            gains_full,
            normed,
            queries,
            key_rows,
            values,
            flat_heads,
            log_totals,
            middle,
            normed_two,
            two_other,
            *transposed,
        ) = forward(
            [
                w.reshape(4, 2, w.shape[0] // 8, w.shape[1])
                for w in (input_proj, output_proj, down_weight, gate_up)
            ],
            jnp.concatenate([gains_low] * 8, axis=0),
            block_in[0],
            cos_table,
            sin_table,
            query_row,
            key_column,
            HEADS,
            S,
            0,
        )
        in_full = in_full.reshape(D, 2 * in_half)
        out_full = out_full.reshape(D, D)
        gains_small = gains_full
        gains_full = gains_full[:, :2].transpose(1, 0, 2).reshape(2, D)
        down_full = down_full.reshape(FF, D)
        gate_full = gate_full.reshape(D, 2 * half_ff)
        gains_wide = gains_full.astype(F32)
    else:
        gate_low = jnp.concatenate(
            [
                lax.dynamic_slice_in_dim(gate_up, side * FF + core * half_ff, half_ff, 1)
                for side in range(2)
            ],
            axis=1,
        )
        in_full, out_full, down_full, gate_full = (
            lax.all_gather(w.astype(BF), "z", axis=0, tiled=True)
            for w in (input_proj, output_proj, down_weight, gate_low)
        )
        gains_full = lax.all_gather(gains_low, "z", axis=1, tiled=True)
        gains_wide = gains_full.astype(F32)
        normed = root_norm(tokens, gains_wide[0]).astype(BF)
        mixed_proj = dot(normed, in_full)
        queries = (
            rotate(mixed_proj[:, :width_q].reshape(piece_len, HEADS, HEAD), positions, 1.0)
            .astype(BF)
            .reshape(piece_len, width_q)
        )
        own_keys = rotate(mixed_proj[:, width_q : width_q + HEAD], positions, 1.0)
        own_pair = jnp.concatenate([own_keys, mixed_proj[:, width_q + HEAD :]], axis=1).astype(BF)
        earlier = []
        for back_step in range(reach_count, 0, -1):
            earlier.append(passed_along(own_pair, "z", back_step))
        key_pairs = jnp.concatenate(earlier + [own_pair], axis=0)
        key_rows = key_pairs[:, :HEAD]
        values = key_pairs[:, HEAD:]
        flat_heads, log_totals = attend(
            query_row, key_column, queries, key_rows, values, HEADS, piece_len
        )
        middle = tokens + dot(flat_heads, out_full)
        normed_two = root_norm(middle, gains_wide[1]).astype(BF)
        two_other = swapped(normed_two, "c")

    upstream = cotangent[0].astype(F32)

    def ordered(mine, other):
        return jnp.concatenate(
            [jnp.where(first_core, mine, other), jnp.where(first_core, other, mine)], axis=0
        )

    def pair(v):
        return ordered(v, swapped(v, "c"))

    def half_pair(v):
        n = v.shape[1] // 2
        keep = lax.dynamic_slice_in_dim(v, core * n, n, 1)
        give = lax.dynamic_slice_in_dim(v, (1 - core) * n, n, 1)
        return ordered(keep, swapped(give, "c"))

    def core_sum(v):
        keep = lax.dynamic_slice_in_dim(v, core * piece_len, piece_len, 0)
        give = lax.dynamic_slice_in_dim(v, (1 - core) * piece_len, piece_len, 0)
        return keep.astype(F32) + swapped(give, "c").astype(F32)

    df_other = swapped(cotangent[0], "c")
    two_t, hid_t, grad_gated, two_sum = mlp_call(
        core.reshape(1).astype(jnp.int32),
        (normed_two, two_other),
        (cotangent[0], df_other),
        gate_full,
        down_full,
    )
    token_total = piece_len * S * Y * 4 * block_in.shape[0]
    step_value = update_count[0].astype(F32)
    rates = optimizer_rates

    if fast:
        sums, block_in_grad, block_out = backward(
            two_t,
            hid_t,
            transposed,
            grad_gated,
            (cotangent[0], df_other),
            two_sum,
            middle,
            out_full,
            gains_small,
            block_in[0],
            in_full,
            down_full,
            (query_row, key_column, queries, key_rows, values, flat_heads, log_totals),
            (cos_table, sin_table),
            HEADS,
            S,
            2,
        )
    else:
        down_mine = lax.dynamic_slice_in_dim(down_full, core * half_ff, half_ff, 0)
        block_out = (middle + core_sum(dot(hid_t.T, down_mine).astype(BF))).astype(BF)
        grad_normed_two = core_sum(two_sum)
        _, norm_pull_two = jax.vjp(root_norm, middle, gains_wide[1])
        grad_middle_norm, grad_gain_two = norm_pull_two(grad_normed_two)
        grad_middle = upstream + grad_middle_norm
        grad_branch = grad_middle.astype(BF)
        grad_flat = dot_t(grad_branch, out_full)
        grad_attended = jnp.where(live_rows[:, None], grad_flat, 0.0).astype(BF)
        grad_query_all, grad_keys, grad_values = attend_back(
            query_row,
            key_column,
            queries,
            key_rows,
            values,
            flat_heads,
            grad_attended,
            log_totals,
            HEADS,
            piece_len // 2,
        )
        grad_pairs = jnp.concatenate([grad_keys, grad_values], axis=1)
        own_grad = grad_pairs[key_span:]
        for back_step in range(1, reach_count + 1):
            sent_rows = grad_pairs[
                key_span - back_step * piece_len : key_span - (back_step - 1) * piece_len
            ]
            own_grad = own_grad + passed_along(sent_rows, "z", -back_step)
        grad_query_raw = rotate(
            grad_query_all.reshape(piece_len, HEADS, HEAD), positions, -1.0
        ).reshape(piece_len, width_q)
        grad_key_raw = rotate(own_grad[:, :HEAD], positions, -1.0)
        grad_mixed = jnp.concatenate(
            [grad_query_raw, grad_key_raw, own_grad[:, HEAD:]], axis=1
        ).astype(BF)
        grad_normed = dot_t(grad_mixed, in_full)
        _, norm_pull_one = jax.vjp(root_norm, tokens, gains_wide[0])
        grad_tokens_norm, grad_gain_one = norm_pull_one(grad_normed)
        block_in_grad = (grad_middle + grad_tokens_norm).astype(BF)

    if fast:

        def adam(weight, moments, *rest, **more):
            return adam_call(
                weight, moments, sums, update_count, rates, float(token_total), *rest, **more
            )

        tiles = half_ff // d_half
        same = (d_half,) * tiles
        gate_grad, gate_new, gate_mom, gain_two = adam(
            gate_up, gate_moments, 0, same, sides=2, gains=True, chips=2
        )
        down_grad, down_new, down_mom = adam(
            down_weight, down_moments, 2 * tiles, (d_half,), tiles=tiles
        )
        out_grad, out_new, out_mom = adam(output_proj, output_moments, 3 * tiles, (d_half,))
        in_grad, in_new, in_mom, gain_one = adam(
            input_proj, input_moments, 3 * tiles + 1, split_widths(in_half, d_half), gains=True
        )
        gain_grad = jnp.stack(
            [jnp.sum(v, axis=1) for v in (gain_one, gain_two)]
        ) / gains_low.astype(F32)
    else:

        def adam(weight, moments, grad):
            grad = grad.astype(F32) / token_total
            change, new = adamw_step(weight, moments, grad, step_value, rates)
            return grad, weight - change, new

        def summed(left, right):
            whole = dot_rows(left.T, right).astype(BF)
            mine = lax.psum_scatter(whole, "z", scatter_dimension=0, tiled=True)
            return lax.psum(mine, ("y", "x"))

        two_both = ordered(normed_two, two_other)
        grad_half = half_pair(grad_branch)
        mixed_half = half_pair(grad_mixed)
        normed_both = pair(normed)
        flat_both = pair(flat_heads)
        df_both = pair(cotangent[0])
        gate_half = [summed(two_both, grad_gated[side]) for side in range(2)]
        gate_sum = jnp.concatenate(
            [lax.all_gather(g, "c", axis=1, tiled=True) for g in gate_half], axis=1
        )
        down_part = lax.psum(dot_rows(hid_t, df_both).astype(BF), ("y", "x"))
        down_part = lax.all_gather(down_part, "c", axis=0, tiled=True)
        down_sum = lax.psum_scatter(down_part, "z", scatter_dimension=0, tiled=True)
        out_total = lax.all_gather(summed(flat_both, grad_half), "c", axis=1, tiled=True)
        in_total = lax.all_gather(summed(normed_both, mixed_half), "c", axis=1, tiled=True)
        out_grad, out_new, out_mom = adam(output_proj, output_moments, out_total)
        in_grad, in_new, in_mom = adam(input_proj, input_moments, in_total)
        gate_grad, gate_new, gate_mom = adam(gate_up, gate_moments, gate_sum)
        down_grad, down_new, down_mom = adam(down_weight, down_moments, down_sum)
        gains_sum = lax.psum(jnp.stack([grad_gain_one, grad_gain_two]), ("y", "x", "c", "z"))
        gain_grad = lax.dynamic_slice_in_dim(gains_sum, seq_place * rows_d, rows_d, 1) / token_total
    gains_step, gain_moments_new = adamw_step(norm_gains, gain_moments, gain_grad, step_value, rates)
    return (
        block_out[None],
        block_in_grad[None],
        in_grad,
        out_grad,
        gate_grad,
        down_grad,
        gain_grad,
        in_new,
        out_new,
        gate_new,
        down_new,
        gains_step,
        in_mom,
        out_mom,
        gate_mom,
        down_mom,
        gain_moments_new,
    )


def solution(mesh):
    dp, S = mesh.shape["dp"], mesh.shape["seq"]
    Y = dp // 4
    grid = Mesh(mesh.devices.reshape(Y, 2, 2, S), ("y", "x", "c", "z"))
    data = ("y", "x", "c")
    tokens = P(data, "z", None)
    rows = P("z", None)
    moments = P(None, "z", None)
    in_specs = (
        (tokens, tokens, P(data, None))
        + (rows,) * 4
        + (P(None, "z"),)
        + (moments,) * 4
        + (P(None, None, "z"), P(), P())
    )
    out_specs = (
        (tokens, tokens)
        + (rows,) * 4
        + (P(None, "z"),)
        + (rows,) * 4
        + (P(None, "z"),)
        + (moments,) * 4
        + (P(None, None, "z"),)
    )

    def device_step(*arrays):
        return on_device(Y, S, *arrays)

    return jax.shard_map(
        device_step, mesh=grid, in_specs=in_specs, out_specs=out_specs, check_vma=False
    )
```

```python
import jax
import jax.numpy as jnp
from jax import lax
from jax.experimental import pallas as pl
from jax.experimental.pallas import tpu as pltpu
from jax.sharding import Mesh
from jax.sharding import PartitionSpec as P

HEADS = 12
HEAD = 128
FF = 4608
WINDOW = 1024


norm_eps = 1e-06
adam_eps = 1e-08
beta_first = 0.9
beta_second = 0.95
BF = jnp.bfloat16
F32 = jnp.float32
MESH_ID = pl.DeviceIdType.MESH
VMEM_BYTES = 60 * 1024 * 1024
BACKWARD_VMEM = 127 * 512 * 1024
ANY = pl.BlockSpec(memory_space=pl.ANY)
VM = pl.BlockSpec(memory_space=pltpu.VMEM)
LOG2E = 1.4426950408889634


def passed_along(block, axis, distance):
    devices = range(lax.axis_size(axis))
    route = [(i - distance, i) for i in devices if i - distance in devices]
    return lax.ppermute(block, axis, route)


def swapped(block, axis):
    return lax.ppermute(block, axis, [(0, 1), (1, 0)])


def rotate(values, positions, sign_value):
    half_width = values.shape[-1] // 2
    frequency = 10000.0 ** (-2.0 * jnp.arange(half_width).astype(jnp.float32) / values.shape[-1])
    angles = positions.astype(jnp.float32)[:, None] * frequency[None, :]
    cosine = jnp.cos(angles)
    sine_part = sign_value * jnp.sin(angles)
    if values.ndim == 3:
        cosine = cosine[:, None, :]
        sine_part = sine_part[:, None, :]
    lower_half = values[..., :half_width]
    upper_half = values[..., half_width:]
    return jnp.concatenate(
        [
            lower_half * cosine - upper_half * sine_part,
            upper_half * cosine + lower_half * sine_part,
        ],
        axis=-1,
    )


def root_norm(values, gain):
    return values * lax.rsqrt(jnp.mean(values * values, axis=-1, keepdims=True) + norm_eps) * gain


def adamw_step(weight, moments, grad, step_value, optimizer_rates):
    fix_first = 1.0 - beta_first**step_value
    fix_second = 1.0 - beta_second**step_value
    first_moment = beta_first * moments[0] + (1.0 - beta_first) * grad
    second = beta_second * moments[1] + (1.0 - beta_second) * grad * grad
    update = (
        first_moment / fix_first / (jnp.sqrt(second / fix_second) + adam_eps)
        + optimizer_rates[1] * weight
    )
    return (optimizer_rates[0] * update, jnp.stack([first_moment, second]))


def gather_kernel(shared, groups, S, own, full, sems, small_own, small_full, prepare, work):
    n = len(shared)
    chunks = [chunk for group in groups for chunk in group]
    members = []
    for group in groups:
        first = members[-1][-1] + 1 if members else 0
        members.append(range(first, first + len(group)))
    ng = len(groups)
    F = S - 1
    loc, zs, zr, xs, xr, ys, yr, cs, cr, ss, sr = sems
    y, x, c, z = (lax.axis_index(a) for a in ("y", "x", "c", "z"))
    k = y * 2 + x
    kx = y * 2 + 1 - x
    ky = (1 - y) * 2 + x
    kxy = 3 - k
    to_x = {"x": 1 - x}
    to_y = {"y": 1 - y}
    to_c = {"c": 1 - c}
    low = z
    high = S - 1 - z
    near_count = jnp.minimum(low, high)
    above = jnp.minimum(z + 1, S - 1)
    below = jnp.maximum(z - 1, 0)
    blocks = []
    for j in range(F):
        near = j < 2 * near_count
        dist = jnp.where(near, j // 2 + 1, j - near_count + 1)
        sign = jnp.where(near, (j % 2) * 2 - 1, jnp.where(high > low, 1, -1))
        blocks.append((z + sign * dist, sign))
    barrier = pltpu.get_barrier_semaphore()
    others = [lax.rem(z + e, S) for e in range(1, S)]
    for target in [to_x, to_y, to_c] + [{"z": zz} for zz in others]:
        pl.semaphore_signal(barrier, inc=1, device_id=target, device_id_type=MESH_ID)
    pl.semaphore_wait(barrier, 3 + F)

    def box(q, half):
        i, r0, rn, c0, cn, _ = chunks[q]
        if shared[i]:
            columns = full[i].shape[-1] // 2
            c0 = pl.multiple_of(half * columns + c0, 128)
        return pl.ds(r0, rn), pl.ds(c0, cn)

    def part(q, zz, kk, h=None, half=c):
        rr, cc = box(q, half)
        held = full[chunks[q][0]]
        if h is None:
            return held.at[zz, kk, :, rr, cc]
        return held.at[zz, kk, h, rr, cc]

    def carried(q):
        route = chunks[q][5]
        if route == "xy":
            return (k,)
        return (x, 2 + x) if route == "x" else (2 * y, 2 * y + 1)

    def exchanged(q):
        if chunks[q][5] == "x":
            return xs, xr, to_x, (1 - x, 3 - x)
        return ys, yr, to_y, (2 - 2 * y, 3 - 2 * y)

    def remote(src, dst, s, r, target):
        return pltpu.make_async_remote_copy(
            src_ref=src,
            dst_ref=dst,
            send_sem=s,
            recv_sem=r,
            device_id=target,
            device_id_type=MESH_ID,
        )

    tail = []
    arriving = {i: [] for i in range(n)}
    arriving[None] = []
    finished = [0] * n

    def begin(g):
        i, r0, rn, c0 = groups[g][0][:4]
        prepare(g)
        rows = pl.ds(r0, rn)
        if shared[i]:
            src, dst = own[i].at[:, :, rows], full[i].at[z, :, :, rows]
        else:
            cc = pl.ds(c0, sum(chunk[4] for chunk in groups[g]))
            src, dst = own[i].at[:, :, rows, cc], full[i].at[z, :, :, rows, cc]
        for q in members[g]:
            z_first(q)
        copy = pltpu.make_async_copy(src, dst, loc.at[g])
        copy.start()
        arriving[i].append(copy.wait)

    def z_first(q):
        i = chunks[q][0]
        rr, cc = box(q, c)
        for m, kk in enumerate(carried(q)):
            for ok, target, slot in ((z + 1 < S, above, F), (z > 0, below, F + 1)):

                def make(target=target, slot=slot, m=m, kk=kk):
                    return remote(
                        own[i].at[kk, :, rr, cc],
                        part(q, z, kk),
                        zs.at[q, slot, m],
                        zr.at[q, z, m],
                        {"z": target},
                    )

                @pl.when(ok)
                def _(make=make):
                    make().start()

                def finish(ok=ok, make=make):
                    @pl.when(ok)
                    def _():
                        make().wait_send()

                tail.append(finish)

    def send(p, s, r, q, j, slot, target):
        copy = remote(p, p, s.at[q, j, slot], r.at[q, j, slot], target)
        copy.start()
        tail.append(copy.wait_send)

    def z_next(q, j):
        zz, sign = blocks[j]
        onward = z - sign
        ok = (onward >= 0) & (onward < S)
        target = jnp.clip(onward, 0, S - 1)
        for m, kk in enumerate(carried(q)):
            piece = part(q, zz, kk)
            remote(piece, piece, zs.at[q, j, m], zr.at[q, zz, m], {"z": above}).wait_recv()

            def make(piece=piece, m=m):
                return remote(piece, piece, zs.at[q, j, m], zr.at[q, zz, m], {"z": target})

            @pl.when(ok)
            def _(make=make):
                make().start()

            def finish(make=make):
                @pl.when(ok)
                def _():
                    make().wait_send()

            tail.append(finish)
            if chunks[q][5] != "xy":
                s, r, neighbour, _ = exchanged(q)
                send(piece, s, r, q, j, m, neighbour)
        if chunks[q][5] == "xy":
            send(part(q, zz, k, 0), xs, xr, q, j, 0, to_x)
            send(part(q, zz, k, 1), ys, yr, q, j, 0, to_y)
            send(part(q, zz, k, 0), ys, yr, q, j, 1, to_y)
            send(part(q, zz, k, 1), xs, xr, q, j, 1, to_x)

    def xy_next(q, j):
        if chunks[q][5] != "xy":
            return
        zz, _ = blocks[j]
        p = part(q, zz, kx, 0)
        remote(p, p, xs.at[q, j, 0], xr.at[q, j, 0], to_x).wait_recv()
        send(p, ys, yr, q, j, 2, to_y)
        p = part(q, zz, ky, 1)
        remote(p, p, ys.at[q, j, 0], yr.at[q, j, 0], to_y).wait_recv()
        send(p, xs, xr, q, j, 2, to_x)

    def last(q, j):
        i = chunks[q][0]
        zz, _ = blocks[j]
        finished[i] += 1
        if chunks[q][5] == "xy":
            for kk, h, s, r, slot, target in (
                (kx, 1, xs, xr, 1, to_x),
                (ky, 0, ys, yr, 1, to_y),
                (kxy, 1, xs, xr, 2, to_x),
                (kxy, 0, ys, yr, 2, to_y),
            ):
                p = part(q, zz, kk, h)
                remote(p, p, s.at[q, j, slot], r.at[q, j, slot], target).wait_recv()
        else:
            s, r, neighbour, theirs = exchanged(q)
            for m, kk in enumerate(theirs):
                p = part(q, zz, kk)
                remote(p, p, s.at[q, j, m], r.at[q, j, m], neighbour).wait_recv()
        if shared[i]:
            rr, cc = box(q, c)
            p = full[i].at[zz, :, :, rr, cc]
            copy = remote(p, p, cs.at[q, j], cr.at[q, j], to_c)
            copy.start()
            tail.append(copy.wait_send)
            rr, cc = box(q, 1 - c)
            other = full[i].at[zz, :, :, rr, cc]

            def finish():
                remote(other, other, cs.at[q, j], cr.at[q, j], to_c).wait_recv()

            arriving[i].append(finish)

    def ready(i):
        if i is not None:
            assert finished[i] == F * sum(chunk[0] == i for chunk in chunks)
        for wait in arriving.pop(i, []):
            wait()

    begin(0)
    if small_own is not None:
        place = pltpu.make_async_copy(small_own, small_full.at[z], ss.at[0])
        place.start()
        arriving[None].append(place.wait)
        for e, zz in enumerate(others, 1):
            copy = remote(small_own, small_full.at[z], ss.at[e], sr.at[S - e], {"z": zz})
            copy.start()
            tail.append(copy.wait_send)
            came = small_full.at[zz]
            arriving[None].append(remote(came, came, ss.at[e], sr.at[e], {"z": zz}).wait_recv)
    for t in range(1, ng + F + 3):
        if t < ng:
            begin(t)
        for lag, stage in ((1, z_next), (2, xy_next), (3, last)):
            for j in reversed(range(F)):
                if 0 <= t - lag - j < ng:
                    for q in members[t - lag - j]:
                        stage(q, j)
        work(t, ready)
    for i in list(arriving):
        ready(i)
    for wait in tail:
        wait()


def gather_sems(ng, nc, S):
    dma = pltpu.SemaphoreType.DMA
    F = S - 1
    return [
        dma((ng,)),
        dma((nc, F + 2, 2)),
        dma((nc, S, 2)),
        dma((nc, F, 3)),
        dma((nc, F, 3)),
        dma((nc, F, 3)),
        dma((nc, F, 3)),
        dma((nc, F)),
        dma((nc, F)),
        dma((S,)),
        dma((S,)),
    ]


def nt(a, b):
    return lax.dot_general(a, b, (((1,), (1,)), ((), ())), preferred_element_type=F32)

def nn(a, b):
    return lax.dot_general(a, b, (((1,), (0,)), ((), ())), preferred_element_type=F32)

def fill_bias(bias, q_ids, k_ids, first, rows, span):
    key = lax.broadcasted_iota(jnp.int32, (span, rows), 0)
    query = lax.broadcasted_iota(jnp.int32, (span, rows), 1)
    distance = query + WINDOW - key
    same = k_ids[pl.ds(first, span), :1] == q_ids[:1, pl.ds(first, rows)]
    allowed = (distance >= 0) & (distance < WINDOW) & same
    bias[...] = jnp.where(allowed, 0.0, -1e30)

def fwd_step(h, first, rows, q_ids, q_ref, k_ref, o_ref, l_ref, bias, vt):
    span = WINDOW + rows
    factor = HEAD**-0.5 * LOG2E
    cols = pl.ds(h * HEAD, HEAD)
    q = q_ref[pl.ds(first, rows), cols]
    s = nt(k_ref[pl.ds(first, span), :], q) * factor + bias[...]
    top = jnp.max(s, axis=0, keepdims=True)
    p = jnp.exp2(s - top)
    total = jnp.sum(p, axis=0, keepdims=True)
    o = nn(vt[:, pl.ds(first, span)], p.astype(BF))
    live = q_ids[:1, pl.ds(first, rows)] != 0
    o = jnp.where(live, o * (1.0 / total), 0.0)
    o_ref[pl.ds(first, rows), cols] = o.T.astype(BF)
    l_ref[h, :, pl.ds(first, rows)] = top + jnp.log2(total)


def fwd_kernel(heads, rows, q_ids, k_ids, q_ref, k_ref, v_ref, o_ref, l_ref, bias, vt):
    vt[...] = v_ref[...].T
    for first in range(0, q_ref.shape[0], rows):
        fill_bias(bias, q_ids, k_ids, first, rows, WINDOW + rows)
        for h in range(heads):
            fwd_step(h, first, rows, q_ids, q_ref, k_ref, o_ref, l_ref, bias, vt)


def norm_rows(source, gain, target):
    rows = 64

    @pl.loop(0, target.shape[0] // rows)
    def _(i):
        at = pl.ds(pl.multiple_of(i * rows, rows), rows)
        u = source[at, :].astype(F32)
        scale = lax.rsqrt(jnp.mean(u * u, axis=1, keepdims=True) + norm_eps)
        target[at, :] = (u * scale * gain).astype(target.dtype)


def turned(u, cos_ref, sin_ref):
    return u * cos_ref[...] + pltpu.roll(u, HEAD // 2, 1) * sin_ref[...]


def remote_copy(src, dst, send, receive, target):
    return pltpu.make_async_remote_copy(
        src_ref=src,
        dst_ref=dst,
        send_sem=send,
        recv_sem=receive,
        device_id=target,
        device_id_type=MESH_ID,
    )


def started(src, dst, sem):
    copy = pltpu.make_async_copy(src, dst, sem)
    copy.start()
    return copy


def forward_kernel(heads, groups, S, *refs):
    masters = refs[:4]
    small_own, x_ref, cos_ref, sin_ref, q_ids, k_ids = refs[4:10]
    full = refs[10:14]
    small_full, h1_ref, q_ref, k_out, v_out, o_ref, l_ref, mid_ref, h2_ref, h2_other = refs[14:24]
    h1_t, h1_t_other, o_t, o_t_other = refs[24:28]
    w_in, w_out, gains, mix, kv, bias, vt, lds, hs, hr, h2_sems = refs[28:39]
    own = refs[39:43]
    stages = refs[43:47]
    stage_sems = refs[47]
    sems = refs[48:]
    z = lax.axis_index("z")
    c = lax.axis_index("c")
    piece = x_ref.shape[0]
    reach = kv.shape[0] // piece - 1
    half = w_in.shape[-1] // 2
    D = x_ref.shape[1]
    half_ff = own[3].shape[-1] // 2
    own_rows = pl.ds(reach * piece, piece)
    kv[...] = jnp.zeros_like(kv)
    sent = []
    loads = {}

    def gain_row(i):
        return jnp.concatenate([gains[zz, i : i + 1, :] for zz in range(S)], axis=1).astype(F32)

    def start_norm(ready):
        ready(None)
        started(small_full, gains, lds.at[0]).wait()
        norm_rows(x_ref, gain_row(0), h1_ref)


    def of_weight(g):
        return sum(group[0][0] == groups[g][0][0] for group in groups[:g])

    def stage(g):
        i, r0, rn, c0 = groups[g][0][:4]
        slot = of_weight(g) % stages[i].shape[0]
        cols = pl.ds(0, masters[i].shape[-1])
        if i == 3:
            first = c0 // half_ff * 2 * half_ff + c * half_ff
            cols = pl.ds(pl.multiple_of(first, 128), half_ff)
        src = masters[i].at[:, :, pl.ds(r0, rn), cols]
        loads["stage", g] = started(src, stages[i].at[slot], stage_sems.at[g])

    for g in range(len(groups)):
        if of_weight(g) < stages[groups[g][0][0]].shape[0]:
            stage(g)

    def prepare(g):
        i, r0, rn, c0 = groups[g][0][:4]
        slot = of_weight(g) % stages[i].shape[0]
        loads.pop(("stage", g)).wait()
        cols = pl.ds(c0, half_ff) if i == 3 else pl.ds(0, own[i].shape[-1])

        @pl.loop(0, 8)
        def _(p):
            kk, h = p // 2, p % 2
            own[i][kk, h, pl.ds(r0, rn), cols] = stages[i][slot, kk, h].astype(BF)

        later = g + stages[i].shape[0]
        if later < len(groups) and groups[later][0][0] == i:
            stage(later)

    def start_project(ready):
        ready(0)
        for i in range(2):
            at = pl.ds(i * half, half)
            loads[i] = started(full[0].at[:, :, :, :, at], w_in.at[:, :, :, :, at], lds.at[1 + i])

    def project(i):
        loads.pop(i).wait()
        weight = w_in[:, :, :, :, i * half : (i + 1) * half].reshape(D, half)
        mix[...] = nn(h1_ref[...], weight)
        for j in range(half // HEAD):
            h = i * (half // HEAD) + j
            u = mix[:, j * HEAD : (j + 1) * HEAD]
            if h < heads:
                q_ref[:, h * HEAD : (h + 1) * HEAD] = turned(u, cos_ref, sin_ref).astype(BF)
            elif h == heads:
                kv[own_rows, :HEAD] = turned(u, cos_ref, sin_ref).astype(BF)
            else:
                kv[own_rows, HEAD:] = u.astype(BF)

    def halo(d, starting):
        there = kv.at[pl.ds((reach - d) * piece, piece)]
        target = {"z": jnp.minimum(z + d, S - 1)}
        copy = remote_copy(kv.at[own_rows], there, hs.at[d - 1], hr.at[d - 1], target)

        @pl.when(z + d < S)
        def _():
            if starting:
                copy.start()
            else:
                copy.wait_send()

        if not starting:

            @pl.when(z >= d)
            def _():
                remote_copy(there, there, hs.at[d - 1], hr.at[d - 1], target).wait_recv()

    def start_attention():
        for d in range(1, reach + 1):
            halo(d, False)
        k_out[...] = kv[:, :HEAD]
        v_out[...] = kv[:, HEAD:]
        vt[...] = kv[:, HEAD:].T
        fill_bias(bias, q_ids, k_ids, 0, piece, WINDOW + piece)

    def attention(first, count):
        for h in range(first, first + count):
            fwd_step(h, 0, piece, q_ids, q_ref, k_out, o_ref, l_ref, bias, vt)

    def start_output(ready):
        ready(1)
        for i in range(2):
            at = pl.ds(i * (D // 2), D // 2)
            loads[i] = started(full[1].at[:, :, :, :, at], w_out.at[:, :, :, :, at], lds.at[3 + i])

    def output():
        n = D // 2
        for i in range(2):
            loads.pop(i).wait()
            at = slice(i * n, (i + 1) * n)
            weight = w_out[:, :, :, :, at].reshape(D, n)
            mid_ref[:, at] = x_ref[:, at].astype(F32) + nn(o_ref[...], weight)

    def finish():
        norm_rows(mid_ref, gain_row(1), h2_ref)
        to_partner(h2_ref, h2_other, 0)

    def to_partner(src, dst, i):
        copy = remote_copy(src, dst, h2_sems.at[2 * i], h2_sems.at[2 * i + 1], {"c": 1 - c})
        copy.start()
        sent.append(copy.wait)

    def transpose(src, dst, there, i):
        for j in range(0, D, HEAD):
            dst[j : j + HEAD, :] = src[:, j : j + HEAD].T
        to_partner(dst, there, i)

    third = heads // 3
    plan = {
        2: lambda ready: start_norm(ready),
        5: lambda ready: start_project(ready),
        6: lambda ready: (project(0), project(1), [halo(d, True) for d in range(1, reach + 1)]),
        7: lambda ready: (start_attention(), attention(0, third), start_output(ready)),
        8: lambda ready: attention(third, third),
        9: lambda ready: attention(2 * third, third),
        10: lambda ready: output(),
        11: lambda ready: (finish(), transpose(h1_ref, h1_t, h1_t_other, 1)),
        12: lambda ready: transpose(o_ref, o_t, o_t_other, 2),
    }

    def work(t, ready):
        if t in plan:
            plan[t](ready)

    gather_kernel(
        [True, True, True, False], groups, S, own, full, sems, small_own, small_full, prepare, work
    )
    for wait in sent:
        wait()


def forward(masters, small, x, cos, sin, q_ids, k_ids, heads, S, cid):
    piece, D = x.shape
    keys = k_ids.shape[0]
    r = masters[0].shape[2]
    rf = masters[2].shape[2]
    all_in, all_out, all_gate = (masters[i].shape[-1] for i in (0, 1, 3))
    half_in, half_out, half_ff = all_in // 2, all_out // 2, all_gate // 4

    def routed(i, r0, rn, c0, cn):
        return [(i, r0, rn, c0, cn, "xy")]

    groups = [routed(0, 0, r, 0, half_in), routed(1, 0, r, 0, half_out)]
    groups += [routed(2, i, 48, 0, half_out) for i in range(0, rf, 48)]
    groups += [routed(3, i, 16, j * half_ff, half_ff) for j in range(2) for i in range(0, r, 16)]

    def body(*refs):
        forward_kernel(heads, groups, S, *refs)

    def shape(*dims, dtype=BF):
        return jax.ShapeDtypeStruct(dims, dtype)

    own = [(4, 2) + masters[i].shape[2:] for i in range(3)] + [(4, 2, r, 2 * half_ff)]
    outs = [shape(S, *o) for o in own]
    outs += [
        shape(S, *small.shape),
        shape(piece, D),
        shape(piece, heads * HEAD),
        shape(keys, HEAD),
        shape(keys, HEAD),
        shape(piece, heads * HEAD),
        shape(heads, 1, piece, dtype=F32),
        shape(piece, D, dtype=F32),
        shape(piece, D),
        shape(piece, D),
        shape(D, piece),
        shape(D, piece),
        shape(D, piece),
        shape(D, piece),
    ]
    dma = pltpu.SemaphoreType.DMA
    return pl.pallas_call(
        body,
        out_shape=tuple(outs),
        in_specs=[ANY] * 4 + [VM] * 6,
        out_specs=tuple([ANY] * 5 + [VM] * 8 + [ANY] + [VM, ANY] * 2),
        scratch_shapes=[
            pltpu.VMEM((S,) + own[0], BF),
            pltpu.VMEM((S,) + own[1], BF),
            pltpu.VMEM((S,) + small.shape, BF),
            pltpu.VMEM((piece, half_in), F32),
            pltpu.VMEM((keys, 2 * HEAD), BF),
            pltpu.VMEM((keys, piece), F32),
            pltpu.VMEM((HEAD, keys), BF),
            dma((5,)),
            dma((2,)),
            dma((2,)),
            dma((6,)),
        ]
        + [pltpu.VMEM(o, BF) for o in own]
        + [
            pltpu.VMEM((1, 4, 2, r, all_in), F32),
            pltpu.VMEM((1, 4, 2, r, all_out), F32),
            pltpu.VMEM((2, 4, 2, 48, all_out), F32),
            pltpu.VMEM((2, 4, 2, 16, half_ff), F32),
            dma((len(groups),)),
        ]
        + gather_sems(len(groups), sum(map(len, groups)), S),
        compiler_params=pltpu.CompilerParams(
            collective_id=cid, has_side_effects=True, vmem_limit_bytes=VMEM_BYTES
        ),
    )(*masters, small, x, cos, sin, q_ids, k_ids)


def back_step(h, first, rows, refs, bias, kt, finish):
    q_ref, k_ref, v_ref, o_ref, do_ref, l_ref, dq_ref, dk_ref, dv_ref = refs
    span = WINDOW + rows
    factor = HEAD**-0.5 * LOG2E
    cols = pl.ds(h * HEAD, HEAD)
    q = q_ref[pl.ds(first, rows), cols]
    do = do_ref[pl.ds(first, rows), cols]
    o = o_ref[pl.ds(first, rows), cols]
    delta = jnp.sum((do.astype(F32) * o.astype(F32)).T, axis=0, keepdims=True)
    s = nt(k_ref[pl.ds(first, span), :], q) * factor + bias[...]
    p = jnp.exp2(s - l_ref[h, :, pl.ds(first, rows)])
    dp = nt(v_ref[pl.ds(first, span), :], do)
    ds = (p * ((dp - delta) * HEAD**-0.5)).astype(BF)
    dv_ref[pl.ds(first, span), :] += nn(p.astype(BF), do)
    dk_ref[pl.ds(first, span), :] += nn(ds, q)
    dq = nn(kt[:, pl.ds(first, span)], ds).T
    dq_ref[pl.ds(first, rows), cols] = finish(dq, first).astype(dq_ref.dtype)


def bwd_kernel(heads, rows, q_ids, k_ids, *refs):
    *arrays, bias, kt = refs
    q_ref, k_ref = arrays[:2]
    dk_ref, dv_ref = arrays[-2:]
    kt[...] = k_ref[...].T
    dk_ref[...] = jnp.zeros_like(dk_ref)
    dv_ref[...] = jnp.zeros_like(dv_ref)
    for first in range(0, q_ref.shape[0], rows):
        fill_bias(bias, q_ids, k_ids, first, rows, WINDOW + rows)
        for h in range(heads):
            back_step(h, first, rows, arrays, bias, kt, lambda dq, first: dq)


def attend(q_ids, k_ids, q, k, v, heads, rows):
    def body(*refs):
        fwd_kernel(heads, rows, *refs)

    return pl.pallas_call(
        body,
        out_shape=(
            jax.ShapeDtypeStruct(q.shape, BF),
            jax.ShapeDtypeStruct((heads, 1, q.shape[0]), F32),
        ),
        in_specs=[VM] * 5,
        out_specs=(VM, VM),
        scratch_shapes=[
            pltpu.VMEM((WINDOW + rows, rows), F32),
            pltpu.VMEM((HEAD, k.shape[0]), BF),
        ],
        compiler_params=pltpu.CompilerParams(vmem_limit_bytes=VMEM_BYTES),
        cost_estimate=pl.CostEstimate(
            flops=4 * q.size * k.shape[0], bytes_accessed=4 * q.size, transcendentals=q.size * 12
        ),
    )(q_ids, k_ids, q, k, v)


def attend_back(q_ids, k_ids, q, k, v, o, do, l, heads, rows):
    def body(*refs):
        bwd_kernel(heads, rows, *refs)

    return pl.pallas_call(
        body,
        out_shape=(
            jax.ShapeDtypeStruct(q.shape, F32),
            jax.ShapeDtypeStruct(k.shape, F32),
            jax.ShapeDtypeStruct(k.shape, F32),
        ),
        in_specs=[VM] * 8,
        out_specs=(VM, VM, VM),
        scratch_shapes=[
            pltpu.VMEM((WINDOW + rows, rows), F32),
            pltpu.VMEM((HEAD, k.shape[0]), BF),
        ],
        compiler_params=pltpu.CompilerParams(vmem_limit_bytes=VMEM_BYTES),
        cost_estimate=pl.CostEstimate(
            flops=10 * q.size * k.shape[0], bytes_accessed=12 * q.size, transcendentals=q.size * 12
        ),
    )(q_ids, k_ids, q, k, v, o, do, l)


def mlp_kernel(
    where, two_own, two_other, df_own, df_other, gate_ref, up_ref, down_ref, *results
):
    two_t, hid_t, grads, back_low, back = results
    step = pl.program_id(0)
    rows, D = two_own.shape
    part = two_t.shape[0]
    core = where[0]
    block = 512

    @pl.when(step == 0)
    def _():
        back[...] = jnp.zeros_like(back)

    @pl.when(step < D // part)
    def _():
        cols = pl.ds(pl.multiple_of(step * part, part), part)
        for two_ref, owner in ((two_own, core), (two_other, 1 - core)):
            at = pl.ds(pl.multiple_of(owner * rows, rows), rows)
            two_t[:, at] = two_ref[:, cols].T

    def tokens(two_ref, df_ref, owner, first):
        here = pl.ds(first, block)
        at = pl.ds(pl.multiple_of(owner * rows + first, block), block)
        two = two_ref[here, :]
        gate = nn(two, gate_ref[...])
        up = nn(two, up_ref[...])
        grad = nt(df_ref[here, :], down_ref[...])
        slope = 0.7978845608028654
        cube = slope * 0.044715
        square = gate * gate
        upper = 0.5 + 0.5 * jnp.tanh(gate * (slope + cube * square))
        act = gate * upper
        act_slope = upper + act * (1.0 - upper) * (2.0 * slope + 6.0 * cube * square)
        hid = (act * up).astype(BF)
        grad_gate = (grad * up * act_slope).astype(BF)
        grad_up = (grad * act).astype(BF)
        hid_t[:, at] = hid.T
        grads[0, at, :] = grad_gate
        grads[1, at, :] = grad_up
        back[at, :] += nt(grad_gate, gate_ref[...]) + nt(grad_up, up_ref[...])

    for two_ref, df_ref, owner in ((two_own, df_own, core), (two_other, df_other, 1 - core)):
        for first in range(0, rows, block):
            tokens(two_ref, df_ref, owner, first)

    @pl.when(step == pl.num_programs(0) - 1)
    def _():
        back_low[...] = back[...].astype(BF)


def mlp_call(core, two, df, gate_full, down_full):
    T, D = 2 * two[0].shape[0], two[0].shape[1]
    half_ff = gate_full.shape[1] // 2
    tile = 256
    tiles = half_ff // tile
    part = max(D // tiles // 128 * 128, 256)
    last = D // part - 1

    def body(*refs):
        mlp_kernel(*refs)

    once = pl.Buffered(1)
    piece = pl.BlockSpec((T // 2, D), lambda i, w: (0, 0), pipeline_mode=once)
    return pl.pallas_call(
        body,
        grid_spec=pltpu.PrefetchScalarGridSpec(
            num_scalar_prefetch=1,
            grid=(tiles,),
            in_specs=[
                piece,
                piece,
                piece,
                piece,
                pl.BlockSpec((D, tile), lambda i, w: (0, i)),
                pl.BlockSpec((D, tile), lambda i, w: (0, tiles + i)),
                pl.BlockSpec((tile, D), lambda i, w: (w[0] * tiles + i, 0)),
            ],
            out_specs=[
                pl.BlockSpec((part, T), lambda i, w: (jnp.minimum(i, last), 0)),
                pl.BlockSpec((tile, T), lambda i, w: (i, 0)),
                pl.BlockSpec((2, T, tile), lambda i, w: (0, 0, i)),
                pl.BlockSpec((T, D), lambda i, w: (0, 0), pipeline_mode=once),
            ],
            scratch_shapes=[pltpu.VMEM((T, D), F32)],
        ),
        out_shape=[
            jax.ShapeDtypeStruct((D, T), BF),
            jax.ShapeDtypeStruct((half_ff, T), BF),
            jax.ShapeDtypeStruct((2, T, half_ff), BF),
            jax.ShapeDtypeStruct((T, D), BF),
        ],
        compiler_params=pltpu.CompilerParams(
            dimension_semantics=("arbitrary",), vmem_limit_bytes=BACKWARD_VMEM
        ),
        cost_estimate=pl.CostEstimate(
            flops=10 * T * D * half_ff, bytes_accessed=40 * 2**20, transcendentals=T * half_ff
        ),
    )(core, *two, *df, gate_full, gate_full, down_full)


def split_widths(total, most):
    first = -(-total // 256) * 128
    assert first <= most
    return (first, total - first)


def backward_kernel(heads, sides, parts, S, *refs):
    two, hid, *flats = refs[:6]
    flat_own, flat_other, norm_own, norm_other = flats[2], flats[3], flats[0], flats[1]
    grads, dy_own, dy_other, back, middle, w_out, gains_ref, x_ref, w_in, w_down = refs[6:16]
    q_ids, k_ids, q_ref, k_ref, v_ref, o_ref, l_ref, cos_ref, sin_ref = refs[16:25]
    out, hid_land, x_grad, y_out, dx_land = refs[25:30]
    left, right, out_right, mix_right, s1, g1, s2, g2, fz, gz, mine, da, do, got = refs[30:44]
    tails, landed_tails, gains, x1, dk, dv, bias, kt, mixed, w_rows, w_tiles = refs[44:55]
    lds, rds, fs, cs_in, hs, hr, s1s, s1r, s2s, s2r, zs, zr, ls, xs, xr, ys, yr, cs, cr = refs[55:]
    _, _, _, r, T = left.shape
    n = right.shape[2]
    piece, D = da.shape
    reach = tails.shape[0]
    wide = sides * parts
    rows_groups = hid.shape[1]
    chunk_out = wide + rows_groups
    mix_half = mix_right.shape[1]
    widths = [n] * (chunk_out + 1) + list(split_widths(mix_half, n))
    nc = len(widths)
    left_slots = left.shape[0]
    right_slots = right.shape[0]
    slots = g1.shape[0]
    y, x, c, z = (lax.axis_index(a) for a in ("y", "x", "c", "z"))
    k = y * 2 + x
    kx = y * 2 + 1 - x
    ky = (1 - y) * 2 + x
    kxy = 3 - k
    to_x = {"x": 1 - x}
    to_y = {"y": 1 - y}
    to_c = {"c": 1 - c}
    place = pl.ds(pl.multiple_of(c * piece, piece), piece)
    other_place = pl.ds(pl.multiple_of((1 - c) * piece, piece), piece)
    loads = {}
    pending = {}

    def fetch(key, src, dst, sem):
        loads.setdefault(key, []).append(started(src, dst, sem))

    def landed(key):
        for copy in loads.pop(key, []):
            copy.wait()

    def launch(key, copy):
        copy.start()
        pending.setdefault(key, []).append(copy)

    def drain(key):
        for copy in pending.pop(key, []):
            copy.wait_send()

    groups = 3 + rows_groups

    def group_of(t):
        if t < wide:
            return 0
        return min(t - wide + 1, groups - 1)

    def fetch_left(g):
        slot = g % left_slots
        for p in range(8):
            h, kk = p // 4, p % 4
            if g == 0:
                fetch(("l", g), two.at[:, kk, h], left.at[slot, p], lds.at[g, p, 0])
                continue
            if g <= rows_groups:
                if g == 1 and p == 0:
                    landed_hid.wait_recv()
                half = left.shape[2] // 2
                pairs = [
                    (hid.at[:, g - 1, kk, h], left.at[slot, p, pl.ds(c * half, half)]),
                    (hid_land.at[:, g - 1, kk, h], left.at[slot, p, pl.ds((1 - c) * half, half)]),
                ]
            else:
                own, other = (flat_own, flat_other) if g == groups - 2 else (norm_own, norm_other)
                pairs = [
                    (own.at[:, kk, h], left.at[slot, p, :, :, place]),
                    (other.at[:, kk, h], left.at[slot, p, :, :, other_place]),
                ]
            for i, (src, dst) in enumerate(pairs):
                fetch(("l", g), src, dst, lds.at[g, p, i])

    def fetch_right(t):
        slot = t % right_slots
        if t < wide:
            src = grads.at[t // parts, :, pl.ds((t % parts) * n, n)]
            fetch(("r", t), src, right.at[slot], rds.at[t, 0])
        elif t == wide:
            keep = pl.ds(pl.multiple_of(c * n, n), n)
            fetch(("r", t), dy_own.at[:, keep], right.at[slot, place], rds.at[t, 0])
            fetch(("r", t), dy_other.at[:, keep], right.at[slot, other_place], rds.at[t, 1])

    fetch_right(0)
    fetch_left(0)
    fetch_right(1)
    landed_tails[...] = jnp.zeros_like(landed_tails)
    barrier = pltpu.get_barrier_semaphore()
    peers = [to_x, to_y, to_c] + [{"z": lax.rem(z + e, S)} for e in range(1, S)]
    for target in peers:
        pl.semaphore_signal(barrier, inc=1, device_id=target, device_id_type=MESH_ID)
    pl.semaphore_wait(barrier, len(peers))
    launch("end", remote_copy(back.at[other_place], got, cs_in.at[0], cs_in.at[1], to_c))
    launch("end", remote_copy(hid, hid_land, cs_in.at[2], cs_in.at[3], to_c))
    landed_hid = remote_copy(hid, hid_land, cs_in.at[2], cs_in.at[3], to_c)
    landed_back = remote_copy(got, got, cs_in.at[0], cs_in.at[1], to_c)

    def product(t, p):
        lhs = left[group_of(t) % left_slots, p].reshape(S * r, T)
        if t <= chunk_out - 1:
            return nn(lhs, right[min(t, wide) % right_slots])
        if t == chunk_out:
            return nn(lhs, out_right[...])
        first = sum(widths[chunk_out + 1 : t])
        return nn(lhs, mix_right[:, first : first + widths[t]])

    def cut(ref, t):
        return ref if widths[t] == n else ref.at[:, pl.ds(0, widths[t])]

    def first(t):
        slot = t % 2
        landed(("l", group_of(t)))
        landed(("r", t))
        drain(("s1", t - 2))
        for i in range(2):
            for j, p, target in ((i, i * 2 + 1 - x, to_x), (2 + i, 4 + (1 - y) * 2 + i, to_y)):
                src, dst = cut(s1.at[slot, j], t), cut(g1.at[t % slots, j], t)
                src[...] = product(t, p).astype(BF)
                launch(("s1", t), remote_copy(src, dst, s1s.at[t, j], s1r.at[t, j], target))

    def second(t):
        slot = t % 2
        drain(("s2", t - 2))
        for j in range(4):
            dst = cut(g1.at[t % slots, j], t)
            remote_copy(dst, dst, s1s.at[t, j], s1r.at[t, j], to_x).wait_recv()
        for h, p, j, target in ((0, (1 - y) * 2 + x, 1 - y, to_y), (1, 4 + y * 2 + 1 - x, 3 - x, to_x)):
            src, dst = cut(s2.at[slot, h], t), cut(g2.at[t % slots, h], t)
            came = cut(g1.at[t % slots, j], t)
            src[...] = (product(t, p) + came[...].astype(F32)).astype(BF)
            launch(("s2", t), remote_copy(src, dst, s2s.at[t, h], s2r.at[t, h], target))

    def third(t):
        slot = t % 2
        w = widths[t]
        drain(("z", t - 2))
        for h, p, j in ((0, k, y), (1, 4 + k, 2 + x)):
            dst = cut(g2.at[t % slots, h], t)
            remote_copy(dst, dst, s2s.at[t, h], s2r.at[t, h], to_x).wait_recv()
            came = cut(g1.at[t % slots, j], t)
            total = (product(t, p) + came[...].astype(F32) + dst[...].astype(F32)).astype(BF)
            for zz in range(S):
                fz[slot, zz, h, :, :w] = total[zz * r : (zz + 1) * r]
        for e in range(1, S):
            src = fz.at[slot, lax.rem(z + e, S), :, :, pl.ds(0, w)]
            dst = gz.at[t, S - e - 1, :, :, pl.ds(0, w)]
            target = {"z": lax.rem(z + e, S)}
            launch(("z", t), remote_copy(src, dst, zs.at[t, e - 1], zr.at[t, S - e - 1], target))

    def fourth(t):
        slot = t % 2
        w = widths[t]
        drain(("ag", t - 2))
        landed(("o", t - 2))
        for e in range(S - 1):
            dst = gz.at[t, e, :, :, pl.ds(0, w)]
            remote_copy(dst, dst, zs.at[t, e], zr.at[t, e], to_x).wait_recv()
        for h in range(2):
            total = fz[slot, z, h, :, :w].astype(F32)
            for e in range(S - 1):
                total = total + gz[t, e, h, :, :w].astype(F32)
            mine[slot, h, :, :w] = total.astype(BF)
        cols = pl.ds(0, w)
        fetch(("o", t), mine.at[slot, :, :, cols], out.at[t, k, c, :, :, cols], ls.at[t])
        for i, hs_ in enumerate(((0, 1), (1, 0))):
            for h, s, r_, target in ((hs_[0], xs, xr, to_x), (hs_[1], ys, yr, to_y)):
                src, dst = mine.at[slot, h, :, cols], out.at[t, k, c, h, :, cols]
                launch(("ag", t), remote_copy(src, dst, s.at[t, i], r_.at[t, i], target))

    def land(t, kk, h, s, r_, j, target):
        p = out.at[t, kk, c, h, :, pl.ds(0, widths[t])]
        remote_copy(p, p, s.at[t, j], r_.at[t, j], target).wait_recv()
        return p

    def fifth(t):
        p = land(t, kx, 0, xs, xr, 0, to_x)
        launch("end", remote_copy(p, p, ys.at[t, 2], yr.at[t, 2], to_y))
        p = land(t, ky, 1, ys, yr, 0, to_y)
        launch("end", remote_copy(p, p, xs.at[t, 2], xr.at[t, 2], to_x))

    def sixth(t):
        land(t, kx, 1, xs, xr, 1, to_x)
        land(t, ky, 0, ys, yr, 1, to_y)
        land(t, kxy, 1, xs, xr, 2, to_x)
        land(t, kxy, 0, ys, yr, 2, to_y)
        landed(("o", t))
        p = out.at[t, :, c, :, :, pl.ds(0, widths[t])]
        launch("end", remote_copy(p, p, cs.at[t], cr.at[t], to_c))


    def norm_back():
        for key in ("near", "x1", "dy", "gains"):
            landed(key)
        landed_back.wait_recv()
        gain = jnp.concatenate([gains[zz, 1:2, :] for zz in range(S)], axis=1).astype(F32)
        step = 64

        @pl.loop(0, piece // step)
        def _(i):
            at = pl.ds(pl.multiple_of(i * step, step), step)
            u = x1[at, :]
            scale = lax.rsqrt(jnp.mean(u * u, axis=1, keepdims=True) + norm_eps)
            hat = u * scale
            e = (do[at, :].astype(F32) + got[at, :].astype(F32)) * gain
            inner = jnp.mean(e * hat, axis=1, keepdims=True)
            dx = mixed[at, :D].astype(F32) + scale * (e - hat * inner)
            x1[at, :] = dx
            da[at, :] = dx.astype(BF)

        fetch("dx", x1, dx_land, fs.at[11])
        launch("da", remote_copy(give_of(da, n), out_right.at[place], cs_in.at[4], cs_in.at[5], to_c))
        out_right[place, :] = keep_of(da, n)[...]
        for i in range(2):
            fetch("w", w_out.at[pl.ds(T, piece), pl.ds(i * n, n)], got.at[:, pl.ds(i * n, n)], fs.at[7 + i])

    def give_of(ref, width):
        return ref.at[:, pl.ds(pl.multiple_of((1 - c) * width, width), width)]

    def keep_of(ref, width):
        return ref.at[:, pl.ds(pl.multiple_of(c * width, width), width)]

    def heads_back():
        landed("w")
        live = k_ids[pl.ds(reach * piece, piece), :1] != 0
        for j in range(0, D, piece):
            if j < T:
                low, high = right[2, j : j + piece, :], right[3, j : j + piece, :]
            else:
                low, high = got[:, :n], got[:, n:]
            part = nt(da[:, :n], low) + nt(da[:, n:], high)
            do[:, j : j + piece] = jnp.where(live, part, 0.0).astype(BF)

    half_rows = piece // 2
    steps = [(block, h) for block in range(2) for h in range(heads)]

    def turn_back(dq, first):
        at = pl.ds(first, half_rows)
        return dq * cos_ref[at, :] - pltpu.roll(dq, HEAD // 2, 1) * sin_ref[at, :]

    def attention(first_step, count):
        arrays = (q_ref, k_ref, v_ref, o_ref, do, l_ref, mixed, dk, dv)
        if first_step == 0:
            kt[...] = k_ref[...].T
            dk[...] = jnp.zeros_like(dk)
            dv[...] = jnp.zeros_like(dv)
        for block, h in steps[first_step : first_step + count]:
            if h == 0:
                fill_bias(bias, q_ids, k_ids, block * half_rows, half_rows, WINDOW + half_rows)
            back_step(h, block * half_rows, half_rows, arrays, bias, kt, turn_back)

    def tail(d):
        target = {"z": jnp.maximum(z - d, 0)}
        return remote_copy(tails.at[d - 1], landed_tails.at[d - 1], hs.at[d - 1], hr.at[d - 1], target)

    def send_tails():
        for d in range(1, reach + 1):
            at = pl.ds((reach - d) * piece, piece)
            tails[d - 1, :, :HEAD] = dk[at, :].astype(BF)
            tails[d - 1, :, HEAD:] = dv[at, :].astype(BF)

            @pl.when(z >= d)
            def _(d=d):
                tail(d).start()

    def mix_back():
        for d in range(1, reach + 1):

            @pl.when(z >= d)
            def _(d=d):
                tail(d).wait_send()

            @pl.when(z + d < S)
            def _(d=d):
                tail(d).wait_recv()

        at = pl.ds(reach * piece, piece)
        keys, values = dk[at, :], dv[at, :]
        for d in range(1, reach + 1):
            keys = keys + landed_tails[d - 1, :, :HEAD].astype(F32)
            values = values + landed_tails[d - 1, :, HEAD:].astype(F32)
        keys = keys * cos_ref[...] - pltpu.roll(keys, HEAD // 2, 1) * sin_ref[...]
        width = heads * HEAD
        mixed[:, width : width + HEAD] = keys.astype(BF)
        mixed[:, width + HEAD :] = values.astype(BF)
        launch("end", remote_copy(give_of(mixed, mix_half), mix_right.at[place], cs_in.at[6], cs_in.at[7], to_c))
        mix_right[place, :] = keep_of(mixed, mix_half)[...]

    step_rows = w_rows.shape[1]

    def fetch_rows(j):
        if j * step_rows < D:
            fetch(("q", j), w_in.at[pl.ds(j * step_rows, step_rows)], w_rows.at[j % 2], fs.at[9 + j % 2])

    def start_input():
        drain("da")
        fetch_rows(0)
        fetch_rows(1)
        fetch("x0", x_ref, got, fs.at[4])

    def project_back(j):
        landed(("q", j))
        da[:, j * step_rows : (j + 1) * step_rows] = nt(mixed[...], w_rows[j % 2]).astype(BF)
        fetch_rows(j + 2)

    def input_back():
        landed("x0")
        landed("dx")
        gain = jnp.concatenate([gains[zz, 0:1, :] for zz in range(S)], axis=1).astype(F32)
        step = 64

        @pl.loop(0, piece // step)
        def _(i):
            at = pl.ds(pl.multiple_of(i * step, step), step)
            u = got[at, :].astype(F32)
            scale = lax.rsqrt(jnp.mean(u * u, axis=1, keepdims=True) + norm_eps)
            hat = u * scale
            e = da[at, :].astype(F32) * gain
            inner = jnp.mean(e * hat, axis=1, keepdims=True)
            do[at, :] = (x1[at, :] + scale * (e - hat * inner)).astype(BF)

        fetch("x_grad", do, x_grad, fs.at[0])

    spread = {6: ((1, 0, 3),), 7: ((1, 3, 6), (2, 0, 3)), 8: ((1, 6, 8), (2, 3, 6), (3, 0, 3))}
    spread.update({9: ((2, 6, 8), (3, 3, 6)), 10: ((3, 6, 8),)})
    out_steps = [(g, p) for t in sorted(spread) for g, a, b in spread[t] for p in range(a, b)]
    out_count = {t: sum(b - a for _, a, b in spread[t]) for t in spread}
    assert rows_groups == 3 and wide == 6

    def fetch_tile(i):
        if i < len(out_steps):
            g, p = out_steps[i]
            fetch(("d", i), w_down.at[:, g - 1, p % 4, p // 4], w_tiles.at[i % 2], fs.at[12 + i % 2])

    def output_step(i):
        g, p = out_steps[i]
        landed(("d", i))
        fetch_tile(i + 1)
        lhs = left[g % left_slots, p, :, :, place].reshape(S * r, piece)
        for j in range(0, D, piece):
            rhs = w_tiles[i % 2, :, :, j : j + piece].reshape(S * r, piece)
            x1[:, j : j + piece] += lax.dot_general(
                lhs, rhs, (((0,), (0,)), ((), ())), preferred_element_type=F32
            )

    def output_work(t):
        if t == 2:
            landed("dx")
            fetch("x1", middle, x1, fs.at[1])
        if t == 5:
            landed("x1")
            fetch_tile(0)
        if t in out_count:
            done = sum(out_count[u] for u in out_count if u < t)
            for i in range(done, done + out_count[t]):
                output_step(i)
        if t == 11:
            do[...] = x1[...].astype(BF)
            fetch("y", do, y_out, fs.at[2])
        if t == 13:
            landed("y")
            fetch("dx", dx_land, x1, fs.at[11])

    def came(ref, i):
        ref = ref.at[other_place]
        remote_copy(ref, ref, cs_in.at[i], cs_in.at[i + 1], to_c).wait_recv()

    stages = (first, second, third, fourth, fifth, sixth)

    fetch("near", back.at[place], do, fs.at[0])
    fetch("x1", middle, x1, fs.at[1])
    fetch("dy", dy_own, mixed.at[:, pl.ds(0, D)], fs.at[2])
    fetch("gains", gains_ref, gains, fs.at[3])
    for i in range(2):
        fetch("w", w_out.at[pl.ds(0, T), pl.ds(i * n, n)], right.at[2 + i], fs.at[5 + i])
    each = 5

    def work(t):
        if t == 0:
            norm_back()
        if t == 1:
            heads_back()
        if t >= 2 and (t - 2) * each < len(steps):
            attention((t - 2) * each, each)
        if t == 7:
            send_tails()
        if t == 8:
            mix_back()
            start_input()
        if t >= 9 and (t - 9) * step_rows < D:
            project_back(t - 9)
        output_work(t)
        if t == 15:
            input_back()

    for t in range(nc + len(stages) - 1):
        for lag, stage in enumerate(stages):
            if lag == 0 and t == chunk_out:
                came(out_right, 4)
            if lag == 0 and t == chunk_out + 1:
                came(mix_right, 6)
            if 0 <= t - lag < nc:
                stage(t - lag)
            if lag == 0:
                work(t)
        if t == 1:
            fetch_right(2)
        if t >= 1:
            fetch_right(t + 2)
        for g in range(1, groups):
            if t == wide + g - (3 if g < left_slots else 2):
                fetch_left(g)
    for t in range(nc):
        p = out.at[t, :, 1 - c, :, :, pl.ds(0, widths[t])]
        remote_copy(p, p, cs.at[t], cr.at[t], to_c).wait_recv()
    for key in list(pending):
        drain(key)
    for key in list(loads):
        landed(key)


def backward(
    two_t, hid_t, transposed, grads, dy, back, middle, w_out, gains, x, w_in, w_down, attention, tables, heads, S, cid
):
    D, T = two_t.shape
    sides, _, half_ff = grads.shape
    piece = middle.shape[0]
    n = D // 2
    r = D // (S * 8)
    parts = half_ff // n
    rows_groups = 2 * half_ff // (S * 8 * r)
    mixed = attention[2].shape[1] + 2 * HEAD
    nc = sides * parts + rows_groups + 3
    m = S * r
    slots = 5
    keys = attention[3].shape[0]
    reach = keys // piece - 1
    dma = pltpu.SemaphoreType.DMA
    hid_shape = (S // 2, rows_groups, 4, 2, r, T)

    def body(*refs):
        backward_kernel(heads, sides, parts, S, *refs)

    def vmem(*shape):
        return pltpu.VMEM(shape, BF)

    results = pl.pallas_call(
        body,
        out_shape=(
            jax.ShapeDtypeStruct((nc, 4, 2, 2, r, n), BF),
            jax.ShapeDtypeStruct(hid_shape, BF),
            jax.ShapeDtypeStruct((piece, D), BF),
            jax.ShapeDtypeStruct((piece, D), BF),
            jax.ShapeDtypeStruct((piece, D), F32),
        ),
        in_specs=[ANY] * 16 + [VM] * 9,
        out_specs=(ANY,) * 5,
        scratch_shapes=[
            vmem(3, 8, S, r, T),
            vmem(4, T, n),
            vmem(T, n),
            vmem(T, mixed // 2),
            vmem(2, 4, m, n),
            vmem(slots, 4, m, n),
            vmem(2, 2, m, n),
            vmem(slots, 2, m, n),
            vmem(2, S, 2, r, n),
            vmem(nc, S - 1, 2, r, n),
            vmem(2, 2, r, n),
            vmem(piece, D),
            vmem(piece, D),
            vmem(piece, D),
            vmem(reach, piece, 2 * HEAD),
            vmem(reach, piece, 2 * HEAD),
            vmem(*gains.shape),
            pltpu.VMEM((piece, D), F32),
            pltpu.VMEM((keys, HEAD), F32),
            pltpu.VMEM((keys, HEAD), F32),
            pltpu.VMEM((WINDOW + piece // 2, piece // 2), F32),
            pltpu.VMEM((HEAD, keys), BF),
            vmem(piece, mixed),
            vmem(2, 256, mixed),
            vmem(2, S, r, D),
            dma((rows_groups + 3, 8, 2)),
            dma((nc, 2)),
            dma((14,)),
            dma((8,)),
            dma((reach,)),
            dma((reach,)),
            dma((nc, 4)),
            dma((nc, 4)),
            dma((nc, 2)),
            dma((nc, 2)),
            dma((nc, S)),
            dma((nc, S)),
            dma((nc,)),
            dma((nc, 3)),
            dma((nc, 3)),
            dma((nc, 3)),
            dma((nc, 3)),
            dma((nc,)),
            dma((nc,)),
        ],
        compiler_params=pltpu.CompilerParams(
            collective_id=cid, has_side_effects=True, vmem_limit_bytes=BACKWARD_VMEM
        ),
    )(
        two_t.reshape(S, 4, 2, r, T),
        hid_t.reshape(hid_shape),
        *[v.reshape(S, 4, 2, r, piece) for v in transposed],
        grads,
        *dy,
        back,
        middle,
        w_out,
        gains,
        x,
        w_in,
        w_down.reshape(S, rows_groups, 4, 2, r, D),
        *attention,
        *tables,
    )
    return results[0], results[2], results[3]


def adam_kernel(total, widths, gains, count_ref, rates_ref, g_ref, w_ref, m_ref, g_out, w_out, m_out, *more):
    step_value = count_ref[0].astype(F32)
    log_first = jnp.log(jnp.full((8, 128), beta_first, F32))
    log_second = jnp.log(jnp.full((8, 128), beta_second, F32))
    unfix_first = (1.0 / (1.0 - jnp.exp(step_value * log_first)))[:1, :1]
    unfix_second = (1.0 / (1.0 - jnp.exp(step_value * log_second)))[:1, :1]
    rate, decay = rates_ref[0], rates_ref[1]
    rows = w_ref.shape[0]

    if gains:

        @pl.when((pl.program_id(1) == 0) & (pl.program_id(2) == 0))
        def _():
            more[0][...] = jnp.zeros_like(more[0])

    for i, n in enumerate(widths):
        at = pl.ds(sum(widths[:i]), n)
        grad = g_ref[i, :, 0, :, :, :n].reshape(rows, n).astype(F32) * (1.0 / total)
        w = w_ref[:, at]
        first = beta_first * m_ref[0, :, at] + (1.0 - beta_first) * grad
        second = beta_second * m_ref[1, :, at] + (1.0 - beta_second) * grad * grad
        step = first * unfix_first / (jnp.sqrt(second * unfix_second) + adam_eps) + decay * w
        g_out[:, at] = grad
        w_out[:, at] = w - rate * step
        m_out[0, :, at] = first
        m_out[1, :, at] = second
        if gains:
            both = w.astype(BF).astype(F32) * grad
            for j in range(0, n, 128):
                more[0][...] += both[:, j : j + 128]


def adam_call(
    weight, moments, grads, count, rates, total, base, widths, sides=1, tiles=1, gains=False, chips=4
):
    _, _, _, _, r, n = grads.shape
    wide = len(widths)

    def g_place(kk, cc, ss, tt):
        return (base // wide + ss + tt, kk, cc, 0, 0, 0)

    def place(kk, cc, ss, tt):
        return (tt * (4 // chips) + kk, ss * 2 + cc)

    def m_place(*at):
        return (0,) + place(*at)

    rows = chips * 2 * r
    w_spec = pl.BlockSpec((rows, sum(widths)), place)
    m_spec = pl.BlockSpec((2, rows, sum(widths)), m_place)
    smem = pl.BlockSpec(memory_space=pltpu.SMEM)
    like = jax.ShapeDtypeStruct(weight.shape, F32)
    out_specs = [w_spec, w_spec, m_spec]
    out_shape = [like, like, jax.ShapeDtypeStruct(moments.shape, F32)]
    if gains:
        out_specs.append(pl.BlockSpec((rows, 128), lambda kk, cc, ss, tt: (kk, 0)))
        out_shape.append(jax.ShapeDtypeStruct((weight.shape[0], 128), F32))

    def body(*refs):
        adam_kernel(total, widths, gains, *refs)

    return pl.pallas_call(
        body,
        grid=(4 // chips, 2, sides, tiles),
        in_specs=[smem, smem, pl.BlockSpec((wide, chips, 1, 2, r, n), g_place), w_spec, m_spec],
        out_specs=out_specs,
        out_shape=out_shape,
        compiler_params=pltpu.CompilerParams(
            dimension_semantics=("arbitrary",) * 4, vmem_limit_bytes=VMEM_BYTES
        ),
        cost_estimate=pl.CostEstimate(
            flops=20 * weight.size,
            bytes_accessed=30 * weight.size,
            transcendentals=weight.size,
        ),
    )(count, rates, grads, weight, moments)


def dot(a, b):
    return jnp.dot(a, b, preferred_element_type=F32)


def dot_rows(a, b):
    return lax.dot_general(a, b, (((1,), (0,)), ((), ())), preferred_element_type=F32)


def dot_t(a, b):
    return lax.dot_general(a, b, (((1,), (1,)), ((), ())), preferred_element_type=F32)


def on_device(
    Y,
    S,
    block_in,
    cotangent,
    segment_ids,
    input_proj,
    output_proj,
    gate_up,
    down_weight,
    norm_gains,
    input_moments,
    output_moments,
    gate_moments,
    down_moments,
    gain_moments,
    update_count,
    optimizer_rates,
):
    seq_place = lax.axis_index("z")
    core = lax.axis_index("c")
    first_core = core == 0
    D = block_in.shape[-1]
    half_ff = FF // 2
    rows_d = input_proj.shape[0]
    rows_f = down_weight.shape[0]
    fast = Y == 2 and rows_d % 128 == 0
    in_half = input_proj.shape[1] // 2
    d_half = D // 2
    r = rows_d // 8

    gains_low = norm_gains.astype(BF)
    tokens = block_in[0].astype(F32)
    piece_len = tokens.shape[0]
    width_q = HEADS * HEAD
    positions = seq_place * piece_len + jnp.arange(piece_len, dtype=jnp.int32)
    reach_count = (WINDOW + piece_len - 2) // piece_len
    key_span = reach_count * piece_len
    segments = segment_ids[0]
    padded_ids = jnp.concatenate([jnp.full((key_span,), -1, jnp.int32), segments])
    query_ids = lax.dynamic_slice_in_dim(segments, seq_place * piece_len, piece_len)
    key_ids = lax.dynamic_slice_in_dim(padded_ids, seq_place * piece_len, key_span + piece_len)
    live_rows = query_ids != 0
    query_row = query_ids[None, :]
    key_column = key_ids[:, None]

    if fast:
        frequency = 10000.0 ** (-2.0 * jnp.arange(HEAD // 2).astype(F32) / HEAD)
        angles = positions.astype(F32)[:, None] * jnp.concatenate([frequency, frequency])[None, :]
        side = jnp.where(jnp.arange(HEAD) < HEAD // 2, -1.0, 1.0)
        cos_table, sin_table = jnp.cos(angles), jnp.sin(angles) * side
        (
            in_full,
            out_full,
            down_full,
            gate_full,
            gains_full,
            normed,
            queries,
            key_rows,
            values,
            flat_heads,
            log_totals,
            middle,
            normed_two,
            two_other,
            *transposed,
        ) = forward(
            [
                w.reshape(4, 2, w.shape[0] // 8, w.shape[1])
                for w in (input_proj, output_proj, down_weight, gate_up)
            ],
            jnp.concatenate([gains_low] * 8, axis=0),
            block_in[0],
            cos_table,
            sin_table,
            query_row,
            key_column,
            HEADS,
            S,
            0,
        )
        in_full = in_full.reshape(D, 2 * in_half)
        out_full = out_full.reshape(D, D)
        gains_small = gains_full
        gains_full = gains_full[:, :2].transpose(1, 0, 2).reshape(2, D)
        down_full = down_full.reshape(FF, D)
        gate_full = gate_full.reshape(D, 2 * half_ff)
        gains_wide = gains_full.astype(F32)
    else:
        gate_low = jnp.concatenate(
            [
                lax.dynamic_slice_in_dim(gate_up, side * FF + core * half_ff, half_ff, 1)
                for side in range(2)
            ],
            axis=1,
        )
        in_full, out_full, down_full, gate_full = (
            lax.all_gather(w.astype(BF), "z", axis=0, tiled=True)
            for w in (input_proj, output_proj, down_weight, gate_low)
        )
        gains_full = lax.all_gather(gains_low, "z", axis=1, tiled=True)
        gains_wide = gains_full.astype(F32)
        normed = root_norm(tokens, gains_wide[0]).astype(BF)
        mixed_proj = dot(normed, in_full)
        queries = (
            rotate(mixed_proj[:, :width_q].reshape(piece_len, HEADS, HEAD), positions, 1.0)
            .astype(BF)
            .reshape(piece_len, width_q)
        )
        own_keys = rotate(mixed_proj[:, width_q : width_q + HEAD], positions, 1.0)
        own_pair = jnp.concatenate([own_keys, mixed_proj[:, width_q + HEAD :]], axis=1).astype(BF)
        earlier = []
        for back_step in range(reach_count, 0, -1):
            earlier.append(passed_along(own_pair, "z", back_step))
        key_pairs = jnp.concatenate(earlier + [own_pair], axis=0)
        key_rows = key_pairs[:, :HEAD]
        values = key_pairs[:, HEAD:]
        flat_heads, log_totals = attend(
            query_row, key_column, queries, key_rows, values, HEADS, piece_len
        )
        middle = tokens + dot(flat_heads, out_full)
        normed_two = root_norm(middle, gains_wide[1]).astype(BF)
        two_other = swapped(normed_two, "c")

    upstream = cotangent[0].astype(F32)

    def ordered(mine, other):
        return jnp.concatenate(
            [jnp.where(first_core, mine, other), jnp.where(first_core, other, mine)], axis=0
        )

    def pair(v):
        return ordered(v, swapped(v, "c"))

    def half_pair(v):
        n = v.shape[1] // 2
        keep = lax.dynamic_slice_in_dim(v, core * n, n, 1)
        give = lax.dynamic_slice_in_dim(v, (1 - core) * n, n, 1)
        return ordered(keep, swapped(give, "c"))

    def core_sum(v):
        keep = lax.dynamic_slice_in_dim(v, core * piece_len, piece_len, 0)
        give = lax.dynamic_slice_in_dim(v, (1 - core) * piece_len, piece_len, 0)
        return keep.astype(F32) + swapped(give, "c").astype(F32)

    df_other = swapped(cotangent[0], "c")
    two_t, hid_t, grad_gated, two_sum = mlp_call(
        core.reshape(1).astype(jnp.int32),
        (normed_two, two_other),
        (cotangent[0], df_other),
        gate_full,
        down_full,
    )
    token_total = piece_len * S * Y * 4 * block_in.shape[0]
    step_value = update_count[0].astype(F32)
    rates = optimizer_rates

    if fast:
        sums, block_in_grad, block_out = backward(
            two_t,
            hid_t,
            transposed,
            grad_gated,
            (cotangent[0], df_other),
            two_sum,
            middle,
            out_full,
            gains_small,
            block_in[0],
            in_full,
            down_full,
            (query_row, key_column, queries, key_rows, values, flat_heads, log_totals),
            (cos_table, sin_table),
            HEADS,
            S,
            2,
        )
    else:
        down_mine = lax.dynamic_slice_in_dim(down_full, core * half_ff, half_ff, 0)
        block_out = (middle + core_sum(dot(hid_t.T, down_mine).astype(BF))).astype(BF)
        grad_normed_two = core_sum(two_sum)
        _, norm_pull_two = jax.vjp(root_norm, middle, gains_wide[1])
        grad_middle_norm, grad_gain_two = norm_pull_two(grad_normed_two)
        grad_middle = upstream + grad_middle_norm
        grad_branch = grad_middle.astype(BF)
        grad_flat = dot_t(grad_branch, out_full)
        grad_attended = jnp.where(live_rows[:, None], grad_flat, 0.0).astype(BF)
        grad_query_all, grad_keys, grad_values = attend_back(
            query_row,
            key_column,
            queries,
            key_rows,
            values,
            flat_heads,
            grad_attended,
            log_totals,
            HEADS,
            piece_len // 2,
        )
        grad_pairs = jnp.concatenate([grad_keys, grad_values], axis=1)
        own_grad = grad_pairs[key_span:]
        for back_step in range(1, reach_count + 1):
            sent_rows = grad_pairs[
                key_span - back_step * piece_len : key_span - (back_step - 1) * piece_len
            ]
            own_grad = own_grad + passed_along(sent_rows, "z", -back_step)
        grad_query_raw = rotate(
            grad_query_all.reshape(piece_len, HEADS, HEAD), positions, -1.0
        ).reshape(piece_len, width_q)
        grad_key_raw = rotate(own_grad[:, :HEAD], positions, -1.0)
        grad_mixed = jnp.concatenate(
            [grad_query_raw, grad_key_raw, own_grad[:, HEAD:]], axis=1
        ).astype(BF)
        grad_normed = dot_t(grad_mixed, in_full)
        _, norm_pull_one = jax.vjp(root_norm, tokens, gains_wide[0])
        grad_tokens_norm, grad_gain_one = norm_pull_one(grad_normed)
        block_in_grad = (grad_middle + grad_tokens_norm).astype(BF)

    if fast:

        def adam(weight, moments, *rest, **more):
            return adam_call(
                weight, moments, sums, update_count, rates, float(token_total), *rest, **more
            )

        tiles = half_ff // d_half
        same = (d_half,) * tiles
        gate_grad, gate_new, gate_mom, gain_two = adam(
            gate_up, gate_moments, 0, same, sides=2, gains=True, chips=2
        )
        down_grad, down_new, down_mom = adam(
            down_weight, down_moments, 2 * tiles, (d_half,), tiles=tiles
        )
        out_grad, out_new, out_mom = adam(output_proj, output_moments, 3 * tiles, (d_half,))
        in_grad, in_new, in_mom, gain_one = adam(
            input_proj, input_moments, 3 * tiles + 1, split_widths(in_half, d_half), gains=True
        )
        gain_grad = jnp.sum(jnp.stack([gain_one, gain_two]), axis=2) / gains_low.astype(F32)
    else:

        def adam(weight, moments, grad):
            grad = grad.astype(F32) / token_total
            change, new = adamw_step(weight, moments, grad, step_value, rates)
            return grad, weight - change, new

        def summed(left, right):
            whole = dot_rows(left.T, right).astype(BF)
            mine = lax.psum_scatter(whole, "z", scatter_dimension=0, tiled=True)
            return lax.psum(mine, ("y", "x"))

        two_both = ordered(normed_two, two_other)
        grad_half = half_pair(grad_branch)
        mixed_half = half_pair(grad_mixed)
        normed_both = pair(normed)
        flat_both = pair(flat_heads)
        df_both = pair(cotangent[0])
        gate_half = [summed(two_both, grad_gated[side]) for side in range(2)]
        gate_sum = jnp.concatenate(
            [lax.all_gather(g, "c", axis=1, tiled=True) for g in gate_half], axis=1
        )
        down_part = lax.psum(dot_rows(hid_t, df_both).astype(BF), ("y", "x"))
        down_part = lax.all_gather(down_part, "c", axis=0, tiled=True)
        down_sum = lax.psum_scatter(down_part, "z", scatter_dimension=0, tiled=True)
        out_total = lax.all_gather(summed(flat_both, grad_half), "c", axis=1, tiled=True)
        in_total = lax.all_gather(summed(normed_both, mixed_half), "c", axis=1, tiled=True)
        out_grad, out_new, out_mom = adam(output_proj, output_moments, out_total)
        in_grad, in_new, in_mom = adam(input_proj, input_moments, in_total)
        gate_grad, gate_new, gate_mom = adam(gate_up, gate_moments, gate_sum)
        down_grad, down_new, down_mom = adam(down_weight, down_moments, down_sum)
        gains_sum = lax.psum(jnp.stack([grad_gain_one, grad_gain_two]), ("y", "x", "c", "z"))
        gain_grad = lax.dynamic_slice_in_dim(gains_sum, seq_place * rows_d, rows_d, 1) / token_total
    gains_step, gain_moments_new = adamw_step(norm_gains, gain_moments, gain_grad, step_value, rates)
    return (
        block_out[None],
        block_in_grad[None],
        in_grad,
        out_grad,
        gate_grad,
        down_grad,
        gain_grad,
        in_new,
        out_new,
        gate_new,
        down_new,
        gains_step,
        in_mom,
        out_mom,
        gate_mom,
        down_mom,
        gain_moments_new,
    )


def solution(mesh):
    dp, S = mesh.shape["dp"], mesh.shape["seq"]
    Y = dp // 4
    grid = Mesh(mesh.devices.reshape(Y, 2, 2, S), ("y", "x", "c", "z"))
    data = ("y", "x", "c")
    tokens = P(data, "z", None)
    rows = P("z", None)
    moments = P(None, "z", None)
    in_specs = (
        (tokens, tokens, P(data, None))
        + (rows,) * 4
        + (P(None, "z"),)
        + (moments,) * 4
        + (P(None, None, "z"), P(), P())
    )
    out_specs = (
        (tokens, tokens)
        + (rows,) * 4
        + (P(None, "z"),)
        + (rows,) * 4
        + (P(None, "z"),)
        + (moments,) * 4
        + (P(None, None, "z"),)
    )

    def device_step(*arrays):
        return on_device(Y, S, *arrays)

    return jax.shard_map(
        device_step, mesh=grid, in_specs=in_specs, out_specs=out_specs, check_vma=False
    )
```
